32 devices in a mesh: dp: 8 (over y, x, core), mp: 4 (over z).
Axes of the slice: x: 2, y: 2, z: 4, core: 2. Of those that a mesh axis runs over, the one named last changes fastest.
Arguments:
- tokens: bfloat16 [16384, 768], P(('dp', 'mp')), may hold values from -6 to 6
- w_qkv: float32 [768, 2304], P('dp', 'mp'), may hold values from -0.21875 to 0.21875
- bias_query: float32 [768], P(('dp', 'mp')), may hold values from -3 to 3
- bias_value: float32 [768], P(('dp', 'mp')), may hold values from -3 to 3
- w_out: float32 [768, 768], P('dp', 'mp'), may hold values from -0.625 to 0.625
- bias_out: float32 [768], P(('dp', 'mp')), may hold values from -2 to 2
- gain_one: float32 [768], P(('dp', 'mp')), may hold values from 0.5 to 1.5
- shift_one: float32 [768], P(('dp', 'mp')), may hold values from -2 to 2
- w_up: float32 [768, 3072], P('dp', 'mp'), may hold values from -0.21875 to 0.21875
- bias_up: float32 [3072], P(('dp', 'mp')), may hold values from -3 to 3
- w_down: float32 [3072, 768], P('dp', 'mp'), may hold values from -0.109375 to 0.109375
- bias_down: float32 [768], P(('dp', 'mp')), may hold values from -2 to 2
- gain_two: float32 [768], P(('dp', 'mp')), may hold values from 0.5 to 1.5
- shift_two: float32 [768], P(('dp', 'mp')), may hold values from -2 to 2
- cluster_order: int32 [32, 12, 512], P(('dp', 'mp')), may hold values from 0 to 511, each once within a row
- segment_ids: int32 [32, 512], P(('dp', 'mp')), may hold values from 0 to 15, never falling along the last dimension, each value on 1 to 256 neighbouring positions
- padding: int32 [32, 512], P(('dp', 'mp')), may hold values 0 or 1
- cotangent: float32 [16384, 768], P(('dp', 'mp')), may hold values from -6 to 6
Outputs:
- layer_out: bfloat16 [16384, 768], P(('dp', 'mp'))
- grad_tokens: float32 [16384, 768], P(('dp', 'mp'))
- grad_w_qkv: float32 [768, 2304], P('dp', 'mp')
- grad_bias_query: float32 [768], P(('dp', 'mp'))
- grad_bias_value: float32 [768], P(('dp', 'mp'))
- grad_w_out: float32 [768, 768], P('dp', 'mp')
- grad_bias_out: float32 [768], P(('dp', 'mp'))
- grad_gain_one: float32 [768], P(('dp', 'mp'))
- grad_shift_one: float32 [768], P(('dp', 'mp'))
- grad_w_up: float32 [768, 3072], P('dp', 'mp')
- grad_bias_up: float32 [3072], P(('dp', 'mp'))
- grad_w_down: float32 [3072, 768], P('dp', 'mp')
- grad_bias_down: float32 [768], P(('dp', 'mp'))
- grad_gain_two: float32 [768], P(('dp', 'mp'))
- grad_shift_two: float32 [768], P(('dp', 'mp'))
The draws below stay inside these ranges and needn't reach their ends.
Inputs may be any that keep to these rules, and one draw needn't show every extreme that they name: Each row cluster_order[s, h, :] lists every position of its sequence exactly once. `segment_ids`: segment numbers never fall along a sequence; every document has 1 to 256 tokens and one has exactly 256.
All inputs are finite; a program needn't handle non-finite values. No bound on the sum of `padding` on one device may be relied on, other than what follows from the above.
Results may differ from the reference program's by a relative error of at most 0.018.
Values may be sent and summed in bfloat16 or wider, within the bound.
No kernel may reach another device: no remote copies, remote signals or barrier semaphores. Data moves between devices by JAX's collectives and lax.ppermute only.
A program may use at most 128 MiB of HBM per device.

```python
import math
import jax
import jax.numpy as jnp
import numpy as np
from jax import lax

D = 768
HEADS = 12
HEAD_DIM = 64
FF = 3072
CLUSTER = 128
TOK_DEV = 512
DOCS = 16
DOC_MAX = 256
SEQS = 32
TOKENS = 16384


def set_ends(values, rng, low, largest):
    extent = values.shape
    place = [jax.random.randint(jax.random.fold_in(rng, axis), (), 0, extent[axis]) for axis in range(len(extent))]
    values = values.at[tuple(place)].set(low)
    longest = extent.index(max(extent))
    place[longest] = (place[longest] + 1) % extent[longest]
    return values.at[tuple(place)].set(largest)


def with_spikes(array, stream_key, source, target, blocks, factor):
    def block_of(position):
        return (jnp.arange(array.shape[position]) // (array.shape[position] // blocks)).reshape((-1,) + (1,) * (array.ndim - 1 - position))

    first = jax.random.permutation(stream_key, blocks)[block_of(target)]
    far = (block_of(target) + blocks // 2) % blocks
    return jnp.where((block_of(source) == first) | (block_of(source) == far), factor * array, array)


def level_of(key, shape, cuts, least, high):
    loudness = 1.0
    for dim, blocks in cuts:
        heights = jax.random.uniform(jax.random.fold_in(jax.random.fold_in(key, 6), dim), (blocks,), jnp.float32, least / len(cuts), high / len(cuts))
        loudness = loudness * jnp.repeat(jnp.exp(heights), shape[dim] // blocks).reshape((-1,) + (1,) * (len(shape) - 1 - dim))
    return loudness


def length_profile(number_of, total, reach, skew):
    portions = [(1 << 20) // math.isqrt(grade ** skew) + 1 for grade in range(2, number_of + 1)]
    spare, given = total - reach - (number_of - 1), [1] * (number_of - 1)
    while spare > 0:
        free = [i for i in range(number_of - 1) if given[i] < reach]
        pool, left = sum([portions[i] for i in free]), spare
        for i in free:
            more = min(reach - given[i], max(1, left * portions[i] // pool), spare)
            given[i] = given[i] + more
            spare = spare - more
    return np.array([reach] + given)


def uneven_parts(rng, number_of, total, limit, lean):
    if number_of == 2:
        one = jax.random.randint(rng, (), max(1, total - limit), min(limit, total - 1) + 1)
        return jnp.stack([one, total - one])
    lengths = jnp.asarray(length_profile(number_of, total, limit, lean), jnp.int32)
    twos = (number_of - 1) // 2
    giver, sink = lengths[1:1 + 2 * twos:2], lengths[2:2 + 2 * twos:2]
    margin = jnp.minimum(giver - 1, limit - sink)
    passed = jax.random.randint(jax.random.fold_in(rng, 1), (twos,), 0, 1 << 20) % (margin + 1)
    lengths = lengths.at[1:1 + 2 * twos:2].set(giver - passed).at[2:2 + 2 * twos:2].set(sink + passed)
    return lengths[jax.random.permutation(jax.random.fold_in(rng, 2), number_of)]


def normal_values(own_key, shape, width, bound, cuts=(), kind=jnp.bfloat16):
    drawn = jax.random.normal(own_key, shape, jnp.float32) * width
    if len(cuts) > 0:
        drawn = level_of(own_key, shape, cuts, -0.22, 0.18) * drawn
    return jnp.clip(drawn, min=-bound, max=bound).astype(kind)


def gaussian_with(rng, extent, width, reach, shards, heavy, kind=jnp.bfloat16):
    entries = width * jax.random.normal(rng, extent, jnp.float32)
    if shards:
        entries = entries * level_of(rng, extent, shards, -0.22, 0.18)
    return jnp.clip(with_spikes(entries, jax.random.fold_in(rng, 3), *heavy), -reach, reach).astype(kind)


def setup_inputs(seed: int = 0) -> dict:
    key_list = jax.random.split(jax.random.key(seed), 19)
    return {
        "tokens": normal_values(key_list[0], (TOKENS, D), 1.0, 6.0, ((0, 32),)),
        "w_qkv": normal_values(key_list[1], (D, 3 * D), D ** -0.5, 0.21875, ((0, 8), (1, 4)), jnp.float32),
        "bias_query": normal_values(key_list[2], (D,), 0.5, 3.0, ((0, 32),), jnp.float32),
        "bias_value": normal_values(key_list[3], (D,), 0.5, 3.0, ((0, 32),), jnp.float32),
        "w_out": normal_values(key_list[4], (D, D), (D // 8) ** -0.5, 0.625, ((0, 8), (1, 4)), jnp.float32),
        "bias_out": normal_values(key_list[5], (D,), 0.3, 2.0, ((0, 32),), jnp.float32),
        "gain_one": jnp.clip(1.0 + 0.1 * jax.random.normal(key_list[6], (D,), jnp.float32), 0.5, 1.5),
        "shift_one": normal_values(key_list[7], (D,), 0.3, 2.0, ((0, 32),), jnp.float32),
        "w_up": normal_values(key_list[8], (D, FF), D ** -0.5, 0.21875, ((0, 8), (1, 4)), jnp.float32),
        "bias_up": normal_values(key_list[9], (FF,), 0.5, 3.0, ((0, 32),), jnp.float32),
        "w_down": normal_values(key_list[10], (FF, D), FF ** -0.5, 0.109375, ((0, 8), (1, 4)), jnp.float32),
        "bias_down": normal_values(key_list[11], (D,), 0.3, 2.0, ((0, 32),), jnp.float32),
        "gain_two": jnp.clip(1.0 + 0.1 * jax.random.normal(key_list[12], (D,), jnp.float32), 0.5, 1.5),
        "shift_two": normal_values(key_list[13], (D,), 0.3, 2.0, ((0, 32),), jnp.float32),
        "cluster_order": jax.vmap(lambda own: jax.random.permutation(own, TOK_DEV))(jax.random.split(key_list[14], SEQS * HEADS)).reshape((SEQS, HEADS, TOK_DEV)).astype(jnp.int32),
        "segment_ids": jax.vmap(lambda own: jnp.searchsorted(jnp.cumsum(uneven_parts(own, DOCS, TOK_DEV, DOC_MAX, 2)), jnp.arange(TOK_DEV), side="right"))(jax.random.split(key_list[15], SEQS)).reshape((SEQS, TOK_DEV)).astype(jnp.int32),
        "padding": set_ends((jax.random.randint(key_list[16], (SEQS, TOK_DEV), 0, 8) < 7).astype(jnp.int32), jax.random.fold_in(key_list[16], 1), 0, 1),
        "cotangent": gaussian_with(key_list[17], (TOKENS, D), 1.0, 6.0, ((0, 32),), (0, 1, 32, 2.75), jnp.float32),
    }


@jax.custom_vjp
def low(v):
    return lax.optimization_barrier(v.astype(jnp.bfloat16)).astype(jnp.float32)

@jax.custom_vjp
def low_back(v):
    return v

def low_keep(v):
    return (low(v), None)

def low_pass(kept, grad):
    return (grad,)

def back_keep(v):
    return (v, None)

def back_low(kept, grad):
    return (low(grad),)
low.defvjp(low_keep, low_pass)
low_back.defvjp(back_keep, back_low)
epsilon = 1e-12
masked_score = -1e+30

def matmul(left_side, right_side):
    return jnp.dot(left_side, right_side, precision=lax.Precision.HIGHEST, preferred_element_type=jnp.float32)

def layer_norm(hidden, norm_gain, norm_shift):
    average = lax.optimization_barrier(jnp.mean(hidden, axis=-1, keepdims=True))
    centred = hidden - average
    variance = lax.optimization_barrier(jnp.mean(centred * centred, axis=-1, keepdims=True))
    return centred * lax.rsqrt(variance + epsilon) * norm_gain + norm_shift

def attend(query, keys, values, ordering, segment, present):
    length = query.shape[0]
    groups = length // CLUSTER

    def to_clusters(matrix):
        per_head = matrix.reshape(length, HEADS, HEAD_DIM).transpose(1, 0, 2)
        return jnp.take_along_axis(per_head, ordering[:, :, None], axis=1).reshape(HEADS, groups, CLUSTER, HEAD_DIM)
    query_blocks = to_clusters(query)
    key_blocks = to_clusters(keys)
    value_blocks = to_clusters(values)
    segment_blocks = jnp.take(segment, ordering).reshape(HEADS, groups, CLUSTER)
    present_blocks = jnp.take(present, ordering).reshape(HEADS, groups, CLUSTER)
    same_doc = segment_blocks[..., :, None] == segment_blocks[..., None, :]
    itself = jnp.eye(CLUSTER, dtype=bool)
    allowed = same_doc & ((present_blocks[..., None, :] == 1) | itself)
    raw_scores = jnp.einsum('hncd,hnmd->hncm', query_blocks, key_blocks, precision=lax.Precision.HIGHEST) * HEAD_DIM ** (-0.5)
    raw_scores = low_back(raw_scores)
    masked = jnp.where(allowed, raw_scores, masked_score)
    highest = lax.optimization_barrier(jnp.max(masked, axis=-1, keepdims=True))
    exponent = jnp.exp(masked - highest)
    attention_weights = low(exponent / lax.optimization_barrier(jnp.sum(exponent, axis=-1, keepdims=True)))
    combined = jnp.einsum('hncm,hnmd->hncd', attention_weights, value_blocks, precision=lax.Precision.HIGHEST)
    combined = combined.reshape(HEADS, length, HEAD_DIM)
    heads_index = jnp.arange(HEADS)[:, None]
    restored = jnp.zeros_like(combined).at[heads_index, ordering].set(combined)
    return restored.transpose(1, 0, 2).reshape(length, HEADS * HEAD_DIM)

def layer_group(inputs, ordering, segment, present, params):
    w_qkv, bias_query, bias_value, w_out, bias_out, gain_one, shift_one, w_up, bias_up, w_down, bias_down, gain_two, shift_two = params
    model_width = HEADS * HEAD_DIM
    sequences = ordering.shape[0]
    projected = matmul(low(inputs), w_qkv)
    query = low(low_back(projected[:, :model_width] + bias_query))
    keys = low(low_back(projected[:, model_width:2 * model_width]))
    values = low(low_back(projected[:, 2 * model_width:] + bias_value))
    combined = jax.vmap(attend)(query.reshape(sequences, -1, model_width), keys.reshape(sequences, -1, model_width), values.reshape(sequences, -1, model_width), ordering, segment, present)
    combined = low(low_back(combined.reshape(-1, model_width)))
    attention = low_back(matmul(combined, w_out) + bias_out)
    first_norm = layer_norm(inputs + attention, gain_one, shift_one)
    hidden = low_back(matmul(low(first_norm), w_up) + bias_up)
    activated = low(jax.nn.gelu(hidden, approximate=False))
    feed_out = low_back(matmul(activated, w_down) + bias_down)
    return layer_norm(first_norm + feed_out, gain_two, shift_two)

def reference(tokens, w_qkv, bias_query, bias_value, w_out, bias_out, gain_one, shift_one, w_up, bias_up, w_down, bias_down, gain_two, shift_two, cluster_order, segment_ids, padding, cotangent):
    group_size = math.gcd(SEQS, max(1, 4096 // TOK_DEV))
    group_count = SEQS // group_size
    inputs = tokens.astype(jnp.float32).reshape(group_count, group_size * TOK_DEV, D)
    orderings = cluster_order.reshape(group_count, group_size, HEADS, TOK_DEV).astype(jnp.int32)
    segments = segment_ids.reshape(group_count, group_size, TOK_DEV).astype(jnp.int32)
    presents = padding.reshape(group_count, group_size, TOK_DEV).astype(jnp.int32)

    def forward(inputs_all, *parameters):
        rounded = tuple((low(parameter) for parameter in parameters))

        def group_step(pieces):
            return layer_group(pieces[0], pieces[1], pieces[2], pieces[3], rounded)
        checked = jax.checkpoint(group_step)

        def advance(state_carry, pieces):
            return (state_carry, checked(pieces))
        final_carry, result = lax.scan(advance, jnp.zeros((), jnp.float32), (inputs_all, orderings, segments, presents))
        return result.reshape(TOKENS, D)
    floats = (w_qkv, bias_query, bias_value, w_out, bias_out, gain_one, shift_one, w_up, bias_up, w_down, bias_down, gain_two, shift_two)
    layer_out, pullback = jax.vjp(forward, inputs, *floats)
    gradients = pullback(cotangent)
    grad_tokens = gradients[0].reshape(TOKENS, D)
    return (layer_out.astype(jnp.bfloat16), grad_tokens, gradients[1], gradients[2], gradients[3], gradients[4], gradients[5], gradients[6], gradients[7], gradients[8], gradients[9], gradients[10], gradients[11], gradients[12], gradients[13])
```

```python
import math

import jax
import jax.numpy as jnp
from jax import lax
from jax.experimental import pallas as pl
from jax.experimental.pallas import tpu as pltpu
from jax.sharding import PartitionSpec as P

HEADS = 12
HEAD_DIM = 64
CLUSTER = 128


epsilon = 1e-12
masked_score = -1e30


def product(left_side, right_side):
    return jnp.dot(left_side, right_side, preferred_element_type=jnp.float32)


def times_back(left_side, right_side):
    return lax.dot_general(
        left_side, right_side, (((1,), (1,)), ((), ())), preferred_element_type=jnp.float32
    )


def outer_sum(left_side, right_side):
    return lax.dot_general(
        left_side, right_side, (((0,), (0,)), ((), ())), preferred_element_type=jnp.float32
    )


def norm_forward(hidden, norm_gain, norm_shift):
    average = jnp.mean(hidden, axis=-1, keepdims=True)
    centred = hidden - average
    variance = jnp.mean(centred * centred, axis=-1, keepdims=True)
    inverse = lax.rsqrt(variance + epsilon)
    normal = centred * inverse
    return (normal * norm_gain + norm_shift, normal, inverse)


def norm_backward(upstream, normal, inverse, norm_gain):
    scaled = upstream * norm_gain
    return inverse * (
        scaled
        - jnp.mean(scaled, axis=-1, keepdims=True)
        - normal * jnp.mean(scaled * normal, axis=-1, keepdims=True)
    )


def gelu_exact(inputs):
    return jax.nn.gelu(inputs, approximate=False)


LANES = 128
QKV_ROWS = 96
UP_TILES = 6
DOWN_TILES = 3
PACK_Q = 4 * QKV_ROWS + QKV_ROWS // 2 + 16
PACK_OU = QKV_ROWS + QKV_ROWS // 2 + UP_TILES * QKV_ROWS
PACK_D = DOWN_TILES * 192
VECTOR_ROW = 4 * QKV_ROWS + QKV_ROWS // 2
UP_ROW = QKV_ROWS + QKV_ROWS // 2


def whole():
    return pl.BlockSpec(memory_space=pltpu.VMEM)


def scalars():
    return pl.BlockSpec(memory_space=pltpu.SMEM)


def call(body, out_shapes, operands, scratch=(), vmem=40, flops=0, nbytes=0, name=None):
    size = sum(x.size * x.dtype.itemsize for x in operands)
    size += sum(math.prod(s.shape) * s.dtype.itemsize for s in out_shapes)
    return pl.pallas_call(
        body,
        out_shape=out_shapes,
        in_specs=[scalars()] + [whole()] * (len(operands) - 1),
        out_specs=[whole()] * len(out_shapes),
        scratch_shapes=list(scratch),
        compiler_params=pltpu.CompilerParams(vmem_limit_bytes=vmem * 1024 * 1024),
        cost_estimate=pl.CostEstimate(
            flops=int(flops), bytes_accessed=int(nbytes or size), transcendentals=0
        ),
        name=name,
    )(*operands)


def shape_of(shape, dtype=jnp.bfloat16):
    return jax.ShapeDtypeStruct(shape, dtype)


def halves_beside(single):
    half = single.shape[0] // 2
    return jnp.concatenate([single[:half], single[half:]], axis=1)


def pack_body(me, w_qkv, w_out, w_up, w_down, *rest):
    vectors, bias_up, to_q, to_ou, to_d = rest[:8], rest[8], rest[9], rest[10], rest[11]
    odd = lax.rem(me[1], 2) == 1

    def columns(source, tiles, base, target):
        width = tiles * LANES
        low = source[...]

        @pl.when(odd)
        def _():
            for t in range(tiles):
                target[base + t * 96 : base + (t + 1) * 96, :] = low[
                    :, 64 + t * LANES : 64 + (t + 1) * LANES
                ].astype(jnp.bfloat16)
            target[base + tiles * 96 : base + tiles * 96 + 48, :] = halves_beside(
                low[:, :64]
            ).astype(jnp.bfloat16)

        @pl.when(jnp.logical_not(odd))
        def _():
            for t in range(tiles):
                target[base + t * 96 : base + (t + 1) * 96, :] = low[
                    :, t * LANES : (t + 1) * LANES
                ].astype(jnp.bfloat16)
            target[base + tiles * 96 : base + tiles * 96 + 48, :] = halves_beside(
                low[:, width : width + 64]
            ).astype(jnp.bfloat16)

    columns(w_qkv, 4, 0, to_q)
    columns(w_out, 1, 0, to_ou)
    for t in range(UP_TILES):
        to_ou[UP_ROW + t * 96 : UP_ROW + (t + 1) * 96, :] = w_up[
            :, t * LANES : (t + 1) * LANES
        ].astype(jnp.bfloat16)
    turned = w_down[...].T
    for t in range(DOWN_TILES):
        to_d[t * 192 : (t + 1) * 192, :] = turned[:, t * LANES : (t + 1) * LANES].astype(
            jnp.bfloat16
        )
    rows = lax.broadcasted_iota(jnp.int32, (16, LANES), 0)
    tail = jnp.zeros((16, LANES), jnp.float32)
    for v in range(8):
        wide = jnp.concatenate(
            [vectors[v][...], jnp.zeros((1, LANES - 24), jnp.float32)], axis=1
        )
        tail = jnp.where(rows == v, jnp.broadcast_to(wide, (16, LANES)), tail)
    wide = jnp.concatenate([bias_up[...], jnp.zeros((1, LANES - 96), jnp.float32)], axis=1)
    tail = jnp.where(rows == 8, jnp.broadcast_to(wide, (16, LANES)), tail)
    to_q[VECTOR_ROW:, :] = tail.astype(jnp.bfloat16)


def pack(me, w_qkv, w_out, w_up, w_down, vectors, bias_up):
    small = [v.reshape(1, -1) for v in vectors] + [bias_up.reshape(1, -1)]
    return call(
        pack_body,
        [shape_of((PACK_Q, LANES)), shape_of((PACK_OU, LANES)), shape_of((PACK_D, LANES))],
        [me, w_qkv, w_out, w_up, w_down, *small],
        name="pack",
    )


def swap(x, axis, bit):
    size = lax.axis_size(axis)
    return lax.ppermute(x, axis, [(i, i ^ bit) for i in range(size)])


CORE, ALONG_X, ALONG_Y = 1, 2, 4


def gather_z(x):
    return [x] + [swap(x, "mp", k) for k in (1, 2, 3)]


def gather_plane(parts):
    first, second = jnp.stack(parts[:2]), jnp.stack(parts[2:])
    first_x, second_y = swap(first, "dp", ALONG_X), swap(second, "dp", ALONG_Y)
    first, second = jnp.stack([first, first_x]), jnp.stack([second, second_y])
    return [first, swap(first, "dp", ALONG_Y), second, swap(second, "dp", ALONG_X)]


def gather_core(parts):
    return parts + [swap(x, "dp", CORE) for x in parts]


def gathered_blocks(me, refs):
    for index, ref in enumerate(refs):
        core, kind, far = index // 4, (index % 4) // 2, index % 2
        for mid in range(2):
            for low in range(2):
                if kind == 0:
                    kx, ky, kz = mid, far, low
                else:
                    kx, ky, kz = far, mid, 2 + low
                k = core + 2 * kx + 4 * ky
                yield me[0] ^ k, me[1] ^ kz, ref.at[mid, low]


def place_columns(block, base, tiles, dp, mp, width, weights, singles):
    start = pl.multiple_of(mp * width + 64 * lax.rem(mp, 2), LANES)
    rows = pl.ds(pl.multiple_of(dp * 96, 32), 96)
    for t in range(tiles):
        weights[rows, pl.ds(pl.multiple_of(start + t * LANES, LANES), LANES)] = block[
            base + t * 96 : base + (t + 1) * 96, :
        ]
    singles[mp, pl.ds(pl.multiple_of(dp * 48, 16), 48), :] = block[
        base + tiles * 96 : base + tiles * 96 + 48, :
    ]


def place_singles(width, weights, singles):
    for pair in range(2):
        column = 2 * pair * width + (width // LANES) * LANES
        for dp in range(8):
            left = singles[2 * pair, dp * 48 : (dp + 1) * 48, :].astype(jnp.float32)
            right = singles[2 * pair + 1, dp * 48 : (dp + 1) * 48, :].astype(jnp.float32)
            upper = jnp.concatenate([left[:, :64], right[:, :64]], axis=1)
            lower = jnp.concatenate([left[:, 64:], right[:, 64:]], axis=1)
            weights[dp * 96 : dp * 96 + 48, column : column + LANES] = upper.astype(jnp.bfloat16)
            weights[dp * 96 + 48 : (dp + 1) * 96, column : column + LANES] = lower.astype(
                jnp.bfloat16
            )


def unpack_q_body(me, *refs):
    blocks, weights, vectors, bias_up, singles, tails = refs[:8], *refs[8:]
    for dp, mp, block in gathered_blocks(me, blocks):
        place_columns(block, 0, 4, dp, mp, 576, weights, singles)
        tails[dp * 4 + mp] = block[VECTOR_ROW:, :].astype(jnp.float32)
    place_singles(576, weights, singles)
    lane = lax.broadcasted_iota(jnp.int32, (16, LANES), 1)

    def spread(width, count):
        found = [jnp.zeros((16, LANES), jnp.float32) for _ in range(count)]
        for device in range(32):
            start, tile = device * width % LANES, device * width // LANES
            piece = tails[device]
            moved = pltpu.roll(piece, start, axis=1) if start else piece
            found[tile] = jnp.where((lane >= start) & (lane < start + width), moved, found[tile])
            if start + width > LANES:
                found[tile + 1] = jnp.where(lane < start + width - LANES, moved, found[tile + 1])
        return found

    for t, value in enumerate(spread(24, 6)):
        vectors[:, t * LANES : (t + 1) * LANES] = value[:8]
    for t, value in enumerate(spread(96, 24)):
        bias_up[:, t * LANES : (t + 1) * LANES] = value[8:9]


def unpack_q(me, parts):
    return call(
        unpack_q_body,
        [shape_of((768, 2304)), shape_of((8, 768), jnp.float32), shape_of((1, 3072), jnp.float32)],
        [me, *parts],
        [pltpu.VMEM((4, 384, LANES), jnp.bfloat16), pltpu.VMEM((32, 16, LANES), jnp.float32)],
        name="unpack_q",
    )


def unpack_ou_body(me, *refs):
    blocks, w_out, w_up, singles = refs[:8], *refs[8:]
    for dp, mp, block in gathered_blocks(me, blocks):
        place_columns(block, 0, 1, dp, mp, 192, w_out, singles)
        rows = pl.ds(pl.multiple_of(dp * 96, 32), 96)
        for t in range(UP_TILES):
            w_up[rows, pl.ds(pl.multiple_of(mp * 768 + t * LANES, LANES), LANES)] = block[
                UP_ROW + t * 96 : UP_ROW + (t + 1) * 96, :
            ]
    place_singles(192, w_out, singles)


def unpack_ou(me, parts):
    return call(
        unpack_ou_body,
        [shape_of((768, 768)), shape_of((768, 3072))],
        [me, *parts],
        [pltpu.VMEM((4, 384, LANES), jnp.bfloat16)],
        name="unpack_ou",
    )


def unpack_d_body(me, *refs):
    blocks, turned = refs[:8], refs[8]
    for dp, mp, block in gathered_blocks(me, blocks):
        rows = pl.ds(pl.multiple_of(mp * 192, 64), 192)
        for t in range(DOWN_TILES):
            turned[rows, pl.ds(pl.multiple_of(dp * 384 + t * LANES, LANES), LANES)] = block[
                t * 192 : (t + 1) * 192, :
            ]


def unpack_d(me, parts):
    return call(unpack_d_body, [shape_of((768, 3072))], [me, *parts], name="unpack_d")[0]


def turned_rows(me, source, target):
    turned = source[...].T
    for dp in range(8):
        k = me[0] ^ dp
        slot = (1 - (k & 1)) * 4 + (k >> 1)
        target[pl.ds(pl.multiple_of(slot * 96, 32), 96), :] = turned[dp * 96 : (dp + 1) * 96, :]


def store_columns(me, target, kp, base, tiles, mp, width, first, value):
    kz = me[1] ^ mp
    start = mp * width + 64 * (mp % 2) - first
    for t in range(tiles):
        target[kp, kz, base + t * 96 : base + (t + 1) * 96, :] = value[
            :, start + t * LANES : start + (t + 1) * LANES
        ].astype(jnp.bfloat16)


def store_single(me, target, kp, base, mp, value):
    kz = me[1] ^ mp
    upper, lower = value[:48], value[48:]
    low_lanes = lax.broadcasted_iota(jnp.int32, (48, LANES), 1) < 64
    if mp % 2 == 0:
        both = jnp.where(low_lanes, upper, pltpu.roll(lower, 64, axis=1))
    else:
        both = jnp.where(low_lanes, pltpu.roll(upper, 64, axis=1), lower)
    target[kp, kz, base : base + 48, :] = both.astype(jnp.bfloat16)


def dot(a, b):
    return jnp.dot(a, b, preferred_element_type=jnp.float32)


def dot_nt(a, b):
    return lax.dot_general(a, b, (((1,), (1,)), ((), ())), preferred_element_type=jnp.float32)


def dot_tn(a, b):
    return lax.dot_general(a, b, (((0,), (0,)), ((), ())), preferred_element_type=jnp.float32)


def column_gradient(me, left, right, target, base, tiles, width):
    for pair in range(2):
        first = 2 * pair * width
        middle = first + tiles * LANES
        for begin, count, mp in ((first, tiles, 2 * pair), (middle + LANES, tiles, 2 * pair + 1)):
            value = dot(left, right[:, begin : begin + count * LANES])
            for kp in range(4):
                store_columns(
                    me, target, kp, base, tiles, mp, width, begin, value[kp * 96 : (kp + 1) * 96]
                )
        value = dot(left, right[:, middle : middle + LANES])
        for kp in range(4):
            for mp in (2 * pair, 2 * pair + 1):
                store_single(me, target, kp, base + tiles * 96, mp, value[kp * 96 : (kp + 1) * 96])


def gradient_q_body(me, tokens, projected_grad, vectors, grad_up, send, own, turned):
    turned_rows(me, tokens, turned)
    lane = lax.broadcasted_iota(jnp.int32, (16, LANES), 1)
    rows = lax.broadcasted_iota(jnp.int32, (16, LANES), 0)
    for half, target in ((0, send), (1, own)):
        left = turned[half * 384 : (half + 1) * 384, :]
        column_gradient(me, left, projected_grad, target, 0, 4, 576)

    def cut(source, count, width, device):
        start, tile = device * width % LANES, device * width // LANES
        value = source[:, tile * LANES : (tile + 1) * LANES]
        moved = pltpu.roll(value, LANES - start, axis=1) if start else value
        if start + width > LANES:
            after = source[:, (tile + 1) * LANES : (tile + 2) * LANES]
            after = pltpu.roll(after, LANES - start, axis=1)
            here = lax.broadcasted_iota(jnp.int32, value.shape, 1)
            moved = jnp.where(here < LANES - start, moved, after)
        return moved

    for device in range(32):
        dp, mp = device // 4, device % 4
        eight = cut(vectors, 8, 24, device)
        one = jnp.broadcast_to(cut(grad_up, 1, 96, device), (8, LANES))
        tail = jnp.concatenate([eight, one], axis=0)
        tail = jnp.where((rows < 8) & (lane >= 24), 0.0, tail).astype(jnp.bfloat16)
        k = me[0] ^ dp
        kz = me[1] ^ mp

        @pl.when((k & 1) == 0)
        def _():
            own[k >> 1, kz, VECTOR_ROW:, :] = tail

        @pl.when((k & 1) == 1)
        def _():
            send[k >> 1, kz, VECTOR_ROW:, :] = tail


def gradient_q(me, tokens, projected_grad, vectors, grad_up):
    return call(
        gradient_q_body,
        [shape_of((4, 4, PACK_Q, LANES))] * 2,
        [me, tokens, projected_grad, vectors, grad_up],
        [pltpu.VMEM((768, tokens.shape[0]), jnp.bfloat16)],
        flops=2 * 512 * 768 * 2304,
        name="gradient_q",
    )


def gradient_ou_body(
    me, combined, attention_grad, first_low, hidden_grad, send, own, turned, turned_too
):
    turned_rows(me, combined, turned)
    turned_rows(me, first_low, turned_too)
    for half, target in ((0, send), (1, own)):
        left = turned[half * 384 : (half + 1) * 384, :]
        column_gradient(me, left, attention_grad, target, 0, 1, 192)
        left = turned_too[half * 384 : (half + 1) * 384, :]
        for mp in range(4):
            value = dot(left, hidden_grad[:, mp * 768 : (mp + 1) * 768])
            kz = me[1] ^ mp
            for kp in range(4):
                for t in range(UP_TILES):
                    target[kp, kz, UP_ROW + t * 96 : UP_ROW + (t + 1) * 96, :] = value[
                        kp * 96 : (kp + 1) * 96, t * LANES : (t + 1) * LANES
                    ].astype(jnp.bfloat16)


def gradient_ou(me, combined, attention_grad, first_low, hidden_grad):
    return call(
        gradient_ou_body,
        [shape_of((4, 4, PACK_OU, LANES))] * 2,
        [me, combined, attention_grad, first_low, hidden_grad],
        [pltpu.VMEM((768, combined.shape[0]), jnp.bfloat16)] * 2,
        flops=2 * 512 * 768 * (3072 + 768),
        name="gradient_ou",
    )


def gradient_d_body(me, feed_grad, activated, send, own, turned):
    turned[...] = feed_grad[...].T
    for core, target in ((1, send), (0, own)):
        for kp in range(4):
            dp = me[0] ^ (2 * kp + core)
            block = activated[:, pl.ds(pl.multiple_of(dp * 384, LANES), 384)]
            value = dot(turned[...], block)
            for mp in range(4):
                kz = me[1] ^ mp
                for t in range(DOWN_TILES):
                    target[kp, kz, t * 192 : (t + 1) * 192, :] = value[
                        mp * 192 : (mp + 1) * 192, t * LANES : (t + 1) * LANES
                    ].astype(jnp.bfloat16)


def gradient_d(me, feed_grad, activated):
    return call(
        gradient_d_body,
        [shape_of((4, 4, PACK_D, LANES))] * 2,
        [me, feed_grad, activated],
        [pltpu.VMEM((768, feed_grad.shape[0]), jnp.bfloat16)],
        flops=2 * 512 * 768 * 3072,
        name="gradient_d",
    )


def add(a, b):
    return a.astype(jnp.float32) + b.astype(jnp.float32)


def add_core_body(me, own, other, first_keep, first_send, second_keep, second_send):
    for kp in range(4):
        ky, kx = kp // 2, kp % 2
        first, second = (first_send if ky else first_keep), (second_send if kx else second_keep)
        for low in range(2):
            first[kx, low] = add(own[kp, low], other[kp, low]).astype(jnp.bfloat16)
            second[ky, low] = add(own[kp, 2 + low], other[kp, 2 + low]).astype(jnp.bfloat16)


def add_plane_body(me, first, first_in, second, second_in, *outs):
    for keep, send, a, b in ((*outs[:2], first, first_in), (*outs[2:], second, second_in)):
        keep[...] = add(a[0], b[0]).astype(jnp.bfloat16)
        send[...] = add(a[1], b[1]).astype(jnp.bfloat16)


def add_last_body(me, first, first_in, second, second_in, *outs):
    for low in range(2):
        outs[low][...] = add(first[low], first_in[low]).astype(jnp.bfloat16)
        outs[2 + low][...] = add(second[low], second_in[low]).astype(jnp.bfloat16)


def scatter_core(me, send, own):
    other = swap(send, "dp", CORE)
    rows = own.shape[2]
    return call(
        add_core_body, [shape_of((2, 2, rows, LANES))] * 4, [me, own, other], name="add_core"
    )


def scatter_plane(me, parts):
    first, first_send, second, second_send = parts
    first_in, second_in = swap(first_send, "dp", ALONG_Y), swap(second_send, "dp", ALONG_X)
    rows = first.shape[2]
    first, first_send, second, second_send = call(
        add_plane_body,
        [shape_of((2, rows, LANES))] * 4,
        [me, first, first_in, second, second_in],
        name="add_plane",
    )
    first_in, second_in = swap(first_send, "dp", ALONG_X), swap(second_send, "dp", ALONG_Y)
    return call(
        add_last_body,
        [shape_of((rows, LANES))] * 4,
        [me, first, first_in, second, second_in],
        name="add_last",
    )


def scatter_z(parts):
    return [parts[0]] + [swap(parts[k], "mp", k) for k in (1, 2, 3)]


def total(refs, rows):
    value = refs[0][rows, :].astype(jnp.float32)
    for ref in refs[1:]:
        value = value + ref[rows, :].astype(jnp.float32)
    return value


def finish_columns(me, refs, base, tiles, out):
    odd = lax.rem(me[1], 2) == 1
    full = [total(refs, pl.ds(base + t * 96, 96)) for t in range(tiles)]
    single = total(refs, pl.ds(base + tiles * 96, 48))
    single = jnp.concatenate([single[:, :64], single[:, 64:]], axis=0)

    @pl.when(odd)
    def _():
        out[...] = jnp.concatenate([single, *full], axis=1)

    @pl.when(jnp.logical_not(odd))
    def _():
        out[...] = jnp.concatenate([*full, single], axis=1)


def finish_q_body(me, *refs):
    parts, out, outs = refs[:4], refs[4], refs[5:]
    finish_columns(me, parts, 0, 4, out)
    tail = total(parts, pl.ds(VECTOR_ROW, 16))
    for v in range(8):
        outs[v][...] = tail[v : v + 1, :24]
    outs[8][...] = tail[8:9, :96]


def finish_q(me, parts):
    f = jnp.float32
    return call(
        finish_q_body,
        [shape_of((96, 576), f)] + [shape_of((1, 24), f)] * 8 + [shape_of((1, 96), f)],
        [me, *parts],
        name="finish_q",
    )


def finish_ou_body(me, *refs):
    parts, w_out, w_up = refs[:4], refs[4], refs[5]
    finish_columns(me, parts, 0, 1, w_out)
    for t in range(UP_TILES):
        w_up[:, t * LANES : (t + 1) * LANES] = total(parts, pl.ds(UP_ROW + t * 96, 96))


def finish_ou(me, parts):
    f = jnp.float32
    return call(
        finish_ou_body, [shape_of((96, 192), f), shape_of((96, 768), f)], [me, *parts],
        name="finish_ou",
    )


def finish_d_body(me, *refs):
    parts, out = refs[:4], refs[4]
    for t in range(DOWN_TILES):
        out[t * LANES : (t + 1) * LANES, :] = total(parts, pl.ds(t * 192, 192)).T


def finish_d(me, parts):
    return call(finish_d_body, [shape_of((384, 192), jnp.float32)], [me, *parts], name="finish_d")[0]


def local_general(
    tokens,
    w_qkv,
    bias_query,
    bias_value,
    w_out,
    bias_out,
    gain_one,
    shift_one,
    w_up,
    bias_up,
    w_down,
    bias_down,
    gain_two,
    shift_two,
    cluster_order,
    segment_ids,
    padding,
    cotangent,
):
    model_width = HEADS * HEAD_DIM
    length = tokens.shape[0]
    groups = length // CLUSTER
    score_scale = HEAD_DIM ** (-0.5)
    vectors = jnp.stack(
        [bias_query, bias_value, bias_out, gain_one, shift_one, bias_down, gain_two, shift_two]
    ).astype(jnp.bfloat16)
    vector_up = bias_up.astype(jnp.bfloat16)[None, :]
    part_qkv = w_qkv.astype(jnp.bfloat16)
    part_out = w_out.astype(jnp.bfloat16)
    part_up = w_up.astype(jnp.bfloat16)
    part_down = w_down.astype(jnp.bfloat16)
    column_qkv, column_out, column_up, column_down, column_vectors, column_bias = (
        lax.all_gather(part_qkv, "mp", axis=1, tiled=True),
        lax.all_gather(part_out, "mp", axis=1, tiled=True),
        lax.all_gather(part_up, "mp", axis=1, tiled=True),
        lax.all_gather(part_down, "mp", axis=1, tiled=True),
        lax.all_gather(vectors, "mp", axis=1, tiled=True),
        lax.all_gather(vector_up, "mp", axis=1, tiled=True),
    )
    full_qkv, full_out, full_up, full_down, full_vectors, full_bias = (
        lax.all_gather(column_qkv, "dp", axis=0, tiled=True),
        lax.all_gather(column_out, "dp", axis=0, tiled=True),
        lax.all_gather(column_up, "dp", axis=0, tiled=True),
        lax.all_gather(column_down, "dp", axis=0, tiled=True),
        lax.all_gather(column_vectors, "dp", axis=1, tiled=True),
        lax.all_gather(column_bias, "dp", axis=1, tiled=True),
    )
    small_params = full_vectors.astype(jnp.float32)
    hidden_bias = full_bias[0].astype(jnp.float32)
    ordering = cluster_order[0]
    segment = segment_ids[0]
    present = padding[0]
    positions = jnp.arange(length, dtype=jnp.int32)
    placement = (ordering[:, :, None] == positions[None, None, :]).astype(jnp.bfloat16)

    def to_clusters(matrix):
        per_head = matrix.reshape(length, HEADS, HEAD_DIM)
        moved = jnp.einsum("hip,phd->hid", placement, per_head, preferred_element_type=jnp.float32)
        return moved.astype(jnp.bfloat16).reshape(HEADS, groups, CLUSTER, HEAD_DIM)

    def from_clusters(blocks):
        per_head = blocks.astype(jnp.bfloat16).reshape(HEADS, length, HEAD_DIM)
        moved = jnp.einsum("hip,hid->phd", placement, per_head, preferred_element_type=jnp.float32)
        return moved.astype(jnp.bfloat16).reshape(length, model_width)

    segment_blocks = jnp.take(segment, ordering).reshape(HEADS, groups, CLUSTER)
    present_blocks = jnp.take(present, ordering).reshape(HEADS, groups, CLUSTER)
    same_doc = segment_blocks[..., :, None] == segment_blocks[..., None, :]
    itself = jnp.eye(CLUSTER, dtype=bool)
    allowed = same_doc & ((present_blocks[..., None, :] == 1) | itself)

    def scores_of(query_blocks, key_blocks):
        raw_scores = (
            jnp.einsum(
                "hncd,hnmd->hncm", query_blocks, key_blocks, preferred_element_type=jnp.float32
            )
            * score_scale
        )
        return jnp.where(allowed, raw_scores, masked_score)

    projected = product(tokens, full_qkv)
    query = (projected[:, :model_width] + small_params[0]).astype(jnp.bfloat16)
    keys = projected[:, model_width : 2 * model_width].astype(jnp.bfloat16)
    values = (projected[:, 2 * model_width :] + small_params[1]).astype(jnp.bfloat16)
    query_blocks = to_clusters(query)
    key_blocks = to_clusters(keys)
    value_blocks = to_clusters(values)
    masked = scores_of(query_blocks, key_blocks)
    highest = jnp.max(masked, axis=-1, keepdims=True)
    exponent = jnp.exp(masked - highest)
    row_total = jnp.sum(exponent, axis=-1, keepdims=True)
    soft_weights = exponent / row_total
    log_total = highest + jnp.log(row_total)
    soft_low = soft_weights.astype(jnp.bfloat16)
    combined = from_clusters(
        jnp.einsum("hncm,hnmd->hncd", soft_low, value_blocks, preferred_element_type=jnp.float32)
    )
    attention = product(combined, full_out) + small_params[2]
    first_norm, first_normal, first_inverse = norm_forward(
        tokens.astype(jnp.float32) + attention, small_params[3], small_params[4]
    )
    first_low = first_norm.astype(jnp.bfloat16)
    hidden = product(first_low, full_up) + hidden_bias
    activated, gelu_pull = jax.vjp(gelu_exact, hidden)
    activated_low = activated.astype(jnp.bfloat16)
    feed_out = product(activated_low, full_down) + small_params[5]
    output, second_normal, second_inverse = norm_forward(
        first_norm + feed_out, small_params[6], small_params[7]
    )
    layer_out = output.astype(jnp.bfloat16)
    again_qkv, again_out, again_up, again_down = (
        lax.all_gather(part_qkv, "mp", axis=1, tiled=True),
        lax.all_gather(part_out, "mp", axis=1, tiled=True),
        lax.all_gather(part_up, "mp", axis=1, tiled=True),
        lax.all_gather(part_down, "mp", axis=1, tiled=True),
    )
    back_qkv, back_out, back_up, back_down = (
        lax.all_gather(again_qkv, "dp", axis=0, tiled=True),
        lax.all_gather(again_out, "dp", axis=0, tiled=True),
        lax.all_gather(again_up, "dp", axis=0, tiled=True),
        lax.all_gather(again_down, "dp", axis=0, tiled=True),
    )
    grad_gain_two = jnp.sum(cotangent * second_normal, axis=0)
    grad_shift_two = jnp.sum(cotangent, axis=0)
    second_grad = norm_backward(cotangent, second_normal, second_inverse, small_params[6])
    feed_grad = second_grad.astype(jnp.bfloat16)
    grad_bias_down = jnp.sum(feed_grad.astype(jnp.float32), axis=0)
    grad_w_down = outer_sum(activated_low, feed_grad)
    hidden_grad = gelu_pull(times_back(feed_grad, back_down))[0].astype(jnp.bfloat16)
    grad_bias_up = jnp.sum(hidden_grad.astype(jnp.float32), axis=0)
    grad_w_up = outer_sum(first_low, hidden_grad)
    first_grad = times_back(hidden_grad, back_up) + second_grad
    grad_gain_one = jnp.sum(first_grad * first_normal, axis=0)
    grad_shift_one = jnp.sum(first_grad, axis=0)
    residual_grad = norm_backward(first_grad, first_normal, first_inverse, small_params[3])
    attention_grad = residual_grad.astype(jnp.bfloat16)
    grad_bias_out = jnp.sum(attention_grad.astype(jnp.float32), axis=0)
    grad_w_out = outer_sum(combined, attention_grad)
    combined_grad = to_clusters(times_back(attention_grad, back_out).astype(jnp.bfloat16))
    masked_again = scores_of(query_blocks, key_blocks)
    soft_again = jnp.exp(masked_again - log_total)
    soft_again_low = soft_again.astype(jnp.bfloat16)
    value_sums = jnp.einsum(
        "hncm,hncd->hnmd", soft_again_low, combined_grad, preferred_element_type=jnp.float32
    )
    soft_grad = jnp.einsum(
        "hncd,hnmd->hncm", combined_grad, value_blocks, preferred_element_type=jnp.float32
    )
    score_grad = (
        soft_again * (soft_grad - jnp.sum(soft_grad * soft_again, axis=-1, keepdims=True))
    ).astype(jnp.bfloat16)
    query_sums = (
        jnp.einsum("hncm,hnmd->hncd", score_grad, key_blocks, preferred_element_type=jnp.float32)
        * score_scale
    )
    key_sums = (
        jnp.einsum("hncm,hncd->hnmd", score_grad, query_blocks, preferred_element_type=jnp.float32)
        * score_scale
    )
    query_grad = from_clusters(query_sums)
    key_grad = from_clusters(key_sums)
    value_grad = from_clusters(value_sums)
    grad_bias_query = jnp.sum(query_grad.astype(jnp.float32), axis=0)
    grad_bias_value = jnp.sum(value_grad.astype(jnp.float32), axis=0)
    projected_grad = jnp.concatenate([query_grad, key_grad, value_grad], axis=1)
    grad_w_qkv = outer_sum(tokens, projected_grad)
    grad_tokens = times_back(projected_grad, back_qkv) + residual_grad
    grad_vectors = jnp.stack(
        [
            grad_bias_query,
            grad_bias_value,
            grad_bias_out,
            grad_gain_one,
            grad_shift_one,
            grad_bias_down,
            grad_gain_two,
            grad_shift_two,
        ]
    )
    grad_up_row = grad_bias_up[None, :]
    row_qkv, row_out, row_up, row_down, row_vectors, row_bias = (
        lax.psum_scatter(
            grad_w_qkv.astype(jnp.bfloat16), "dp", scatter_dimension=0, tiled=True
        ).astype(jnp.float32),
        lax.psum_scatter(
            grad_w_out.astype(jnp.bfloat16), "dp", scatter_dimension=0, tiled=True
        ).astype(jnp.float32),
        lax.psum_scatter(
            grad_w_up.astype(jnp.bfloat16), "dp", scatter_dimension=0, tiled=True
        ).astype(jnp.float32),
        lax.psum_scatter(
            grad_w_down.astype(jnp.bfloat16), "dp", scatter_dimension=0, tiled=True
        ).astype(jnp.float32),
        lax.psum_scatter(
            grad_vectors.astype(jnp.bfloat16), "dp", scatter_dimension=1, tiled=True
        ).astype(jnp.float32),
        lax.psum_scatter(
            grad_up_row.astype(jnp.bfloat16), "dp", scatter_dimension=1, tiled=True
        ).astype(jnp.float32),
    )
    shard_qkv, shard_out, shard_up, shard_down, shard_vectors, shard_bias = (
        lax.psum_scatter(
            row_qkv.astype(jnp.bfloat16), "mp", scatter_dimension=1, tiled=True
        ).astype(jnp.float32),
        lax.psum_scatter(
            row_out.astype(jnp.bfloat16), "mp", scatter_dimension=1, tiled=True
        ).astype(jnp.float32),
        lax.psum_scatter(row_up.astype(jnp.bfloat16), "mp", scatter_dimension=1, tiled=True).astype(
            jnp.float32
        ),
        lax.psum_scatter(
            row_down.astype(jnp.bfloat16), "mp", scatter_dimension=1, tiled=True
        ).astype(jnp.float32),
        lax.psum_scatter(
            row_vectors.astype(jnp.bfloat16), "mp", scatter_dimension=1, tiled=True
        ).astype(jnp.float32),
        lax.psum_scatter(
            row_bias.astype(jnp.bfloat16), "mp", scatter_dimension=1, tiled=True
        ).astype(jnp.float32),
    )
    return (
        layer_out,
        grad_tokens,
        shard_qkv,
        shard_vectors[0],
        shard_vectors[1],
        shard_out,
        shard_vectors[2],
        shard_vectors[3],
        shard_vectors[4],
        shard_up,
        shard_bias[0],
        shard_down,
        shard_vectors[5],
        shard_vectors[6],
        shard_vectors[7],
    )


def local_block(
    tokens,
    w_qkv,
    bias_query,
    bias_value,
    w_out,
    bias_out,
    gain_one,
    shift_one,
    w_up,
    bias_up,
    w_down,
    bias_down,
    gain_two,
    shift_two,
    cluster_order,
    segment_ids,
    padding,
    cotangent,
):
    model_width = HEADS * HEAD_DIM
    length = tokens.shape[0]
    groups = length // CLUSTER
    score_scale = HEAD_DIM ** (-0.5)
    me = jnp.stack([lax.axis_index("dp"), lax.axis_index("mp")]).astype(jnp.int32)
    vector_list = [
        bias_query, bias_value, bias_out, gain_one, shift_one, bias_down, gain_two, shift_two
    ]
    packed_q, packed_ou, packed_d = pack(me, w_qkv, w_out, w_up, w_down, vector_list, bias_up)
    parts_q = gather_z(packed_q)
    parts_ou = gather_z(packed_ou)
    parts_d = gather_z(packed_d)
    parts_q = gather_core(gather_plane(parts_q))
    parts_ou = gather_core(gather_plane(parts_ou))
    parts_d = gather_core(gather_plane(parts_d))
    full_qkv, small_params, hidden_bias = unpack_q(me, parts_q)
    full_out, full_up = unpack_ou(me, parts_ou)
    turned_down = unpack_d(me, parts_d)
    ordering = cluster_order[0]
    segment = segment_ids[0]
    present = padding[0]
    positions = jnp.arange(length, dtype=jnp.int32)
    placement = (ordering[:, :, None] == positions[None, None, :]).astype(jnp.bfloat16)

    def to_clusters(matrix):
        per_head = matrix.reshape(length, HEADS, HEAD_DIM)
        moved = jnp.einsum("hip,phd->hid", placement, per_head, preferred_element_type=jnp.float32)
        return moved.astype(jnp.bfloat16).reshape(HEADS, groups, CLUSTER, HEAD_DIM)

    def from_clusters(blocks):
        per_head = blocks.astype(jnp.bfloat16).reshape(HEADS, length, HEAD_DIM)
        moved = jnp.einsum("hip,hid->phd", placement, per_head, preferred_element_type=jnp.float32)
        return moved.astype(jnp.bfloat16).reshape(length, model_width)

    facts = jnp.stack([segment, present]).astype(jnp.bfloat16)
    moved_facts = jnp.einsum("hip,fp->fhi", placement, facts, preferred_element_type=jnp.float32)
    segment_blocks = moved_facts[0].reshape(HEADS, groups, CLUSTER)
    present_blocks = moved_facts[1].reshape(HEADS, groups, CLUSTER)
    same_doc = segment_blocks[..., :, None] == segment_blocks[..., None, :]
    itself = jnp.eye(CLUSTER, dtype=bool)
    allowed = same_doc & ((present_blocks[..., None, :] == 1) | itself)

    def scores_of(query_blocks, key_blocks):
        raw_scores = (
            jnp.einsum(
                "hncd,hnmd->hncm", query_blocks, key_blocks, preferred_element_type=jnp.float32
            )
            * score_scale
        )
        return jnp.where(allowed, raw_scores, masked_score)

    projected = product(tokens, full_qkv)
    query = (projected[:, :model_width] + small_params[0]).astype(jnp.bfloat16)
    keys = projected[:, model_width : 2 * model_width].astype(jnp.bfloat16)
    values = (projected[:, 2 * model_width :] + small_params[1]).astype(jnp.bfloat16)
    query_blocks = to_clusters(query)
    key_blocks = to_clusters(keys)
    value_blocks = to_clusters(values)
    masked = scores_of(query_blocks, key_blocks)
    highest = jnp.max(masked, axis=-1, keepdims=True)
    exponent = jnp.exp(masked - highest)
    row_total = jnp.sum(exponent, axis=-1, keepdims=True)
    soft_weights = exponent / row_total
    log_total = highest + jnp.log(row_total)
    soft_low = soft_weights.astype(jnp.bfloat16)
    combined = from_clusters(
        jnp.einsum("hncm,hnmd->hncd", soft_low, value_blocks, preferred_element_type=jnp.float32)
    )
    attention = product(combined, full_out) + small_params[2]
    first_norm, first_normal, first_inverse = norm_forward(
        tokens.astype(jnp.float32) + attention, small_params[3], small_params[4]
    )
    first_low = first_norm.astype(jnp.bfloat16)
    hidden = product(first_low, full_up) + hidden_bias
    activated, gelu_pull = jax.vjp(gelu_exact, hidden)
    activated_low = activated.astype(jnp.bfloat16)
    feed_out = times_back(activated_low, turned_down) + small_params[5]
    output, second_normal, second_inverse = norm_forward(
        first_norm + feed_out, small_params[6], small_params[7]
    )
    layer_out = output.astype(jnp.bfloat16)
    grad_gain_two = jnp.sum(cotangent * second_normal, axis=0)
    grad_shift_two = jnp.sum(cotangent, axis=0)
    second_grad = norm_backward(cotangent, second_normal, second_inverse, small_params[6])
    feed_grad = second_grad.astype(jnp.bfloat16)
    grad_bias_down = jnp.sum(feed_grad.astype(jnp.float32), axis=0)
    sums_d = scatter_core(me, *gradient_d(me, feed_grad, activated_low))
    sums_d = scatter_z(scatter_plane(me, sums_d))
    hidden_grad = gelu_pull(product(feed_grad, turned_down))[0].astype(jnp.bfloat16)
    grad_bias_up = jnp.sum(hidden_grad.astype(jnp.float32), axis=0)
    first_grad = times_back(hidden_grad, full_up) + second_grad
    grad_gain_one = jnp.sum(first_grad * first_normal, axis=0)
    grad_shift_one = jnp.sum(first_grad, axis=0)
    residual_grad = norm_backward(first_grad, first_normal, first_inverse, small_params[3])
    attention_grad = residual_grad.astype(jnp.bfloat16)
    grad_bias_out = jnp.sum(attention_grad.astype(jnp.float32), axis=0)
    sums_ou = scatter_core(me, *gradient_ou(me, combined, attention_grad, first_low, hidden_grad))
    sums_ou = scatter_z(scatter_plane(me, sums_ou))
    combined_grad = to_clusters(times_back(attention_grad, full_out).astype(jnp.bfloat16))
    masked_again = scores_of(query_blocks, key_blocks)
    soft_again = jnp.exp(masked_again - log_total)
    soft_again_low = soft_again.astype(jnp.bfloat16)
    value_sums = jnp.einsum(
        "hncm,hncd->hnmd", soft_again_low, combined_grad, preferred_element_type=jnp.float32
    )
    soft_grad = jnp.einsum(
        "hncd,hnmd->hncm", combined_grad, value_blocks, preferred_element_type=jnp.float32
    )
    score_grad = (
        soft_again * (soft_grad - jnp.sum(soft_grad * soft_again, axis=-1, keepdims=True))
    ).astype(jnp.bfloat16)
    query_sums = (
        jnp.einsum("hncm,hnmd->hncd", score_grad, key_blocks, preferred_element_type=jnp.float32)
        * score_scale
    )
    key_sums = (
        jnp.einsum("hncm,hncd->hnmd", score_grad, query_blocks, preferred_element_type=jnp.float32)
        * score_scale
    )
    query_grad = from_clusters(query_sums)
    key_grad = from_clusters(key_sums)
    value_grad = from_clusters(value_sums)
    grad_bias_query = jnp.sum(query_grad.astype(jnp.float32), axis=0)
    grad_bias_value = jnp.sum(value_grad.astype(jnp.float32), axis=0)
    projected_grad = jnp.concatenate([query_grad, key_grad, value_grad], axis=1)
    grad_tokens = times_back(projected_grad, full_qkv) + residual_grad
    grad_vectors = jnp.stack(
        [
            grad_bias_query,
            grad_bias_value,
            grad_bias_out,
            grad_gain_one,
            grad_shift_one,
            grad_bias_down,
            grad_gain_two,
            grad_shift_two,
        ]
    )
    grad_up_row = grad_bias_up[None, :]
    sums_q = scatter_core(me, *gradient_q(me, tokens, projected_grad, grad_vectors, grad_up_row))
    sums_q = scatter_z(scatter_plane(me, sums_q))
    shard_down = finish_d(me, sums_d)
    shard_out, shard_up = finish_ou(me, sums_ou)
    shard_qkv, *shard_vectors = finish_q(me, sums_q)
    shard_vectors = [v.reshape(-1) for v in shard_vectors]
    shard_bias = shard_vectors[8:]
    return (
        layer_out,
        grad_tokens,
        shard_qkv,
        shard_vectors[0],
        shard_vectors[1],
        shard_out,
        shard_vectors[2],
        shard_vectors[3],
        shard_vectors[4],
        shard_up,
        shard_bias[0],
        shard_down,
        shard_vectors[5],
        shard_vectors[6],
        shard_vectors[7],
    )


def solution(mesh):
    in_specs = (
        P(("dp", "mp"), None),
        P("dp", "mp"),
        P(("dp", "mp")),
        P(("dp", "mp")),
        P("dp", "mp"),
        P(("dp", "mp")),
        P(("dp", "mp")),
        P(("dp", "mp")),
        P("dp", "mp"),
        P(("dp", "mp")),
        P("dp", "mp"),
        P(("dp", "mp")),
        P(("dp", "mp")),
        P(("dp", "mp")),
        P(("dp", "mp"), None, None),
        P(("dp", "mp"), None),
        P(("dp", "mp"), None),
        P(("dp", "mp"), None),
    )
    out_specs = (
        P(("dp", "mp"), None),
        P(("dp", "mp"), None),
        P("dp", "mp"),
        P(("dp", "mp")),
        P(("dp", "mp")),
        P("dp", "mp"),
        P(("dp", "mp")),
        P(("dp", "mp")),
        P(("dp", "mp")),
        P("dp", "mp"),
        P(("dp", "mp")),
        P("dp", "mp"),
        P(("dp", "mp")),
        P(("dp", "mp")),
        P(("dp", "mp")),
    )
    blocks = mesh.shape["dp"] == 8 and mesh.shape["mp"] == 4
    local = local_block if blocks else local_general
    return jax.shard_map(local, mesh=mesh, in_specs=in_specs, out_specs=out_specs, check_vma=False)
```

```python
import functools
import math

import jax
import jax.numpy as jnp
from jax import lax
from jax.experimental import pallas as pl
from jax.experimental.pallas import tpu as pltpu
from jax.sharding import PartitionSpec as P

HEADS = 12
HEAD_DIM = 64
CLUSTER = 128


epsilon = 1e-12
masked_score = -1e30


def product(left_side, right_side):
    return jnp.dot(left_side, right_side, preferred_element_type=jnp.float32)


def times_back(left_side, right_side):
    return lax.dot_general(
        left_side, right_side, (((1,), (1,)), ((), ())), preferred_element_type=jnp.float32
    )


def outer_sum(left_side, right_side):
    return lax.dot_general(
        left_side, right_side, (((0,), (0,)), ((), ())), preferred_element_type=jnp.float32
    )


def norm_forward(hidden, norm_gain, norm_shift):
    average = jnp.mean(hidden, axis=-1, keepdims=True)
    centred = hidden - average
    variance = jnp.mean(centred * centred, axis=-1, keepdims=True)
    inverse = lax.rsqrt(variance + epsilon)
    normal = centred * inverse
    return (normal * norm_gain + norm_shift, normal, inverse)


def norm_backward(upstream, normal, inverse, norm_gain):
    scaled = upstream * norm_gain
    return inverse * (
        scaled
        - jnp.mean(scaled, axis=-1, keepdims=True)
        - normal * jnp.mean(scaled * normal, axis=-1, keepdims=True)
    )


def gelu_exact(inputs):
    return jax.nn.gelu(inputs, approximate=False)


def local_general(
    tokens,
    w_qkv,
    bias_query,
    bias_value,
    w_out,
    bias_out,
    gain_one,
    shift_one,
    w_up,
    bias_up,
    w_down,
    bias_down,
    gain_two,
    shift_two,
    cluster_order,
    segment_ids,
    padding,
    cotangent,
):
    model_width = HEADS * HEAD_DIM
    length = tokens.shape[0]
    groups = length // CLUSTER
    score_scale = HEAD_DIM ** (-0.5)
    vectors = jnp.stack(
        [bias_query, bias_value, bias_out, gain_one, shift_one, bias_down, gain_two, shift_two]
    ).astype(jnp.bfloat16)
    vector_up = bias_up.astype(jnp.bfloat16)[None, :]
    part_qkv = w_qkv.astype(jnp.bfloat16)
    part_out = w_out.astype(jnp.bfloat16)
    part_up = w_up.astype(jnp.bfloat16)
    part_down = w_down.astype(jnp.bfloat16)
    column_qkv, column_out, column_up, column_down, column_vectors, column_bias = (
        lax.all_gather(part_qkv, "mp", axis=1, tiled=True),
        lax.all_gather(part_out, "mp", axis=1, tiled=True),
        lax.all_gather(part_up, "mp", axis=1, tiled=True),
        lax.all_gather(part_down, "mp", axis=1, tiled=True),
        lax.all_gather(vectors, "mp", axis=1, tiled=True),
        lax.all_gather(vector_up, "mp", axis=1, tiled=True),
    )
    full_qkv, full_out, full_up, full_down, full_vectors, full_bias = (
        lax.all_gather(column_qkv, "dp", axis=0, tiled=True),
        lax.all_gather(column_out, "dp", axis=0, tiled=True),
        lax.all_gather(column_up, "dp", axis=0, tiled=True),
        lax.all_gather(column_down, "dp", axis=0, tiled=True),
        lax.all_gather(column_vectors, "dp", axis=1, tiled=True),
        lax.all_gather(column_bias, "dp", axis=1, tiled=True),
    )
    small_params = full_vectors.astype(jnp.float32)
    hidden_bias = full_bias[0].astype(jnp.float32)
    ordering = cluster_order[0]
    segment = segment_ids[0]
    present = padding[0]
    positions = jnp.arange(length, dtype=jnp.int32)
    placement = (ordering[:, :, None] == positions[None, None, :]).astype(jnp.bfloat16)

    def to_clusters(matrix):
        per_head = matrix.reshape(length, HEADS, HEAD_DIM)
        moved = jnp.einsum("hip,phd->hid", placement, per_head, preferred_element_type=jnp.float32)
        return moved.astype(jnp.bfloat16).reshape(HEADS, groups, CLUSTER, HEAD_DIM)

    def from_clusters(blocks):
        per_head = blocks.astype(jnp.bfloat16).reshape(HEADS, length, HEAD_DIM)
        moved = jnp.einsum("hip,hid->phd", placement, per_head, preferred_element_type=jnp.float32)
        return moved.astype(jnp.bfloat16).reshape(length, model_width)

    segment_blocks = jnp.take(segment, ordering).reshape(HEADS, groups, CLUSTER)
    present_blocks = jnp.take(present, ordering).reshape(HEADS, groups, CLUSTER)
    same_doc = segment_blocks[..., :, None] == segment_blocks[..., None, :]
    itself = jnp.eye(CLUSTER, dtype=bool)
    allowed = same_doc & ((present_blocks[..., None, :] == 1) | itself)

    def scores_of(query_blocks, key_blocks):
        raw_scores = (
            jnp.einsum(
                "hncd,hnmd->hncm", query_blocks, key_blocks, preferred_element_type=jnp.float32
            )
            * score_scale
        )
        return jnp.where(allowed, raw_scores, masked_score)

    projected = product(tokens, full_qkv)
    query = (projected[:, :model_width] + small_params[0]).astype(jnp.bfloat16)
    keys = projected[:, model_width : 2 * model_width].astype(jnp.bfloat16)
    values = (projected[:, 2 * model_width :] + small_params[1]).astype(jnp.bfloat16)
    query_blocks = to_clusters(query)
    key_blocks = to_clusters(keys)
    value_blocks = to_clusters(values)
    masked = scores_of(query_blocks, key_blocks)
    highest = jnp.max(masked, axis=-1, keepdims=True)
    exponent = jnp.exp(masked - highest)
    row_total = jnp.sum(exponent, axis=-1, keepdims=True)
    soft_weights = exponent / row_total
    log_total = highest + jnp.log(row_total)
    soft_low = soft_weights.astype(jnp.bfloat16)
    combined = from_clusters(
        jnp.einsum("hncm,hnmd->hncd", soft_low, value_blocks, preferred_element_type=jnp.float32)
    )
    attention = product(combined, full_out) + small_params[2]
    first_norm, first_normal, first_inverse = norm_forward(
        tokens.astype(jnp.float32) + attention, small_params[3], small_params[4]
    )
    first_low = first_norm.astype(jnp.bfloat16)
    hidden = product(first_low, full_up) + hidden_bias
    activated, gelu_pull = jax.vjp(gelu_exact, hidden)
    activated_low = activated.astype(jnp.bfloat16)
    feed_out = product(activated_low, full_down) + small_params[5]
    output, second_normal, second_inverse = norm_forward(
        first_norm + feed_out, small_params[6], small_params[7]
    )
    layer_out = output.astype(jnp.bfloat16)
    again_qkv, again_out, again_up, again_down = (
        lax.all_gather(part_qkv, "mp", axis=1, tiled=True),
        lax.all_gather(part_out, "mp", axis=1, tiled=True),
        lax.all_gather(part_up, "mp", axis=1, tiled=True),
        lax.all_gather(part_down, "mp", axis=1, tiled=True),
    )
    back_qkv, back_out, back_up, back_down = (
        lax.all_gather(again_qkv, "dp", axis=0, tiled=True),
        lax.all_gather(again_out, "dp", axis=0, tiled=True),
        lax.all_gather(again_up, "dp", axis=0, tiled=True),
        lax.all_gather(again_down, "dp", axis=0, tiled=True),
    )
    grad_gain_two = jnp.sum(cotangent * second_normal, axis=0)
    grad_shift_two = jnp.sum(cotangent, axis=0)
    second_grad = norm_backward(cotangent, second_normal, second_inverse, small_params[6])
    feed_grad = second_grad.astype(jnp.bfloat16)
    grad_bias_down = jnp.sum(feed_grad.astype(jnp.float32), axis=0)
    grad_w_down = outer_sum(activated_low, feed_grad)
    hidden_grad = gelu_pull(times_back(feed_grad, back_down))[0].astype(jnp.bfloat16)
    grad_bias_up = jnp.sum(hidden_grad.astype(jnp.float32), axis=0)
    grad_w_up = outer_sum(first_low, hidden_grad)
    first_grad = times_back(hidden_grad, back_up) + second_grad
    grad_gain_one = jnp.sum(first_grad * first_normal, axis=0)
    grad_shift_one = jnp.sum(first_grad, axis=0)
    residual_grad = norm_backward(first_grad, first_normal, first_inverse, small_params[3])
    attention_grad = residual_grad.astype(jnp.bfloat16)
    grad_bias_out = jnp.sum(attention_grad.astype(jnp.float32), axis=0)
    grad_w_out = outer_sum(combined, attention_grad)
    combined_grad = to_clusters(times_back(attention_grad, back_out).astype(jnp.bfloat16))
    masked_again = scores_of(query_blocks, key_blocks)
    soft_again = jnp.exp(masked_again - log_total)
    soft_again_low = soft_again.astype(jnp.bfloat16)
    value_sums = jnp.einsum(
        "hncm,hncd->hnmd", soft_again_low, combined_grad, preferred_element_type=jnp.float32
    )
    soft_grad = jnp.einsum(
        "hncd,hnmd->hncm", combined_grad, value_blocks, preferred_element_type=jnp.float32
    )
    score_grad = (
        soft_again * (soft_grad - jnp.sum(soft_grad * soft_again, axis=-1, keepdims=True))
    ).astype(jnp.bfloat16)
    query_sums = (
        jnp.einsum("hncm,hnmd->hncd", score_grad, key_blocks, preferred_element_type=jnp.float32)
        * score_scale
    )
    key_sums = (
        jnp.einsum("hncm,hncd->hnmd", score_grad, query_blocks, preferred_element_type=jnp.float32)
        * score_scale
    )
    query_grad = from_clusters(query_sums)
    key_grad = from_clusters(key_sums)
    value_grad = from_clusters(value_sums)
    grad_bias_query = jnp.sum(query_grad.astype(jnp.float32), axis=0)
    grad_bias_value = jnp.sum(value_grad.astype(jnp.float32), axis=0)
    projected_grad = jnp.concatenate([query_grad, key_grad, value_grad], axis=1)
    grad_w_qkv = outer_sum(tokens, projected_grad)
    grad_tokens = times_back(projected_grad, back_qkv) + residual_grad
    grad_vectors = jnp.stack(
        [
            grad_bias_query,
            grad_bias_value,
            grad_bias_out,
            grad_gain_one,
            grad_shift_one,
            grad_bias_down,
            grad_gain_two,
            grad_shift_two,
        ]
    )
    grad_up_row = grad_bias_up[None, :]
    row_qkv, row_out, row_up, row_down, row_vectors, row_bias = (
        lax.psum_scatter(
            grad_w_qkv.astype(jnp.bfloat16), "dp", scatter_dimension=0, tiled=True
        ).astype(jnp.float32),
        lax.psum_scatter(
            grad_w_out.astype(jnp.bfloat16), "dp", scatter_dimension=0, tiled=True
        ).astype(jnp.float32),
        lax.psum_scatter(
            grad_w_up.astype(jnp.bfloat16), "dp", scatter_dimension=0, tiled=True
        ).astype(jnp.float32),
        lax.psum_scatter(
            grad_w_down.astype(jnp.bfloat16), "dp", scatter_dimension=0, tiled=True
        ).astype(jnp.float32),
        lax.psum_scatter(
            grad_vectors.astype(jnp.bfloat16), "dp", scatter_dimension=1, tiled=True
        ).astype(jnp.float32),
        lax.psum_scatter(
            grad_up_row.astype(jnp.bfloat16), "dp", scatter_dimension=1, tiled=True
        ).astype(jnp.float32),
    )
    shard_qkv, shard_out, shard_up, shard_down, shard_vectors, shard_bias = (
        lax.psum_scatter(
            row_qkv.astype(jnp.bfloat16), "mp", scatter_dimension=1, tiled=True
        ).astype(jnp.float32),
        lax.psum_scatter(
            row_out.astype(jnp.bfloat16), "mp", scatter_dimension=1, tiled=True
        ).astype(jnp.float32),
        lax.psum_scatter(row_up.astype(jnp.bfloat16), "mp", scatter_dimension=1, tiled=True).astype(
            jnp.float32
        ),
        lax.psum_scatter(
            row_down.astype(jnp.bfloat16), "mp", scatter_dimension=1, tiled=True
        ).astype(jnp.float32),
        lax.psum_scatter(
            row_vectors.astype(jnp.bfloat16), "mp", scatter_dimension=1, tiled=True
        ).astype(jnp.float32),
        lax.psum_scatter(
            row_bias.astype(jnp.bfloat16), "mp", scatter_dimension=1, tiled=True
        ).astype(jnp.float32),
    )
    return (
        layer_out,
        grad_tokens,
        shard_qkv,
        shard_vectors[0],
        shard_vectors[1],
        shard_out,
        shard_vectors[2],
        shard_vectors[3],
        shard_vectors[4],
        shard_up,
        shard_bias[0],
        shard_down,
        shard_vectors[5],
        shard_vectors[6],
        shard_vectors[7],
    )


LANES = 128
QKV_ROWS = 96
UP_TILES = 6
DOWN_TILES = 3
PACK_Q = 4 * QKV_ROWS + QKV_ROWS // 2 + 16
PACK_OU = QKV_ROWS + QKV_ROWS // 2 + UP_TILES * QKV_ROWS
PACK_D = DOWN_TILES * 192
VECTOR_ROW = 4 * QKV_ROWS + QKV_ROWS // 2
UP_ROW = QKV_ROWS + QKV_ROWS // 2


def whole():
    return pl.BlockSpec(memory_space=pltpu.VMEM)


def far():
    return pl.BlockSpec(memory_space=pltpu.HBM)


def kept_far(arrays):
    return [pltpu.with_memory_space_constraint(x, pltpu.HBM) for x in arrays]


def waited(after):
    return [kept_far([x.token])[0] if isinstance(x, Results) else x for x in after]


def anywhere(after):
    return [far() if isinstance(x, Results) else pl.BlockSpec(memory_space=pl.ANY) for x in after]


class Results(list):
    token = None


TOKEN = pltpu.HBM((8, 128), jnp.float32)


def place():
    return lax.axis_index("dp"), lax.axis_index("mp")


SHORT = pl.CostEstimate(flops=1, bytes_accessed=1, transcendentals=0)


class Place(tuple):
    def arrived(self, index):
        copy, here = self.late[index]
        if copy is not None:
            copy.wait()
            self.late[index] = (None, here)
        return here

    def send(self, index, where=None, source=None):
        here, there = self.far[index]
        source = here if source is None else source
        if where is not None:
            source, there = source.at[where], there.at[where]
        copy = pltpu.make_async_copy(source, there, self.sems.at[len(self.sent)])
        copy.start()
        self.sent.append(copy)


def call(
    body, out_shapes, operands, scratch=(), staged=0, late=0, far_outs=None, sends=None, after=(),
    aliases=None, vmem=14, name=None,
):
    operands = operands[1:]
    far_outs = far_outs or {}
    sends = len(far_outs) if sends is None else sends
    count, outs, copied = len(operands), len(out_shapes), staged + late

    def with_copies(*refs):
        sources, rest = refs[:copied], refs[copied:count]
        results = list(refs[count + len(after) : count + len(after) + outs])
        own = refs[count + len(after) + outs + 1 :]
        mine, own = own[: len(scratch)], own[len(scratch) :]
        arrived, own = own[:copied], list(own[copied:])
        me = Place(place())
        me.sent, me.far = [], {}
        if copied:
            sem = own.pop(0)
            copies = [
                pltpu.make_async_copy(source, here, sem.at[i])
                for i, (source, here) in enumerate(zip(sources, arrived))
            ]
            for copy in copies:
                copy.start()
            for copy in copies[:staged]:
                copy.wait()
            me.late = list(zip(copies[staged:], arrived[staged:]))
        if far_outs:
            me.sems = own.pop(0)
            for index, has_room in far_outs.items():
                here = own.pop(0) if has_room else None
                me.far[index] = (here, results[index])
                results[index] = here
        body(me, *arrived[:staged], *rest, *results, *mine)
        for copy in me.sent:
            copy.wait()

    room = [pltpu.VMEM(x.shape, x.dtype) for x in operands[:copied]]
    if copied:
        room.append(pltpu.SemaphoreType.DMA((copied,)))
    if far_outs:
        room.append(pltpu.SemaphoreType.DMA((sends,)))
        room += [pltpu.VMEM(out_shapes[i].shape, out_shapes[i].dtype) for i in far_outs if far_outs[i]]
    given = [
        pltpu.HBM(x.shape, x.dtype) if i in far_outs else x for i, x in enumerate(out_shapes)
    ]
    *results, token = pl.pallas_call(
        with_copies,
        out_shape=[*given, TOKEN],
        in_specs=[pl.BlockSpec(memory_space=pl.ANY)] * staged
        + [far()] * late
        + [whole()] * (count - copied)
        + anywhere(after),
        out_specs=[far() if i in far_outs else whole() for i in range(outs)] + [far()],
        scratch_shapes=list(scratch) + room,
        input_output_aliases=aliases or {},
        compiler_params=pltpu.CompilerParams(vmem_limit_bytes=vmem * 1024 * 1024),
        cost_estimate=SHORT,
        name=name,
    )(
        *operands[:staged],
        *kept_far(operands[staged:copied]),
        *operands[copied:],
        *waited(after),
    )
    results = Results(results)
    results.token = token
    return results


def tie(arrays, after):
    count = len(arrays)

    def body(*refs):
        pass

    return pl.pallas_call(
        body,
        out_shape=[shape_of(x.shape, x.dtype) for x in arrays],
        in_specs=[pl.BlockSpec(memory_space=pl.ANY)] * count + anywhere(after),
        out_specs=[pl.BlockSpec(memory_space=pl.ANY)] * count,
        input_output_aliases={i: i for i in range(count)},
        compiler_params=pltpu.CompilerParams(vmem_limit_bytes=1024 * 1024),
        cost_estimate=SHORT,
        name="tie",
    )(*arrays, *waited(after))


def shape_of(shape, dtype=jnp.bfloat16):
    return jax.ShapeDtypeStruct(shape, dtype)


def halves_beside(single):
    half = single.shape[0] // 2
    return jnp.concatenate([single[:half], single[half:]], axis=1)


def pack_columns(odd, low, tiles, base, target):
    @pl.when(odd)
    def _():
        for t in range(tiles):
            target[base + t * 96 : base + (t + 1) * 96, :] = low[
                :, 64 + t * LANES : 64 + (t + 1) * LANES
            ].astype(jnp.bfloat16)
        target[base + tiles * 96 : base + tiles * 96 + 48, :] = halves_beside(low[:, :64]).astype(
            jnp.bfloat16
        )

    @pl.when(jnp.logical_not(odd))
    def _():
        for t in range(tiles):
            target[base + t * 96 : base + (t + 1) * 96, :] = low[
                :, t * LANES : (t + 1) * LANES
            ].astype(jnp.bfloat16)
        target[base + tiles * 96 : base + tiles * 96 + 48, :] = halves_beside(
            low[:, tiles * LANES : tiles * LANES + 64]
        ).astype(jnp.bfloat16)


def pack_q_body(me, *refs):
    w_qkv, vectors, target, own = refs[0], refs[1:10], refs[10], refs[11]
    pack_columns(lax.rem(me[1], 2) == 1, w_qkv[...], 4, 0, target)
    rows = lax.broadcasted_iota(jnp.int32, (16, LANES), 0)
    tail = jnp.zeros((16, LANES), jnp.float32)
    for v in range(9):
        value = vectors[v][...]
        wide = jnp.concatenate(
            [value, jnp.zeros((1, LANES - value.shape[1]), jnp.float32)], axis=1
        )
        tail = jnp.where(rows == v, jnp.broadcast_to(wide, (16, LANES)), tail)
    target[VECTOR_ROW:, :] = tail.astype(jnp.bfloat16)
    me.send(0)
    own[...] = target[...]


def pack_q(me, w_qkv, vectors, bias_up):
    small = [v.reshape(1, -1) for v in (*vectors, bias_up)]
    return call(
        pack_q_body, [shape_of((PACK_Q, LANES))] * 2, [me, *kept_far([w_qkv, *small])], staged=10, far_outs={0: True},
        name="pack_q",
    )


def pack_rest_body(me, w_out, w_up, w_down, to_ou, to_d):
    for t in range(DOWN_TILES):
        to_d[t * 192 : (t + 1) * 192, :] = w_down[:, t * LANES : (t + 1) * LANES].astype(
            jnp.bfloat16
        )
    me.send(1)
    pack_columns(lax.rem(me[1], 2) == 1, w_out[...], 1, 0, to_ou)
    for t in range(UP_TILES):
        to_ou[UP_ROW + t * 96 : UP_ROW + (t + 1) * 96, :] = w_up[
            :, t * LANES : (t + 1) * LANES
        ].astype(jnp.bfloat16)
    me.send(0)


def pack_rest(me, w_out, w_up, w_down, after):
    return call(
        pack_rest_body,
        [
            shape_of((PACK_OU, LANES)),
            shape_of((PACK_D, LANES)),
        ],
        [me, *kept_far([w_out, w_up, w_down.T])],
        staged=3,
        far_outs={0: True, 1: True},
        after=after,
        name="pack_rest",
    )


def swap(x, axis, bit):
    size = lax.axis_size(axis)
    return lax.ppermute(x, axis, [(i, i ^ bit) for i in range(size)])


CORE, ALONG_X, ALONG_Y = 1, 2, 4


def gather_z(x, own=None):
    return [x if own is None else own] + [swap(x, "mp", k) for k in (1, 2, 3)]


def beside(me, groups, shapes, after=(), name="beside"):
    sources = []
    for x, _ in groups:
        if all(x is not y for y in sources):
            sources.append(x)

    def body(me, *refs):
        for x, (index, where) in groups:
            source = refs[next(n for n, y in enumerate(sources) if x is y)]
            refs[len(sources) + index][where] = source[...]

    return call(body, [shape_of(s) for s in shapes], [me, *sources], after=after, name=name)


def gather_near(me, parts, after=()):
    shape = (2, *parts[0].shape)
    found = beside(
        me,
        [(parts[0], (0, 0)), (parts[1], (0, 1)), (parts[2], (1, 0)), (parts[3], (1, 1))],
        [shape, shape],
        after,
        "beside_z",
    )
    first, second = found
    result = Results([first, swap(first, "dp", ALONG_X), second, swap(second, "dp", ALONG_Y)])
    result.token = found.token
    return result


def gather_far(me, parts, after=()):
    shape = (2, *parts[0].shape)
    groups = [(parts[i], (i // 2, i % 2)) for i in range(4)]
    groups += [(parts[i], (2, (i // 2, i % 2))) for i in range(4)]
    found = beside(me, groups, [shape, shape, (2, *shape)], after, "beside_near")
    first, second, both = found
    result = Results([both, swap(first, "dp", ALONG_Y), swap(second, "dp", ALONG_X)])
    result.token = found.token
    return result


def gather_core(parts):
    return list(parts) + [swap(x, "dp", CORE) for x in parts]


def gathered_blocks(me, refs):
    for core in range(2):
        both, far_y, far_x = refs[3 * core : 3 * core + 3]
        for mid in range(2):
            for low in range(2):
                for kx, ky, kz, block in (
                    (mid, 0, low, both.at[0, mid, low]),
                    (0, mid, 2 + low, both.at[1, mid, low]),
                    (mid, 1, low, far_y.at[mid, low]),
                    (1, mid, 2 + low, far_x.at[mid, low]),
                ):
                    yield me[0] ^ (core + 2 * kx + 4 * ky), me[1] ^ kz, block


def place_columns(block, base, tiles, dp, mp, width, weights, singles):
    start = pl.multiple_of(mp * width + 64 * lax.rem(mp, 2), LANES)
    rows = pl.ds(pl.multiple_of(dp * 96, 32), 96)
    for t in range(tiles):
        weights[rows, pl.ds(pl.multiple_of(start + t * LANES, LANES), LANES)] = block[
            base + t * 96 : base + (t + 1) * 96, :
        ]
    singles[mp, pl.ds(pl.multiple_of(dp * 48, 16), 48), :] = block[
        base + tiles * 96 : base + tiles * 96 + 48, :
    ]


def place_singles(width, weights, singles):
    for pair in range(2):
        column = 2 * pair * width + (width // LANES) * LANES
        for dp in range(8):
            left = singles[2 * pair, dp * 48 : (dp + 1) * 48, :].astype(jnp.float32)
            right = singles[2 * pair + 1, dp * 48 : (dp + 1) * 48, :].astype(jnp.float32)
            upper = jnp.concatenate([left[:, :64], right[:, :64]], axis=1)
            lower = jnp.concatenate([left[:, 64:], right[:, 64:]], axis=1)
            weights[dp * 96 : dp * 96 + 48, column : column + LANES] = upper.astype(jnp.bfloat16)
            weights[dp * 96 + 48 : (dp + 1) * 96, column : column + LANES] = lower.astype(
                jnp.bfloat16
            )


def unpack_q_body(me, *refs):
    blocks, weights, vectors, bias_up, singles, tails = refs[:6], *refs[6:]
    for dp, mp, block in gathered_blocks(me, blocks):
        place_columns(block, 0, 4, dp, mp, 576, weights, singles)
        tails[dp * 4 + mp] = block[VECTOR_ROW:, :].astype(jnp.float32)
    place_singles(576, weights, singles)
    lane = lax.broadcasted_iota(jnp.int32, (16, LANES), 1)

    def spread(width, count):
        found = [jnp.zeros((16, LANES), jnp.float32) for _ in range(count)]
        for device in range(32):
            start, tile = device * width % LANES, device * width // LANES
            piece = tails[device]
            moved = pltpu.roll(piece, start, axis=1) if start else piece
            found[tile] = jnp.where((lane >= start) & (lane < start + width), moved, found[tile])
            if start + width > LANES:
                found[tile + 1] = jnp.where(lane < start + width - LANES, moved, found[tile + 1])
        return found

    for t, value in enumerate(spread(24, 6)):
        vectors[:, t * LANES : (t + 1) * LANES] = value[:8]
    for t, value in enumerate(spread(96, 24)):
        bias_up[:, t * LANES : (t + 1) * LANES] = value[8:9]


def unpack_ou_body(me, *refs):
    blocks, w_out, w_up, _, _, singles = refs[:6], *refs[6:]
    for dp, mp, block in gathered_blocks(me, blocks):
        place_columns(block, 0, 1, dp, mp, 192, w_out, singles)
        rows = pl.ds(pl.multiple_of(dp * 96, 32), 96)
        for t in range(UP_TILES):
            w_up[rows, pl.ds(pl.multiple_of(mp * 768 + t * LANES, LANES), LANES)] = block[
                UP_ROW + t * 96 : UP_ROW + (t + 1) * 96, :
            ]
    me.send(3, source=w_up)
    place_singles(192, w_out, singles)
    me.send(2, source=w_out)


def unpack_ou(me, parts, after=()):
    return call(
        unpack_ou_body,
        [shape_of((768, 768)), shape_of((768, 3072))] * 2,
        [me, *parts],
        [pltpu.VMEM((4, 384, LANES), jnp.bfloat16)],
        far_outs={2: False, 3: False},
        staged=6,
        after=after,
        name="unpack_ou",
    )


def unpack_d_body(me, blocks, turned):
    for device in range(32):
        dp, mp = device // 4, device % 4
        for t in range(DOWN_TILES):
            column = dp * 384 + t * LANES
            turned[mp * 192 : (mp + 1) * 192, column : column + LANES] = blocks[
                device, t * 192 : (t + 1) * 192, :
            ]


def unpack_d(me, blocks, after=()):
    return call(
        unpack_d_body, [shape_of((768, 3072))], [me, blocks], staged=1, after=after,
        name="unpack_d",
    )


def turned_rows(me, source, target):
    turned = source[...].T
    for dp in range(8):
        k = me[0] ^ dp
        slot = (1 - (k & 1)) * 4 + (k >> 1)
        target[pl.ds(pl.multiple_of(slot * 96, 32), 96), :] = turned[dp * 96 : (dp + 1) * 96, :]


def store_columns(me, target, kp, base, tiles, mp, width, first, value):
    kz = me[1] ^ mp
    start = mp * width + 64 * (mp % 2) - first
    for t in range(tiles):
        target[kp, kz, base + t * 96 : base + (t + 1) * 96, :] = value[
            :, start + t * LANES : start + (t + 1) * LANES
        ].astype(jnp.bfloat16)


def store_single(me, target, kp, base, mp, value):
    kz = me[1] ^ mp
    upper, lower = value[:48], value[48:]
    low_lanes = lax.broadcasted_iota(jnp.int32, (48, LANES), 1) < 64
    if mp % 2 == 0:
        both = jnp.where(low_lanes, upper, pltpu.roll(lower, 64, axis=1))
    else:
        both = jnp.where(low_lanes, pltpu.roll(upper, 64, axis=1), lower)
    target[kp, kz, base : base + 48, :] = both.astype(jnp.bfloat16)


def dot(a, b):
    return jnp.dot(a, b, preferred_element_type=jnp.float32)


def dot_nt(a, b):
    return lax.dot_general(a, b, (((1,), (1,)), ((), ())), preferred_element_type=jnp.float32)


def dot_tn(a, b):
    return lax.dot_general(a, b, (((0,), (0,)), ((), ())), preferred_element_type=jnp.float32)


def column_gradient(me, left, right, target, base, tiles, width):
    for pair in range(2):
        first = 2 * pair * width
        middle = first + tiles * LANES
        for begin, count, mp in ((first, tiles, 2 * pair), (middle + LANES, tiles, 2 * pair + 1)):
            value = dot(left, right[:, begin : begin + count * LANES])
            for kp in range(4):
                store_columns(
                    me, target, kp, base, tiles, mp, width, begin, value[kp * 96 : (kp + 1) * 96]
                )
        value = dot(left, right[:, middle : middle + LANES])
        for kp in range(4):
            for mp in (2 * pair, 2 * pair + 1):
                store_single(me, target, kp, base + tiles * 96, mp, value[kp * 96 : (kp + 1) * 96])


def gradient_q_body(me, tokens, projected_grad, vectors, grad_up, send, own, turned):
    turned_rows(me, tokens, turned)
    lane = lax.broadcasted_iota(jnp.int32, (16, LANES), 1)
    rows = lax.broadcasted_iota(jnp.int32, (16, LANES), 0)
    for half, target in ((0, send), (1, own)):
        left = turned[half * 384 : (half + 1) * 384, :]
        column_gradient(me, left, projected_grad, target, 0, 4, 576)

    def cut(source, count, width, device):
        start, tile = device * width % LANES, device * width // LANES
        value = source[:, tile * LANES : (tile + 1) * LANES]
        moved = pltpu.roll(value, LANES - start, axis=1) if start else value
        if start + width > LANES:
            after = source[:, (tile + 1) * LANES : (tile + 2) * LANES]
            after = pltpu.roll(after, LANES - start, axis=1)
            here = lax.broadcasted_iota(jnp.int32, value.shape, 1)
            moved = jnp.where(here < LANES - start, moved, after)
        return moved

    for device in range(32):
        dp, mp = device // 4, device % 4
        eight = cut(vectors, 8, 24, device)
        one = jnp.broadcast_to(cut(grad_up, 1, 96, device), (8, LANES))
        tail = jnp.concatenate([eight, one], axis=0)
        tail = jnp.where((rows < 8) & (lane >= 24), 0.0, tail).astype(jnp.bfloat16)
        k = me[0] ^ dp
        kz = me[1] ^ mp

        @pl.when((k & 1) == 0)
        def _():
            own[k >> 1, kz, VECTOR_ROW:, :] = tail

        @pl.when((k & 1) == 1)
        def _():
            send[k >> 1, kz, VECTOR_ROW:, :] = tail


def gradient_q(me, tokens, projected_grad, vectors, grad_up, after=()):
    return call(
        gradient_q_body,
        [shape_of((4, 4, PACK_Q, LANES))] * 2,
        [me, tokens, projected_grad, vectors, grad_up],
        [pltpu.VMEM((768, tokens.shape[0]), jnp.bfloat16)],
        after=after,
        name="gradient_q",
    )


def gradient_ou_body(
    me, combined, attention_grad, hidden_grad, send, own, turned, turned_too
):
    turned_rows(me, combined, turned)
    turned_rows(me, me.arrived(0), turned_too)
    for half, target in ((0, send), (1, own)):
        left = turned[half * 384 : (half + 1) * 384, :]
        column_gradient(me, left, attention_grad, target, 0, 1, 192)
        left = turned_too[half * 384 : (half + 1) * 384, :]
        for mp in range(4):
            value = dot(left, hidden_grad[:, mp * 768 : (mp + 1) * 768])
            kz = me[1] ^ mp
            for kp in range(4):
                for t in range(UP_TILES):
                    target[kp, kz, UP_ROW + t * 96 : UP_ROW + (t + 1) * 96, :] = value[
                        kp * 96 : (kp + 1) * 96, t * LANES : (t + 1) * LANES
                    ].astype(jnp.bfloat16)


def gradient_ou(me, combined, attention_grad, first_low, hidden_grad, after=()):
    return call(
        gradient_ou_body,
        [shape_of((4, 4, PACK_OU, LANES))] * 2,
        [me, first_low, combined, attention_grad, hidden_grad],
        [pltpu.VMEM((768, combined.shape[0]), jnp.bfloat16)] * 2,
        late=1,
        after=after,
        name="gradient_ou",
    )


def gradient_d_body(me, feed_grad, activated, out, turned):
    turned[...] = feed_grad[...].T
    for dp in range(8):
        value = dot(turned[...], activated[:, dp * 384 : (dp + 1) * 384])
        for mp in range(4):
            for t in range(DOWN_TILES):
                out[dp, mp, t * 192 : (t + 1) * 192, :] = value[
                    mp * 192 : (mp + 1) * 192, t * LANES : (t + 1) * LANES
                ].astype(jnp.bfloat16)
        me.send(0, dp)


def gradient_d(me, feed_grad, activated, after=()):
    return call(
        gradient_d_body,
        [shape_of((8, 4, PACK_D, LANES))],
        [me, feed_grad, activated],
        [pltpu.VMEM((768, feed_grad.shape[0]), jnp.bfloat16)],
        far_outs={0: True},
        sends=8,
        after=after,
        name="gradient_d",
    )


def add(a, b):
    return a.astype(jnp.float32) + b.astype(jnp.float32)


def add_core_body(me, own, other, first_keep, first_send, second_keep, second_send):
    for kp in range(4):
        ky, kx = kp // 2, kp % 2
        first, second = (first_send if ky else first_keep), (second_send if kx else second_keep)
        for low in range(2):
            first[kx, low] = add(own[kp, low], other[kp, low]).astype(jnp.bfloat16)
            second[ky, low] = add(own[kp, 2 + low], other[kp, 2 + low]).astype(jnp.bfloat16)


def add_plane_body(me, first, first_in, second, second_in, *outs):
    for keep, send, a, b in ((*outs[:2], first, first_in), (*outs[2:], second, second_in)):
        keep[...] = add(a[0], b[0]).astype(jnp.bfloat16)
        send[...] = add(a[1], b[1]).astype(jnp.bfloat16)


def add_last_body(me, first, first_in, second, second_in, *outs):
    for low in range(2):
        outs[low][...] = add(first[low], first_in[low]).astype(jnp.bfloat16)
        outs[2 + low][...] = add(second[low], second_in[low]).astype(jnp.bfloat16)


def add_core(me, own, other, after=()):
    rows = own.shape[2]
    return call(
        add_core_body,
        [shape_of((2, 2, rows, LANES))] * 4,
        [me, own, other],
        after=after,
        name="add_core",
    )


def scatter_near(parts):
    first, first_send, second, second_send = parts
    return first, swap(first_send, "dp", ALONG_Y), second, swap(second_send, "dp", ALONG_X)


def add_plane(me, parts, after=()):
    rows = parts[0].shape[2]
    return call(
        add_plane_body,
        [shape_of((2, rows, LANES))] * 4,
        [me, *parts],
        after=after,
        name="add_plane",
    )


def scatter_far(parts):
    first, first_send, second, second_send = parts
    return first, swap(first_send, "dp", ALONG_X), second, swap(second_send, "dp", ALONG_Y)


def add_last(me, parts, after=()):
    rows = parts[0].shape[1]
    return call(
        add_last_body, [shape_of((rows, LANES))] * 4, [me, *parts], after=after, name="add_last"
    )


def scatter_z(parts):
    return [parts[0]] + [swap(parts[k], "mp", k) for k in (1, 2, 3)]


def total(refs, rows):
    value = refs[0][rows, :].astype(jnp.float32)
    for ref in refs[1:]:
        value = value + ref[rows, :].astype(jnp.float32)
    return value


def finish_columns(me, refs, base, tiles, out):
    odd = lax.rem(me[1], 2) == 1
    full = [total(refs, pl.ds(base + t * 96, 96)) for t in range(tiles)]
    single = total(refs, pl.ds(base + tiles * 96, 48))
    single = jnp.concatenate([single[:, :64], single[:, 64:]], axis=0)

    @pl.when(odd)
    def _():
        out[...] = jnp.concatenate([single, *full], axis=1)

    @pl.when(jnp.logical_not(odd))
    def _():
        out[...] = jnp.concatenate([*full, single], axis=1)


def finish_q_body(me, *refs):
    parts, out, outs = refs[:4], refs[4], refs[5:]
    finish_columns(me, parts, 0, 4, out)
    tail = total(parts, pl.ds(VECTOR_ROW, 16))
    for v in range(8):
        outs[v][...] = tail[v : v + 1, :24]
    outs[8][...] = tail[8:9, :96]


def finish_q(me, parts):
    f = jnp.float32
    return call(
        finish_q_body,
        [shape_of((96, 576), f)] + [shape_of((1, 24), f)] * 8 + [shape_of((1, 96), f)],
        [me, *parts],
        name="finish_q",
    )


def finish_ou_body(me, *refs):
    parts, w_out, w_up = refs[:4], refs[4], refs[5]
    finish_columns(me, parts, 0, 1, w_out)
    for t in range(UP_TILES):
        w_up[:, t * LANES : (t + 1) * LANES] = total(parts, pl.ds(UP_ROW + t * 96, 96))


def finish_ou(me, parts):
    f = jnp.float32
    return call(
        finish_ou_body, [shape_of((96, 192), f), shape_of((96, 768), f)], [me, *parts],
        name="finish_ou",
    )


def finish_d_body(me, part, out):
    for t in range(DOWN_TILES):
        out[:, t * LANES : (t + 1) * LANES] = part[t * 192 : (t + 1) * 192, :].astype(jnp.float32)


def finish_d(me, part, after=()):
    f = jnp.float32
    return call(finish_d_body, [shape_of((192, 384), f)], [me, part], after=after, name="finish_d")


PAIRS = HEADS // 2


def iota(shape, axis):
    return lax.broadcasted_iota(jnp.int32, shape, axis)


def place_matrix(order, head):
    length = order.shape[1]
    row = order[head : head + 1, :].astype(jnp.int16)
    token = iota((length, length), 0).astype(jnp.int16)
    return jnp.where(token == row, jnp.bfloat16(1.0), jnp.bfloat16(0.0))


def project_body(me, *refs):
    blocks, tokens = refs[:6], refs[6]
    weights, vectors, bias_up, qkv, singles, tails = refs[7:]
    unpack_q_body(me, *blocks, weights, vectors, bias_up, singles, tails)
    me.send(0)
    for c in range(9):
        columns = slice(c * 256, (c + 1) * 256)
        value = dot(tokens[...], weights[:, columns])
        if c < 3:
            value = value + vectors[0:1, c * 256 : (c + 1) * 256]
        elif c >= 6:
            value = value + vectors[1:2, (c - 6) * 256 : (c - 5) * 256]
        qkv[:, columns] = value.astype(jnp.bfloat16)


def project(me, parts, tokens, after=()):
    return call(
        project_body,
        [
            shape_of((768, 2304)),
            shape_of((8, 768), jnp.float32),
            shape_of((1, 3072), jnp.float32),
            shape_of((tokens.shape[0], 2304)),
        ],
        [me, *parts, tokens],
        [pltpu.VMEM((4, 384, LANES), jnp.bfloat16), pltpu.VMEM((32, 16, LANES), jnp.float32)],
        staged=6,
        far_outs={0: True},
        after=after,
        name="project",
    )


def attend_body(first_pair, pairs, me, qkv, order, facts, *refs):
    swapped, values, soft, combined = refs[-4:]
    length = qkv.shape[0]
    groups = length // CLUSTER
    blocks = [slice(g * CLUSTER, (g + 1) * CLUSTER) for g in range(groups)]
    low = iota((length, LANES), 1) < 64
    itself = iota((CLUSTER, CLUSTER), 0) == iota((CLUSTER, CLUSTER), 1)
    pick = [
        jnp.where(iota((16, LANES), 1) == lane, 1.0, 0.0).astype(jnp.bfloat16) for lane in (64, 0)
    ]
    scale = HEAD_DIM ** (-0.5)

    for place in range(pairs):
        pair = first_pair + place

        def columns(base, pair=pair):
            return slice(base + pair * LANES, base + (pair + 1) * LANES)

        query = qkv[:, columns(0)].astype(jnp.float32)
        keys = qkv[:, columns(768)].astype(jnp.float32)
        value = qkv[:, columns(1536)].astype(jnp.float32)
        known = facts[...]
        tiles = (
            (jnp.where(low, query, pltpu.roll(keys, 64, axis=1)), jnp.where(low, value, known)),
            (jnp.where(low, pltpu.roll(query, 64, axis=1), keys), jnp.where(low, known, value)),
        )
        moved, to_tokens = [], []
        for h in range(2):
            back = place_matrix(order, 2 * pair + h)
            to_tokens.append(back)
            tile = jnp.concatenate([t.astype(jnp.bfloat16) for t in tiles[h]], axis=1)
            moved.append(dot_tn(back, tile))
        query_slots, key_slots, value_slots, codes, rows_of = [], [], [], [], []
        for h in range(2):
            both = moved[h][:, :LANES]
            query_slots.append(jnp.where(low, both, 0.0).astype(jnp.bfloat16))
            key_slots.append(pltpu.roll(both, 64, axis=1).astype(jnp.bfloat16))
            value_slots.append(moved[h][:, LANES:].astype(jnp.bfloat16))
            swapped[2 * place + h] = key_slots[h]
            values[2 * place + h] = value_slots[h]
            me.send(0, 2 * place + h)
            me.send(1, 2 * place + h)
            lane = 64 * (1 - h)
            code = moved[h][:, LANES + lane : LANES + lane + 1]
            row = dot_nt(pick[h], value_slots[h])[0:1]
            codes.append(jnp.where(code >= 32.0, code - 32.0, code))
            rows_of.append(row)
        scores = [
            [dot_nt(query_slots[h][b], key_slots[h][b]) for b in blocks] for h in range(2)
        ]
        found = []
        for h in range(2):
            outs = []
            for g, b in enumerate(blocks):
                allowed = (codes[h][b] == rows_of[h][:, b]) | itself
                value = jnp.where(allowed, scores[h][g] * scale, masked_score)
                value = jnp.exp(value - jnp.max(value, axis=1, keepdims=True))
                weights = value / jnp.sum(value, axis=1, keepdims=True)
                soft[2 * place + h, b, :] = weights
                outs.append(weights.astype(jnp.bfloat16))
            me.send(2, 2 * place + h)
            found.append(
                [dot(outs[g], value_slots[h][b]) for g, b in enumerate(blocks)]
            )
        result = None
        for h in range(2):
            value = jnp.concatenate(found[h], axis=0)
            value = jnp.where(low if h == 0 else jnp.logical_not(low), value, 0.0)
            value = dot(to_tokens[h], value.astype(jnp.bfloat16))
            result = value if result is None else result + value
        combined[:, columns(0)] = result.astype(jnp.bfloat16)


def attend(me, qkv, order, facts, first_pair, pairs, combined=None, after=()):
    length = qkv.shape[0]
    operands = [me, qkv, order, facts]
    if combined is not None:
        operands.append(combined)
    return call(
        functools.partial(attend_body, first_pair, pairs),
        [
            shape_of((2 * pairs, length, LANES)),
            shape_of((2 * pairs, length, LANES)),
            shape_of((2 * pairs, length, CLUSTER), jnp.float32),
            shape_of((length, 768)),
        ],
        operands,
        after=after,
        aliases={3: 3} if combined is not None else None,
        far_outs={0: True, 1: True, 2: True},
        sends=6 * pairs,
        name="attend",
    )


def by_rows(count, step, body):
    def one(i, carry):
        body(pl.ds(pl.multiple_of(i * step, step), step))
        return carry

    lax.fori_loop(0, count // step, one, 0)


def mean(value):
    return jnp.mean(value, axis=1, keepdims=True)


def fold(value):
    return jnp.sum(value.reshape(value.shape[0] // 8, 8, value.shape[1]), axis=0)


def out_norm_body(me, combined, w_out, tokens, vectors, first_low, normal, *refs):
    inverse, total_ref = refs[0], refs[3]
    total_ref[...] = dot(combined[...], w_out[...])

    def rows_of(rows):
        value = total_ref[rows, :] + vectors[2:3] + tokens[rows, :].astype(jnp.float32)
        centred = value - mean(value)
        scale = lax.rsqrt(mean(centred * centred) + epsilon)
        norm = centred * scale
        normal[rows, :] = norm
        inverse[rows, :] = jnp.broadcast_to(scale, (scale.shape[0], LANES))
        first_low[rows, :] = (norm * vectors[3:4] + vectors[4:5]).astype(jnp.bfloat16)

    by_rows(tokens.shape[0], 32, rows_of)
    me.send(2)
    me.send(3, source=normal)
    me.send(4, source=first_low)


def out_norm(me, combined, w_out, tokens, vectors, after=()):
    n = tokens.shape[0]
    f = jnp.float32
    return call(
        out_norm_body,
        [
            shape_of((n, 768)),
            shape_of((n, 768), f),
            shape_of((n, LANES), f),
            shape_of((n, 768), f),
            shape_of((n, 768)),
        ],
        [me, combined, w_out, tokens, vectors],
        [pltpu.VMEM((n, 768), jnp.float32)],
        far_outs={2: True, 3: False, 4: False},
        after=after,
        name="out_norm",
    )


def up_body(me, first_low, w_up, bias_up, activated, slope):
    for i in range(w_up.shape[1] // 256):
        columns = slice(i * 256, (i + 1) * 256)
        hidden = dot(first_low[...], w_up[:, columns]) + bias_up[:, columns]
        half = 0.5 + 0.5 * lax.erf(hidden * (0.5**0.5))
        activated[:, columns] = (hidden * half).astype(jnp.bfloat16)
        bell = jnp.exp(-0.5 * hidden * hidden) * (2.0 * math.pi) ** (-0.5)
        slope[:, columns] = (half + hidden * bell).astype(jnp.bfloat16)
        if i % 3 == 2:
            me.send(1, (slice(None), slice((i - 2) * 256, (i + 1) * 256)))


def up(me, first_low, w_up, bias_up, after=()):
    shape = (first_low.shape[0], w_up.shape[1])
    return call(
        up_body,
        [shape_of(shape), shape_of(shape)],
        [me, first_low, w_up, bias_up],
        far_outs={1: True},
        sends=4,
        after=after,
        name="up",
    )


def down_norm_body(
    me, activated, turned, normal, vectors, out, feed_grad, second_grad, sums, feed, acc
):
    feed[...] = dot_nt(activated[...], turned[...])
    cotangent = me.arrived(0)
    acc[...] = jnp.zeros_like(acc)

    def rows_of(rows):
        value = normal[rows, :] * vectors[3:4] + vectors[4:5] + feed[rows, :] + vectors[5:6]
        centred = value - mean(value)
        inverse = lax.rsqrt(mean(centred * centred) + epsilon)
        norm = centred * inverse
        out[rows, :] = (norm * vectors[6:7] + vectors[7:8]).astype(jnp.bfloat16)
        upstream = cotangent[rows, :]
        scaled = upstream * vectors[6:7]
        back = inverse * (scaled - mean(scaled) - norm * mean(scaled * norm))
        second_grad[rows, :] = back
        low = back.astype(jnp.bfloat16)
        feed_grad[rows, :] = low
        acc[0] += fold(low.astype(jnp.float32))
        acc[1] += fold(upstream * norm)
        acc[2] += fold(upstream)

    by_rows(cotangent.shape[0], 32, rows_of)
    me.send(0)
    me.send(2)
    for i in range(3):
        sums[i : i + 1, :] = jnp.sum(acc[i], axis=0, keepdims=True)


def down_norm(me, activated, turned, normal, vectors, cotangent, after=()):
    n = cotangent.shape[0]
    return call(
        down_norm_body,
        [
            shape_of((n, 768)),
            shape_of((n, 768)),
            shape_of((n, 768), jnp.float32),
            shape_of((3, 768), jnp.float32),
        ],
        [me, cotangent, activated, turned, normal, vectors],
        [pltpu.VMEM((n, 768), jnp.float32), pltpu.VMEM((3, 8, 768), jnp.float32)],
        late=1,
        far_outs={0: True, 2: True},
        after=after,
        name="down_norm",
    )


def hidden_back_body(me, feed_grad, turned, hidden_grad, sums):
    for i in range(turned.shape[1] // 256):
        columns = slice(i * 256, (i + 1) * 256)
        value = dot(feed_grad[...], turned[:, columns])
        value = value * me.arrived(0)[:, columns].astype(jnp.float32)
        low = value.astype(jnp.bfloat16)
        hidden_grad[:, columns] = low
        sums[:, columns] = jnp.sum(low.astype(jnp.float32), axis=0, keepdims=True)


def hidden_back(me, feed_grad, turned, slope, after=()):
    return call(
        hidden_back_body,
        [shape_of(slope.shape), shape_of((1, slope.shape[1]), jnp.float32)],
        [me, slope, feed_grad, turned],
        late=1,
        after=after,
        name="hidden_back",
    )


def first_back_body(
    me, hidden_grad, vectors, residual, low_out, sums, back, acc
):
    w_up = me.arrived(0)
    back[...] = dot_nt(hidden_grad[...], w_up[...])
    second_grad, normal, inverse = me.arrived(1), me.arrived(2), me.arrived(3)
    acc[...] = jnp.zeros_like(acc)

    def rows_of(rows):
        upstream = back[rows, :] + second_grad[rows, :]
        norm = normal[rows, :]
        scaled = upstream * vectors[3:4]
        value = inverse[rows, 0:1] * (scaled - mean(scaled) - norm * mean(scaled * norm))
        residual[rows, :] = value
        low = value.astype(jnp.bfloat16)
        low_out[rows, :] = low
        acc[0] += fold(low.astype(jnp.float32))
        acc[1] += fold(upstream * norm)
        acc[2] += fold(upstream)

    by_rows(normal.shape[0], 32, rows_of)
    me.send(0)
    for i in range(3):
        sums[i : i + 1, :] = jnp.sum(acc[i], axis=0, keepdims=True)


def first_back(me, hidden_grad, w_up, second_grad, normal, inverse, vectors, after=()):
    n = normal.shape[0]
    return call(
        first_back_body,
        [shape_of((n, 768), jnp.float32), shape_of((n, 768)), shape_of((3, 768), jnp.float32)],
        [me, w_up, second_grad, normal, inverse, hidden_grad, vectors],
        [pltpu.VMEM((n, 768), jnp.float32), pltpu.VMEM((3, 8, 768), jnp.float32)],
        late=4,
        far_outs={0: True},
        vmem=20,
        after=after,
        name="first_back",
    )


def attend_back_body(
    first_pair, pairs, me, attention_grad, w_out, order, *refs
):
    grads, sums, upstream = refs[-3:]
    length = attention_grad.shape[0]
    groups = length // CLUSTER
    blocks = [slice(g * CLUSTER, (g + 1) * CLUSTER) for g in range(groups)]
    low = iota((length, LANES), 1) < 64
    low_rows = iota((CLUSTER, LANES), 1) < 64
    scale = HEAD_DIM ** (-0.5)
    mine = slice(first_pair * LANES, (first_pair + pairs) * LANES)
    upstream[...] = dot_nt(attention_grad[...], w_out[mine, :]).astype(jnp.bfloat16)

    for place in range(pairs):
        pair = first_pair + place

        def columns(base, pair=pair):
            return slice(base + pair * LANES, base + (pair + 1) * LANES)

        both = upstream[:, slice(place * LANES, (place + 1) * LANES)]
        to_tokens, moved = [], []
        for h in range(2):
            to_tokens.append(place_matrix(order, 2 * pair + h))
            value = dot_tn(to_tokens[h], both)
            value = jnp.where(low if h == 0 else jnp.logical_not(low), value, 0.0)
            moved.append(value.astype(jnp.bfloat16))
        swapped, values, soft = me.arrived(0), me.arrived(1), me.arrived(2)
        back = []
        for h in range(2):
            kept = 2 * place + h
            keys = [swapped[kept, b, :] for b in blocks]
            weights = [soft[kept, b, :] for b in blocks]
            soft_grad = [dot_nt(moved[h][b], values[kept, b, :]) for b in blocks]
            value_grad = [
                dot_tn(weights[g].astype(jnp.bfloat16), moved[h][b]) for g, b in enumerate(blocks)
            ]
            score_grad = []
            for g in range(groups):
                middle = jnp.sum(soft_grad[g] * weights[g], axis=1, keepdims=True)
                score_grad.append((weights[g] * (soft_grad[g] - middle)).astype(jnp.bfloat16))
            query_grad = [dot(score_grad[g], keys[g]) for g in range(groups)]
            key_grad = [dot_tn(score_grad[g], keys[g]) for g in range(groups)]
            parts = [
                jnp.concatenate(
                    [
                        (jnp.where(low_rows, query_grad[g], key_grad[g]) * scale).astype(
                            jnp.bfloat16
                        ),
                        value_grad[g].astype(jnp.bfloat16),
                    ],
                    axis=1,
                )
                for g in range(groups)
            ]
            back.append(dot(to_tokens[h], jnp.concatenate(parts, axis=0)))
        first, second = back[0][:, :LANES], back[1][:, :LANES]
        query = jnp.where(low, first, pltpu.roll(second, 64, axis=1))
        keys = jnp.where(low, pltpu.roll(first, 64, axis=1), second)
        value = back[0][:, LANES:] + back[1][:, LANES:]
        grads[:, columns(0)] = query.astype(jnp.bfloat16)
        grads[:, columns(768)] = keys.astype(jnp.bfloat16)
        grads[:, columns(1536)] = value.astype(jnp.bfloat16)
        sums[0:1, columns(0)] = jnp.sum(query, axis=0, keepdims=True)
        sums[1:2, columns(0)] = jnp.sum(value, axis=0, keepdims=True)


def attend_back(
    me, attention_grad, w_out, order, kept, first_pair, pairs, before=(), after=()
):
    length = attention_grad.shape[0]
    return call(
        functools.partial(attend_back_body, first_pair, pairs),
        [shape_of((length, 2304)), shape_of((2, 768), jnp.float32)],
        [me, *kept, attention_grad, w_out, order, *before],
        [pltpu.VMEM((length, pairs * LANES), jnp.bfloat16)],
        after=after,
        aliases={6: 0, 7: 1} if before else None,
        late=3,
        name="attend_back",
    )


def tokens_back_body(me, grads, out):
    weights = me.arrived(0)
    for c in range(3):
        columns = slice(c * 256, (c + 1) * 256)
        value = dot_nt(grads[...], weights[columns, :])
        out[:, columns] = value + me.arrived(1)[:, columns]
        me.send(0, (slice(None), columns))


def tokens_back(me, grads, weights, residual, after=()):
    return call(
        tokens_back_body,
        [shape_of(residual.shape, jnp.float32)],
        [me, weights, residual, grads],
        late=2,
        far_outs={0: True},
        sends=3,
        after=after,
        name="tokens_back",
    )


def local_block(
    tokens,
    w_qkv,
    bias_query,
    bias_value,
    w_out,
    bias_out,
    gain_one,
    shift_one,
    w_up,
    bias_up,
    w_down,
    bias_down,
    gain_two,
    shift_two,
    cluster_order,
    segment_ids,
    padding,
    cotangent,
):
    length = tokens.shape[0]
    me = None
    vector_list = [
        bias_query, bias_value, bias_out, gain_one, shift_one, bias_down, gain_two, shift_two
    ]
    order = cluster_order[0]
    facts = (segment_ids[0] + 32 * (1 - padding[0])).astype(jnp.float32)
    facts = jnp.broadcast_to(facts[:, None], (length, 128))

    blocks_q = pack_q(me, w_qkv, vector_list, bias_up)
    z_q = gather_z(*blocks_q)
    blocks_rest = pack_rest(me, w_out, w_up, w_down, after=[blocks_q])
    all_d = lax.all_gather(blocks_rest[1], ("dp", "mp"), axis=0, tiled=False)
    near_q = gather_near(me, z_q, after=[blocks_rest])
    (block_ou,) = tie([blocks_rest[0]], [near_q])
    middle_ou = swap(block_ou, "mp", 2)
    far_q = gather_far(me, near_q, after=[middle_ou])
    (block_ou,) = tie([block_ou], [far_q])
    z_ou = [block_ou, swap(block_ou, "mp", 1), middle_ou, swap(block_ou, "mp", 3)]
    near_ou = gather_near(me, z_ou, after=far_q[1:])
    projected = project(me, gather_core(far_q), tokens, after=[near_ou])
    full_qkv, vectors, full_bias_up, qkv = projected

    pairs = PAIRS // 3

    def forward(part, before, after):
        return attend(
            me, qkv, order, facts, part * pairs, pairs, before, after=after
        )

    seen_a = forward(0, None, [projected])
    far_ou = gather_far(me, near_ou, after=[seen_a])
    seen_b = forward(1, seen_a[-1], [far_ou])
    tied_ou = tie(far_ou, [seen_b])
    seen_c = forward(2, seen_b[-1], tied_ou[:1])
    combined = seen_c[-1]
    near_out, near_up, full_out, full_up = unpack_ou(me, gather_core(tied_ou), after=[seen_c])
    first_near, normal_near, inverse, normal, first_low = out_norm(
        me, combined, near_out, tokens, vectors
    )
    upper = up(me, first_near, near_up, full_bias_up)
    activated, slope = upper
    turned_down = unpack_d(me, all_d, after=[upper])[0]
    layer_out, feed_grad, second_grad, sums_two = down_norm(
        me, activated, turned_down, normal_near, vectors, cotangent
    )

    both_d = gradient_d(me, feed_grad, activated)
    sum_d = lax.psum_scatter(both_d[0], "dp", scatter_dimension=0, tiled=False)
    sum_d = lax.psum_scatter(sum_d, "mp", scatter_dimension=0, tiled=False)
    hidden_grad, sums_up = hidden_back(me, feed_grad, turned_down, slope, after=[both_d])
    residual_grad, attention_grad, sums_one = first_back(
        me, hidden_grad, full_up, second_grad, normal, inverse, vectors
    )
    both_ou = gradient_ou(me, combined, attention_grad, first_low, hidden_grad)
    send_ou, own_ou = both_ou
    other_ou = swap(send_ou, "dp", CORE)

    def back(part, kept, before, after):
        return attend_back(
            me, attention_grad, full_out, order, kept,
            part * pairs, pairs, before, after,
        )

    grads_a = back(0, seen_a[:3], (), [both_ou])
    added_ou = add_core(me, own_ou, other_ou, after=[grads_a])
    core_ou = scatter_near(added_ou)
    grads_b = back(1, seen_b[:3], grads_a, [added_ou])
    grads_c = back(2, seen_c[:3], grads_b, [])
    half_ou = add_plane(me, core_ou, after=[grads_c])
    plane_ou = scatter_far(half_ou)
    projected_grad, sums_bias = grads_c
    grad_vectors = jnp.concatenate([sums_bias, sums_one, sums_two], axis=0)
    both_q = gradient_q(me, tokens, projected_grad, grad_vectors, sums_up, after=[half_ou])
    send_q, own_q = both_q
    other_q = swap(send_q, "dp", CORE)
    moved = tokens_back(me, projected_grad, full_qkv, residual_grad, after=[both_q])
    grad_tokens = moved[0]
    last_ou = add_last(me, plane_ou, after=[moved])
    added_q = add_core(me, own_q, other_q, after=[last_ou])
    core_q = scatter_near(added_q)
    sums_ou = scatter_z(last_ou)
    done_ou = finish_ou(me, sums_ou)
    shard_out, shard_up = done_ou
    half_q = add_plane(me, core_q, after=[done_ou])
    plane_q = scatter_far(half_q)
    last_q = add_last(me, plane_q)
    sums_q = scatter_z(last_q)
    shard_qkv, *shard_vectors = finish_q(me, sums_q)
    shard_down = finish_d(me, sum_d)[0].T
    grad_list = [v.reshape(-1) for v in shard_vectors]
    return (
        layer_out,
        grad_tokens,
        shard_qkv,
        grad_list[0],
        grad_list[1],
        shard_out,
        grad_list[2],
        grad_list[3],
        grad_list[4],
        shard_up,
        grad_list[8],
        shard_down,
        grad_list[5],
        grad_list[6],
        grad_list[7],
    )


def solution(mesh):
    in_specs = (
        P(("dp", "mp"), None),
        P("dp", "mp"),
        P(("dp", "mp")),
        P(("dp", "mp")),
        P("dp", "mp"),
        P(("dp", "mp")),
        P(("dp", "mp")),
        P(("dp", "mp")),
        P("dp", "mp"),
        P(("dp", "mp")),
        P("dp", "mp"),
        P(("dp", "mp")),
        P(("dp", "mp")),
        P(("dp", "mp")),
        P(("dp", "mp"), None, None),
        P(("dp", "mp"), None),
        P(("dp", "mp"), None),
        P(("dp", "mp"), None),
    )
    out_specs = (
        P(("dp", "mp"), None),
        P(("dp", "mp"), None),
        P("dp", "mp"),
        P(("dp", "mp")),
        P(("dp", "mp")),
        P("dp", "mp"),
        P(("dp", "mp")),
        P(("dp", "mp")),
        P(("dp", "mp")),
        P("dp", "mp"),
        P(("dp", "mp")),
        P("dp", "mp"),
        P(("dp", "mp")),
        P(("dp", "mp")),
        P(("dp", "mp")),
    )
    blocks = mesh.shape["dp"] == 8 and mesh.shape["mp"] == 4
    local = local_block if blocks else local_general
    return jax.shard_map(local, mesh=mesh, in_specs=in_specs, out_specs=out_specs, check_vma=False)
```

```python
import functools
import math

import jax
import jax.numpy as jnp
from jax import lax
from jax.experimental import pallas as pl
from jax.experimental.pallas import tpu as pltpu
from jax.sharding import PartitionSpec as P

HEADS = 12
HEAD_DIM = 64
CLUSTER = 128


epsilon = 1e-12
masked_score = -1e30


def product(left_side, right_side):
    return jnp.dot(left_side, right_side, preferred_element_type=jnp.float32)


def times_back(left_side, right_side):
    return lax.dot_general(
        left_side, right_side, (((1,), (1,)), ((), ())), preferred_element_type=jnp.float32
    )


def outer_sum(left_side, right_side):
    return lax.dot_general(
        left_side, right_side, (((0,), (0,)), ((), ())), preferred_element_type=jnp.float32
    )


def norm_forward(hidden, norm_gain, norm_shift):
    average = jnp.mean(hidden, axis=-1, keepdims=True)
    centred = hidden - average
    variance = jnp.mean(centred * centred, axis=-1, keepdims=True)
    inverse = lax.rsqrt(variance + epsilon)
    normal = centred * inverse
    return (normal * norm_gain + norm_shift, normal, inverse)


def norm_backward(upstream, normal, inverse, norm_gain):
    scaled = upstream * norm_gain
    return inverse * (
        scaled
        - jnp.mean(scaled, axis=-1, keepdims=True)
        - normal * jnp.mean(scaled * normal, axis=-1, keepdims=True)
    )


def gelu_exact(inputs):
    return jax.nn.gelu(inputs, approximate=False)


def local_general(
    tokens,
    w_qkv,
    bias_query,
    bias_value,
    w_out,
    bias_out,
    gain_one,
    shift_one,
    w_up,
    bias_up,
    w_down,
    bias_down,
    gain_two,
    shift_two,
    cluster_order,
    segment_ids,
    padding,
    cotangent,
):
    model_width = HEADS * HEAD_DIM
    length = tokens.shape[0]
    groups = length // CLUSTER
    score_scale = HEAD_DIM ** (-0.5)
    vectors = jnp.stack(
        [bias_query, bias_value, bias_out, gain_one, shift_one, bias_down, gain_two, shift_two]
    ).astype(jnp.bfloat16)
    vector_up = bias_up.astype(jnp.bfloat16)[None, :]
    part_qkv = w_qkv.astype(jnp.bfloat16)
    part_out = w_out.astype(jnp.bfloat16)
    part_up = w_up.astype(jnp.bfloat16)
    part_down = w_down.astype(jnp.bfloat16)
    column_qkv, column_out, column_up, column_down, column_vectors, column_bias = (
        lax.all_gather(part_qkv, "mp", axis=1, tiled=True),
        lax.all_gather(part_out, "mp", axis=1, tiled=True),
        lax.all_gather(part_up, "mp", axis=1, tiled=True),
        lax.all_gather(part_down, "mp", axis=1, tiled=True),
        lax.all_gather(vectors, "mp", axis=1, tiled=True),
        lax.all_gather(vector_up, "mp", axis=1, tiled=True),
    )
    full_qkv, full_out, full_up, full_down, full_vectors, full_bias = (
        lax.all_gather(column_qkv, "dp", axis=0, tiled=True),
        lax.all_gather(column_out, "dp", axis=0, tiled=True),
        lax.all_gather(column_up, "dp", axis=0, tiled=True),
        lax.all_gather(column_down, "dp", axis=0, tiled=True),
        lax.all_gather(column_vectors, "dp", axis=1, tiled=True),
        lax.all_gather(column_bias, "dp", axis=1, tiled=True),
    )
    small_params = full_vectors.astype(jnp.float32)
    hidden_bias = full_bias[0].astype(jnp.float32)
    ordering = cluster_order[0]
    segment = segment_ids[0]
    present = padding[0]
    positions = jnp.arange(length, dtype=jnp.int32)
    placement = (ordering[:, :, None] == positions[None, None, :]).astype(jnp.bfloat16)

    def to_clusters(matrix):
        per_head = matrix.reshape(length, HEADS, HEAD_DIM)
        moved = jnp.einsum("hip,phd->hid", placement, per_head, preferred_element_type=jnp.float32)
        return moved.astype(jnp.bfloat16).reshape(HEADS, groups, CLUSTER, HEAD_DIM)

    def from_clusters(blocks):
        per_head = blocks.astype(jnp.bfloat16).reshape(HEADS, length, HEAD_DIM)
        moved = jnp.einsum("hip,hid->phd", placement, per_head, preferred_element_type=jnp.float32)
        return moved.astype(jnp.bfloat16).reshape(length, model_width)

    segment_blocks = jnp.take(segment, ordering).reshape(HEADS, groups, CLUSTER)
    present_blocks = jnp.take(present, ordering).reshape(HEADS, groups, CLUSTER)
    same_doc = segment_blocks[..., :, None] == segment_blocks[..., None, :]
    itself = jnp.eye(CLUSTER, dtype=bool)
    allowed = same_doc & ((present_blocks[..., None, :] == 1) | itself)

    def scores_of(query_blocks, key_blocks):
        raw_scores = (
            jnp.einsum(
                "hncd,hnmd->hncm", query_blocks, key_blocks, preferred_element_type=jnp.float32
            )
            * score_scale
        )
        return jnp.where(allowed, raw_scores, masked_score)

    projected = product(tokens, full_qkv)
    query = (projected[:, :model_width] + small_params[0]).astype(jnp.bfloat16)
    keys = projected[:, model_width : 2 * model_width].astype(jnp.bfloat16)
    values = (projected[:, 2 * model_width :] + small_params[1]).astype(jnp.bfloat16)
    query_blocks = to_clusters(query)
    key_blocks = to_clusters(keys)
    value_blocks = to_clusters(values)
    masked = scores_of(query_blocks, key_blocks)
    highest = jnp.max(masked, axis=-1, keepdims=True)
    exponent = jnp.exp(masked - highest)
    row_total = jnp.sum(exponent, axis=-1, keepdims=True)
    soft_weights = exponent / row_total
    log_total = highest + jnp.log(row_total)
    soft_low = soft_weights.astype(jnp.bfloat16)
    combined = from_clusters(
        jnp.einsum("hncm,hnmd->hncd", soft_low, value_blocks, preferred_element_type=jnp.float32)
    )
    attention = product(combined, full_out) + small_params[2]
    first_norm, first_normal, first_inverse = norm_forward(
        tokens.astype(jnp.float32) + attention, small_params[3], small_params[4]
    )
    first_low = first_norm.astype(jnp.bfloat16)
    hidden = product(first_low, full_up) + hidden_bias
    activated, gelu_pull = jax.vjp(gelu_exact, hidden)
    activated_low = activated.astype(jnp.bfloat16)
    feed_out = product(activated_low, full_down) + small_params[5]
    output, second_normal, second_inverse = norm_forward(
        first_norm + feed_out, small_params[6], small_params[7]
    )
    layer_out = output.astype(jnp.bfloat16)
    again_qkv, again_out, again_up, again_down = (
        lax.all_gather(part_qkv, "mp", axis=1, tiled=True),
        lax.all_gather(part_out, "mp", axis=1, tiled=True),
        lax.all_gather(part_up, "mp", axis=1, tiled=True),
        lax.all_gather(part_down, "mp", axis=1, tiled=True),
    )
    back_qkv, back_out, back_up, back_down = (
        lax.all_gather(again_qkv, "dp", axis=0, tiled=True),
        lax.all_gather(again_out, "dp", axis=0, tiled=True),
        lax.all_gather(again_up, "dp", axis=0, tiled=True),
        lax.all_gather(again_down, "dp", axis=0, tiled=True),
    )
    grad_gain_two = jnp.sum(cotangent * second_normal, axis=0)
    grad_shift_two = jnp.sum(cotangent, axis=0)
    second_grad = norm_backward(cotangent, second_normal, second_inverse, small_params[6])
    feed_grad = second_grad.astype(jnp.bfloat16)
    grad_bias_down = jnp.sum(feed_grad.astype(jnp.float32), axis=0)
    grad_w_down = outer_sum(activated_low, feed_grad)
    hidden_grad = gelu_pull(times_back(feed_grad, back_down))[0].astype(jnp.bfloat16)
    grad_bias_up = jnp.sum(hidden_grad.astype(jnp.float32), axis=0)
    grad_w_up = outer_sum(first_low, hidden_grad)
    first_grad = times_back(hidden_grad, back_up) + second_grad
    grad_gain_one = jnp.sum(first_grad * first_normal, axis=0)
    grad_shift_one = jnp.sum(first_grad, axis=0)
    residual_grad = norm_backward(first_grad, first_normal, first_inverse, small_params[3])
    attention_grad = residual_grad.astype(jnp.bfloat16)
    grad_bias_out = jnp.sum(attention_grad.astype(jnp.float32), axis=0)
    grad_w_out = outer_sum(combined, attention_grad)
    combined_grad = to_clusters(times_back(attention_grad, back_out).astype(jnp.bfloat16))
    masked_again = scores_of(query_blocks, key_blocks)
    soft_again = jnp.exp(masked_again - log_total)
    soft_again_low = soft_again.astype(jnp.bfloat16)
    value_sums = jnp.einsum(
        "hncm,hncd->hnmd", soft_again_low, combined_grad, preferred_element_type=jnp.float32
    )
    soft_grad = jnp.einsum(
        "hncd,hnmd->hncm", combined_grad, value_blocks, preferred_element_type=jnp.float32
    )
    score_grad = (
        soft_again * (soft_grad - jnp.sum(soft_grad * soft_again, axis=-1, keepdims=True))
    ).astype(jnp.bfloat16)
    query_sums = (
        jnp.einsum("hncm,hnmd->hncd", score_grad, key_blocks, preferred_element_type=jnp.float32)
        * score_scale
    )
    key_sums = (
        jnp.einsum("hncm,hncd->hnmd", score_grad, query_blocks, preferred_element_type=jnp.float32)
        * score_scale
    )
    query_grad = from_clusters(query_sums)
    key_grad = from_clusters(key_sums)
    value_grad = from_clusters(value_sums)
    grad_bias_query = jnp.sum(query_grad.astype(jnp.float32), axis=0)
    grad_bias_value = jnp.sum(value_grad.astype(jnp.float32), axis=0)
    projected_grad = jnp.concatenate([query_grad, key_grad, value_grad], axis=1)
    grad_w_qkv = outer_sum(tokens, projected_grad)
    grad_tokens = times_back(projected_grad, back_qkv) + residual_grad
    grad_vectors = jnp.stack(
        [
            grad_bias_query,
            grad_bias_value,
            grad_bias_out,
            grad_gain_one,
            grad_shift_one,
            grad_bias_down,
            grad_gain_two,
            grad_shift_two,
        ]
    )
    grad_up_row = grad_bias_up[None, :]
    row_qkv, row_out, row_up, row_down, row_vectors, row_bias = (
        lax.psum_scatter(
            grad_w_qkv.astype(jnp.bfloat16), "dp", scatter_dimension=0, tiled=True
        ).astype(jnp.float32),
        lax.psum_scatter(
            grad_w_out.astype(jnp.bfloat16), "dp", scatter_dimension=0, tiled=True
        ).astype(jnp.float32),
        lax.psum_scatter(
            grad_w_up.astype(jnp.bfloat16), "dp", scatter_dimension=0, tiled=True
        ).astype(jnp.float32),
        lax.psum_scatter(
            grad_w_down.astype(jnp.bfloat16), "dp", scatter_dimension=0, tiled=True
        ).astype(jnp.float32),
        lax.psum_scatter(
            grad_vectors.astype(jnp.bfloat16), "dp", scatter_dimension=1, tiled=True
        ).astype(jnp.float32),
        lax.psum_scatter(
            grad_up_row.astype(jnp.bfloat16), "dp", scatter_dimension=1, tiled=True
        ).astype(jnp.float32),
    )
    shard_qkv, shard_out, shard_up, shard_down, shard_vectors, shard_bias = (
        lax.psum_scatter(
            row_qkv.astype(jnp.bfloat16), "mp", scatter_dimension=1, tiled=True
        ).astype(jnp.float32),
        lax.psum_scatter(
            row_out.astype(jnp.bfloat16), "mp", scatter_dimension=1, tiled=True
        ).astype(jnp.float32),
        lax.psum_scatter(row_up.astype(jnp.bfloat16), "mp", scatter_dimension=1, tiled=True).astype(
            jnp.float32
        ),
        lax.psum_scatter(
            row_down.astype(jnp.bfloat16), "mp", scatter_dimension=1, tiled=True
        ).astype(jnp.float32),
        lax.psum_scatter(
            row_vectors.astype(jnp.bfloat16), "mp", scatter_dimension=1, tiled=True
        ).astype(jnp.float32),
        lax.psum_scatter(
            row_bias.astype(jnp.bfloat16), "mp", scatter_dimension=1, tiled=True
        ).astype(jnp.float32),
    )
    return (
        layer_out,
        grad_tokens,
        shard_qkv,
        shard_vectors[0],
        shard_vectors[1],
        shard_out,
        shard_vectors[2],
        shard_vectors[3],
        shard_vectors[4],
        shard_up,
        shard_bias[0],
        shard_down,
        shard_vectors[5],
        shard_vectors[6],
        shard_vectors[7],
    )


LANES = 128
QKV_ROWS = 96
UP_TILES = 6
DOWN_TILES = 3
PACK_Q = 4 * QKV_ROWS + QKV_ROWS // 2 + 16
PACK_OU = QKV_ROWS + QKV_ROWS // 2 + UP_TILES * QKV_ROWS
PACK_D = DOWN_TILES * 192
VECTOR_ROW = 4 * QKV_ROWS + QKV_ROWS // 2
UP_ROW = QKV_ROWS + QKV_ROWS // 2


def whole():
    return pl.BlockSpec(memory_space=pltpu.VMEM)


def far():
    return pl.BlockSpec(memory_space=pltpu.HBM)


def kept_far(arrays):
    return [pltpu.with_memory_space_constraint(x, pltpu.HBM) for x in arrays]


def near(x):
    return pltpu.with_memory_space_constraint(x, pltpu.VMEM)


def near_shape(shape, dtype=jnp.bfloat16):
    return pltpu.VMEM(shape, dtype)


def waited(after):
    return [kept_far([x.token])[0] if isinstance(x, Results) else x for x in after]


def anywhere(after):
    return [far() if isinstance(x, Results) else pl.BlockSpec(memory_space=pl.ANY) for x in after]


class Results(list):
    token = None


TOKEN = pltpu.HBM((8, 128), jnp.float32)


def place():
    return lax.axis_index("dp"), lax.axis_index("mp")


SHORT = pl.CostEstimate(flops=1, bytes_accessed=1, transcendentals=0)
MICROSECOND = 1_153_000_000


class Place(tuple):
    def arrived(self, index, part=None):
        copies, here = self.late[index]
        for i in range(len(copies)) if part is None else [part]:
            if copies[i] is not None:
                copies[i].wait()
                copies[i] = None
        return here

    def send(self, index, where=None, source=None):
        here, there = self.far[index]
        source = here if source is None else source
        if where is not None:
            source, there = source.at[where], there.at[where]
        copy = pltpu.make_async_copy(source, there, self.sems.at[len(self.sent)])
        copy.start()
        self.sent.append(copy)


def call(
    body, out_shapes, operands, scratch=(), staged=0, late=(), far_outs=None, sends=None, after=(),
    aliases=None, vmem=10, cost=0, name=None,
):
    operands = operands[1:]
    far_outs = far_outs or {}
    sends = len(far_outs) if sends is None else sends
    count, outs, copied = len(operands), len(out_shapes), staged + len(late)
    spread = [(0, 1)] * staged + [x or (0, 1) for x in late]
    starts = [sum(n for _, n in spread[:i]) for i in range(copied)]

    def with_copies(*refs):
        sources, rest = refs[:copied], refs[copied:count]
        results = list(refs[count + len(after) : count + len(after) + outs])
        own = refs[count + len(after) + outs + 1 :]
        mine, own = own[: len(scratch)], own[len(scratch) :]
        arrived, own = own[:copied], list(own[copied:])
        me = Place(place())
        me.sent, me.far = [], {}
        if copied:
            sem = own.pop(0)
            copies = []
            for source, here, (axis, parts), start in zip(sources, arrived, spread, starts):
                size = here.shape[axis] // parts
                copies.append([])
                for i in range(parts):
                    cut = (slice(None),) * axis + (slice(i * size, (i + 1) * size),)
                    copies[-1].append(
                        pltpu.make_async_copy(source.at[cut], here.at[cut], sem.at[start + i])
                    )
            for copy in sum(copies, []):
                copy.start()
            for (copy,) in copies[:staged]:
                copy.wait()
            me.late = list(zip(copies[staged:], arrived[staged:]))
        if far_outs:
            me.sems = own.pop(0)
            for index, has_room in far_outs.items():
                here = own.pop(0) if has_room else None
                me.far[index] = (here, results[index])
                results[index] = here
        body(me, *arrived[:staged], *rest, *results, *mine)
        for copy in me.sent:
            copy.wait()

    room = [pltpu.VMEM(x.shape, x.dtype) for x in operands[:copied]]
    if copied:
        room.append(pltpu.SemaphoreType.DMA((sum(n for _, n in spread),)))
    if far_outs:
        room.append(pltpu.SemaphoreType.DMA((sends,)))
        room += [pltpu.VMEM(out_shapes[i].shape, out_shapes[i].dtype) for i in far_outs if far_outs[i]]
    given = [
        pltpu.HBM(x.shape, x.dtype) if i in far_outs else x for i, x in enumerate(out_shapes)
    ]
    *results, token = pl.pallas_call(
        with_copies,
        out_shape=[*given, TOKEN],
        in_specs=[pl.BlockSpec(memory_space=pl.ANY)] * staged
        + [far()] * len(late)
        + [whole()] * (count - copied)
        + anywhere(after),
        out_specs=[far() if i in far_outs else whole() for i in range(outs)] + [far()],
        scratch_shapes=list(scratch) + room,
        input_output_aliases=aliases or {},
        compiler_params=pltpu.CompilerParams(vmem_limit_bytes=vmem * 1024 * 1024),
        cost_estimate=SHORT if not cost else pl.CostEstimate(cost, 1, 0),
        name=name,
    )(
        *operands[:staged],
        *kept_far(operands[staged:copied]),
        *operands[copied:],
        *waited(after),
    )
    results = Results(results)
    results.token = token
    return results


def tie(arrays, after):
    count = len(arrays)

    def body(*refs):
        pass

    return pl.pallas_call(
        body,
        out_shape=[shape_of(x.shape, x.dtype) for x in arrays],
        in_specs=[pl.BlockSpec(memory_space=pl.ANY)] * count + anywhere(after),
        out_specs=[pl.BlockSpec(memory_space=pl.ANY)] * count,
        input_output_aliases={i: i for i in range(count)},
        compiler_params=pltpu.CompilerParams(vmem_limit_bytes=1024 * 1024),
        cost_estimate=SHORT,
        name="tie",
    )(*arrays, *waited(after))


def shape_of(shape, dtype=jnp.bfloat16):
    return jax.ShapeDtypeStruct(shape, dtype)


def halves_beside(single):
    half = single.shape[0] // 2
    return jnp.concatenate([single[:half], single[half:]], axis=1)


def pack_columns(odd, low, tiles, base, target):
    @pl.when(odd)
    def _():
        for t in range(tiles):
            target[base + t * 96 : base + (t + 1) * 96, :] = low[
                :, 64 + t * LANES : 64 + (t + 1) * LANES
            ].astype(jnp.bfloat16)
        target[base + tiles * 96 : base + tiles * 96 + 48, :] = halves_beside(low[:, :64]).astype(
            jnp.bfloat16
        )

    @pl.when(jnp.logical_not(odd))
    def _():
        for t in range(tiles):
            target[base + t * 96 : base + (t + 1) * 96, :] = low[
                :, t * LANES : (t + 1) * LANES
            ].astype(jnp.bfloat16)
        target[base + tiles * 96 : base + tiles * 96 + 48, :] = halves_beside(
            low[:, tiles * LANES : tiles * LANES + 64]
        ).astype(jnp.bfloat16)


def pack_q_body(me, *refs):
    w_qkv, vectors, target, own = refs[0], refs[1:10], refs[10], refs[11]
    pack_columns(lax.rem(me[1], 2) == 1, w_qkv[...], 4, 0, target)
    rows = lax.broadcasted_iota(jnp.int32, (16, LANES), 0)
    tail = jnp.zeros((16, LANES), jnp.float32)
    for v in range(9):
        value = vectors[v][...]
        wide = jnp.concatenate(
            [value, jnp.zeros((1, LANES - value.shape[1]), jnp.float32)], axis=1
        )
        tail = jnp.where(rows == v, jnp.broadcast_to(wide, (16, LANES)), tail)
    target[VECTOR_ROW:, :] = tail.astype(jnp.bfloat16)
    me.send(0)
    own[...] = target[...]


def pack_q(me, w_qkv, vectors, bias_up):
    small = [v.reshape(1, -1) for v in (*vectors, bias_up)]
    return call(
        pack_q_body, [shape_of((PACK_Q, LANES))] * 2, [me, *kept_far([w_qkv, *small])], staged=10, far_outs={0: True},
        name="pack_q",
    )


def pack_rest_body(me, w_out, w_up, w_down, to_ou, to_d):
    for t in range(DOWN_TILES):
        to_d[t * 192 : (t + 1) * 192, :] = w_down[:, t * LANES : (t + 1) * LANES].astype(
            jnp.bfloat16
        )
    me.send(1)
    pack_columns(lax.rem(me[1], 2) == 1, w_out[...], 1, 0, to_ou)
    for t in range(UP_TILES):
        to_ou[UP_ROW + t * 96 : UP_ROW + (t + 1) * 96, :] = w_up[
            :, t * LANES : (t + 1) * LANES
        ].astype(jnp.bfloat16)
    me.send(0)


def pack_rest(me, w_out, w_up, w_down, after):
    return call(
        pack_rest_body,
        [
            shape_of((PACK_OU, LANES)),
            shape_of((PACK_D, LANES)),
        ],
        [me, *kept_far([w_out, w_up, w_down.T])],
        staged=3,
        far_outs={0: True, 1: True},
        after=after,
        name="pack_rest",
    )


def swap(x, axis, bit):
    size = lax.axis_size(axis)
    return lax.ppermute(x, axis, [(i, i ^ bit) for i in range(size)])


CORE, ALONG_X, ALONG_Y = 1, 2, 4


def gather_z(x, own=None):
    return [x if own is None else own] + [swap(x, "mp", k) for k in (1, 2, 3)]


def beside(me, groups, shapes, after=(), name="beside"):
    sources = []
    for x, _ in groups:
        if all(x is not y for y in sources):
            sources.append(x)

    def body(me, *refs):
        for x, (index, where) in groups:
            source = refs[next(n for n, y in enumerate(sources) if x is y)]
            refs[len(sources) + index][where] = source[...]

    return call(body, [shape_of(s) for s in shapes], [me, *sources], after=after, name=name)


def beside_two(me, a, b, after=()):
    return beside(me, [(a, (0, 0)), (b, (0, 1))], [(2, *a.shape)], after, "beside_two")


def gather_near(me, parts, after=()):
    shape = (2, *parts[0].shape)
    found = beside(
        me,
        [(parts[0], (0, 0)), (parts[1], (0, 1)), (parts[2], (1, 0)), (parts[3], (1, 1))],
        [shape, shape],
        after,
        "beside_z",
    )
    first, second = found
    result = Results([first, swap(first, "dp", ALONG_X), second, swap(second, "dp", ALONG_Y)])
    result.token = found.token
    return result


def gather_far(me, parts, after=()):
    shape = (2, *parts[0].shape)
    groups = [(parts[i], (i // 2, i % 2)) for i in range(4)]
    groups += [(parts[i], (2, (i // 2, i % 2))) for i in range(4)]
    found = beside(me, groups, [shape, shape, (2, *shape)], after, "beside_near")
    first, second, both = found
    result = Results([both, swap(first, "dp", ALONG_Y), swap(second, "dp", ALONG_X)])
    result.token = found.token
    return result


def gather_core(parts):
    return list(parts) + [swap(x, "dp", CORE) for x in parts]


def gathered_blocks(me, refs):
    for core in range(2):
        for kind, ref in enumerate(refs[3 * core : 3 * core + 3]):
            for mid in range(2):
                for low in range(2):
                    if kind == 0:
                        found = (
                            (mid, 0, low, ref.at[0, mid, low]), (0, mid, 2 + low, ref.at[1, mid, low])
                        )
                    elif kind == 1:
                        found = ((mid, 1, low, ref.at[mid, low]),)
                    else:
                        found = ((1, mid, 2 + low, ref.at[mid, low]),)
                    for kx, ky, kz, block in found:
                        yield me[0] ^ (core + 2 * kx + 4 * ky), me[1] ^ kz, block


def place_columns(block, base, tiles, dp, mp, width, weights, singles):
    start = pl.multiple_of(mp * width + 64 * lax.rem(mp, 2), LANES)
    rows = pl.ds(pl.multiple_of(dp * 96, 32), 96)
    for t in range(tiles):
        weights[rows, pl.ds(pl.multiple_of(start + t * LANES, LANES), LANES)] = block[
            base + t * 96 : base + (t + 1) * 96, :
        ]
    singles[mp, pl.ds(pl.multiple_of(dp * 48, 16), 48), :] = block[
        base + tiles * 96 : base + tiles * 96 + 48, :
    ]


def place_singles(width, weights, singles):
    for pair in range(2):
        column = 2 * pair * width + (width // LANES) * LANES
        for dp in range(8):
            left = singles[2 * pair, dp * 48 : (dp + 1) * 48, :].astype(jnp.float32)
            right = singles[2 * pair + 1, dp * 48 : (dp + 1) * 48, :].astype(jnp.float32)
            upper = jnp.concatenate([left[:, :64], right[:, :64]], axis=1)
            lower = jnp.concatenate([left[:, 64:], right[:, 64:]], axis=1)
            weights[dp * 96 : dp * 96 + 48, column : column + LANES] = upper.astype(jnp.bfloat16)
            weights[dp * 96 + 48 : (dp + 1) * 96, column : column + LANES] = lower.astype(
                jnp.bfloat16
            )


def unpack_q_body(me, *refs):
    blocks, weights, vectors, bias_up, singles, tails = refs[:6], *refs[6:]
    for dp, mp, block in gathered_blocks(me, blocks):
        place_columns(block, 0, 4, dp, mp, 576, weights, singles)
        tails[dp * 4 + mp] = block[VECTOR_ROW:, :].astype(jnp.float32)
    place_singles(576, weights, singles)
    lane = lax.broadcasted_iota(jnp.int32, (16, LANES), 1)

    def spread(width, count):
        found = [jnp.zeros((16, LANES), jnp.float32) for _ in range(count)]
        for device in range(32):
            start, tile = device * width % LANES, device * width // LANES
            piece = tails[device]
            moved = pltpu.roll(piece, start, axis=1) if start else piece
            found[tile] = jnp.where((lane >= start) & (lane < start + width), moved, found[tile])
            if start + width > LANES:
                found[tile + 1] = jnp.where(lane < start + width - LANES, moved, found[tile + 1])
        return found

    for t, value in enumerate(spread(24, 6)):
        vectors[:, t * LANES : (t + 1) * LANES] = value[:8]
    for t, value in enumerate(spread(96, 24)):
        bias_up[:, t * LANES : (t + 1) * LANES] = value[8:9]


def unpack_ou_body(me, *refs):
    blocks, w_out, w_up, singles = refs[:6], *refs[6:]
    for dp, mp, block in gathered_blocks(me, blocks):
        place_columns(block, 0, 1, dp, mp, 192, w_out, singles)
        rows = pl.ds(pl.multiple_of(dp * 96, 32), 96)
        for t in range(UP_TILES):
            w_up[rows, pl.ds(pl.multiple_of(mp * 768 + t * LANES, LANES), LANES)] = block[
                UP_ROW + t * 96 : UP_ROW + (t + 1) * 96, :
            ]
    place_singles(192, w_out, singles)


def unpack_ou(me, parts, after=()):
    return call(
        unpack_ou_body,
        [near_shape((768, 768)), near_shape((768, 3072))],
        [me, *parts],
        [pltpu.VMEM((4, 384, LANES), jnp.bfloat16)],
        after=after,
        name="unpack_ou",
    )


def unpack_d_body(me, *refs):
    blocks, turned = refs[:6], refs[6]
    for dp, mp, block in gathered_blocks(me, blocks):
        rows = pl.ds(pl.multiple_of(mp * 192, 64), 192)
        for t in range(DOWN_TILES):
            turned[rows, pl.ds(pl.multiple_of(dp * 384 + t * LANES, LANES), LANES)] = block[
                t * 192 : (t + 1) * 192, :
            ]


def unpack_d(me, parts, after=()):
    return call(
        unpack_d_body, [near_shape((768, 3072))], [me, *parts], after=after, name="unpack_d"
    )


def turn_body(me, source, send, keep, turned):
    value = source[...].T
    for dp in range(8):
        k = me[0] ^ dp
        slot = (1 - (k & 1)) * 4 + (k >> 1)
        turned[pl.ds(pl.multiple_of(slot * 96, 32), 96), :] = value[dp * 96 : (dp + 1) * 96, :]
    send[...] = turned[:384, :]
    keep[...] = turned[384:, :]


def turn(me, source, after=()):
    n = source.shape[0]
    return call(
        turn_body,
        [shape_of((384, n)), near_shape((384, n))],
        [me, source],
        [pltpu.VMEM((768, n), jnp.bfloat16)],
        after=after,
        name="turn",
    )


def dot(a, b):
    return jnp.dot(a, b, preferred_element_type=jnp.float32)


def dot_nt(a, b):
    return lax.dot_general(a, b, (((1,), (1,)), ((), ())), preferred_element_type=jnp.float32)


def dot_tn(a, b):
    return lax.dot_general(a, b, (((0,), (0,)), ((), ())), preferred_element_type=jnp.float32)


def part_of(targets, kp, mp):
    ky, kx = kp // 2, kp % 2
    if mp < 2:
        return targets[ky].at[kx, mp]
    return targets[2 + kx].at[ky, mp - 2]


def store_columns(target, base, tiles, first, value):
    for t in range(tiles):
        target[base + t * 96 : base + (t + 1) * 96, :] = value[
            :, first + t * LANES : first + (t + 1) * LANES
        ].astype(jnp.bfloat16)


def store_single(target, base, odd, value):
    upper, lower = value[:48], value[48:]
    low_lanes = lax.broadcasted_iota(jnp.int32, (48, LANES), 1) < 64
    if odd:
        both = jnp.where(low_lanes, pltpu.roll(upper, 64, axis=1), lower)
    else:
        both = jnp.where(low_lanes, upper, pltpu.roll(lower, 64, axis=1))
    target[base : base + 48, :] = both.astype(jnp.bfloat16)


def column_gradient(lefts, rights, targets, base, tiles, width):
    def product(columns):
        return dot(lefts[0], rights[0][:, columns]) + dot(lefts[1], rights[1][:, columns])

    for pair in range(2):
        first = 2 * pair * width
        middle = first + tiles * LANES
        for begin, mp in ((first, 2 * pair), (middle + LANES, 2 * pair + 1)):
            value = product(slice(begin, begin + tiles * LANES))
            for kp in range(4):
                store_columns(
                    part_of(targets, kp, mp), base, tiles, 0, value[kp * 96 : (kp + 1) * 96]
                )
        value = product(slice(middle, middle + LANES))
        for kp in range(4):
            for mp in (2 * pair, 2 * pair + 1):
                store_single(
                    part_of(targets, kp, mp), base + tiles * 96, mp % 2,
                    value[kp * 96 : (kp + 1) * 96],
                )


def parts_shape(rows):
    return [near_shape((2, 2, rows, LANES)), shape_of((2, 2, rows, LANES))] * 2


def gradient_q_body(me, keep, other_keep, grads, other_grads, vectors, other_vectors, *targets):
    lefts, rights = (keep[...], other_keep[...]), (grads, other_grads)
    column_gradient(lefts, rights, targets, 0, 4, 576)
    sums = vectors[...] + other_vectors[...]
    lane = lax.broadcasted_iota(jnp.int32, (16, LANES), 1)
    rows = lax.broadcasted_iota(jnp.int32, (16, LANES), 0)

    def cut(source, width, device):
        start, tile = device * width % LANES, device * width // LANES
        value = source[:, tile * LANES : (tile + 1) * LANES]
        moved = pltpu.roll(value, LANES - start, axis=1) if start else value
        if start + width > LANES:
            after = source[:, (tile + 1) * LANES : (tile + 2) * LANES]
            after = pltpu.roll(after, LANES - start, axis=1)
            here = lax.broadcasted_iota(jnp.int32, value.shape, 1)
            moved = jnp.where(here < LANES - start, moved, after)
        return moved

    for kp in range(4):
        plane = (me[0] >> 1) ^ kp
        for mp in range(4):
            tail = jnp.zeros((16, LANES), jnp.float32)
            for dp in range(8):
                device = dp * 4 + mp
                row = 8 + device // 8
                up = jnp.broadcast_to(cut(sums[row : row + 1], 96, device % 8), (8, LANES))
                found = jnp.concatenate([cut(sums[:8], 24, device), up], axis=0)
                mine = dp == 2 * plane + (me[0] & 1)
                tail = jnp.where(mine, found, tail)
            tail = jnp.where((rows < 8) & (lane >= 24), 0.0, tail).astype(jnp.bfloat16)
            part_of(targets, kp, mp)[VECTOR_ROW:, :] = tail


def gradient_q(me, keep, other_keep, grads, other_grads, vectors, other_vectors, after=()):
    return call(
        gradient_q_body,
        parts_shape(PACK_Q),
        [me, keep, other_keep, grads, other_grads, vectors, other_vectors],
        after=after,
        name="gradient_q",
    )


def gradient_ou_body(me, *refs):
    combined, first_low, hidden_grad = (refs[i : i + 2] for i in (0, 2, 4))
    attention_grad, targets, room = (refs[6], refs[13]), refs[9:13], refs[13]
    room[:, :384] = refs[7][...]
    room[:, 384:] = refs[8][...]
    column_gradient([x[...] for x in combined], attention_grad, targets, 0, 1, 192)
    lefts = [x[...] for x in first_low]
    for mp in range(4):
        columns = slice(mp * 768, (mp + 1) * 768)
        value = dot(lefts[0], hidden_grad[0][:, columns])
        value = value + dot(lefts[1], hidden_grad[1][:, columns])
        for kp in range(4):
            store_columns(
                part_of(targets, kp, mp), UP_ROW, UP_TILES, 0, value[kp * 96 : (kp + 1) * 96]
            )


def gradient_ou(me, combined, first_low, hidden_grad, attention_grad, after=()):
    return call(
        gradient_ou_body,
        parts_shape(PACK_OU),
        [me, *combined, *first_low, *hidden_grad, *attention_grad],
        [pltpu.VMEM(attention_grad[0].shape, jnp.bfloat16)],
        after=after,
        name="gradient_ou",
    )


def gradient_d_body(me, feed_grad, other_feed_grad, activated, other_activated, *refs):
    targets, turned, other_turned = refs[:4], refs[4], refs[5]
    turned[...] = feed_grad[...].T
    other_turned[...] = other_feed_grad[...].T
    for kp in range(4):
        dp = me[0] ^ (2 * kp)
        block = activated[:, pl.ds(pl.multiple_of(dp * 384, LANES), 384)]
        value = dot(turned[...], block)
        value = value + dot(other_turned[...], other_activated[:, kp * 384 : (kp + 1) * 384])
        for mp in range(4):
            target = part_of(targets, kp, mp)
            for t in range(DOWN_TILES):
                target[t * 192 : (t + 1) * 192, :] = value[
                    mp * 192 : (mp + 1) * 192, t * LANES : (t + 1) * LANES
                ].astype(jnp.bfloat16)


def gradient_d(me, feed_grad, other_feed_grad, activated, other_activated, after=()):
    return call(
        gradient_d_body,
        parts_shape(PACK_D),
        [me, feed_grad, other_feed_grad, activated, other_activated],
        [pltpu.VMEM((768, feed_grad.shape[0]), jnp.bfloat16)] * 2,
        after=after,
        name="gradient_d",
    )


def sums_body(me, bias, one, two, up, out):
    out[0:2, :], out[2:5, :], out[5:8, :] = bias[...], one[...], two[...]
    for i in range(4):
        out[8 + i : 9 + i, :] = up[:, i * 768 : (i + 1) * 768]


def all_sums(me, *sums):
    return call(sums_body, [shape_of((12, 768), jnp.float32)], [me, *sums], name="sums")[0]


def add(a, b):
    return a.astype(jnp.float32) + b.astype(jnp.float32)


def add_plane_body(me, first, first_in, second, second_in, *outs):
    for keep, send, a, b in ((*outs[:2], first, first_in), (*outs[2:], second, second_in)):
        keep[...] = add(a[0], b[0]).astype(jnp.bfloat16)
        send[...] = add(a[1], b[1]).astype(jnp.bfloat16)


def add_last_body(me, first, first_in, second, second_in, *refs):
    keep, send, room = refs
    for mp in range(4):
        a, b = (first, first_in) if mp < 2 else (second, second_in)
        room[me[1] ^ mp] = add(a[mp % 2], b[mp % 2]).astype(jnp.bfloat16)
    for k in range(4):
        (send if k % 2 else keep)[k // 2] = room[k]


def add_z_body(me, mine, arrived, keep, send):
    keep[...] = add(mine[0], arrived[0])
    send[...] = add(mine[1], arrived[1]).astype(jnp.bfloat16)


def scatter_near(parts):
    first, first_send, second, second_send = parts
    return first, swap(first_send, "dp", ALONG_Y), second, swap(second_send, "dp", ALONG_X)


def add_plane(me, parts, after=()):
    rows = parts[0].shape[2]
    return call(
        add_plane_body,
        [near_shape((2, rows, LANES)), shape_of((2, rows, LANES))] * 2,
        [me, *parts],
        after=after,
        name="add_plane",
    )


def scatter_far(parts):
    first, first_send, second, second_send = parts
    return first, swap(first_send, "dp", ALONG_X), second, swap(second_send, "dp", ALONG_Y)


def add_last(me, parts, after=(), cost=0):
    rows = parts[0].shape[1]
    return call(
        add_last_body,
        [near_shape((2, rows, LANES)), shape_of((2, rows, LANES))],
        [me, *parts],
        [pltpu.VMEM((4, rows, LANES), jnp.bfloat16)],
        after=after,
        cost=cost,
        name="add_last",
    )


def scatter_z(parts):
    return parts[0], swap(parts[1], "mp", 1)


def add_z(me, parts, after=()):
    rows = parts[0].shape[1]
    return call(
        add_z_body,
        [near_shape((rows, LANES), jnp.float32), shape_of((rows, LANES))],
        [me, *parts],
        after=after,
        name="add_z",
    )


def scatter_z_far(parts):
    return parts[0], swap(parts[1], "mp", 2)


def total(refs, rows):
    value = refs[0][rows, :].astype(jnp.float32)
    for ref in refs[1:]:
        value = value + ref[rows, :].astype(jnp.float32)
    return value


def finish_columns(me, refs, base, tiles, out):
    odd = lax.rem(me[1], 2) == 1
    full = [total(refs, pl.ds(base + t * 96, 96)) for t in range(tiles)]
    single = total(refs, pl.ds(base + tiles * 96, 48))
    single = jnp.concatenate([single[:, :64], single[:, 64:]], axis=0)

    @pl.when(odd)
    def _():
        out[...] = jnp.concatenate([single, *full], axis=1)

    @pl.when(jnp.logical_not(odd))
    def _():
        out[...] = jnp.concatenate([*full, single], axis=1)


def finish_q_body(me, *refs):
    parts, out, outs = refs[:2], refs[2], refs[3:]
    finish_columns(me, parts, 0, 4, out)
    tail = total(parts, pl.ds(VECTOR_ROW, 16))
    for v in range(8):
        outs[v][...] = tail[v : v + 1, :24]
    outs[8][...] = tail[8:9, :96]


def finish_q(me, parts):
    f = jnp.float32
    return call(
        finish_q_body,
        [shape_of((96, 576), f)] + [shape_of((1, 24), f)] * 8 + [shape_of((1, 96), f)],
        [me, *parts],
        name="finish_q",
    )


def finish_ou_body(me, *refs):
    parts, w_out, w_up = refs[:2], refs[2], refs[3]
    finish_columns(me, parts, 0, 1, w_out)
    for t in range(UP_TILES):
        w_up[:, t * LANES : (t + 1) * LANES] = total(parts, pl.ds(UP_ROW + t * 96, 96))


def finish_ou(me, parts):
    f = jnp.float32
    return call(
        finish_ou_body, [shape_of((96, 192), f), shape_of((96, 768), f)], [me, *parts],
        name="finish_ou",
    )


def finish_d_body(me, *refs):
    parts, out = refs[:2], refs[2]
    for t in range(DOWN_TILES):
        out[:, t * LANES : (t + 1) * LANES] = total(parts, pl.ds(t * 192, 192))


def finish_d(me, parts, after=()):
    f = jnp.float32
    return call(finish_d_body, [shape_of((192, 384), f)], [me, *parts], after=after, name="finish_d")


PAIRS = HEADS // 2


def iota(shape, axis):
    return lax.broadcasted_iota(jnp.int32, shape, axis)


def place_matrix(order, head):
    length = order.shape[1]
    row = order[head : head + 1, :].astype(jnp.int16)
    token = iota((length, length), 0).astype(jnp.int16)
    return jnp.where(token == row, jnp.bfloat16(1.0), jnp.bfloat16(0.0))


def project_body(me, *refs):
    blocks, tokens = refs[:6], refs[6]
    weights, vectors, bias_up, qkv, singles, tails = refs[7:]
    unpack_q_body(me, *blocks, weights, vectors, bias_up, singles, tails)
    for c in range(9):
        columns = slice(c * 256, (c + 1) * 256)
        value = dot(tokens[...], weights[:, columns])
        if c < 3:
            value = value + vectors[0:1, c * 256 : (c + 1) * 256]
        elif c >= 6:
            value = value + vectors[1:2, (c - 6) * 256 : (c - 5) * 256]
        qkv[:, columns] = value.astype(jnp.bfloat16)


def project(me, parts, tokens, after=()):
    return call(
        project_body,
        [
            near_shape((768, 2304)),
            near_shape((8, 768), jnp.float32),
            near_shape((1, 3072), jnp.float32),
            near_shape((tokens.shape[0], 2304)),
        ],
        [me, *parts, tokens],
        [pltpu.VMEM((4, 384, LANES), jnp.bfloat16), pltpu.VMEM((32, 16, LANES), jnp.float32)],
        after=after,
        name="project",
    )


def attend_body(first_pair, pairs, me, qkv, order, facts, *refs):
    swapped, values, soft, combined = refs[-4:]
    length = qkv.shape[0]
    groups = length // CLUSTER
    blocks = [slice(g * CLUSTER, (g + 1) * CLUSTER) for g in range(groups)]
    low = iota((length, LANES), 1) < 64
    itself = iota((CLUSTER, CLUSTER), 0) == iota((CLUSTER, CLUSTER), 1)
    pick = [
        jnp.where(iota((16, LANES), 1) == lane, 1.0, 0.0).astype(jnp.bfloat16) for lane in (64, 0)
    ]
    scale = HEAD_DIM ** (-0.5)

    for place in range(pairs):
        pair = first_pair + place

        def columns(base, pair=pair):
            return slice(base + pair * LANES, base + (pair + 1) * LANES)

        query = qkv[:, columns(0)].astype(jnp.float32)
        keys = qkv[:, columns(768)].astype(jnp.float32)
        value = qkv[:, columns(1536)].astype(jnp.float32)
        known = facts[...]
        tiles = (
            (jnp.where(low, query, pltpu.roll(keys, 64, axis=1)), jnp.where(low, value, known)),
            (jnp.where(low, pltpu.roll(query, 64, axis=1), keys), jnp.where(low, known, value)),
        )
        moved, to_tokens = [], []
        for h in range(2):
            back = place_matrix(order, 2 * pair + h)
            to_tokens.append(back)
            tile = jnp.concatenate([t.astype(jnp.bfloat16) for t in tiles[h]], axis=1)
            moved.append(dot_tn(back, tile))
        query_slots, key_slots, value_slots, codes, rows_of = [], [], [], [], []
        for h in range(2):
            both = moved[h][:, :LANES]
            query_slots.append(jnp.where(low, both, 0.0).astype(jnp.bfloat16))
            key_slots.append(pltpu.roll(both, 64, axis=1).astype(jnp.bfloat16))
            value_slots.append(moved[h][:, LANES:].astype(jnp.bfloat16))
            swapped[2 * place + h] = key_slots[h]
            values[2 * place + h] = value_slots[h]
            lane = 64 * (1 - h)
            code = moved[h][:, LANES + lane : LANES + lane + 1]
            row = dot_nt(pick[h], value_slots[h])[0:1]
            codes.append(jnp.where(code >= 32.0, code - 32.0, code))
            rows_of.append(row)
        scores = [
            [dot_nt(query_slots[h][b], key_slots[h][b]) for b in blocks] for h in range(2)
        ]
        found = []
        for h in range(2):
            outs = []
            for g, b in enumerate(blocks):
                allowed = (codes[h][b] == rows_of[h][:, b]) | itself
                value = jnp.where(allowed, scores[h][g] * scale, masked_score)
                value = jnp.exp(value - jnp.max(value, axis=1, keepdims=True))
                weights = value / jnp.sum(value, axis=1, keepdims=True)
                soft[2 * place + h, b, :] = weights
                outs.append(weights.astype(jnp.bfloat16))
            found.append(
                [dot(outs[g], value_slots[h][b]) for g, b in enumerate(blocks)]
            )
        result = None
        for h in range(2):
            value = jnp.concatenate(found[h], axis=0)
            value = jnp.where(low if h == 0 else jnp.logical_not(low), value, 0.0)
            value = dot(to_tokens[h], value.astype(jnp.bfloat16))
            result = value if result is None else result + value
        combined[:, columns(0)] = result.astype(jnp.bfloat16)


def attend(me, qkv, order, facts, first_pair, pairs, combined=None, after=()):
    length = qkv.shape[0]
    operands = [me, qkv, order, facts]
    if combined is not None:
        operands.append(combined)
    return call(
        functools.partial(attend_body, first_pair, pairs),
        [
            near_shape((2 * pairs, length, LANES)),
            near_shape((2 * pairs, length, LANES)),
            near_shape((2 * pairs, length, CLUSTER), jnp.float32),
            near_shape((length, 768)),
        ],
        operands,
        after=after,
        aliases={3: 3} if combined is not None else None,
        name="attend",
    )


def by_rows(first, count, step, body):
    for i in range(first, first + count, step):
        body(slice(i, i + step))


def mean(value):
    return jnp.mean(value, axis=1, keepdims=True)


def fold(value):
    return jnp.sum(value.reshape(value.shape[0] // 8, 8, value.shape[1]), axis=0)


def out_norm_body(me, combined, w_out, tokens, vectors, first_low, normal, inverse, total_ref):

    def rows_of(rows):
        value = total_ref[rows, :] + vectors[2:3] + tokens[rows, :].astype(jnp.float32)
        centred = value - mean(value)
        scale = lax.rsqrt(mean(centred * centred) + epsilon)
        norm = centred * scale
        normal[rows, :] = norm
        inverse[rows, :] = jnp.broadcast_to(scale, (scale.shape[0], LANES))
        first_low[rows, :] = (norm * vectors[3:4] + vectors[4:5]).astype(jnp.bfloat16)

    half = tokens.shape[0] // 2
    for first in (0, half):
        rows = slice(first, first + half)
        total_ref[rows, :] = dot(combined[rows, :], w_out[...])
        by_rows(first, half, 32, rows_of)


def out_norm(me, combined, w_out, tokens, vectors, after=()):
    n = tokens.shape[0]
    f = jnp.float32
    return call(
        out_norm_body,
        [near_shape((n, 768)), near_shape((n, 768), f), near_shape((n, LANES), f)],
        [me, combined, w_out, tokens, vectors],
        [pltpu.VMEM((n, 768), jnp.float32)],
        after=after,
        name="out_norm",
    )


def up_body(me, first_low, w_up, bias_up, activated, slope, send):
    width = w_up.shape[1] // 8
    for i in range(8):
        columns = slice(i * width, (i + 1) * width)
        hidden = dot(first_low[...], w_up[:, columns]) + bias_up[:, columns]
        half = 0.5 + 0.5 * lax.erf(hidden * (0.5**0.5))
        low = (hidden * half).astype(jnp.bfloat16)
        activated[:, columns] = low
        bell = jnp.exp(-0.5 * hidden * hidden) * (2.0 * math.pi) ** (-0.5)
        slope[:, columns] = (half + hidden * bell).astype(jnp.bfloat16)
    for i in range(8):
        k = me[0] ^ i

        @pl.when((k & 1) == 1)
        def _():
            there = pl.ds(pl.multiple_of((k >> 1) * width, LANES), width)
            send[:, there] = activated[:, i * width : (i + 1) * width]


def up(me, first_low, w_up, bias_up, after=()):
    n, width = first_low.shape[0], w_up.shape[1]
    return call(
        up_body,
        [near_shape((n, width)), near_shape((n, width)), shape_of((n, width // 2))],
        [me, first_low, w_up, bias_up],
        after=after,
        name="up",
    )


def down_norm_body(
    me, activated, turned, normal, vectors, out, feed_grad, second_grad, sums, feed, acc
):
    acc[...] = jnp.zeros_like(acc)

    def rows_of(rows):
        value = normal[rows, :] * vectors[3:4] + vectors[4:5] + feed[rows, :] + vectors[5:6]
        centred = value - mean(value)
        inverse = lax.rsqrt(mean(centred * centred) + epsilon)
        norm = centred * inverse
        out[rows, :] = (norm * vectors[6:7] + vectors[7:8]).astype(jnp.bfloat16)
        upstream = me.arrived(0)[rows, :]
        scaled = upstream * vectors[6:7]
        back = inverse * (scaled - mean(scaled) - norm * mean(scaled * norm))
        second_grad[rows, :] = back
        low = back.astype(jnp.bfloat16)
        feed_grad[rows, :] = low
        acc[0] += fold(low.astype(jnp.float32))
        acc[1] += fold(upstream * norm)
        acc[2] += fold(upstream)

    half = out.shape[0] // 2
    for first in (0, half):
        rows = slice(first, first + half)
        feed[rows, :] = dot_nt(activated[rows, :], turned[...])
        by_rows(first, half, 32, rows_of)
    me.send(0)
    for i in range(3):
        sums[i : i + 1, :] = jnp.sum(acc[i], axis=0, keepdims=True)


def down_norm(me, activated, turned, normal, vectors, cotangent, after=()):
    n = cotangent.shape[0]
    return call(
        down_norm_body,
        [
            shape_of((n, 768)),
            near_shape((n, 768)),
            near_shape((n, 768), jnp.float32),
            near_shape((3, 768), jnp.float32),
        ],
        [me, cotangent, activated, turned, normal, vectors],
        [pltpu.VMEM((n, 768), jnp.float32), pltpu.VMEM((3, 8, 768), jnp.float32)],
        late=[None],
        far_outs={0: True},
        after=after,
        name="down_norm",
    )


def hidden_back_body(me, feed_grad, turned, slope, hidden_grad, sums):
    for i in range(hidden_grad.shape[1] // 256):
        columns = slice(i * 256, (i + 1) * 256)
        value = dot(feed_grad[...], turned[:, columns]) * slope[:, columns].astype(jnp.float32)
        low = value.astype(jnp.bfloat16)
        hidden_grad[:, columns] = low
        sums[:, columns] = jnp.sum(low.astype(jnp.float32), axis=0, keepdims=True)


def hidden_back(me, feed_grad, turned, slope, after=()):
    return call(
        hidden_back_body,
        [near_shape(slope.shape), near_shape((1, slope.shape[1]), jnp.float32)],
        [me, feed_grad, turned, slope],
        after=after,
        name="hidden_back",
    )


def first_back_body(
    me, hidden_grad, w_up, second_grad, normal, inverse, vectors, residual, low_out, left, right, sums, back,
    acc,
):
    acc[...] = jnp.zeros_like(acc)

    def rows_of(rows):
        upstream = back[rows, :] + second_grad[rows, :]
        norm = normal[rows, :]
        scaled = upstream * vectors[3:4]
        value = inverse[rows, 0:1] * (scaled - mean(scaled) - norm * mean(scaled * norm))
        residual[rows, :] = value
        low = value.astype(jnp.bfloat16)
        low_out[rows, :] = low
        left[rows, :] = low[:, :384]
        right[rows, :] = low[:, 384:]
        acc[0] += fold(low.astype(jnp.float32))
        acc[1] += fold(upstream * norm)
        acc[2] += fold(upstream)

    half = normal.shape[0] // 2
    for first in (0, half):
        rows = slice(first, first + half)
        back[rows, :] = dot_nt(hidden_grad[rows, :], w_up[...])
        by_rows(first, half, 32, rows_of)
    for i in range(3):
        sums[i : i + 1, :] = jnp.sum(acc[i], axis=0, keepdims=True)


def first_back(me, hidden_grad, w_up, second_grad, normal, inverse, vectors, after=()):
    n = normal.shape[0]
    return call(
        first_back_body,
        [
            near_shape((n, 768), jnp.float32),
            near_shape((n, 768)),
            shape_of((n, 384)),
            shape_of((n, 384)),
            near_shape((3, 768), jnp.float32),
        ],
        [me, hidden_grad, w_up, second_grad, normal, inverse, vectors],
        [pltpu.VMEM((n, 768), jnp.float32), pltpu.VMEM((3, 8, 768), jnp.float32)],
        after=after,
        name="first_back",
    )


def attend_back_body(
    first_pair, pairs, me, attention_grad, w_out, order, swapped, values, soft, *refs
):
    grads, sums, upstream = refs[-3:]
    length = attention_grad.shape[0]
    groups = length // CLUSTER
    blocks = [slice(g * CLUSTER, (g + 1) * CLUSTER) for g in range(groups)]
    low = iota((length, LANES), 1) < 64
    low_rows = iota((CLUSTER, LANES), 1) < 64
    scale = HEAD_DIM ** (-0.5)
    mine = slice(first_pair * LANES, (first_pair + pairs) * LANES)
    upstream[...] = dot_nt(attention_grad[...], w_out[mine, :]).astype(jnp.bfloat16)

    for place in range(pairs):
        pair = first_pair + place

        def columns(base, pair=pair):
            return slice(base + pair * LANES, base + (pair + 1) * LANES)

        both = upstream[:, slice(place * LANES, (place + 1) * LANES)]
        to_tokens, moved = [], []
        for h in range(2):
            to_tokens.append(place_matrix(order, 2 * pair + h))
            value = dot_tn(to_tokens[h], both)
            value = jnp.where(low if h == 0 else jnp.logical_not(low), value, 0.0)
            moved.append(value.astype(jnp.bfloat16))
        back = []
        for h in range(2):
            kept = 2 * place + h
            keys = [swapped[kept, b, :] for b in blocks]
            weights = [soft[kept, b, :] for b in blocks]
            soft_grad = [dot_nt(moved[h][b], values[kept, b, :]) for b in blocks]
            value_grad = [
                dot_tn(weights[g].astype(jnp.bfloat16), moved[h][b]) for g, b in enumerate(blocks)
            ]
            score_grad = []
            for g in range(groups):
                middle = jnp.sum(soft_grad[g] * weights[g], axis=1, keepdims=True)
                score_grad.append((weights[g] * (soft_grad[g] - middle)).astype(jnp.bfloat16))
            query_grad = [dot(score_grad[g], keys[g]) for g in range(groups)]
            key_grad = [dot_tn(score_grad[g], keys[g]) for g in range(groups)]
            parts = [
                jnp.concatenate(
                    [
                        (jnp.where(low_rows, query_grad[g], key_grad[g]) * scale).astype(
                            jnp.bfloat16
                        ),
                        value_grad[g].astype(jnp.bfloat16),
                    ],
                    axis=1,
                )
                for g in range(groups)
            ]
            back.append(dot(to_tokens[h], jnp.concatenate(parts, axis=0)))
        first, second = back[0][:, :LANES], back[1][:, :LANES]
        query = jnp.where(low, first, pltpu.roll(second, 64, axis=1))
        keys = jnp.where(low, pltpu.roll(first, 64, axis=1), second)
        value = back[0][:, LANES:] + back[1][:, LANES:]
        grads[:, columns(0)] = query.astype(jnp.bfloat16)
        grads[:, columns(768)] = keys.astype(jnp.bfloat16)
        grads[:, columns(1536)] = value.astype(jnp.bfloat16)
        sums[0:1, columns(0)] = jnp.sum(query, axis=0, keepdims=True)
        sums[1:2, columns(0)] = jnp.sum(value, axis=0, keepdims=True)


def attend_back(
    me, attention_grad, w_out, order, kept, first_pair, pairs, before=(), after=()
):
    length = attention_grad.shape[0]
    return call(
        functools.partial(attend_back_body, first_pair, pairs),
        [near_shape((length, 2304)), near_shape((2, 768), jnp.float32)],
        [me, attention_grad, w_out, order, *kept, *before],
        [pltpu.VMEM((length, pairs * LANES), jnp.bfloat16)],
        after=after,
        aliases={6: 0, 7: 1} if before else None,
        name="attend_back",
    )


def tokens_back_body(me, grads, weights, residual, out):
    for c in range(3):
        columns = slice(c * 256, (c + 1) * 256)
        out[:, columns] = dot_nt(grads[...], weights[columns, :]) + residual[:, columns]
        me.send(0, (slice(None), columns))


def tokens_back(me, grads, weights, residual, after=()):
    return call(
        tokens_back_body,
        [shape_of(residual.shape, jnp.float32)],
        [me, grads, weights, residual],
        far_outs={0: True},
        sends=3,
        after=after,
        name="tokens_back",
    )


def local_block(
    tokens,
    w_qkv,
    bias_query,
    bias_value,
    w_out,
    bias_out,
    gain_one,
    shift_one,
    w_up,
    bias_up,
    w_down,
    bias_down,
    gain_two,
    shift_two,
    cluster_order,
    segment_ids,
    padding,
    cotangent,
):
    length = tokens.shape[0]
    me = None
    vector_list = [
        bias_query, bias_value, bias_out, gain_one, shift_one, bias_down, gain_two, shift_two
    ]
    order = cluster_order[0]
    facts = (segment_ids[0] + 32 * (1 - padding[0])).astype(jnp.float32)
    facts = jnp.broadcast_to(facts[:, None], (length, 128))

    def other(x):
        return swap(x, "dp", CORE)

    blocks_q = pack_q(me, w_qkv, vector_list, bias_up)
    z_q = gather_z(*blocks_q)
    blocks_rest = pack_rest(me, w_out, w_up, w_down, after=[blocks_q])
    tokens_turned = turn(me, tokens, after=[blocks_rest])
    other_tokens = other(tie([tokens_turned[0]], [blocks_rest])[0])
    near_q = gather_near(me, z_q, after=[tokens_turned, other_tokens])
    (block_ou,) = tie([blocks_rest[0]], [near_q])
    z_ou = gather_z(block_ou)
    far_q = gather_far(me, near_q, after=z_ou[1:])
    (block_d,) = tie([blocks_rest[1]], [far_q])
    z_d = gather_z(block_d)
    near_ou = gather_near(me, z_ou, after=[*far_q[1:], *z_d[1:]])
    far_q = tie(far_q, [near_ou])
    projected = project(me, gather_core(far_q), tokens, after=[near_ou])
    full_qkv, vectors, full_bias_up, qkv = projected

    pairs = PAIRS // 3

    def forward(part, before, after):
        return attend(
            me, qkv, order, facts, part * pairs, pairs, before, after=after
        )

    seen_a = forward(0, None, [projected])
    far_ou = gather_far(me, near_ou, after=[seen_a])
    near_d = gather_near(me, z_d, after=[far_ou])
    seen_b = forward(1, seen_a[-1], [near_d])
    seen_c = forward(2, seen_b[-1], [seen_b])
    combined = seen_c[-1]
    far_d = gather_far(me, near_d, after=[seen_c, *far_ou[1:]])
    far_ou = tie(far_ou, [far_d])
    combined_turned = turn(me, combined, after=[far_d])
    full_out, full_up = unpack_ou(me, gather_core(far_ou), after=[combined_turned])
    normed = out_norm(me, combined, full_out, tokens, vectors)
    first_low, normal, inverse = normed
    first_turned = turn(me, first_low)
    upper = up(me, first_low, full_up, full_bias_up, after=[first_turned])
    activated, slope, send_activated = upper
    far_d = tie(far_d, [upper])
    unpacked = unpack_d(me, gather_core(far_d), after=[upper])
    turned_down = unpacked[0]
    sends = tie([combined_turned[0], first_turned[0], send_activated], [unpacked])
    others = [other(x) for x in sends]
    downed = down_norm(me, activated, turned_down, normal, vectors, cotangent)
    layer_out, feed_grad, second_grad, sums_two = downed

    other_feed = other(feed_grad)
    hidden = hidden_back(me, feed_grad, turned_down, slope, after=[downed, *others])
    hidden_grad, sums_up = hidden
    (hidden_grad,) = tie([hidden_grad], [hidden, other_feed])
    other_hidden = other(hidden_grad)
    grad_d = gradient_d(
        me, feed_grad, other_feed, activated, others[2], after=[hidden]
    )
    core_d = scatter_near(grad_d)
    first = first_back(
        me, hidden_grad, full_up, second_grad, normal, inverse, vectors, after=[grad_d]
    )
    residual_grad, attention_grad, *halves, sums_one = first
    halves = [other(x) for x in halves]

    def back(part, kept, before, after):
        return attend_back(
            me, attention_grad, full_out, order, kept,
            part * pairs, pairs, before, after,
        )

    grads_a = back(0, seen_a[:3], (), [first])
    grads_b = back(1, seen_b[:3], grads_a, [])
    grads_c = back(2, seen_c[:3], grads_b, halves)
    half_d = add_plane(me, core_d, after=[grads_c])
    plane_d = scatter_far(half_d)
    projected_grad, sums_bias = grads_c
    grad_vectors = all_sums(me, sums_bias, sums_one, sums_two, sums_up)
    projected_grad, grad_vectors = tie([projected_grad, grad_vectors], [half_d])
    other_grads = other(projected_grad), other(grad_vectors)
    grad_ou = gradient_ou(
        me,
        (combined_turned[1], others[0]),
        (first_turned[1], others[1]),
        (hidden_grad, other_hidden),
        (attention_grad, *halves),
        after=[half_d],
    )
    core_ou = scatter_near(grad_ou)
    last_d = add_last(me, plane_d, after=[grad_ou], cost=22 * MICROSECOND)
    z_d = scatter_z(last_d)
    grad_q = gradient_q(
        me, tokens_turned[1], other_tokens, projected_grad, other_grads[0], grad_vectors,
        other_grads[1], after=[last_d],
    )
    core_q = scatter_near(grad_q)
    moved = tokens_back(me, projected_grad, full_qkv, residual_grad, after=[grad_q])
    grad_tokens = moved[0]
    half_ou = add_plane(me, core_ou, after=[moved])
    plane_ou = scatter_far(half_ou)
    near_d = add_z(me, z_d, after=[half_ou])
    sum_d = scatter_z_far(near_d)
    half_q = add_plane(me, core_q, after=[near_d])
    plane_q = scatter_far(half_q)
    last_ou = add_last(me, plane_ou, after=[half_q])
    z_ou = scatter_z(last_ou)
    done_d = finish_d(me, sum_d, after=[last_ou])
    last_q = add_last(me, plane_q, after=[done_d])
    z_q = scatter_z(last_q)
    near_ou = add_z(me, z_ou, after=[last_q])
    sum_ou = scatter_z_far(near_ou)
    near_q = add_z(me, z_q, after=[near_ou])
    sum_q = scatter_z_far(near_q)
    shard_out, shard_up = finish_ou(me, sum_ou)
    shard_qkv, *shard_vectors = finish_q(me, sum_q)
    shard_down = done_d[0].T
    grad_list = [v.reshape(-1) for v in shard_vectors]
    return (
        layer_out,
        grad_tokens,
        shard_qkv,
        grad_list[0],
        grad_list[1],
        shard_out,
        grad_list[2],
        grad_list[3],
        grad_list[4],
        shard_up,
        grad_list[8],
        shard_down,
        grad_list[5],
        grad_list[6],
        grad_list[7],
    )


def solution(mesh):
    in_specs = (
        P(("dp", "mp"), None),
        P("dp", "mp"),
        P(("dp", "mp")),
        P(("dp", "mp")),
        P("dp", "mp"),
        P(("dp", "mp")),
        P(("dp", "mp")),
        P(("dp", "mp")),
        P("dp", "mp"),
        P(("dp", "mp")),
        P("dp", "mp"),
        P(("dp", "mp")),
        P(("dp", "mp")),
        P(("dp", "mp")),
        P(("dp", "mp"), None, None),
        P(("dp", "mp"), None),
        P(("dp", "mp"), None),
        P(("dp", "mp"), None),
    )
    out_specs = (
        P(("dp", "mp"), None),
        P(("dp", "mp"), None),
        P("dp", "mp"),
        P(("dp", "mp")),
        P(("dp", "mp")),
        P("dp", "mp"),
        P(("dp", "mp")),
        P(("dp", "mp")),
        P(("dp", "mp")),
        P("dp", "mp"),
        P(("dp", "mp")),
        P("dp", "mp"),
        P(("dp", "mp")),
        P(("dp", "mp")),
        P(("dp", "mp")),
    )
    blocks = mesh.shape["dp"] == 8 and mesh.shape["mp"] == 4
    local = local_block if blocks else local_general
    return jax.shard_map(local, mesh=mesh, in_specs=in_specs, out_specs=out_specs, check_vma=False)
```

```python
import functools
import math

import jax
import jax.numpy as jnp
from jax import lax
from jax.experimental import pallas as pl
from jax.experimental.pallas import tpu as pltpu
from jax.sharding import PartitionSpec as P

HEADS = 12
HEAD_DIM = 64
CLUSTER = 128


epsilon = 1e-12
masked_score = -1e30


def product(left_side, right_side):
    return jnp.dot(left_side, right_side, preferred_element_type=jnp.float32)


def times_back(left_side, right_side):
    return lax.dot_general(
        left_side, right_side, (((1,), (1,)), ((), ())), preferred_element_type=jnp.float32
    )


def outer_sum(left_side, right_side):
    return lax.dot_general(
        left_side, right_side, (((0,), (0,)), ((), ())), preferred_element_type=jnp.float32
    )


def norm_forward(hidden, norm_gain, norm_shift):
    average = jnp.mean(hidden, axis=-1, keepdims=True)
    centred = hidden - average
    variance = jnp.mean(centred * centred, axis=-1, keepdims=True)
    inverse = lax.rsqrt(variance + epsilon)
    normal = centred * inverse
    return (normal * norm_gain + norm_shift, normal, inverse)


def norm_backward(upstream, normal, inverse, norm_gain):
    scaled = upstream * norm_gain
    return inverse * (
        scaled
        - jnp.mean(scaled, axis=-1, keepdims=True)
        - normal * jnp.mean(scaled * normal, axis=-1, keepdims=True)
    )


def gelu_exact(inputs):
    return jax.nn.gelu(inputs, approximate=False)


def local_general(
    tokens,
    w_qkv,
    bias_query,
    bias_value,
    w_out,
    bias_out,
    gain_one,
    shift_one,
    w_up,
    bias_up,
    w_down,
    bias_down,
    gain_two,
    shift_two,
    cluster_order,
    segment_ids,
    padding,
    cotangent,
):
    model_width = HEADS * HEAD_DIM
    length = tokens.shape[0]
    groups = length // CLUSTER
    score_scale = HEAD_DIM ** (-0.5)
    vectors = jnp.stack(
        [bias_query, bias_value, bias_out, gain_one, shift_one, bias_down, gain_two, shift_two]
    ).astype(jnp.bfloat16)
    vector_up = bias_up.astype(jnp.bfloat16)[None, :]
    part_qkv = w_qkv.astype(jnp.bfloat16)
    part_out = w_out.astype(jnp.bfloat16)
    part_up = w_up.astype(jnp.bfloat16)
    part_down = w_down.astype(jnp.bfloat16)
    column_qkv, column_out, column_up, column_down, column_vectors, column_bias = (
        lax.all_gather(part_qkv, "mp", axis=1, tiled=True),
        lax.all_gather(part_out, "mp", axis=1, tiled=True),
        lax.all_gather(part_up, "mp", axis=1, tiled=True),
        lax.all_gather(part_down, "mp", axis=1, tiled=True),
        lax.all_gather(vectors, "mp", axis=1, tiled=True),
        lax.all_gather(vector_up, "mp", axis=1, tiled=True),
    )
    full_qkv, full_out, full_up, full_down, full_vectors, full_bias = (
        lax.all_gather(column_qkv, "dp", axis=0, tiled=True),
        lax.all_gather(column_out, "dp", axis=0, tiled=True),
        lax.all_gather(column_up, "dp", axis=0, tiled=True),
        lax.all_gather(column_down, "dp", axis=0, tiled=True),
        lax.all_gather(column_vectors, "dp", axis=1, tiled=True),
        lax.all_gather(column_bias, "dp", axis=1, tiled=True),
    )
    small_params = full_vectors.astype(jnp.float32)
    hidden_bias = full_bias[0].astype(jnp.float32)
    ordering = cluster_order[0]
    segment = segment_ids[0]
    present = padding[0]
    positions = jnp.arange(length, dtype=jnp.int32)
    placement = (ordering[:, :, None] == positions[None, None, :]).astype(jnp.bfloat16)

    def to_clusters(matrix):
        per_head = matrix.reshape(length, HEADS, HEAD_DIM)
        moved = jnp.einsum("hip,phd->hid", placement, per_head, preferred_element_type=jnp.float32)
        return moved.astype(jnp.bfloat16).reshape(HEADS, groups, CLUSTER, HEAD_DIM)

    def from_clusters(blocks):
        per_head = blocks.astype(jnp.bfloat16).reshape(HEADS, length, HEAD_DIM)
        moved = jnp.einsum("hip,hid->phd", placement, per_head, preferred_element_type=jnp.float32)
        return moved.astype(jnp.bfloat16).reshape(length, model_width)

    segment_blocks = jnp.take(segment, ordering).reshape(HEADS, groups, CLUSTER)
    present_blocks = jnp.take(present, ordering).reshape(HEADS, groups, CLUSTER)
    same_doc = segment_blocks[..., :, None] == segment_blocks[..., None, :]
    itself = jnp.eye(CLUSTER, dtype=bool)
    allowed = same_doc & ((present_blocks[..., None, :] == 1) | itself)

    def scores_of(query_blocks, key_blocks):
        raw_scores = (
            jnp.einsum(
                "hncd,hnmd->hncm", query_blocks, key_blocks, preferred_element_type=jnp.float32
            )
            * score_scale
        )
        return jnp.where(allowed, raw_scores, masked_score)

    projected = product(tokens, full_qkv)
    query = (projected[:, :model_width] + small_params[0]).astype(jnp.bfloat16)
    keys = projected[:, model_width : 2 * model_width].astype(jnp.bfloat16)
    values = (projected[:, 2 * model_width :] + small_params[1]).astype(jnp.bfloat16)
    query_blocks = to_clusters(query)
    key_blocks = to_clusters(keys)
    value_blocks = to_clusters(values)
    masked = scores_of(query_blocks, key_blocks)
    highest = jnp.max(masked, axis=-1, keepdims=True)
    exponent = jnp.exp(masked - highest)
    row_total = jnp.sum(exponent, axis=-1, keepdims=True)
    soft_weights = exponent / row_total
    log_total = highest + jnp.log(row_total)
    soft_low = soft_weights.astype(jnp.bfloat16)
    combined = from_clusters(
        jnp.einsum("hncm,hnmd->hncd", soft_low, value_blocks, preferred_element_type=jnp.float32)
    )
    attention = product(combined, full_out) + small_params[2]
    first_norm, first_normal, first_inverse = norm_forward(
        tokens.astype(jnp.float32) + attention, small_params[3], small_params[4]
    )
    first_low = first_norm.astype(jnp.bfloat16)
    hidden = product(first_low, full_up) + hidden_bias
    activated, gelu_pull = jax.vjp(gelu_exact, hidden)
    activated_low = activated.astype(jnp.bfloat16)
    feed_out = product(activated_low, full_down) + small_params[5]
    output, second_normal, second_inverse = norm_forward(
        first_norm + feed_out, small_params[6], small_params[7]
    )
    layer_out = output.astype(jnp.bfloat16)
    again_qkv, again_out, again_up, again_down = (
        lax.all_gather(part_qkv, "mp", axis=1, tiled=True),
        lax.all_gather(part_out, "mp", axis=1, tiled=True),
        lax.all_gather(part_up, "mp", axis=1, tiled=True),
        lax.all_gather(part_down, "mp", axis=1, tiled=True),
    )
    back_qkv, back_out, back_up, back_down = (
        lax.all_gather(again_qkv, "dp", axis=0, tiled=True),
        lax.all_gather(again_out, "dp", axis=0, tiled=True),
        lax.all_gather(again_up, "dp", axis=0, tiled=True),
        lax.all_gather(again_down, "dp", axis=0, tiled=True),
    )
    grad_gain_two = jnp.sum(cotangent * second_normal, axis=0)
    grad_shift_two = jnp.sum(cotangent, axis=0)
    second_grad = norm_backward(cotangent, second_normal, second_inverse, small_params[6])
    feed_grad = second_grad.astype(jnp.bfloat16)
    grad_bias_down = jnp.sum(feed_grad.astype(jnp.float32), axis=0)
    grad_w_down = outer_sum(activated_low, feed_grad)
    hidden_grad = gelu_pull(times_back(feed_grad, back_down))[0].astype(jnp.bfloat16)
    grad_bias_up = jnp.sum(hidden_grad.astype(jnp.float32), axis=0)
    grad_w_up = outer_sum(first_low, hidden_grad)
    first_grad = times_back(hidden_grad, back_up) + second_grad
    grad_gain_one = jnp.sum(first_grad * first_normal, axis=0)
    grad_shift_one = jnp.sum(first_grad, axis=0)
    residual_grad = norm_backward(first_grad, first_normal, first_inverse, small_params[3])
    attention_grad = residual_grad.astype(jnp.bfloat16)
    grad_bias_out = jnp.sum(attention_grad.astype(jnp.float32), axis=0)
    grad_w_out = outer_sum(combined, attention_grad)
    combined_grad = to_clusters(times_back(attention_grad, back_out).astype(jnp.bfloat16))
    masked_again = scores_of(query_blocks, key_blocks)
    soft_again = jnp.exp(masked_again - log_total)
    soft_again_low = soft_again.astype(jnp.bfloat16)
    value_sums = jnp.einsum(
        "hncm,hncd->hnmd", soft_again_low, combined_grad, preferred_element_type=jnp.float32
    )
    soft_grad = jnp.einsum(
        "hncd,hnmd->hncm", combined_grad, value_blocks, preferred_element_type=jnp.float32
    )
    score_grad = (
        soft_again * (soft_grad - jnp.sum(soft_grad * soft_again, axis=-1, keepdims=True))
    ).astype(jnp.bfloat16)
    query_sums = (
        jnp.einsum("hncm,hnmd->hncd", score_grad, key_blocks, preferred_element_type=jnp.float32)
        * score_scale
    )
    key_sums = (
        jnp.einsum("hncm,hncd->hnmd", score_grad, query_blocks, preferred_element_type=jnp.float32)
        * score_scale
    )
    query_grad = from_clusters(query_sums)
    key_grad = from_clusters(key_sums)
    value_grad = from_clusters(value_sums)
    grad_bias_query = jnp.sum(query_grad.astype(jnp.float32), axis=0)
    grad_bias_value = jnp.sum(value_grad.astype(jnp.float32), axis=0)
    projected_grad = jnp.concatenate([query_grad, key_grad, value_grad], axis=1)
    grad_w_qkv = outer_sum(tokens, projected_grad)
    grad_tokens = times_back(projected_grad, back_qkv) + residual_grad
    grad_vectors = jnp.stack(
        [
            grad_bias_query,
            grad_bias_value,
            grad_bias_out,
            grad_gain_one,
            grad_shift_one,
            grad_bias_down,
            grad_gain_two,
            grad_shift_two,
        ]
    )
    grad_up_row = grad_bias_up[None, :]
    row_qkv, row_out, row_up, row_down, row_vectors, row_bias = (
        lax.psum_scatter(
            grad_w_qkv.astype(jnp.bfloat16), "dp", scatter_dimension=0, tiled=True
        ).astype(jnp.float32),
        lax.psum_scatter(
            grad_w_out.astype(jnp.bfloat16), "dp", scatter_dimension=0, tiled=True
        ).astype(jnp.float32),
        lax.psum_scatter(
            grad_w_up.astype(jnp.bfloat16), "dp", scatter_dimension=0, tiled=True
        ).astype(jnp.float32),
        lax.psum_scatter(
            grad_w_down.astype(jnp.bfloat16), "dp", scatter_dimension=0, tiled=True
        ).astype(jnp.float32),
        lax.psum_scatter(
            grad_vectors.astype(jnp.bfloat16), "dp", scatter_dimension=1, tiled=True
        ).astype(jnp.float32),
        lax.psum_scatter(
            grad_up_row.astype(jnp.bfloat16), "dp", scatter_dimension=1, tiled=True
        ).astype(jnp.float32),
    )
    shard_qkv, shard_out, shard_up, shard_down, shard_vectors, shard_bias = (
        lax.psum_scatter(
            row_qkv.astype(jnp.bfloat16), "mp", scatter_dimension=1, tiled=True
        ).astype(jnp.float32),
        lax.psum_scatter(
            row_out.astype(jnp.bfloat16), "mp", scatter_dimension=1, tiled=True
        ).astype(jnp.float32),
        lax.psum_scatter(row_up.astype(jnp.bfloat16), "mp", scatter_dimension=1, tiled=True).astype(
            jnp.float32
        ),
        lax.psum_scatter(
            row_down.astype(jnp.bfloat16), "mp", scatter_dimension=1, tiled=True
        ).astype(jnp.float32),
        lax.psum_scatter(
            row_vectors.astype(jnp.bfloat16), "mp", scatter_dimension=1, tiled=True
        ).astype(jnp.float32),
        lax.psum_scatter(
            row_bias.astype(jnp.bfloat16), "mp", scatter_dimension=1, tiled=True
        ).astype(jnp.float32),
    )
    return (
        layer_out,
        grad_tokens,
        shard_qkv,
        shard_vectors[0],
        shard_vectors[1],
        shard_out,
        shard_vectors[2],
        shard_vectors[3],
        shard_vectors[4],
        shard_up,
        shard_bias[0],
        shard_down,
        shard_vectors[5],
        shard_vectors[6],
        shard_vectors[7],
    )


LANES = 128
QKV_ROWS = 96
UP_TILES = 6
DOWN_TILES = 3
PACK_Q = 4 * QKV_ROWS + QKV_ROWS // 2 + 16
PACK_OU = QKV_ROWS + QKV_ROWS // 2 + UP_TILES * QKV_ROWS
PACK_D = DOWN_TILES * 192
VECTOR_ROW = 4 * QKV_ROWS + QKV_ROWS // 2
UP_ROW = QKV_ROWS + QKV_ROWS // 2


def whole():
    return pl.BlockSpec(memory_space=pltpu.VMEM)


def far():
    return pl.BlockSpec(memory_space=pltpu.HBM)


def kept_far(arrays):
    return [pltpu.with_memory_space_constraint(x, pltpu.HBM) for x in arrays]


def near(x):
    return pltpu.with_memory_space_constraint(x, pltpu.VMEM)


def near_shape(shape, dtype=jnp.bfloat16):
    return pltpu.VMEM(shape, dtype)


def waited(after):
    return [kept_far([x.token])[0] if isinstance(x, Results) else x for x in after]


def anywhere(after):
    return [far() if isinstance(x, Results) else pl.BlockSpec(memory_space=pl.ANY) for x in after]


class Results(list):
    token = None


TOKEN = pltpu.HBM((8, 128), jnp.float32)


def place():
    return lax.axis_index("dp"), lax.axis_index("mp")


SHORT = pl.CostEstimate(flops=1, bytes_accessed=1, transcendentals=0)
MICROSECOND = 1_153_000_000


class Place(tuple):
    def arrived(self, index, part=None):
        copies, here = self.late[index]
        for i in range(len(copies)) if part is None else [part]:
            if copies[i] is not None:
                copies[i].wait()
                copies[i] = None
        return here

    def send(self, index, where=None, source=None):
        here, there = self.far[index]
        source = here if source is None else source
        if where is not None:
            source, there = source.at[where], there.at[where]
        copy = pltpu.make_async_copy(source, there, self.sems.at[len(self.sent)])
        copy.start()
        self.sent.append(copy)


def call(
    body, out_shapes, operands, scratch=(), staged=0, late=(), far_outs=None, sends=None, after=(),
    aliases=None, vmem=10, cost=0, name=None,
):
    operands = operands[1:]
    far_outs = far_outs or {}
    sends = len(far_outs) if sends is None else sends
    count, outs, copied = len(operands), len(out_shapes), staged + len(late)
    spread = [(0, 1)] * staged + [x or (0, 1) for x in late]
    starts = [sum(n for _, n in spread[:i]) for i in range(copied)]

    def with_copies(*refs):
        sources, rest = refs[:copied], refs[copied:count]
        results = list(refs[count + len(after) : count + len(after) + outs])
        own = refs[count + len(after) + outs + 1 :]
        mine, own = own[: len(scratch)], own[len(scratch) :]
        arrived, own = own[:copied], list(own[copied:])
        me = Place(place())
        me.sent, me.far = [], {}
        if copied:
            sem = own.pop(0)
            copies = []
            for source, here, (axis, parts), start in zip(sources, arrived, spread, starts):
                size = here.shape[axis] // parts
                copies.append([])
                for i in range(parts):
                    cut = (slice(None),) * axis + (slice(i * size, (i + 1) * size),)
                    copies[-1].append(
                        pltpu.make_async_copy(source.at[cut], here.at[cut], sem.at[start + i])
                    )
            for copy in sum(copies, []):
                copy.start()
            for (copy,) in copies[:staged]:
                copy.wait()
            me.late = list(zip(copies[staged:], arrived[staged:]))
        if far_outs:
            me.sems = own.pop(0)
            for index, has_room in far_outs.items():
                here = own.pop(0) if has_room else None
                me.far[index] = (here, results[index])
                results[index] = here
        body(me, *arrived[:staged], *rest, *results, *mine)
        for copy in me.sent:
            copy.wait()

    room = [pltpu.VMEM(x.shape, x.dtype) for x in operands[:copied]]
    if copied:
        room.append(pltpu.SemaphoreType.DMA((sum(n for _, n in spread),)))
    if far_outs:
        room.append(pltpu.SemaphoreType.DMA((sends,)))
        room += [pltpu.VMEM(out_shapes[i].shape, out_shapes[i].dtype) for i in far_outs if far_outs[i]]
    given = [
        pltpu.HBM(x.shape, x.dtype) if i in far_outs else x for i, x in enumerate(out_shapes)
    ]
    *results, token = pl.pallas_call(
        with_copies,
        out_shape=[*given, TOKEN],
        in_specs=[pl.BlockSpec(memory_space=pl.ANY)] * staged
        + [far()] * len(late)
        + [whole()] * (count - copied)
        + anywhere(after),
        out_specs=[far() if i in far_outs else whole() for i in range(outs)] + [far()],
        scratch_shapes=list(scratch) + room,
        input_output_aliases=aliases or {},
        compiler_params=pltpu.CompilerParams(vmem_limit_bytes=vmem * 1024 * 1024),
        cost_estimate=SHORT if not cost else pl.CostEstimate(cost, 1, 0),
        name=name,
    )(
        *operands[:staged],
        *kept_far(operands[staged:copied]),
        *operands[copied:],
        *waited(after),
    )
    results = Results(results)
    results.token = token
    return results


def tie(arrays, after):
    count = len(arrays)

    def body(*refs):
        pass

    return pl.pallas_call(
        body,
        out_shape=[shape_of(x.shape, x.dtype) for x in arrays],
        in_specs=[pl.BlockSpec(memory_space=pl.ANY)] * count + anywhere(after),
        out_specs=[pl.BlockSpec(memory_space=pl.ANY)] * count,
        input_output_aliases={i: i for i in range(count)},
        compiler_params=pltpu.CompilerParams(vmem_limit_bytes=1024 * 1024),
        cost_estimate=SHORT,
        name="tie",
    )(*arrays, *waited(after))


def shape_of(shape, dtype=jnp.bfloat16):
    return jax.ShapeDtypeStruct(shape, dtype)


def halves_beside(single):
    half = single.shape[0] // 2
    return jnp.concatenate([single[:half], single[half:]], axis=1)


def pack_columns(odd, low, tiles, base, target):
    @pl.when(odd)
    def _():
        for t in range(tiles):
            target[base + t * 96 : base + (t + 1) * 96, :] = low[
                :, 64 + t * LANES : 64 + (t + 1) * LANES
            ].astype(jnp.bfloat16)
        target[base + tiles * 96 : base + tiles * 96 + 48, :] = halves_beside(low[:, :64]).astype(
            jnp.bfloat16
        )

    @pl.when(jnp.logical_not(odd))
    def _():
        for t in range(tiles):
            target[base + t * 96 : base + (t + 1) * 96, :] = low[
                :, t * LANES : (t + 1) * LANES
            ].astype(jnp.bfloat16)
        target[base + tiles * 96 : base + tiles * 96 + 48, :] = halves_beside(
            low[:, tiles * LANES : tiles * LANES + 64]
        ).astype(jnp.bfloat16)


def pack_q_body(me, *refs):
    w_qkv, vectors, target, own = refs[0], refs[1:10], refs[10], refs[11]
    pack_columns(lax.rem(me[1], 2) == 1, w_qkv[...], 4, 0, target)
    rows = lax.broadcasted_iota(jnp.int32, (16, LANES), 0)
    tail = jnp.zeros((16, LANES), jnp.float32)
    for v in range(9):
        value = vectors[v][...]
        wide = jnp.concatenate(
            [value, jnp.zeros((1, LANES - value.shape[1]), jnp.float32)], axis=1
        )
        tail = jnp.where(rows == v, jnp.broadcast_to(wide, (16, LANES)), tail)
    target[VECTOR_ROW:, :] = tail.astype(jnp.bfloat16)
    me.send(0)
    own[...] = target[...]


def pack_q(me, w_qkv, vectors, bias_up):
    small = [v.reshape(1, -1) for v in (*vectors, bias_up)]
    return call(
        pack_q_body, [shape_of((PACK_Q, LANES))] * 2, [me, *kept_far([w_qkv, *small])], staged=10, far_outs={0: True},
        name="pack_q",
    )


def pack_rest_body(me, w_out, w_up, w_down, to_ou, upper_d, lower_d, to_d):
    for t in range(DOWN_TILES):
        to_d[t * 192 : (t + 1) * 192, :] = w_down[:, t * LANES : (t + 1) * LANES].astype(
            jnp.bfloat16
        )
    upper_d[...] = to_d[: PACK_D // 2, :]
    lower_d[...] = to_d[PACK_D // 2 :, :]
    me.send(1)
    me.send(2)
    pack_columns(lax.rem(me[1], 2) == 1, w_out[...], 1, 0, to_ou)
    for t in range(UP_TILES):
        to_ou[UP_ROW + t * 96 : UP_ROW + (t + 1) * 96, :] = w_up[
            :, t * LANES : (t + 1) * LANES
        ].astype(jnp.bfloat16)
    me.send(0)


def pack_rest(me, w_out, w_up, w_down, after):
    return call(
        pack_rest_body,
        [
            shape_of((PACK_OU, LANES)),
            shape_of((PACK_D // 2, LANES)),
            shape_of((PACK_D // 2, LANES)),
            near_shape((PACK_D, LANES)),
        ],
        [me, *kept_far([w_out, w_up, w_down.T])],
        staged=3,
        far_outs={0: True, 1: True, 2: True},
        after=after,
        name="pack_rest",
    )


def swap(x, axis, bit):
    size = lax.axis_size(axis)
    return lax.ppermute(x, axis, [(i, i ^ bit) for i in range(size)])


CORE, ALONG_X, ALONG_Y = 1, 2, 4


def gather_z(x, own=None):
    return [x if own is None else own] + [swap(x, "mp", k) for k in (1, 2, 3)]


def beside(me, groups, shapes, after=(), name="beside"):
    sources = []
    for x, _ in groups:
        if all(x is not y for y in sources):
            sources.append(x)

    def body(me, *refs):
        for x, (index, where) in groups:
            source = refs[next(n for n, y in enumerate(sources) if x is y)]
            refs[len(sources) + index][where] = source[...]

    return call(body, [shape_of(s) for s in shapes], [me, *sources], after=after, name=name)


def beside_two(me, a, b, after=()):
    return beside(me, [(a, (0, 0)), (b, (0, 1))], [(2, *a.shape)], after, "beside_two")


def gather_near(me, parts, after=()):
    shape = (2, *parts[0].shape)
    found = beside(
        me,
        [(parts[0], (0, 0)), (parts[1], (0, 1)), (parts[2], (1, 0)), (parts[3], (1, 1))],
        [shape, shape],
        after,
        "beside_z",
    )
    first, second = found
    result = Results([first, swap(first, "dp", ALONG_X), second, swap(second, "dp", ALONG_Y)])
    result.token = found.token
    return result


def gather_far(me, parts, after=()):
    shape = (2, *parts[0].shape)
    groups = [(parts[i], (i // 2, i % 2)) for i in range(4)]
    found = beside(me, groups, [shape, shape], after, "beside_near")
    first, second = found
    result = Results([first, second, swap(first, "dp", ALONG_Y), swap(second, "dp", ALONG_X)])
    result.token = found.token
    return result


def gather_core(parts):
    return list(parts) + [swap(x, "dp", CORE) for x in parts]


def gathered_blocks(me, refs, steps=(1, 2)):
    for index, ref in enumerate(refs):
        core, far, half = index // 4, index % 4 // 2, index % 2
        for mid in range(2):
            for low in range(2):
                kx, ky = (far, mid) if half else (mid, far)
                along_z = steps[0] * low + steps[1] * half
                yield me[0] ^ (core + 2 * kx + 4 * ky), me[1] ^ along_z, ref.at[mid, low]


def split_pairs(refs):
    return [ref.at[i] for ref in refs for i in range(2)]


def place_columns(block, base, tiles, dp, mp, width, weights, singles):
    start = pl.multiple_of(mp * width + 64 * lax.rem(mp, 2), LANES)
    rows = pl.ds(pl.multiple_of(dp * 96, 32), 96)
    for t in range(tiles):
        weights[rows, pl.ds(pl.multiple_of(start + t * LANES, LANES), LANES)] = block[
            base + t * 96 : base + (t + 1) * 96, :
        ]
    singles[mp, pl.ds(pl.multiple_of(dp * 48, 16), 48), :] = block[
        base + tiles * 96 : base + tiles * 96 + 48, :
    ]


def place_singles(width, weights, singles):
    for pair in range(2):
        column = 2 * pair * width + (width // LANES) * LANES
        for dp in range(8):
            left = singles[2 * pair, dp * 48 : (dp + 1) * 48, :].astype(jnp.float32)
            right = singles[2 * pair + 1, dp * 48 : (dp + 1) * 48, :].astype(jnp.float32)
            upper = jnp.concatenate([left[:, :64], right[:, :64]], axis=1)
            lower = jnp.concatenate([left[:, 64:], right[:, 64:]], axis=1)
            weights[dp * 96 : dp * 96 + 48, column : column + LANES] = upper.astype(jnp.bfloat16)
            weights[dp * 96 + 48 : (dp + 1) * 96, column : column + LANES] = lower.astype(
                jnp.bfloat16
            )


def unpack_q_body(me, *refs):
    blocks, weights, vectors, bias_up, singles, tails = refs[:8], *refs[8:]
    for dp, mp, block in gathered_blocks(me, blocks):
        place_columns(block, 0, 4, dp, mp, 576, weights, singles)
        tails[dp * 4 + mp] = block[VECTOR_ROW:, :].astype(jnp.float32)
    place_singles(576, weights, singles)
    lane = lax.broadcasted_iota(jnp.int32, (16, LANES), 1)

    def spread(width, count):
        found = [jnp.zeros((16, LANES), jnp.float32) for _ in range(count)]
        for device in range(32):
            start, tile = device * width % LANES, device * width // LANES
            piece = tails[device]
            moved = pltpu.roll(piece, start, axis=1) if start else piece
            found[tile] = jnp.where((lane >= start) & (lane < start + width), moved, found[tile])
            if start + width > LANES:
                found[tile + 1] = jnp.where(lane < start + width - LANES, moved, found[tile + 1])
        return found

    for t, value in enumerate(spread(24, 6)):
        vectors[:, t * LANES : (t + 1) * LANES] = value[:8]
    for t, value in enumerate(spread(96, 24)):
        bias_up[:, t * LANES : (t + 1) * LANES] = value[8:9]


def unpack_ou_body(me, *refs):
    blocks, w_out, w_up, singles = refs[:8], *refs[8:]
    for dp, mp, block in gathered_blocks(me, blocks, (2, 1)):
        place_columns(block, 0, 1, dp, mp, 192, w_out, singles)
        rows = pl.ds(pl.multiple_of(dp * 96, 32), 96)
        for t in range(UP_TILES):
            w_up[rows, pl.ds(pl.multiple_of(mp * 768 + t * LANES, LANES), LANES)] = block[
                UP_ROW + t * 96 : UP_ROW + (t + 1) * 96, :
            ]
    place_singles(192, w_out, singles)


def unpack_ou(me, parts, after=()):
    return call(
        unpack_ou_body,
        [near_shape((768, 768)), near_shape((768, 3072))],
        [me, *parts],
        [pltpu.VMEM((4, 384, LANES), jnp.bfloat16)],
        after=after,
        name="unpack_ou",
    )


def spread_d_body(me, mine, upper_x, lower_y, upper, lower):
    half = PACK_D // 2
    upper[0], upper[1] = mine[:half, :], upper_x[...]
    lower[0], lower[1] = mine[half:, :], lower_y[...]


def spread_d(me, mine, upper_x, lower_y, after=()):
    shape = near_shape((2, PACK_D // 2, LANES))
    return call(
        spread_d_body, [shape, shape], [me, mine, upper_x, lower_y], after=after, name="spread_d"
    )


def whole_d_body(me, upper, upper_y, lower, lower_x, out):
    half = PACK_D // 2
    for kx in range(2):
        for ky in range(2):
            out[2 * ky + kx, :half, :] = (upper_y if ky else upper)[kx]
            out[2 * ky + kx, half:, :] = (lower_x if kx else lower)[ky]


def whole_d(me, upper, upper_y, lower, lower_x, after=()):
    return call(
        whole_d_body, [near_shape((4, PACK_D, LANES))], [me, upper, upper_y, lower, lower_x],
        after=after, name="whole_d",
    )


def unpack_d_body(me, *refs):
    blocks, turned = refs[:4], refs[4]
    for index, ref in enumerate(blocks):
        for far in range(2):
            for plane in range(4):
                dp, mp = me[0] ^ (2 * plane + index // 2), me[1] ^ (2 * far + index % 2)
                rows = pl.ds(pl.multiple_of(mp * 192, 64), 192)
                for t in range(DOWN_TILES):
                    turned[rows, pl.ds(pl.multiple_of(dp * 384 + t * LANES, LANES), LANES)] = ref[
                        far, plane, t * 192 : (t + 1) * 192, :
                    ]


def unpack_d(me, parts, after=()):
    return call(
        unpack_d_body, [near_shape((768, 3072))], [me, *parts], after=after, name="unpack_d"
    )


def turn_body(me, source, send, keep, turned):
    value = source[...].T
    for dp in range(8):
        k = me[0] ^ dp
        slot = (1 - (k & 1)) * 4 + (k >> 1)
        turned[pl.ds(pl.multiple_of(slot * 96, 32), 96), :] = value[dp * 96 : (dp + 1) * 96, :]
    send[...] = turned[:384, :]
    keep[...] = turned[384:, :]


def turn(me, source, after=()):
    n = source.shape[0]
    return call(
        turn_body,
        [shape_of((384, n)), near_shape((384, n))],
        [me, source],
        [pltpu.VMEM((768, n), jnp.bfloat16)],
        after=after,
        name="turn",
    )


def dot(a, b):
    return jnp.dot(a, b, preferred_element_type=jnp.float32)


def dot_nt(a, b):
    return lax.dot_general(a, b, (((1,), (1,)), ((), ())), preferred_element_type=jnp.float32)


def dot_tn(a, b):
    return lax.dot_general(a, b, (((0,), (0,)), ((), ())), preferred_element_type=jnp.float32)


def part_of(targets, kp, mp):
    ky, kx = kp // 2, kp % 2
    if mp < 2:
        return targets[ky].at[kx, mp]
    return targets[2 + kx].at[ky, mp - 2]


def store_columns(target, base, tiles, first, value):
    for t in range(tiles):
        target[base + t * 96 : base + (t + 1) * 96, :] = value[
            :, first + t * LANES : first + (t + 1) * LANES
        ].astype(jnp.bfloat16)


def store_single(target, base, odd, value):
    upper, lower = value[:48], value[48:]
    low_lanes = lax.broadcasted_iota(jnp.int32, (48, LANES), 1) < 64
    if odd:
        both = jnp.where(low_lanes, pltpu.roll(upper, 64, axis=1), lower)
    else:
        both = jnp.where(low_lanes, upper, pltpu.roll(lower, 64, axis=1))
    target[base : base + 48, :] = both.astype(jnp.bfloat16)


def column_gradient(lefts, rights, targets, base, tiles, width):
    def product(columns):
        return dot(lefts[0], rights[0][:, columns]) + dot(lefts[1], rights[1][:, columns])

    for pair in range(2):
        first = 2 * pair * width
        middle = first + tiles * LANES
        for begin, mp in ((first, 2 * pair), (middle + LANES, 2 * pair + 1)):
            value = product(slice(begin, begin + tiles * LANES))
            for kp in range(4):
                store_columns(
                    part_of(targets, kp, mp), base, tiles, 0, value[kp * 96 : (kp + 1) * 96]
                )
        value = product(slice(middle, middle + LANES))
        for kp in range(4):
            for mp in (2 * pair, 2 * pair + 1):
                store_single(
                    part_of(targets, kp, mp), base + tiles * 96, mp % 2,
                    value[kp * 96 : (kp + 1) * 96],
                )


def parts_shape(rows):
    return [near_shape((2, 2, rows, LANES)), shape_of((2, 2, rows, LANES))] * 2


def gradient_q_body(me, keep, other_keep, grads, other_grads, vectors, other_vectors, *targets):
    lefts, rights = (keep[...], other_keep[...]), (grads, other_grads)
    column_gradient(lefts, rights, targets, 0, 4, 576)
    sums = vectors[...] + other_vectors[...]
    lane = lax.broadcasted_iota(jnp.int32, (16, LANES), 1)
    rows = lax.broadcasted_iota(jnp.int32, (16, LANES), 0)

    def cut(source, width, device):
        start, tile = device * width % LANES, device * width // LANES
        value = source[:, tile * LANES : (tile + 1) * LANES]
        moved = pltpu.roll(value, LANES - start, axis=1) if start else value
        if start + width > LANES:
            after = source[:, (tile + 1) * LANES : (tile + 2) * LANES]
            after = pltpu.roll(after, LANES - start, axis=1)
            here = lax.broadcasted_iota(jnp.int32, value.shape, 1)
            moved = jnp.where(here < LANES - start, moved, after)
        return moved

    for kp in range(4):
        plane = (me[0] >> 1) ^ kp
        for mp in range(4):
            tail = jnp.zeros((16, LANES), jnp.float32)
            for dp in range(8):
                device = dp * 4 + mp
                row = 8 + device // 8
                up = jnp.broadcast_to(cut(sums[row : row + 1], 96, device % 8), (8, LANES))
                found = jnp.concatenate([cut(sums[:8], 24, device), up], axis=0)
                mine = dp == 2 * plane + (me[0] & 1)
                tail = jnp.where(mine, found, tail)
            tail = jnp.where((rows < 8) & (lane >= 24), 0.0, tail).astype(jnp.bfloat16)
            part_of(targets, kp, mp)[VECTOR_ROW:, :] = tail


def gradient_q(me, keep, other_keep, grads, other_grads, vectors, other_vectors, after=()):
    return call(
        gradient_q_body,
        parts_shape(PACK_Q),
        [me, keep, other_keep, grads, other_grads, vectors, other_vectors],
        after=after,
        name="gradient_q",
    )


def gradient_ou_body(me, *refs):
    combined, first_low, hidden_grad = (refs[i : i + 2] for i in (0, 2, 4))
    attention_grad, targets, room = (refs[6], refs[13]), refs[9:13], refs[13]
    room[:, :384] = refs[7][...]
    room[:, 384:] = refs[8][...]
    column_gradient([x[...] for x in combined], attention_grad, targets, 0, 1, 192)
    lefts = [x[...] for x in first_low]
    for mp in range(4):
        columns = slice(mp * 768, (mp + 1) * 768)
        value = dot(lefts[0], hidden_grad[0][:, columns])
        value = value + dot(lefts[1], hidden_grad[1][:, columns])
        for kp in range(4):
            store_columns(
                part_of(targets, kp, mp), UP_ROW, UP_TILES, 0, value[kp * 96 : (kp + 1) * 96]
            )


def gradient_ou(me, combined, first_low, hidden_grad, attention_grad, after=()):
    return call(
        gradient_ou_body,
        parts_shape(PACK_OU),
        [me, *combined, *first_low, *hidden_grad, *attention_grad],
        [pltpu.VMEM(attention_grad[0].shape, jnp.bfloat16)],
        after=after,
        name="gradient_ou",
    )


def gradient_d_body(me, feed_grad, other_feed_grad, activated, other_activated, *refs):
    targets, turned, other_turned = refs[:4], refs[4], refs[5]
    turned[...] = feed_grad[...].T
    other_turned[...] = other_feed_grad[...].T
    for kp in range(4):
        dp = me[0] ^ (2 * kp)
        block = activated[:, pl.ds(pl.multiple_of(dp * 384, LANES), 384)]
        value = dot(turned[...], block)
        value = value + dot(other_turned[...], other_activated[:, kp * 384 : (kp + 1) * 384])
        for mp in range(4):
            target = part_of(targets, kp, mp)
            for t in range(DOWN_TILES):
                target[t * 192 : (t + 1) * 192, :] = value[
                    mp * 192 : (mp + 1) * 192, t * LANES : (t + 1) * LANES
                ].astype(jnp.bfloat16)


def gradient_d(me, feed_grad, other_feed_grad, activated, other_activated, after=()):
    return call(
        gradient_d_body,
        parts_shape(PACK_D),
        [me, feed_grad, other_feed_grad, activated, other_activated],
        [pltpu.VMEM((768, feed_grad.shape[0]), jnp.bfloat16)] * 2,
        after=after,
        name="gradient_d",
    )


def sums_body(me, bias, one, two, up, out):
    out[0:2, :], out[2:5, :], out[5:8, :] = bias[...], one[...], two[...]
    for i in range(4):
        out[8 + i : 9 + i, :] = up[:, i * 768 : (i + 1) * 768]


def all_sums(me, *sums):
    return call(sums_body, [shape_of((12, 768), jnp.float32)], [me, *sums], name="sums")[0]


def add(a, b):
    return a.astype(jnp.float32) + b.astype(jnp.float32)


def add_plane_body(me, first, first_in, second, second_in, *outs):
    for keep, send, a, b in ((*outs[:2], first, first_in), (*outs[2:], second, second_in)):
        keep[...] = add(a[0], b[0]).astype(jnp.bfloat16)
        send[...] = add(a[1], b[1]).astype(jnp.bfloat16)


def add_last_body(me, first, first_in, second, second_in, *refs):
    keep, send, room = refs
    for mp in range(4):
        a, b = (first, first_in) if mp < 2 else (second, second_in)
        room[me[1] ^ mp] = add(a[mp % 2], b[mp % 2]).astype(jnp.bfloat16)
    for k in range(4):
        (send if k % 2 else keep)[k // 2] = room[k]


def add_z_body(me, mine, arrived, keep, send):
    keep[...] = add(mine[0], arrived[0])
    send[...] = add(mine[1], arrived[1]).astype(jnp.bfloat16)


def scatter_near(parts):
    first, first_send, second, second_send = parts
    return first, swap(first_send, "dp", ALONG_Y), second, swap(second_send, "dp", ALONG_X)


def add_plane(me, parts, after=()):
    rows = parts[0].shape[2]
    return call(
        add_plane_body,
        [near_shape((2, rows, LANES)), shape_of((2, rows, LANES))] * 2,
        [me, *parts],
        after=after,
        name="add_plane",
    )


def scatter_far(parts):
    first, first_send, second, second_send = parts
    return first, swap(first_send, "dp", ALONG_X), second, swap(second_send, "dp", ALONG_Y)


def add_last(me, parts, after=(), cost=0):
    rows = parts[0].shape[1]
    return call(
        add_last_body,
        [near_shape((2, rows, LANES)), shape_of((2, rows, LANES))],
        [me, *parts],
        [pltpu.VMEM((4, rows, LANES), jnp.bfloat16)],
        after=after,
        cost=cost,
        name="add_last",
    )


def scatter_z(parts):
    return parts[0], swap(parts[1], "mp", 1)


def add_z(me, parts, after=()):
    rows = parts[0].shape[1]
    return call(
        add_z_body,
        [near_shape((rows, LANES), jnp.float32), shape_of((rows, LANES))],
        [me, *parts],
        after=after,
        name="add_z",
    )


def scatter_z_far(parts):
    return parts[0], swap(parts[1], "mp", 2)


def total(refs, rows):
    value = refs[0][rows, :].astype(jnp.float32)
    for ref in refs[1:]:
        value = value + ref[rows, :].astype(jnp.float32)
    return value


def finish_columns(me, refs, base, tiles, out):
    odd = lax.rem(me[1], 2) == 1
    full = [total(refs, pl.ds(base + t * 96, 96)) for t in range(tiles)]
    single = total(refs, pl.ds(base + tiles * 96, 48))
    single = jnp.concatenate([single[:, :64], single[:, 64:]], axis=0)

    @pl.when(odd)
    def _():
        out[...] = jnp.concatenate([single, *full], axis=1)

    @pl.when(jnp.logical_not(odd))
    def _():
        out[...] = jnp.concatenate([*full, single], axis=1)


def finish_q_body(me, *refs):
    parts, out, outs = refs[:2], refs[2], refs[3:]
    finish_columns(me, parts, 0, 4, out)
    tail = total(parts, pl.ds(VECTOR_ROW, 16))
    for v in range(8):
        outs[v][...] = tail[v : v + 1, :24]
    outs[8][...] = tail[8:9, :96]


def finish_q(me, parts):
    f = jnp.float32
    return call(
        finish_q_body,
        [shape_of((96, 576), f)] + [shape_of((1, 24), f)] * 8 + [shape_of((1, 96), f)],
        [me, *parts],
        name="finish_q",
    )


def finish_ou_body(me, *refs):
    parts, w_out, w_up = refs[:2], refs[2], refs[3]
    finish_columns(me, parts, 0, 1, w_out)
    for t in range(UP_TILES):
        w_up[:, t * LANES : (t + 1) * LANES] = total(parts, pl.ds(UP_ROW + t * 96, 96))


def finish_ou(me, parts):
    f = jnp.float32
    return call(
        finish_ou_body, [shape_of((96, 192), f), shape_of((96, 768), f)], [me, *parts],
        name="finish_ou",
    )


def finish_d_body(me, *refs):
    parts, out = refs[:2], refs[2]
    for t in range(DOWN_TILES):
        out[:, t * LANES : (t + 1) * LANES] = total(parts, pl.ds(t * 192, 192))


def finish_d(me, parts, after=()):
    f = jnp.float32
    return call(finish_d_body, [shape_of((192, 384), f)], [me, *parts], after=after, name="finish_d")


PAIRS = HEADS // 2


def iota(shape, axis):
    return lax.broadcasted_iota(jnp.int32, shape, axis)


def place_matrix(order, head):
    length = order.shape[1]
    row = order[head : head + 1, :].astype(jnp.int16)
    token = iota((length, length), 0).astype(jnp.int16)
    return jnp.where(token == row, jnp.bfloat16(1.0), jnp.bfloat16(0.0))


def project_body(me, *refs):
    blocks, tokens = split_pairs(refs[:4]), refs[4]
    weights, vectors, bias_up, qkv, singles, tails = refs[5:]
    unpack_q_body(me, *blocks, weights, vectors, bias_up, singles, tails)
    for c in range(9):
        columns = slice(c * 256, (c + 1) * 256)
        value = dot(tokens[...], weights[:, columns])
        if c < 3:
            value = value + vectors[0:1, c * 256 : (c + 1) * 256]
        elif c >= 6:
            value = value + vectors[1:2, (c - 6) * 256 : (c - 5) * 256]
        qkv[:, columns] = value.astype(jnp.bfloat16)


def project(me, parts, tokens, after=()):
    return call(
        project_body,
        [
            near_shape((768, 2304)),
            near_shape((8, 768), jnp.float32),
            near_shape((1, 3072), jnp.float32),
            near_shape((tokens.shape[0], 2304)),
        ],
        [me, *parts, tokens],
        [pltpu.VMEM((4, 384, LANES), jnp.bfloat16), pltpu.VMEM((32, 16, LANES), jnp.float32)],
        after=after,
        name="project",
    )


def attend_body(first_pair, pairs, me, qkv, order, facts, *refs):
    swapped, values, soft, combined = refs[-4:]
    length = qkv.shape[0]
    groups = length // CLUSTER
    blocks = [slice(g * CLUSTER, (g + 1) * CLUSTER) for g in range(groups)]
    low = iota((length, LANES), 1) < 64
    itself = iota((CLUSTER, CLUSTER), 0) == iota((CLUSTER, CLUSTER), 1)
    pick = [
        jnp.where(iota((16, LANES), 1) == lane, 1.0, 0.0).astype(jnp.bfloat16) for lane in (64, 0)
    ]
    scale = HEAD_DIM ** (-0.5)

    for place in range(pairs):
        pair = first_pair + place

        def columns(base, pair=pair):
            return slice(base + pair * LANES, base + (pair + 1) * LANES)

        query = qkv[:, columns(0)].astype(jnp.float32)
        keys = qkv[:, columns(768)].astype(jnp.float32)
        value = qkv[:, columns(1536)].astype(jnp.float32)
        known = facts[...]
        tiles = (
            (jnp.where(low, query, pltpu.roll(keys, 64, axis=1)), jnp.where(low, value, known)),
            (jnp.where(low, pltpu.roll(query, 64, axis=1), keys), jnp.where(low, known, value)),
        )
        moved, to_tokens = [], []
        for h in range(2):
            back = place_matrix(order, 2 * pair + h)
            to_tokens.append(back)
            tile = jnp.concatenate([t.astype(jnp.bfloat16) for t in tiles[h]], axis=1)
            moved.append(dot_tn(back, tile))
        query_slots, key_slots, value_slots, codes, rows_of = [], [], [], [], []
        for h in range(2):
            both = moved[h][:, :LANES]
            query_slots.append(jnp.where(low, both, 0.0).astype(jnp.bfloat16))
            key_slots.append(pltpu.roll(both, 64, axis=1).astype(jnp.bfloat16))
            value_slots.append(moved[h][:, LANES:].astype(jnp.bfloat16))
            swapped[2 * place + h] = key_slots[h]
            values[2 * place + h] = value_slots[h]
            lane = 64 * (1 - h)
            code = moved[h][:, LANES + lane : LANES + lane + 1]
            row = dot_nt(pick[h], value_slots[h])[0:1]
            codes.append(jnp.where(code >= 32.0, code - 32.0, code))
            rows_of.append(row)
        scores = [
            [dot_nt(query_slots[h][b], key_slots[h][b]) for b in blocks] for h in range(2)
        ]
        found = []
        for h in range(2):
            outs = []
            for g, b in enumerate(blocks):
                allowed = (codes[h][b] == rows_of[h][:, b]) | itself
                value = jnp.where(allowed, scores[h][g] * scale, masked_score)
                value = jnp.exp(value - jnp.max(value, axis=1, keepdims=True))
                weights = value / jnp.sum(value, axis=1, keepdims=True)
                soft[2 * place + h, b, :] = weights
                outs.append(weights.astype(jnp.bfloat16))
            found.append(
                [dot(outs[g], value_slots[h][b]) for g, b in enumerate(blocks)]
            )
        result = None
        for h in range(2):
            value = jnp.concatenate(found[h], axis=0)
            value = jnp.where(low if h == 0 else jnp.logical_not(low), value, 0.0)
            value = dot(to_tokens[h], value.astype(jnp.bfloat16))
            result = value if result is None else result + value
        combined[:, columns(0)] = result.astype(jnp.bfloat16)


def attend(me, qkv, order, facts, first_pair, pairs, combined=None, after=()):
    length = qkv.shape[0]
    operands = [me, qkv, order, facts]
    if combined is not None:
        operands.append(combined)
    return call(
        functools.partial(attend_body, first_pair, pairs),
        [
            near_shape((2 * pairs, length, LANES)),
            near_shape((2 * pairs, length, LANES)),
            near_shape((2 * pairs, length, CLUSTER), jnp.float32),
            near_shape((length, 768)),
        ],
        operands,
        after=after,
        aliases={3: 3} if combined is not None else None,
        name="attend",
    )


def by_rows(first, count, step, body):
    for i in range(first, first + count, step):
        body(slice(i, i + step))


def mean(value):
    return jnp.mean(value, axis=1, keepdims=True)


def fold(value):
    return jnp.sum(value.reshape(value.shape[0] // 8, 8, value.shape[1]), axis=0)


def out_norm_body(me, combined, w_out, tokens, vectors, first_low, normal, inverse, total_ref):

    def rows_of(rows):
        value = total_ref[rows, :] + vectors[2:3] + tokens[rows, :].astype(jnp.float32)
        centred = value - mean(value)
        scale = lax.rsqrt(mean(centred * centred) + epsilon)
        norm = centred * scale
        normal[rows, :] = norm
        inverse[rows, :] = jnp.broadcast_to(scale, (scale.shape[0], LANES))
        first_low[rows, :] = (norm * vectors[3:4] + vectors[4:5]).astype(jnp.bfloat16)

    half = tokens.shape[0] // 2
    for first in (0, half):
        rows = slice(first, first + half)
        total_ref[rows, :] = dot(combined[rows, :], w_out[...])
        by_rows(first, half, 32, rows_of)


def out_norm(me, combined, w_out, tokens, vectors, after=()):
    n = tokens.shape[0]
    f = jnp.float32
    return call(
        out_norm_body,
        [near_shape((n, 768)), near_shape((n, 768), f), near_shape((n, LANES), f)],
        [me, combined, w_out, tokens, vectors],
        [pltpu.VMEM((n, 768), jnp.float32)],
        after=after,
        name="out_norm",
    )


def up_body(me, first_low, w_up, bias_up, activated, slope, send):
    width = w_up.shape[1] // 8
    for i in range(8):
        columns = slice(i * width, (i + 1) * width)
        hidden = dot(first_low[...], w_up[:, columns]) + bias_up[:, columns]
        half = 0.5 + 0.5 * lax.erf(hidden * (0.5**0.5))
        low = (hidden * half).astype(jnp.bfloat16)
        activated[:, columns] = low
        bell = jnp.exp(-0.5 * hidden * hidden) * (2.0 * math.pi) ** (-0.5)
        slope[:, columns] = (half + hidden * bell).astype(jnp.bfloat16)
    for i in range(8):
        k = me[0] ^ i

        @pl.when((k & 1) == 1)
        def _():
            there = pl.ds(pl.multiple_of((k >> 1) * width, LANES), width)
            send[:, there] = activated[:, i * width : (i + 1) * width]


def up(me, first_low, w_up, bias_up, after=()):
    n, width = first_low.shape[0], w_up.shape[1]
    return call(
        up_body,
        [near_shape((n, width)), near_shape((n, width)), shape_of((n, width // 2))],
        [me, first_low, w_up, bias_up],
        after=after,
        name="up",
    )


def down_norm_body(
    me, activated, turned, normal, vectors, out, feed_grad, second_grad, sums, feed, acc
):
    acc[...] = jnp.zeros_like(acc)

    def rows_of(rows):
        value = normal[rows, :] * vectors[3:4] + vectors[4:5] + feed[rows, :] + vectors[5:6]
        centred = value - mean(value)
        inverse = lax.rsqrt(mean(centred * centred) + epsilon)
        norm = centred * inverse
        out[rows, :] = (norm * vectors[6:7] + vectors[7:8]).astype(jnp.bfloat16)
        upstream = me.arrived(0)[rows, :]
        scaled = upstream * vectors[6:7]
        back = inverse * (scaled - mean(scaled) - norm * mean(scaled * norm))
        second_grad[rows, :] = back
        low = back.astype(jnp.bfloat16)
        feed_grad[rows, :] = low
        acc[0] += fold(low.astype(jnp.float32))
        acc[1] += fold(upstream * norm)
        acc[2] += fold(upstream)

    half = out.shape[0] // 2
    for first in (0, half):
        rows = slice(first, first + half)
        feed[rows, :] = dot_nt(activated[rows, :], turned[...])
        by_rows(first, half, 32, rows_of)
    me.send(0)
    for i in range(3):
        sums[i : i + 1, :] = jnp.sum(acc[i], axis=0, keepdims=True)


def down_norm(me, activated, turned, normal, vectors, cotangent, after=()):
    n = cotangent.shape[0]
    return call(
        down_norm_body,
        [
            shape_of((n, 768)),
            near_shape((n, 768)),
            near_shape((n, 768), jnp.float32),
            near_shape((3, 768), jnp.float32),
        ],
        [me, cotangent, activated, turned, normal, vectors],
        [pltpu.VMEM((n, 768), jnp.float32), pltpu.VMEM((3, 8, 768), jnp.float32)],
        late=[None],
        far_outs={0: True},
        after=after,
        name="down_norm",
    )


def hidden_back_body(me, feed_grad, turned, slope, hidden_grad, sums):
    for i in range(hidden_grad.shape[1] // 256):
        columns = slice(i * 256, (i + 1) * 256)
        value = dot(feed_grad[...], turned[:, columns]) * slope[:, columns].astype(jnp.float32)
        low = value.astype(jnp.bfloat16)
        hidden_grad[:, columns] = low
        sums[:, columns] = jnp.sum(low.astype(jnp.float32), axis=0, keepdims=True)


def hidden_back(me, feed_grad, turned, slope, after=()):
    return call(
        hidden_back_body,
        [near_shape(slope.shape), near_shape((1, slope.shape[1]), jnp.float32)],
        [me, feed_grad, turned, slope],
        after=after,
        name="hidden_back",
    )


def first_back_body(
    me, hidden_grad, w_up, second_grad, normal, inverse, vectors, residual, low_out, left, right, sums, back,
    acc,
):
    acc[...] = jnp.zeros_like(acc)

    def rows_of(rows):
        upstream = back[rows, :] + second_grad[rows, :]
        norm = normal[rows, :]
        scaled = upstream * vectors[3:4]
        value = inverse[rows, 0:1] * (scaled - mean(scaled) - norm * mean(scaled * norm))
        residual[rows, :] = value
        low = value.astype(jnp.bfloat16)
        low_out[rows, :] = low
        left[rows, :] = low[:, :384]
        right[rows, :] = low[:, 384:]
        acc[0] += fold(low.astype(jnp.float32))
        acc[1] += fold(upstream * norm)
        acc[2] += fold(upstream)

    half = normal.shape[0] // 2
    for first in (0, half):
        rows = slice(first, first + half)
        back[rows, :] = dot_nt(hidden_grad[rows, :], w_up[...])
        by_rows(first, half, 32, rows_of)
    for i in range(3):
        sums[i : i + 1, :] = jnp.sum(acc[i], axis=0, keepdims=True)


def first_back(me, hidden_grad, w_up, second_grad, normal, inverse, vectors, after=()):
    n = normal.shape[0]
    return call(
        first_back_body,
        [
            near_shape((n, 768), jnp.float32),
            near_shape((n, 768)),
            shape_of((n, 384)),
            shape_of((n, 384)),
            near_shape((3, 768), jnp.float32),
        ],
        [me, hidden_grad, w_up, second_grad, normal, inverse, vectors],
        [pltpu.VMEM((n, 768), jnp.float32), pltpu.VMEM((3, 8, 768), jnp.float32)],
        after=after,
        name="first_back",
    )


def attend_back_body(
    first_pair, pairs, me, attention_grad, w_out, order, swapped, values, soft, *refs
):
    grads, sums, upstream = refs[-3:]
    length = attention_grad.shape[0]
    groups = length // CLUSTER
    blocks = [slice(g * CLUSTER, (g + 1) * CLUSTER) for g in range(groups)]
    low = iota((length, LANES), 1) < 64
    low_rows = iota((CLUSTER, LANES), 1) < 64
    scale = HEAD_DIM ** (-0.5)
    mine = slice(first_pair * LANES, (first_pair + pairs) * LANES)
    upstream[...] = dot_nt(attention_grad[...], w_out[mine, :]).astype(jnp.bfloat16)

    for place in range(pairs):
        pair = first_pair + place

        def columns(base, pair=pair):
            return slice(base + pair * LANES, base + (pair + 1) * LANES)

        both = upstream[:, slice(place * LANES, (place + 1) * LANES)]
        to_tokens, moved = [], []
        for h in range(2):
            to_tokens.append(place_matrix(order, 2 * pair + h))
            value = dot_tn(to_tokens[h], both)
            value = jnp.where(low if h == 0 else jnp.logical_not(low), value, 0.0)
            moved.append(value.astype(jnp.bfloat16))
        back = []
        for h in range(2):
            kept = 2 * place + h
            keys = [swapped[kept, b, :] for b in blocks]
            weights = [soft[kept, b, :] for b in blocks]
            soft_grad = [dot_nt(moved[h][b], values[kept, b, :]) for b in blocks]
            value_grad = [
                dot_tn(weights[g].astype(jnp.bfloat16), moved[h][b]) for g, b in enumerate(blocks)
            ]
            score_grad = []
            for g in range(groups):
                middle = jnp.sum(soft_grad[g] * weights[g], axis=1, keepdims=True)
                score_grad.append((weights[g] * (soft_grad[g] - middle)).astype(jnp.bfloat16))
            query_grad = [dot(score_grad[g], keys[g]) for g in range(groups)]
            key_grad = [dot_tn(score_grad[g], keys[g]) for g in range(groups)]
            parts = [
                jnp.concatenate(
                    [
                        (jnp.where(low_rows, query_grad[g], key_grad[g]) * scale).astype(
                            jnp.bfloat16
                        ),
                        value_grad[g].astype(jnp.bfloat16),
                    ],
                    axis=1,
                )
                for g in range(groups)
            ]
            back.append(dot(to_tokens[h], jnp.concatenate(parts, axis=0)))
        first, second = back[0][:, :LANES], back[1][:, :LANES]
        query = jnp.where(low, first, pltpu.roll(second, 64, axis=1))
        keys = jnp.where(low, pltpu.roll(first, 64, axis=1), second)
        value = back[0][:, LANES:] + back[1][:, LANES:]
        grads[:, columns(0)] = query.astype(jnp.bfloat16)
        grads[:, columns(768)] = keys.astype(jnp.bfloat16)
        grads[:, columns(1536)] = value.astype(jnp.bfloat16)
        sums[0:1, columns(0)] = jnp.sum(query, axis=0, keepdims=True)
        sums[1:2, columns(0)] = jnp.sum(value, axis=0, keepdims=True)


def attend_back(
    me, attention_grad, w_out, order, kept, first_pair, pairs, before=(), after=()
):
    length = attention_grad.shape[0]
    return call(
        functools.partial(attend_back_body, first_pair, pairs),
        [near_shape((length, 2304)), near_shape((2, 768), jnp.float32)],
        [me, attention_grad, w_out, order, *kept, *before],
        [pltpu.VMEM((length, pairs * LANES), jnp.bfloat16)],
        after=after,
        aliases={6: 0, 7: 1} if before else None,
        name="attend_back",
    )


def tokens_back_body(me, grads, weights, residual, out):
    for c in range(3):
        columns = slice(c * 256, (c + 1) * 256)
        out[:, columns] = dot_nt(grads[...], weights[columns, :]) + residual[:, columns]
        me.send(0, (slice(None), columns))


def tokens_back(me, grads, weights, residual, after=()):
    return call(
        tokens_back_body,
        [shape_of(residual.shape, jnp.float32)],
        [me, grads, weights, residual],
        far_outs={0: True},
        sends=3,
        after=after,
        name="tokens_back",
    )


def local_block(
    tokens,
    w_qkv,
    bias_query,
    bias_value,
    w_out,
    bias_out,
    gain_one,
    shift_one,
    w_up,
    bias_up,
    w_down,
    bias_down,
    gain_two,
    shift_two,
    cluster_order,
    segment_ids,
    padding,
    cotangent,
):
    length = tokens.shape[0]
    me = None
    vector_list = [
        bias_query, bias_value, bias_out, gain_one, shift_one, bias_down, gain_two, shift_two
    ]
    order = cluster_order[0]
    facts = (segment_ids[0] + 32 * (1 - padding[0])).astype(jnp.float32)
    facts = jnp.broadcast_to(facts[:, None], (length, 128))

    def other(x):
        return swap(x, "dp", CORE)

    blocks_q = pack_q(me, w_qkv, vector_list, bias_up)
    z_q = gather_z(*blocks_q)
    blocks_rest = pack_rest(me, w_out, w_up, w_down, after=[blocks_q])
    block_ou, upper, lower, block_d = blocks_rest
    upper_x, lower_y = swap(upper, "dp", ALONG_X), swap(lower, "dp", ALONG_Y)
    tokens_turned = turn(me, tokens, after=[blocks_rest])
    near_q = gather_near(me, z_q, after=[tokens_turned, upper_x, lower_y])
    upper, lower = spread_d(me, block_d, upper_x, lower_y, after=[near_q])
    upper_y, lower_x = swap(upper, "dp", ALONG_Y), swap(lower, "dp", ALONG_X)
    (block_ou,) = tie([block_ou], [near_q])
    far_z_ou = swap(block_ou, "mp", 2)
    near_d = whole_d(me, upper, upper_y, lower, lower_x)
    far_q = gather_far(me, near_q, after=[near_d, far_z_ou])
    far_d = swap(near_d[0], "mp", 2)
    near_z_ou = beside_two(me, block_ou, far_z_ou, after=[far_q])
    z_ou = tie([near_z_ou[0], swap(near_z_ou[0], "mp", 1)], [near_z_ou])
    near_ou = [z_ou[0], swap(z_ou[0], "dp", ALONG_X), z_ou[1], swap(z_ou[1], "dp", ALONG_Y)]
    far_ou = gather_far(me, near_ou, after=far_q[2:])
    both_d = beside_two(me, near_d[0], far_d, after=[far_ou])
    z_d = swap(both_d[0], "mp", 1)
    pairs_q = beside(
        me,
        [(x, (i // 2, i % 2)) for i, x in enumerate(far_q)],
        [(2, *far_q[0].shape)] * 2,
        [both_d],
        "beside_far",
    )
    parts_q = list(pairs_q)
    parts_q = [*parts_q, *[other(x) for x in parts_q]]
    projected = project(me, parts_q, tokens)
    full_qkv, vectors, full_bias_up, qkv = projected

    pairs = PAIRS // 3

    def forward(part, before, after):
        return attend(
            me, qkv, order, facts, part * pairs, pairs, before, after=after
        )

    seen_a = forward(0, None, [projected])
    seen_b = forward(1, seen_a[-1], [seen_a])
    far_ou = tie(far_ou, [seen_b])
    seen_c = forward(2, seen_b[-1], far_ou[:1])
    combined = seen_c[-1]
    combined_turned = turn(me, combined)
    full_out, full_up = unpack_ou(me, gather_core(far_ou), after=[combined_turned])
    normed = out_norm(me, combined, full_out, tokens, vectors)
    first_low, normal, inverse = normed
    first_turned = turn(me, first_low)
    upper = up(me, first_low, full_up, full_bias_up, after=[first_turned])
    activated, slope, send_activated = upper
    sends = tie(
        [combined_turned[0], first_turned[0], send_activated, tokens_turned[0]], [upper]
    )
    others = [other(x) for x in sends]
    parts_d = tie([both_d[0], z_d], [upper])
    parts_d = [*parts_d, *[other(x) for x in parts_d]]
    unpacked = unpack_d(me, parts_d, after=others)
    turned_down = unpacked[0]
    downed = down_norm(me, activated, turned_down, normal, vectors, cotangent)
    layer_out, feed_grad, second_grad, sums_two = downed
    other_tokens = others[3]

    other_feed = other(feed_grad)
    hidden = hidden_back(me, feed_grad, turned_down, slope, after=[downed])
    hidden_grad, sums_up = hidden
    (hidden_grad,) = tie([hidden_grad], [hidden, other_feed])
    other_hidden = other(hidden_grad)
    grad_d = gradient_d(
        me, feed_grad, other_feed, activated, others[2], after=[hidden]
    )
    core_d = scatter_near(grad_d)
    first = first_back(
        me, hidden_grad, full_up, second_grad, normal, inverse, vectors, after=[grad_d]
    )
    residual_grad, attention_grad, *halves, sums_one = first
    halves = [other(x) for x in halves]

    def back(part, kept, before, after):
        return attend_back(
            me, attention_grad, full_out, order, kept,
            part * pairs, pairs, before, after,
        )

    grads_a = back(0, seen_a[:3], (), [first])
    grads_b = back(1, seen_b[:3], grads_a, [])
    grads_c = back(2, seen_c[:3], grads_b, halves)
    half_d = add_plane(me, core_d, after=[grads_c])
    plane_d = scatter_far(half_d)
    projected_grad, sums_bias = grads_c
    grad_vectors = all_sums(me, sums_bias, sums_one, sums_two, sums_up)
    projected_grad, grad_vectors = tie([projected_grad, grad_vectors], [half_d])
    other_grads = other(projected_grad), other(grad_vectors)
    grad_ou = gradient_ou(
        me,
        (combined_turned[1], others[0]),
        (first_turned[1], others[1]),
        (hidden_grad, other_hidden),
        (attention_grad, *halves),
        after=[half_d],
    )
    core_ou = scatter_near(grad_ou)
    last_d = add_last(me, plane_d, after=[grad_ou], cost=22 * MICROSECOND)
    z_d = scatter_z(last_d)
    grad_q = gradient_q(
        me, tokens_turned[1], other_tokens, projected_grad, other_grads[0], grad_vectors,
        other_grads[1], after=[last_d],
    )
    core_q = scatter_near(grad_q)
    moved = tokens_back(me, projected_grad, full_qkv, residual_grad, after=[grad_q])
    grad_tokens = moved[0]
    near_d = add_z(me, z_d, after=[moved])
    sum_d = scatter_z_far(near_d)
    half_ou = add_plane(me, core_ou, after=[near_d])
    plane_ou = scatter_far(half_ou)
    half_q = add_plane(me, core_q, after=[half_ou])
    plane_q = scatter_far(half_q)
    last_ou = add_last(me, plane_ou, after=[half_q])
    z_ou = scatter_z(last_ou)
    done_d = finish_d(me, sum_d, after=[last_ou])
    last_q = add_last(me, plane_q, after=[done_d])
    z_q = scatter_z(last_q)
    near_ou = add_z(me, z_ou, after=[last_q])
    sum_ou = scatter_z_far(near_ou)
    near_q = add_z(me, z_q, after=[near_ou])
    sum_q = scatter_z_far(near_q)
    shard_out, shard_up = finish_ou(me, sum_ou)
    shard_qkv, *shard_vectors = finish_q(me, sum_q)
    shard_down = done_d[0].T
    grad_list = [v.reshape(-1) for v in shard_vectors]
    return (
        layer_out,
        grad_tokens,
        shard_qkv,
        grad_list[0],
        grad_list[1],
        shard_out,
        grad_list[2],
        grad_list[3],
        grad_list[4],
        shard_up,
        grad_list[8],
        shard_down,
        grad_list[5],
        grad_list[6],
        grad_list[7],
    )


def solution(mesh):
    in_specs = (
        P(("dp", "mp"), None),
        P("dp", "mp"),
        P(("dp", "mp")),
        P(("dp", "mp")),
        P("dp", "mp"),
        P(("dp", "mp")),
        P(("dp", "mp")),
        P(("dp", "mp")),
        P("dp", "mp"),
        P(("dp", "mp")),
        P("dp", "mp"),
        P(("dp", "mp")),
        P(("dp", "mp")),
        P(("dp", "mp")),
        P(("dp", "mp"), None, None),
        P(("dp", "mp"), None),
        P(("dp", "mp"), None),
        P(("dp", "mp"), None),
    )
    out_specs = (
        P(("dp", "mp"), None),
        P(("dp", "mp"), None),
        P("dp", "mp"),
        P(("dp", "mp")),
        P(("dp", "mp")),
        P("dp", "mp"),
        P(("dp", "mp")),
        P(("dp", "mp")),
        P(("dp", "mp")),
        P("dp", "mp"),
        P(("dp", "mp")),
        P("dp", "mp"),
        P(("dp", "mp")),
        P(("dp", "mp")),
        P(("dp", "mp")),
    )
    blocks = mesh.shape["dp"] == 8 and mesh.shape["mp"] == 4
    local = local_block if blocks else local_general
    return jax.shard_map(local, mesh=mesh, in_specs=in_specs, out_specs=out_specs, check_vma=False)
```

```python
import functools
import math

import jax
import jax.numpy as jnp
from jax import lax
from jax.experimental import pallas as pl
from jax.experimental.pallas import tpu as pltpu
from jax.sharding import PartitionSpec as P

HEADS = 12
HEAD_DIM = 64
CLUSTER = 128


epsilon = 1e-12
masked_score = -1e30


def product(left_side, right_side):
    return jnp.dot(left_side, right_side, preferred_element_type=jnp.float32)


def times_back(left_side, right_side):
    return lax.dot_general(
        left_side, right_side, (((1,), (1,)), ((), ())), preferred_element_type=jnp.float32
    )


def outer_sum(left_side, right_side):
    return lax.dot_general(
        left_side, right_side, (((0,), (0,)), ((), ())), preferred_element_type=jnp.float32
    )


def norm_forward(hidden, norm_gain, norm_shift):
    average = jnp.mean(hidden, axis=-1, keepdims=True)
    centred = hidden - average
    variance = jnp.mean(centred * centred, axis=-1, keepdims=True)
    inverse = lax.rsqrt(variance + epsilon)
    normal = centred * inverse
    return (normal * norm_gain + norm_shift, normal, inverse)


def norm_backward(upstream, normal, inverse, norm_gain):
    scaled = upstream * norm_gain
    return inverse * (
        scaled
        - jnp.mean(scaled, axis=-1, keepdims=True)
        - normal * jnp.mean(scaled * normal, axis=-1, keepdims=True)
    )


def gelu_exact(inputs):
    return jax.nn.gelu(inputs, approximate=False)


def local_general(
    tokens,
    w_qkv,
    bias_query,
    bias_value,
    w_out,
    bias_out,
    gain_one,
    shift_one,
    w_up,
    bias_up,
    w_down,
    bias_down,
    gain_two,
    shift_two,
    cluster_order,
    segment_ids,
    padding,
    cotangent,
):
    model_width = HEADS * HEAD_DIM
    length = tokens.shape[0]
    groups = length // CLUSTER
    score_scale = HEAD_DIM ** (-0.5)
    vectors = jnp.stack(
        [bias_query, bias_value, bias_out, gain_one, shift_one, bias_down, gain_two, shift_two]
    ).astype(jnp.bfloat16)
    vector_up = bias_up.astype(jnp.bfloat16)[None, :]
    part_qkv = w_qkv.astype(jnp.bfloat16)
    part_out = w_out.astype(jnp.bfloat16)
    part_up = w_up.astype(jnp.bfloat16)
    part_down = w_down.astype(jnp.bfloat16)
    column_qkv, column_out, column_up, column_down, column_vectors, column_bias = (
        lax.all_gather(part_qkv, "mp", axis=1, tiled=True),
        lax.all_gather(part_out, "mp", axis=1, tiled=True),
        lax.all_gather(part_up, "mp", axis=1, tiled=True),
        lax.all_gather(part_down, "mp", axis=1, tiled=True),
        lax.all_gather(vectors, "mp", axis=1, tiled=True),
        lax.all_gather(vector_up, "mp", axis=1, tiled=True),
    )
    full_qkv, full_out, full_up, full_down, full_vectors, full_bias = (
        lax.all_gather(column_qkv, "dp", axis=0, tiled=True),
        lax.all_gather(column_out, "dp", axis=0, tiled=True),
        lax.all_gather(column_up, "dp", axis=0, tiled=True),
        lax.all_gather(column_down, "dp", axis=0, tiled=True),
        lax.all_gather(column_vectors, "dp", axis=1, tiled=True),
        lax.all_gather(column_bias, "dp", axis=1, tiled=True),
    )
    small_params = full_vectors.astype(jnp.float32)
    hidden_bias = full_bias[0].astype(jnp.float32)
    ordering = cluster_order[0]
    segment = segment_ids[0]
    present = padding[0]
    positions = jnp.arange(length, dtype=jnp.int32)
    placement = (ordering[:, :, None] == positions[None, None, :]).astype(jnp.bfloat16)

    def to_clusters(matrix):
        per_head = matrix.reshape(length, HEADS, HEAD_DIM)
        moved = jnp.einsum("hip,phd->hid", placement, per_head, preferred_element_type=jnp.float32)
        return moved.astype(jnp.bfloat16).reshape(HEADS, groups, CLUSTER, HEAD_DIM)

    def from_clusters(blocks):
        per_head = blocks.astype(jnp.bfloat16).reshape(HEADS, length, HEAD_DIM)
        moved = jnp.einsum("hip,hid->phd", placement, per_head, preferred_element_type=jnp.float32)
        return moved.astype(jnp.bfloat16).reshape(length, model_width)

    segment_blocks = jnp.take(segment, ordering).reshape(HEADS, groups, CLUSTER)
    present_blocks = jnp.take(present, ordering).reshape(HEADS, groups, CLUSTER)
    same_doc = segment_blocks[..., :, None] == segment_blocks[..., None, :]
    itself = jnp.eye(CLUSTER, dtype=bool)
    allowed = same_doc & ((present_blocks[..., None, :] == 1) | itself)

    def scores_of(query_blocks, key_blocks):
        raw_scores = (
            jnp.einsum(
                "hncd,hnmd->hncm", query_blocks, key_blocks, preferred_element_type=jnp.float32
            )
            * score_scale
        )
        return jnp.where(allowed, raw_scores, masked_score)

    projected = product(tokens, full_qkv)
    query = (projected[:, :model_width] + small_params[0]).astype(jnp.bfloat16)
    keys = projected[:, model_width : 2 * model_width].astype(jnp.bfloat16)
    values = (projected[:, 2 * model_width :] + small_params[1]).astype(jnp.bfloat16)
    query_blocks = to_clusters(query)
    key_blocks = to_clusters(keys)
    value_blocks = to_clusters(values)
    masked = scores_of(query_blocks, key_blocks)
    highest = jnp.max(masked, axis=-1, keepdims=True)
    exponent = jnp.exp(masked - highest)
    row_total = jnp.sum(exponent, axis=-1, keepdims=True)
    soft_weights = exponent / row_total
    log_total = highest + jnp.log(row_total)
    soft_low = soft_weights.astype(jnp.bfloat16)
    combined = from_clusters(
        jnp.einsum("hncm,hnmd->hncd", soft_low, value_blocks, preferred_element_type=jnp.float32)
    )
    attention = product(combined, full_out) + small_params[2]
    first_norm, first_normal, first_inverse = norm_forward(
        tokens.astype(jnp.float32) + attention, small_params[3], small_params[4]
    )
    first_low = first_norm.astype(jnp.bfloat16)
    hidden = product(first_low, full_up) + hidden_bias
    activated, gelu_pull = jax.vjp(gelu_exact, hidden)
    activated_low = activated.astype(jnp.bfloat16)
    feed_out = product(activated_low, full_down) + small_params[5]
    output, second_normal, second_inverse = norm_forward(
        first_norm + feed_out, small_params[6], small_params[7]
    )
    layer_out = output.astype(jnp.bfloat16)
    again_qkv, again_out, again_up, again_down = (
        lax.all_gather(part_qkv, "mp", axis=1, tiled=True),
        lax.all_gather(part_out, "mp", axis=1, tiled=True),
        lax.all_gather(part_up, "mp", axis=1, tiled=True),
        lax.all_gather(part_down, "mp", axis=1, tiled=True),
    )
    back_qkv, back_out, back_up, back_down = (
        lax.all_gather(again_qkv, "dp", axis=0, tiled=True),
        lax.all_gather(again_out, "dp", axis=0, tiled=True),
        lax.all_gather(again_up, "dp", axis=0, tiled=True),
        lax.all_gather(again_down, "dp", axis=0, tiled=True),
    )
    grad_gain_two = jnp.sum(cotangent * second_normal, axis=0)
    grad_shift_two = jnp.sum(cotangent, axis=0)
    second_grad = norm_backward(cotangent, second_normal, second_inverse, small_params[6])
    feed_grad = second_grad.astype(jnp.bfloat16)
    grad_bias_down = jnp.sum(feed_grad.astype(jnp.float32), axis=0)
    grad_w_down = outer_sum(activated_low, feed_grad)
    hidden_grad = gelu_pull(times_back(feed_grad, back_down))[0].astype(jnp.bfloat16)
    grad_bias_up = jnp.sum(hidden_grad.astype(jnp.float32), axis=0)
    grad_w_up = outer_sum(first_low, hidden_grad)
    first_grad = times_back(hidden_grad, back_up) + second_grad
    grad_gain_one = jnp.sum(first_grad * first_normal, axis=0)
    grad_shift_one = jnp.sum(first_grad, axis=0)
    residual_grad = norm_backward(first_grad, first_normal, first_inverse, small_params[3])
    attention_grad = residual_grad.astype(jnp.bfloat16)
    grad_bias_out = jnp.sum(attention_grad.astype(jnp.float32), axis=0)
    grad_w_out = outer_sum(combined, attention_grad)
    combined_grad = to_clusters(times_back(attention_grad, back_out).astype(jnp.bfloat16))
    masked_again = scores_of(query_blocks, key_blocks)
    soft_again = jnp.exp(masked_again - log_total)
    soft_again_low = soft_again.astype(jnp.bfloat16)
    value_sums = jnp.einsum(
        "hncm,hncd->hnmd", soft_again_low, combined_grad, preferred_element_type=jnp.float32
    )
    soft_grad = jnp.einsum(
        "hncd,hnmd->hncm", combined_grad, value_blocks, preferred_element_type=jnp.float32
    )
    score_grad = (
        soft_again * (soft_grad - jnp.sum(soft_grad * soft_again, axis=-1, keepdims=True))
    ).astype(jnp.bfloat16)
    query_sums = (
        jnp.einsum("hncm,hnmd->hncd", score_grad, key_blocks, preferred_element_type=jnp.float32)
        * score_scale
    )
    key_sums = (
        jnp.einsum("hncm,hncd->hnmd", score_grad, query_blocks, preferred_element_type=jnp.float32)
        * score_scale
    )
    query_grad = from_clusters(query_sums)
    key_grad = from_clusters(key_sums)
    value_grad = from_clusters(value_sums)
    grad_bias_query = jnp.sum(query_grad.astype(jnp.float32), axis=0)
    grad_bias_value = jnp.sum(value_grad.astype(jnp.float32), axis=0)
    projected_grad = jnp.concatenate([query_grad, key_grad, value_grad], axis=1)
    grad_w_qkv = outer_sum(tokens, projected_grad)
    grad_tokens = times_back(projected_grad, back_qkv) + residual_grad
    grad_vectors = jnp.stack(
        [
            grad_bias_query,
            grad_bias_value,
            grad_bias_out,
            grad_gain_one,
            grad_shift_one,
            grad_bias_down,
            grad_gain_two,
            grad_shift_two,
        ]
    )
    grad_up_row = grad_bias_up[None, :]
    row_qkv, row_out, row_up, row_down, row_vectors, row_bias = (
        lax.psum_scatter(
            grad_w_qkv.astype(jnp.bfloat16), "dp", scatter_dimension=0, tiled=True
        ).astype(jnp.float32),
        lax.psum_scatter(
            grad_w_out.astype(jnp.bfloat16), "dp", scatter_dimension=0, tiled=True
        ).astype(jnp.float32),
        lax.psum_scatter(
            grad_w_up.astype(jnp.bfloat16), "dp", scatter_dimension=0, tiled=True
        ).astype(jnp.float32),
        lax.psum_scatter(
            grad_w_down.astype(jnp.bfloat16), "dp", scatter_dimension=0, tiled=True
        ).astype(jnp.float32),
        lax.psum_scatter(
            grad_vectors.astype(jnp.bfloat16), "dp", scatter_dimension=1, tiled=True
        ).astype(jnp.float32),
        lax.psum_scatter(
            grad_up_row.astype(jnp.bfloat16), "dp", scatter_dimension=1, tiled=True
        ).astype(jnp.float32),
    )
    shard_qkv, shard_out, shard_up, shard_down, shard_vectors, shard_bias = (
        lax.psum_scatter(
            row_qkv.astype(jnp.bfloat16), "mp", scatter_dimension=1, tiled=True
        ).astype(jnp.float32),
        lax.psum_scatter(
            row_out.astype(jnp.bfloat16), "mp", scatter_dimension=1, tiled=True
        ).astype(jnp.float32),
        lax.psum_scatter(row_up.astype(jnp.bfloat16), "mp", scatter_dimension=1, tiled=True).astype(
            jnp.float32
        ),
        lax.psum_scatter(
            row_down.astype(jnp.bfloat16), "mp", scatter_dimension=1, tiled=True
        ).astype(jnp.float32),
        lax.psum_scatter(
            row_vectors.astype(jnp.bfloat16), "mp", scatter_dimension=1, tiled=True
        ).astype(jnp.float32),
        lax.psum_scatter(
            row_bias.astype(jnp.bfloat16), "mp", scatter_dimension=1, tiled=True
        ).astype(jnp.float32),
    )
    return (
        layer_out,
        grad_tokens,
        shard_qkv,
        shard_vectors[0],
        shard_vectors[1],
        shard_out,
        shard_vectors[2],
        shard_vectors[3],
        shard_vectors[4],
        shard_up,
        shard_bias[0],
        shard_down,
        shard_vectors[5],
        shard_vectors[6],
        shard_vectors[7],
    )


LANES = 128
QKV_ROWS = 96
UP_TILES = 6
DOWN_TILES = 3
PACK_Q = 4 * QKV_ROWS + QKV_ROWS // 2 + 16
PACK_OU = QKV_ROWS + QKV_ROWS // 2 + UP_TILES * QKV_ROWS
PACK_D = DOWN_TILES * 192
VECTOR_ROW = 4 * QKV_ROWS + QKV_ROWS // 2
UP_ROW = QKV_ROWS + QKV_ROWS // 2


def whole():
    return pl.BlockSpec(memory_space=pltpu.VMEM)


def far():
    return pl.BlockSpec(memory_space=pltpu.HBM)


def kept_far(arrays):
    return [pltpu.with_memory_space_constraint(x, pltpu.HBM) for x in arrays]


def near(x):
    return pltpu.with_memory_space_constraint(x, pltpu.VMEM)


def near_shape(shape, dtype=jnp.bfloat16):
    return pltpu.VMEM(shape, dtype)


def waited(after):
    return [kept_far([x.token])[0] if isinstance(x, Results) else x for x in after]


def anywhere(after):
    return [far() if isinstance(x, Results) else pl.BlockSpec(memory_space=pl.ANY) for x in after]


class Results(list):
    token = None


TOKEN = pltpu.HBM((8, 128), jnp.float32)


def place():
    return lax.axis_index("dp"), lax.axis_index("mp")


SHORT = pl.CostEstimate(flops=1, bytes_accessed=1, transcendentals=0)
MICROSECOND = 1_153_000_000


class Place(tuple):
    def arrived(self, index, part=None):
        copies, here = self.late[index]
        for i in range(len(copies)) if part is None else [part]:
            if copies[i] is not None:
                copies[i].wait()
                copies[i] = None
        return here

    def send(self, index, where=None, source=None):
        here, there = self.far[index]
        source = here if source is None else source
        if where is not None:
            source, there = source.at[where], there.at[where]
        copy = pltpu.make_async_copy(source, there, self.sems.at[len(self.sent)])
        copy.start()
        self.sent.append(copy)


def call(
    body, out_shapes, operands, scratch=(), staged=0, late=(), far_outs=None, sends=None, after=(),
    aliases=None, vmem=10, cost=0, name=None,
):
    operands = operands[1:]
    far_outs = far_outs or {}
    sends = len(far_outs) if sends is None else sends
    count, outs, copied = len(operands), len(out_shapes), staged + len(late)
    spread = [(0, 1)] * staged + [x or (0, 1) for x in late]
    starts = [sum(n for _, n in spread[:i]) for i in range(copied)]

    def with_copies(*refs):
        sources, rest = refs[:copied], refs[copied:count]
        results = list(refs[count + len(after) : count + len(after) + outs])
        own = refs[count + len(after) + outs + 1 :]
        mine, own = own[: len(scratch)], own[len(scratch) :]
        arrived, own = own[:copied], list(own[copied:])
        me = Place(place())
        me.sent, me.far = [], {}
        if copied:
            sem = own.pop(0)
            copies = []
            for source, here, (axis, parts), start in zip(sources, arrived, spread, starts):
                size = here.shape[axis] // parts
                copies.append([])
                for i in range(parts):
                    cut = (slice(None),) * axis + (slice(i * size, (i + 1) * size),)
                    copies[-1].append(
                        pltpu.make_async_copy(source.at[cut], here.at[cut], sem.at[start + i])
                    )
            for copy in sum(copies, []):
                copy.start()
            for (copy,) in copies[:staged]:
                copy.wait()
            me.late = list(zip(copies[staged:], arrived[staged:]))
        if far_outs:
            me.sems = own.pop(0)
            for index, has_room in far_outs.items():
                here = own.pop(0) if has_room else None
                me.far[index] = (here, results[index])
                results[index] = here
        body(me, *arrived[:staged], *rest, *results, *mine)
        for copy in me.sent:
            copy.wait()

    room = [pltpu.VMEM(x.shape, x.dtype) for x in operands[:copied]]
    if copied:
        room.append(pltpu.SemaphoreType.DMA((sum(n for _, n in spread),)))
    if far_outs:
        room.append(pltpu.SemaphoreType.DMA((sends,)))
        room += [pltpu.VMEM(out_shapes[i].shape, out_shapes[i].dtype) for i in far_outs if far_outs[i]]
    given = [
        pltpu.HBM(x.shape, x.dtype) if i in far_outs else x for i, x in enumerate(out_shapes)
    ]
    *results, token = pl.pallas_call(
        with_copies,
        out_shape=[*given, TOKEN],
        in_specs=[pl.BlockSpec(memory_space=pl.ANY)] * staged
        + [far()] * len(late)
        + [whole()] * (count - copied)
        + anywhere(after),
        out_specs=[far() if i in far_outs else whole() for i in range(outs)] + [far()],
        scratch_shapes=list(scratch) + room,
        input_output_aliases=aliases or {},
        compiler_params=pltpu.CompilerParams(vmem_limit_bytes=vmem * 1024 * 1024),
        cost_estimate=SHORT if not cost else pl.CostEstimate(cost, 1, 0),
        name=name,
    )(
        *operands[:staged],
        *kept_far(operands[staged:copied]),
        *operands[copied:],
        *waited(after),
    )
    results = Results(results)
    results.token = token
    return results


def tie(arrays, after):
    count = len(arrays)

    def body(*refs):
        pass

    return pl.pallas_call(
        body,
        out_shape=[shape_of(x.shape, x.dtype) for x in arrays],
        in_specs=[pl.BlockSpec(memory_space=pl.ANY)] * count + anywhere(after),
        out_specs=[pl.BlockSpec(memory_space=pl.ANY)] * count,
        input_output_aliases={i: i for i in range(count)},
        compiler_params=pltpu.CompilerParams(vmem_limit_bytes=1024 * 1024),
        cost_estimate=SHORT,
        name="tie",
    )(*arrays, *waited(after))


def shape_of(shape, dtype=jnp.bfloat16):
    return jax.ShapeDtypeStruct(shape, dtype)


def halves_beside(single):
    half = single.shape[0] // 2
    return jnp.concatenate([single[:half], single[half:]], axis=1)


def pack_columns(odd, low, tiles, base, target):
    @pl.when(odd)
    def _():
        for t in range(tiles):
            target[base + t * 96 : base + (t + 1) * 96, :] = low[
                :, 64 + t * LANES : 64 + (t + 1) * LANES
            ].astype(jnp.bfloat16)
        target[base + tiles * 96 : base + tiles * 96 + 48, :] = halves_beside(low[:, :64]).astype(
            jnp.bfloat16
        )

    @pl.when(jnp.logical_not(odd))
    def _():
        for t in range(tiles):
            target[base + t * 96 : base + (t + 1) * 96, :] = low[
                :, t * LANES : (t + 1) * LANES
            ].astype(jnp.bfloat16)
        target[base + tiles * 96 : base + tiles * 96 + 48, :] = halves_beside(
            low[:, tiles * LANES : tiles * LANES + 64]
        ).astype(jnp.bfloat16)


def pack_q_body(me, *refs):
    w_qkv, vectors, target, own = refs[0], refs[1:10], refs[10], refs[11]
    pack_columns(lax.rem(me[1], 2) == 1, w_qkv[...], 4, 0, target)
    rows = lax.broadcasted_iota(jnp.int32, (16, LANES), 0)
    tail = jnp.zeros((16, LANES), jnp.float32)
    for v in range(9):
        value = vectors[v][...]
        wide = jnp.concatenate(
            [value, jnp.zeros((1, LANES - value.shape[1]), jnp.float32)], axis=1
        )
        tail = jnp.where(rows == v, jnp.broadcast_to(wide, (16, LANES)), tail)
    target[VECTOR_ROW:, :] = tail.astype(jnp.bfloat16)
    me.send(0)
    own[...] = target[...]


def pack_q(me, w_qkv, vectors, bias_up):
    small = [v.reshape(1, -1) for v in (*vectors, bias_up)]
    return call(
        pack_q_body, [shape_of((PACK_Q, LANES))] * 2, [me, *kept_far([w_qkv, *small])], staged=10, far_outs={0: True},
        name="pack_q",
    )


def pack_rest_body(me, w_out, w_up, w_down, to_ou, upper_d, lower_d, to_d):
    for t in range(DOWN_TILES):
        to_d[t * 192 : (t + 1) * 192, :] = w_down[:, t * LANES : (t + 1) * LANES].astype(
            jnp.bfloat16
        )
    upper_d[...] = to_d[: PACK_D // 2, :]
    lower_d[...] = to_d[PACK_D // 2 :, :]
    me.send(1)
    me.send(2)
    pack_columns(lax.rem(me[1], 2) == 1, w_out[...], 1, 0, to_ou)
    for t in range(UP_TILES):
        to_ou[UP_ROW + t * 96 : UP_ROW + (t + 1) * 96, :] = w_up[
            :, t * LANES : (t + 1) * LANES
        ].astype(jnp.bfloat16)


def pack_rest(me, w_out, w_up, w_down, after):
    return call(
        pack_rest_body,
        [
            near_shape((PACK_OU, LANES)),
            shape_of((PACK_D // 2, LANES)),
            shape_of((PACK_D // 2, LANES)),
            near_shape((PACK_D, LANES)),
        ],
        [me, *kept_far([w_out, w_up, w_down.T])],
        staged=3,
        far_outs={1: True, 2: True},
        after=after,
        name="pack_rest",
    )


def swap(x, axis, bit):
    size = lax.axis_size(axis)
    return lax.ppermute(x, axis, [(i, i ^ bit) for i in range(size)])


CORE, ALONG_X, ALONG_Y = 1, 2, 4


def gather_z(x, own=None):
    return [x if own is None else own] + [swap(x, "mp", k) for k in (1, 2, 3)]


def beside(me, groups, shapes, after=(), name="beside"):
    sources = []
    for x, _ in groups:
        if all(x is not y for y in sources):
            sources.append(x)

    def body(me, *refs):
        for x, (index, where) in groups:
            source = refs[next(n for n, y in enumerate(sources) if x is y)]
            refs[len(sources) + index][where] = source[...]

    return call(body, [shape_of(s) for s in shapes], [me, *sources], after=after, name=name)


def beside_two(me, a, b, after=()):
    return beside(me, [(a, (0, 0)), (b, (0, 1))], [(2, *a.shape)], after, "beside_two")


def gather_near(me, parts, after=()):
    shape = (2, *parts[0].shape)
    found = beside(
        me,
        [(parts[0], (0, 0)), (parts[1], (0, 1)), (parts[2], (1, 0)), (parts[3], (1, 1))],
        [shape, shape],
        after,
        "beside_z",
    )
    first, second = found
    result = Results([first, swap(first, "dp", ALONG_X), second, swap(second, "dp", ALONG_Y)])
    result.token = found.token
    return result


def gather_far(me, parts, after=()):
    shape = (2, *parts[0].shape)
    groups = [(parts[i], (i // 2, i % 2)) for i in range(4)]
    found = beside(me, groups, [shape, shape], after, "beside_near")
    first, second = found
    result = Results([first, second, swap(first, "dp", ALONG_Y), swap(second, "dp", ALONG_X)])
    result.token = found.token
    return result


def gather_core(parts):
    return list(parts) + [swap(x, "dp", CORE) for x in parts]


def gathered_blocks(me, refs, steps=(1, 2)):
    for index, ref in enumerate(refs):
        core, far, half = index // 4, index % 4 // 2, index % 2
        for mid in range(2):
            for low in range(2):
                kx, ky = (far, mid) if half else (mid, far)
                along_z = steps[0] * low + steps[1] * half
                yield me[0] ^ (core + 2 * kx + 4 * ky), me[1] ^ along_z, ref.at[mid, low]


def split_pairs(refs):
    return [ref.at[i] for ref in refs for i in range(2)]


def place_columns(block, base, tiles, dp, mp, width, weights, singles):
    start = pl.multiple_of(mp * width + 64 * lax.rem(mp, 2), LANES)
    rows = pl.ds(pl.multiple_of(dp * 96, 32), 96)
    for t in range(tiles):
        weights[rows, pl.ds(pl.multiple_of(start + t * LANES, LANES), LANES)] = block[
            base + t * 96 : base + (t + 1) * 96, :
        ]
    singles[mp, pl.ds(pl.multiple_of(dp * 48, 16), 48), :] = block[
        base + tiles * 96 : base + tiles * 96 + 48, :
    ]


def place_singles(width, weights, singles):
    for pair in range(2):
        column = 2 * pair * width + (width // LANES) * LANES
        for dp in range(8):
            left = singles[2 * pair, dp * 48 : (dp + 1) * 48, :].astype(jnp.float32)
            right = singles[2 * pair + 1, dp * 48 : (dp + 1) * 48, :].astype(jnp.float32)
            upper = jnp.concatenate([left[:, :64], right[:, :64]], axis=1)
            lower = jnp.concatenate([left[:, 64:], right[:, 64:]], axis=1)
            weights[dp * 96 : dp * 96 + 48, column : column + LANES] = upper.astype(jnp.bfloat16)
            weights[dp * 96 + 48 : (dp + 1) * 96, column : column + LANES] = lower.astype(
                jnp.bfloat16
            )


def unpack_q_body(me, *refs):
    blocks, weights, vectors, bias_up, singles, tails = refs[:8], *refs[8:]
    for dp, mp, block in gathered_blocks(me, blocks):
        place_columns(block, 0, 4, dp, mp, 576, weights, singles)
        tails[dp * 4 + mp] = block[VECTOR_ROW:, :].astype(jnp.float32)
    place_singles(576, weights, singles)
    lane = lax.broadcasted_iota(jnp.int32, (16, LANES), 1)

    def spread(width, count):
        found = [jnp.zeros((16, LANES), jnp.float32) for _ in range(count)]
        for device in range(32):
            start, tile = device * width % LANES, device * width // LANES
            piece = tails[device]
            moved = pltpu.roll(piece, start, axis=1) if start else piece
            found[tile] = jnp.where((lane >= start) & (lane < start + width), moved, found[tile])
            if start + width > LANES:
                found[tile + 1] = jnp.where(lane < start + width - LANES, moved, found[tile + 1])
        return found

    for t, value in enumerate(spread(24, 6)):
        vectors[:, t * LANES : (t + 1) * LANES] = value[:8]
    for t, value in enumerate(spread(96, 24)):
        bias_up[:, t * LANES : (t + 1) * LANES] = value[8:9]


def unpack_ou_body(me, *refs):
    blocks, w_out, w_up, singles = refs[:8], *refs[8:]
    for dp, mp, block in gathered_blocks(me, blocks, (2, 1)):
        place_columns(block, 0, 1, dp, mp, 192, w_out, singles)
        rows = pl.ds(pl.multiple_of(dp * 96, 32), 96)
        for t in range(UP_TILES):
            w_up[rows, pl.ds(pl.multiple_of(mp * 768 + t * LANES, LANES), LANES)] = block[
                UP_ROW + t * 96 : UP_ROW + (t + 1) * 96, :
            ]
    place_singles(192, w_out, singles)


def unpack_ou(me, parts, after=()):
    return call(
        unpack_ou_body,
        [near_shape((768, 768)), near_shape((768, 3072))],
        [me, *parts],
        [pltpu.VMEM((4, 384, LANES), jnp.bfloat16)],
        after=after,
        name="unpack_ou",
    )


def spread_d_body(me, mine, upper_x, lower_y, upper, lower):
    half = PACK_D // 2
    upper[0], upper[1] = mine[:half, :], upper_x[...]
    lower[0], lower[1] = mine[half:, :], lower_y[...]


def spread_d(me, mine, upper_x, lower_y, after=()):
    shape = near_shape((2, PACK_D // 2, LANES))
    return call(
        spread_d_body, [shape, shape], [me, mine, upper_x, lower_y], after=after, name="spread_d"
    )


def whole_d_body(me, upper, upper_y, lower, lower_x, out):
    half = PACK_D // 2
    for kx in range(2):
        for ky in range(2):
            out[2 * ky + kx, :half, :] = (upper_y if ky else upper)[kx]
            out[2 * ky + kx, half:, :] = (lower_x if kx else lower)[ky]


def whole_d(me, upper, upper_y, lower, lower_x, after=()):
    return call(
        whole_d_body, [near_shape((4, PACK_D, LANES))], [me, upper, upper_y, lower, lower_x],
        after=after, name="whole_d",
    )


def unpack_d_body(me, *refs):
    blocks, turned = refs[:4], refs[4]
    for index, ref in enumerate(blocks):
        for far in range(2):
            for plane in range(4):
                dp, mp = me[0] ^ (2 * plane + index // 2), me[1] ^ (2 * far + index % 2)
                rows = pl.ds(pl.multiple_of(mp * 192, 64), 192)
                for t in range(DOWN_TILES):
                    turned[rows, pl.ds(pl.multiple_of(dp * 384 + t * LANES, LANES), LANES)] = ref[
                        far, plane, t * 192 : (t + 1) * 192, :
                    ]


def unpack_d(me, parts, after=()):
    return call(
        unpack_d_body, [near_shape((768, 3072))], [me, *parts], after=after, name="unpack_d"
    )


def turn_body(me, source, send, keep, turned):
    value = source[...].T
    for dp in range(8):
        k = me[0] ^ dp
        slot = (1 - (k & 1)) * 4 + (k >> 1)
        turned[pl.ds(pl.multiple_of(slot * 96, 32), 96), :] = value[dp * 96 : (dp + 1) * 96, :]
    send[...] = turned[:384, :]
    keep[...] = turned[384:, :]


def turn(me, source, after=()):
    n = source.shape[0]
    return call(
        turn_body,
        [shape_of((384, n)), near_shape((384, n))],
        [me, source],
        [pltpu.VMEM((768, n), jnp.bfloat16)],
        after=after,
        name="turn",
    )


def dot(a, b):
    return jnp.dot(a, b, preferred_element_type=jnp.float32)


def dot_nt(a, b):
    return lax.dot_general(a, b, (((1,), (1,)), ((), ())), preferred_element_type=jnp.float32)


def dot_tn(a, b):
    return lax.dot_general(a, b, (((0,), (0,)), ((), ())), preferred_element_type=jnp.float32)


def part_of(targets, kp, mp):
    ky, kx = kp // 2, kp % 2
    if mp < 2:
        return targets[ky].at[kx, mp]
    return targets[2 + kx].at[ky, mp - 2]


def store_columns(target, base, tiles, first, value):
    for t in range(tiles):
        target[base + t * 96 : base + (t + 1) * 96, :] = value[
            :, first + t * LANES : first + (t + 1) * LANES
        ].astype(jnp.bfloat16)


def store_single(target, base, odd, value):
    upper, lower = value[:48], value[48:]
    low_lanes = lax.broadcasted_iota(jnp.int32, (48, LANES), 1) < 64
    if odd:
        both = jnp.where(low_lanes, pltpu.roll(upper, 64, axis=1), lower)
    else:
        both = jnp.where(low_lanes, upper, pltpu.roll(lower, 64, axis=1))
    target[base : base + 48, :] = both.astype(jnp.bfloat16)


def column_gradient(lefts, rights, targets, base, tiles, width):
    def product(columns):
        return dot(lefts[0], rights[0][:, columns]) + dot(lefts[1], rights[1][:, columns])

    for pair in range(2):
        first = 2 * pair * width
        middle = first + tiles * LANES
        for begin, mp in ((first, 2 * pair), (middle + LANES, 2 * pair + 1)):
            value = product(slice(begin, begin + tiles * LANES))
            for kp in range(4):
                store_columns(
                    targets(kp, mp), base, tiles, 0, value[kp * 96 : (kp + 1) * 96]
                )
        value = product(slice(middle, middle + LANES))
        for kp in range(4):
            for mp in (2 * pair, 2 * pair + 1):
                store_single(
                    targets(kp, mp), base + tiles * 96, mp % 2,
                    value[kp * 96 : (kp + 1) * 96],
                )


def parts_shape(rows):
    return [near_shape((2, 2, rows, LANES)), shape_of((2, 2, rows, LANES))] * 2


def gradient_q_body(
    me, keep, other_keep, grads, other_grads, vectors, other_vectors, mine, send, room
):
    targets = lambda kp, mp: room.at[me[1] ^ mp, kp]
    lefts, rights = (keep[...], other_keep[...]), (grads, other_grads)
    column_gradient(lefts, rights, targets, 0, 4, 576)
    sums = vectors[...] + other_vectors[...]
    lane = lax.broadcasted_iota(jnp.int32, (16, LANES), 1)
    rows = lax.broadcasted_iota(jnp.int32, (16, LANES), 0)

    def cut(source, width, device):
        start, tile = device * width % LANES, device * width // LANES
        value = source[:, tile * LANES : (tile + 1) * LANES]
        moved = pltpu.roll(value, LANES - start, axis=1) if start else value
        if start + width > LANES:
            after = source[:, (tile + 1) * LANES : (tile + 2) * LANES]
            after = pltpu.roll(after, LANES - start, axis=1)
            here = lax.broadcasted_iota(jnp.int32, value.shape, 1)
            moved = jnp.where(here < LANES - start, moved, after)
        return moved

    for kp in range(4):
        plane = (me[0] >> 1) ^ kp
        for mp in range(4):
            tail = jnp.zeros((16, LANES), jnp.float32)
            for dp in range(8):
                device = dp * 4 + mp
                row = 8 + device // 8
                up = jnp.broadcast_to(cut(sums[row : row + 1], 96, device % 8), (8, LANES))
                found = jnp.concatenate([cut(sums[:8], 24, device), up], axis=0)
                owner = dp == 2 * plane + (me[0] & 1)
                tail = jnp.where(owner, found, tail)
            tail = jnp.where((rows < 8) & (lane >= 24), 0.0, tail).astype(jnp.bfloat16)
            targets(kp, mp)[VECTOR_ROW:, :] = tail
    for kz in range(4):
        (send if kz % 2 else mine)[kz // 2] = room[kz]


def gradient_q(me, keep, other_keep, grads, other_grads, vectors, other_vectors, after=()):
    return call(
        gradient_q_body,
        [near_shape((2, 4, PACK_Q, LANES)), shape_of((2, 4, PACK_Q, LANES))],
        [me, keep, other_keep, grads, other_grads, vectors, other_vectors],
        [pltpu.VMEM((4, 4, PACK_Q, LANES), jnp.bfloat16)],
        after=after,
        name="gradient_q",
    )


def gradient_ou_body(me, *refs):
    combined, first_low, hidden_grad = (refs[i : i + 2] for i in (0, 2, 4))
    attention_grad, room = (refs[6], refs[13]), refs[13]
    targets = functools.partial(part_of, refs[9:13])
    room[:, :384] = refs[7][...]
    room[:, 384:] = refs[8][...]
    column_gradient([x[...] for x in combined], attention_grad, targets, 0, 1, 192)
    lefts = [x[...] for x in first_low]
    for mp in range(4):
        columns = slice(mp * 768, (mp + 1) * 768)
        value = dot(lefts[0], hidden_grad[0][:, columns])
        value = value + dot(lefts[1], hidden_grad[1][:, columns])
        for kp in range(4):
            store_columns(
                targets(kp, mp), UP_ROW, UP_TILES, 0, value[kp * 96 : (kp + 1) * 96]
            )


def gradient_ou(me, combined, first_low, hidden_grad, attention_grad, after=()):
    return call(
        gradient_ou_body,
        parts_shape(PACK_OU),
        [me, *combined, *first_low, *hidden_grad, *attention_grad],
        [pltpu.VMEM(attention_grad[0].shape, jnp.bfloat16)],
        after=after,
        name="gradient_ou",
    )


def gradient_d_body(me, feed_grad, other_feed_grad, activated, other_activated, *refs):
    targets, turned, other_turned = refs[:4], refs[4], refs[5]
    turned[...] = feed_grad[...].T
    other_turned[...] = other_feed_grad[...].T
    for kp in range(4):
        dp = me[0] ^ (2 * kp)
        block = activated[:, pl.ds(pl.multiple_of(dp * 384, LANES), 384)]
        value = dot(turned[...], block)
        value = value + dot(other_turned[...], other_activated[:, kp * 384 : (kp + 1) * 384])
        for mp in range(4):
            target = part_of(targets, kp, mp)
            for t in range(DOWN_TILES):
                target[t * 192 : (t + 1) * 192, :] = value[
                    mp * 192 : (mp + 1) * 192, t * LANES : (t + 1) * LANES
                ].astype(jnp.bfloat16)


def gradient_d(me, feed_grad, other_feed_grad, activated, other_activated, after=()):
    return call(
        gradient_d_body,
        parts_shape(PACK_D),
        [me, feed_grad, other_feed_grad, activated, other_activated],
        [pltpu.VMEM((768, feed_grad.shape[0]), jnp.bfloat16)] * 2,
        after=after,
        name="gradient_d",
    )


def sums_body(me, bias, one, two, up, out):
    out[0:2, :], out[2:5, :], out[5:8, :] = bias[...], one[...], two[...]
    for i in range(4):
        out[8 + i : 9 + i, :] = up[:, i * 768 : (i + 1) * 768]


def all_sums(me, *sums):
    return call(sums_body, [shape_of((12, 768), jnp.float32)], [me, *sums], name="sums")[0]


def add(a, b):
    return a.astype(jnp.float32) + b.astype(jnp.float32)


def add_plane_body(me, first, first_in, second, second_in, *outs):
    for keep, send, a, b in ((*outs[:2], first, first_in), (*outs[2:], second, second_in)):
        keep[...] = add(a[0], b[0]).astype(jnp.bfloat16)
        send[...] = add(a[1], b[1]).astype(jnp.bfloat16)


def add_last_body(me, first, first_in, second, second_in, *refs):
    keep, send, room = refs
    for mp in range(4):
        a, b = (first, first_in) if mp < 2 else (second, second_in)
        room[me[1] ^ mp] = add(a[mp % 2], b[mp % 2]).astype(jnp.bfloat16)
    for k in range(4):
        (send if k % 2 else keep)[k // 2] = room[k]


def add_first_body(me, mine, arrived, *outs):
    for kp in range(4):
        ky, kx = kp // 2, kp % 2
        outs[ky][kx] = add(mine[0, kp], arrived[0, kp]).astype(jnp.bfloat16)
        outs[2 + kx][ky] = add(mine[1, kp], arrived[1, kp]).astype(jnp.bfloat16)


def add_first(me, mine, arrived, after=()):
    rows = mine.shape[2]
    return call(
        add_first_body,
        [near_shape((2, rows, LANES)), shape_of((2, rows, LANES))] * 2,
        [me, mine, arrived],
        after=after,
        name="add_first",
    )


def add_both_body(me, first, first_in, second, second_in, keep, send):
    keep[...] = add(first[...], first_in[...])
    send[...] = add(second[...], second_in[...]).astype(jnp.bfloat16)


def add_both(me, parts, after=()):
    shape = parts[0].shape
    return call(
        add_both_body,
        [near_shape(shape, jnp.float32), shape_of(shape)],
        [me, *parts],
        after=after,
        name="add_both",
    )


def add_z_body(me, mine, arrived, keep, send):
    keep[...] = add(mine[0], arrived[0])
    send[...] = add(mine[1], arrived[1]).astype(jnp.bfloat16)


def scatter_near(parts):
    first, first_send, second, second_send = parts
    return first, swap(first_send, "dp", ALONG_Y), second, swap(second_send, "dp", ALONG_X)


def add_plane(me, parts, after=(), cost=0):
    shape = parts[0].shape[1:]
    return call(
        add_plane_body,
        [near_shape(shape), shape_of(shape)] * 2,
        [me, *parts],
        after=after,
        cost=cost,
        name="add_plane",
    )


def scatter_far(parts):
    first, first_send, second, second_send = parts
    return first, swap(first_send, "dp", ALONG_X), second, swap(second_send, "dp", ALONG_Y)


def add_last(me, parts, after=(), cost=0):
    rows = parts[0].shape[1]
    return call(
        add_last_body,
        [near_shape((2, rows, LANES)), shape_of((2, rows, LANES))],
        [me, *parts],
        [pltpu.VMEM((4, rows, LANES), jnp.bfloat16)],
        after=after,
        cost=cost,
        name="add_last",
    )


def scatter_z(parts):
    return parts[0], swap(parts[1], "mp", 1)


def add_z(me, parts, after=()):
    rows = parts[0].shape[1]
    return call(
        add_z_body,
        [near_shape((rows, LANES), jnp.float32), shape_of((rows, LANES))],
        [me, *parts],
        after=after,
        name="add_z",
    )


def scatter_z_far(parts):
    return parts[0], swap(parts[1], "mp", 2)


def total(refs, rows):
    value = refs[0][rows, :].astype(jnp.float32)
    for ref in refs[1:]:
        value = value + ref[rows, :].astype(jnp.float32)
    return value


def finish_columns(me, refs, base, tiles, out):
    odd = lax.rem(me[1], 2) == 1
    full = [total(refs, pl.ds(base + t * 96, 96)) for t in range(tiles)]
    single = total(refs, pl.ds(base + tiles * 96, 48))
    single = jnp.concatenate([single[:, :64], single[:, 64:]], axis=0)

    @pl.when(odd)
    def _():
        out[...] = jnp.concatenate([single, *full], axis=1)

    @pl.when(jnp.logical_not(odd))
    def _():
        out[...] = jnp.concatenate([*full, single], axis=1)


def finish_q_body(me, *refs):
    parts, out, outs = refs[:2], refs[2], refs[3:]
    finish_columns(me, parts, 0, 4, out)
    tail = total(parts, pl.ds(VECTOR_ROW, 16))
    for v in range(8):
        outs[v][...] = tail[v : v + 1, :24]
    outs[8][...] = tail[8:9, :96]


def finish_q(me, parts):
    f = jnp.float32
    return call(
        finish_q_body,
        [shape_of((96, 576), f)] + [shape_of((1, 24), f)] * 8 + [shape_of((1, 96), f)],
        [me, *parts],
        name="finish_q",
    )


def finish_ou_body(me, *refs):
    parts, w_out, w_up = refs[:2], refs[2], refs[3]
    finish_columns(me, parts, 0, 1, w_out)
    for t in range(UP_TILES):
        w_up[:, t * LANES : (t + 1) * LANES] = total(parts, pl.ds(UP_ROW + t * 96, 96))


def finish_ou(me, parts, after=()):
    f = jnp.float32
    return call(
        finish_ou_body, [shape_of((96, 192), f), shape_of((96, 768), f)], [me, *parts],
        after=after, name="finish_ou",
    )


def finish_d_body(me, *refs):
    parts, out = refs[:2], refs[2]
    for t in range(DOWN_TILES):
        out[:, t * LANES : (t + 1) * LANES] = total(parts, pl.ds(t * 192, 192))


def finish_d(me, parts, after=()):
    f = jnp.float32
    return call(finish_d_body, [shape_of((192, 384), f)], [me, *parts], after=after, name="finish_d")


PAIRS = HEADS // 2


def iota(shape, axis):
    return lax.broadcasted_iota(jnp.int32, shape, axis)


def place_matrix(order, head):
    length = order.shape[1]
    row = order[head : head + 1, :].astype(jnp.int16)
    token = iota((length, length), 0).astype(jnp.int16)
    return jnp.where(token == row, jnp.bfloat16(1.0), jnp.bfloat16(0.0))


def project_body(me, *refs):
    blocks, tokens = split_pairs(refs[:4]), refs[4]
    weights, vectors, bias_up, qkv, singles, tails = refs[5:]
    unpack_q_body(me, *blocks, weights, vectors, bias_up, singles, tails)
    for c in range(9):
        columns = slice(c * 256, (c + 1) * 256)
        value = dot(tokens[...], weights[:, columns])
        if c < 3:
            value = value + vectors[0:1, c * 256 : (c + 1) * 256]
        elif c >= 6:
            value = value + vectors[1:2, (c - 6) * 256 : (c - 5) * 256]
        qkv[:, columns] = value.astype(jnp.bfloat16)


def project(me, parts, tokens, after=()):
    return call(
        project_body,
        [
            near_shape((768, 2304)),
            near_shape((8, 768), jnp.float32),
            near_shape((1, 3072), jnp.float32),
            near_shape((tokens.shape[0], 2304)),
        ],
        [me, *parts, tokens],
        [pltpu.VMEM((4, 384, LANES), jnp.bfloat16), pltpu.VMEM((32, 16, LANES), jnp.float32)],
        after=after,
        name="project",
    )


def attend_body(first_pair, pairs, me, qkv, order, facts, *refs):
    swapped, values, soft, combined = refs[-4:]
    length = qkv.shape[0]
    groups = length // CLUSTER
    blocks = [slice(g * CLUSTER, (g + 1) * CLUSTER) for g in range(groups)]
    low = iota((length, LANES), 1) < 64
    itself = iota((CLUSTER, CLUSTER), 0) == iota((CLUSTER, CLUSTER), 1)
    pick = [
        jnp.where(iota((16, LANES), 1) == lane, 1.0, 0.0).astype(jnp.bfloat16) for lane in (64, 0)
    ]
    scale = HEAD_DIM ** (-0.5)

    for place in range(pairs):
        pair = first_pair + place

        def columns(base, pair=pair):
            return slice(base + pair * LANES, base + (pair + 1) * LANES)

        query = qkv[:, columns(0)].astype(jnp.float32)
        keys = qkv[:, columns(768)].astype(jnp.float32)
        value = qkv[:, columns(1536)].astype(jnp.float32)
        known = facts[...]
        tiles = (
            (jnp.where(low, query, pltpu.roll(keys, 64, axis=1)), jnp.where(low, value, known)),
            (jnp.where(low, pltpu.roll(query, 64, axis=1), keys), jnp.where(low, known, value)),
        )
        moved, to_tokens = [], []
        for h in range(2):
            back = place_matrix(order, 2 * pair + h)
            to_tokens.append(back)
            tile = jnp.concatenate([t.astype(jnp.bfloat16) for t in tiles[h]], axis=1)
            moved.append(dot_tn(back, tile))
        query_slots, key_slots, value_slots, codes, rows_of = [], [], [], [], []
        for h in range(2):
            both = moved[h][:, :LANES]
            query_slots.append(jnp.where(low, both, 0.0).astype(jnp.bfloat16))
            key_slots.append(pltpu.roll(both, 64, axis=1).astype(jnp.bfloat16))
            value_slots.append(moved[h][:, LANES:].astype(jnp.bfloat16))
            swapped[2 * place + h] = key_slots[h]
            values[2 * place + h] = value_slots[h]
            lane = 64 * (1 - h)
            code = moved[h][:, LANES + lane : LANES + lane + 1]
            row = dot_nt(pick[h], value_slots[h])[0:1]
            codes.append(jnp.where(code >= 32.0, code - 32.0, code))
            rows_of.append(row)
        scores = [
            [dot_nt(query_slots[h][b], key_slots[h][b]) for b in blocks] for h in range(2)
        ]
        found = []
        for h in range(2):
            outs = []
            for g, b in enumerate(blocks):
                allowed = (codes[h][b] == rows_of[h][:, b]) | itself
                value = jnp.where(allowed, scores[h][g] * scale, masked_score)
                value = jnp.exp(value - jnp.max(value, axis=1, keepdims=True))
                weights = value / jnp.sum(value, axis=1, keepdims=True)
                soft[2 * place + h, b, :] = weights
                outs.append(weights.astype(jnp.bfloat16))
            found.append(
                [dot(outs[g], value_slots[h][b]) for g, b in enumerate(blocks)]
            )
        result = None
        for h in range(2):
            value = jnp.concatenate(found[h], axis=0)
            value = jnp.where(low if h == 0 else jnp.logical_not(low), value, 0.0)
            value = dot(to_tokens[h], value.astype(jnp.bfloat16))
            result = value if result is None else result + value
        combined[:, columns(0)] = result.astype(jnp.bfloat16)


def attend(me, qkv, order, facts, first_pair, pairs, combined=None, after=()):
    length = qkv.shape[0]
    operands = [me, qkv, order, facts]
    if combined is not None:
        operands.append(combined)
    return call(
        functools.partial(attend_body, first_pair, pairs),
        [
            near_shape((2 * pairs, length, LANES)),
            near_shape((2 * pairs, length, LANES)),
            near_shape((2 * pairs, length, CLUSTER), jnp.float32),
            near_shape((length, 768)),
        ],
        operands,
        after=after,
        aliases={3: 3} if combined is not None else None,
        name="attend",
    )


def by_rows(first, count, step, body):
    for i in range(first, first + count, step):
        body(slice(i, i + step))


def mean(value):
    return jnp.mean(value, axis=1, keepdims=True)


def fold(value):
    return jnp.sum(value.reshape(value.shape[0] // 8, 8, value.shape[1]), axis=0)


def out_norm_body(me, combined, w_out, tokens, vectors, first_low, normal, inverse, total_ref):

    def rows_of(rows):
        value = total_ref[rows, :] + vectors[2:3] + tokens[rows, :].astype(jnp.float32)
        centred = value - mean(value)
        scale = lax.rsqrt(mean(centred * centred) + epsilon)
        norm = centred * scale
        normal[rows, :] = norm
        inverse[rows, :] = jnp.broadcast_to(scale, (scale.shape[0], LANES))
        first_low[rows, :] = (norm * vectors[3:4] + vectors[4:5]).astype(jnp.bfloat16)

    half = tokens.shape[0] // 2
    for first in (0, half):
        rows = slice(first, first + half)
        total_ref[rows, :] = dot(combined[rows, :], w_out[...])
        by_rows(first, half, 32, rows_of)


def out_norm(me, combined, w_out, tokens, vectors, after=()):
    n = tokens.shape[0]
    f = jnp.float32
    return call(
        out_norm_body,
        [near_shape((n, 768)), near_shape((n, 768), f), near_shape((n, LANES), f)],
        [me, combined, w_out, tokens, vectors],
        [pltpu.VMEM((n, 768), jnp.float32)],
        after=after,
        name="out_norm",
    )


def up_body(me, first_low, w_up, bias_up, activated, slope, send):
    width = w_up.shape[1] // 8
    for i in range(8):
        columns = slice(i * width, (i + 1) * width)
        hidden = dot(first_low[...], w_up[:, columns]) + bias_up[:, columns]
        half = 0.5 + 0.5 * lax.erf(hidden * (0.5**0.5))
        low = (hidden * half).astype(jnp.bfloat16)
        activated[:, columns] = low
        bell = jnp.exp(-0.5 * hidden * hidden) * (2.0 * math.pi) ** (-0.5)
        slope[:, columns] = (half + hidden * bell).astype(jnp.bfloat16)
    for i in range(8):
        k = me[0] ^ i

        @pl.when((k & 1) == 1)
        def _():
            there = pl.ds(pl.multiple_of((k >> 1) * width, LANES), width)
            send[:, there] = activated[:, i * width : (i + 1) * width]


def up(me, first_low, w_up, bias_up, after=()):
    n, width = first_low.shape[0], w_up.shape[1]
    return call(
        up_body,
        [near_shape((n, width)), near_shape((n, width)), shape_of((n, width // 2))],
        [me, first_low, w_up, bias_up],
        after=after,
        name="up",
    )


def down_norm_body(
    me, activated, turned, normal, vectors, out, feed_grad, second_grad, sums, feed, acc
):
    acc[...] = jnp.zeros_like(acc)

    def rows_of(rows):
        value = normal[rows, :] * vectors[3:4] + vectors[4:5] + feed[rows, :] + vectors[5:6]
        centred = value - mean(value)
        inverse = lax.rsqrt(mean(centred * centred) + epsilon)
        norm = centred * inverse
        out[rows, :] = (norm * vectors[6:7] + vectors[7:8]).astype(jnp.bfloat16)
        upstream = me.arrived(0)[rows, :]
        scaled = upstream * vectors[6:7]
        back = inverse * (scaled - mean(scaled) - norm * mean(scaled * norm))
        second_grad[rows, :] = back
        low = back.astype(jnp.bfloat16)
        feed_grad[rows, :] = low
        acc[0] += fold(low.astype(jnp.float32))
        acc[1] += fold(upstream * norm)
        acc[2] += fold(upstream)

    half = out.shape[0] // 2
    for first in (0, half):
        rows = slice(first, first + half)
        feed[rows, :] = dot_nt(activated[rows, :], turned[...])
        by_rows(first, half, 32, rows_of)
    me.send(0)
    for i in range(3):
        sums[i : i + 1, :] = jnp.sum(acc[i], axis=0, keepdims=True)


def down_norm(me, activated, turned, normal, vectors, cotangent, after=()):
    n = cotangent.shape[0]
    return call(
        down_norm_body,
        [
            shape_of((n, 768)),
            near_shape((n, 768)),
            near_shape((n, 768), jnp.float32),
            near_shape((3, 768), jnp.float32),
        ],
        [me, cotangent, activated, turned, normal, vectors],
        [pltpu.VMEM((n, 768), jnp.float32), pltpu.VMEM((3, 8, 768), jnp.float32)],
        late=[None],
        far_outs={0: True},
        after=after,
        name="down_norm",
    )


def hidden_back_body(me, feed_grad, turned, slope, hidden_grad, sums):
    for i in range(hidden_grad.shape[1] // 256):
        columns = slice(i * 256, (i + 1) * 256)
        value = dot(feed_grad[...], turned[:, columns]) * slope[:, columns].astype(jnp.float32)
        low = value.astype(jnp.bfloat16)
        hidden_grad[:, columns] = low
        sums[:, columns] = jnp.sum(low.astype(jnp.float32), axis=0, keepdims=True)


def hidden_back(me, feed_grad, turned, slope, after=()):
    return call(
        hidden_back_body,
        [near_shape(slope.shape), near_shape((1, slope.shape[1]), jnp.float32)],
        [me, feed_grad, turned, slope],
        after=after,
        name="hidden_back",
    )


def first_back_body(
    me, hidden_grad, w_up, second_grad, normal, inverse, vectors, residual, low_out, left, right, sums, back,
    acc,
):
    acc[...] = jnp.zeros_like(acc)

    def rows_of(rows):
        upstream = back[rows, :] + second_grad[rows, :]
        norm = normal[rows, :]
        scaled = upstream * vectors[3:4]
        value = inverse[rows, 0:1] * (scaled - mean(scaled) - norm * mean(scaled * norm))
        residual[rows, :] = value
        low = value.astype(jnp.bfloat16)
        low_out[rows, :] = low
        left[rows, :] = low[:, :384]
        right[rows, :] = low[:, 384:]
        acc[0] += fold(low.astype(jnp.float32))
        acc[1] += fold(upstream * norm)
        acc[2] += fold(upstream)

    half = normal.shape[0] // 2
    for first in (0, half):
        rows = slice(first, first + half)
        back[rows, :] = dot_nt(hidden_grad[rows, :], w_up[...])
        by_rows(first, half, 32, rows_of)
    for i in range(3):
        sums[i : i + 1, :] = jnp.sum(acc[i], axis=0, keepdims=True)


def first_back(me, hidden_grad, w_up, second_grad, normal, inverse, vectors, after=()):
    n = normal.shape[0]
    return call(
        first_back_body,
        [
            near_shape((n, 768), jnp.float32),
            near_shape((n, 768)),
            shape_of((n, 384)),
            shape_of((n, 384)),
            near_shape((3, 768), jnp.float32),
        ],
        [me, hidden_grad, w_up, second_grad, normal, inverse, vectors],
        [pltpu.VMEM((n, 768), jnp.float32), pltpu.VMEM((3, 8, 768), jnp.float32)],
        after=after,
        name="first_back",
    )


def attend_back_body(
    first_pair, pairs, me, attention_grad, w_out, order, swapped, values, soft, *refs
):
    grads, sums, upstream = refs[-3:]
    length = attention_grad.shape[0]
    groups = length // CLUSTER
    blocks = [slice(g * CLUSTER, (g + 1) * CLUSTER) for g in range(groups)]
    low = iota((length, LANES), 1) < 64
    low_rows = iota((CLUSTER, LANES), 1) < 64
    scale = HEAD_DIM ** (-0.5)
    mine = slice(first_pair * LANES, (first_pair + pairs) * LANES)
    upstream[...] = dot_nt(attention_grad[...], w_out[mine, :]).astype(jnp.bfloat16)

    for place in range(pairs):
        pair = first_pair + place

        def columns(base, pair=pair):
            return slice(base + pair * LANES, base + (pair + 1) * LANES)

        both = upstream[:, slice(place * LANES, (place + 1) * LANES)]
        to_tokens, moved = [], []
        for h in range(2):
            to_tokens.append(place_matrix(order, 2 * pair + h))
            value = dot_tn(to_tokens[h], both)
            value = jnp.where(low if h == 0 else jnp.logical_not(low), value, 0.0)
            moved.append(value.astype(jnp.bfloat16))
        back = []
        for h in range(2):
            kept = 2 * place + h
            keys = [swapped[kept, b, :] for b in blocks]
            weights = [soft[kept, b, :] for b in blocks]
            soft_grad = [dot_nt(moved[h][b], values[kept, b, :]) for b in blocks]
            value_grad = [
                dot_tn(weights[g].astype(jnp.bfloat16), moved[h][b]) for g, b in enumerate(blocks)
            ]
            score_grad = []
            for g in range(groups):
                middle = jnp.sum(soft_grad[g] * weights[g], axis=1, keepdims=True)
                score_grad.append((weights[g] * (soft_grad[g] - middle)).astype(jnp.bfloat16))
            query_grad = [dot(score_grad[g], keys[g]) for g in range(groups)]
            key_grad = [dot_tn(score_grad[g], keys[g]) for g in range(groups)]
            parts = [
                jnp.concatenate(
                    [
                        (jnp.where(low_rows, query_grad[g], key_grad[g]) * scale).astype(
                            jnp.bfloat16
                        ),
                        value_grad[g].astype(jnp.bfloat16),
                    ],
                    axis=1,
                )
                for g in range(groups)
            ]
            back.append(dot(to_tokens[h], jnp.concatenate(parts, axis=0)))
        first, second = back[0][:, :LANES], back[1][:, :LANES]
        query = jnp.where(low, first, pltpu.roll(second, 64, axis=1))
        keys = jnp.where(low, pltpu.roll(first, 64, axis=1), second)
        value = back[0][:, LANES:] + back[1][:, LANES:]
        grads[:, columns(0)] = query.astype(jnp.bfloat16)
        grads[:, columns(768)] = keys.astype(jnp.bfloat16)
        grads[:, columns(1536)] = value.astype(jnp.bfloat16)
        sums[0:1, columns(0)] = jnp.sum(query, axis=0, keepdims=True)
        sums[1:2, columns(0)] = jnp.sum(value, axis=0, keepdims=True)


def attend_back(
    me, attention_grad, w_out, order, kept, first_pair, pairs, before=(), after=()
):
    length = attention_grad.shape[0]
    return call(
        functools.partial(attend_back_body, first_pair, pairs),
        [near_shape((length, 2304)), near_shape((2, 768), jnp.float32)],
        [me, attention_grad, w_out, order, *kept, *before],
        [pltpu.VMEM((length, pairs * LANES), jnp.bfloat16)],
        after=after,
        aliases={6: 0, 7: 1} if before else None,
        name="attend_back",
    )


def tokens_back_body(me, grads, weights, residual, out):
    for c in range(3):
        columns = slice(c * 256, (c + 1) * 256)
        out[:, columns] = dot_nt(grads[...], weights[columns, :]) + residual[:, columns]
        me.send(0, (slice(None), columns))


def tokens_back(me, grads, weights, residual, after=()):
    return call(
        tokens_back_body,
        [shape_of(residual.shape, jnp.float32)],
        [me, grads, weights, residual],
        far_outs={0: True},
        sends=3,
        after=after,
        name="tokens_back",
    )


def local_block(
    tokens,
    w_qkv,
    bias_query,
    bias_value,
    w_out,
    bias_out,
    gain_one,
    shift_one,
    w_up,
    bias_up,
    w_down,
    bias_down,
    gain_two,
    shift_two,
    cluster_order,
    segment_ids,
    padding,
    cotangent,
):
    length = tokens.shape[0]
    me = None
    vector_list = [
        bias_query, bias_value, bias_out, gain_one, shift_one, bias_down, gain_two, shift_two
    ]
    order = cluster_order[0]
    facts = (segment_ids[0] + 32 * (1 - padding[0])).astype(jnp.float32)
    facts = jnp.broadcast_to(facts[:, None], (length, 128))

    def other(x):
        return swap(x, "dp", CORE)

    blocks_q = pack_q(me, w_qkv, vector_list, bias_up)
    z_q = gather_z(*blocks_q)
    blocks_rest = pack_rest(me, w_out, w_up, w_down, after=[blocks_q])
    block_ou, upper, lower, block_d = blocks_rest
    upper_x, lower_y = swap(upper, "dp", ALONG_X), swap(lower, "dp", ALONG_Y)
    tokens_turned = turn(me, tokens, after=[blocks_rest])
    near_q = gather_near(me, z_q, after=[tokens_turned, upper_x, lower_y])
    upper, lower = spread_d(me, block_d, upper_x, lower_y, after=[near_q])
    upper_y, lower_x = swap(upper, "dp", ALONG_Y), swap(lower, "dp", ALONG_X)
    (block_ou,) = tie([block_ou], [near_q])
    far_z_ou = swap(block_ou, "mp", 2)
    near_d = whole_d(me, upper, upper_y, lower, lower_x)
    far_q = gather_far(me, near_q, after=[near_d, far_z_ou])
    far_d = swap(near_d[0], "mp", 2)
    near_z_ou = beside_two(me, block_ou, far_z_ou, after=[far_q])
    z_ou = tie([near_z_ou[0], swap(near_z_ou[0], "mp", 1)], [near_z_ou])
    near_ou = [z_ou[0], swap(z_ou[0], "dp", ALONG_X), z_ou[1], swap(z_ou[1], "dp", ALONG_Y)]
    far_ou = gather_far(me, near_ou, after=far_q[2:])
    both_d = beside_two(me, near_d[0], far_d, after=[far_ou])
    z_d = swap(both_d[0], "mp", 1)
    pairs_q = beside(
        me,
        [(x, (i // 2, i % 2)) for i, x in enumerate(far_q)],
        [(2, *far_q[0].shape)] * 2,
        [both_d],
        "beside_far",
    )
    parts_q = list(pairs_q)
    parts_q = [*parts_q, *[other(x) for x in parts_q]]
    projected = project(me, parts_q, tokens)
    full_qkv, vectors, full_bias_up, qkv = projected

    pairs = PAIRS // 3

    def forward(part, before, after):
        return attend(
            me, qkv, order, facts, part * pairs, pairs, before, after=after
        )

    seen_a = forward(0, None, [projected])
    seen_b = forward(1, seen_a[-1], [seen_a])
    far_ou = tie(far_ou, [seen_b])
    seen_c = forward(2, seen_b[-1], far_ou[:1])
    combined = seen_c[-1]
    combined_turned = turn(me, combined)
    full_out, full_up = unpack_ou(me, gather_core(far_ou), after=[combined_turned])
    normed = out_norm(me, combined, full_out, tokens, vectors)
    first_low, normal, inverse = normed
    first_turned = turn(me, first_low)
    upper = up(me, first_low, full_up, full_bias_up, after=[first_turned])
    activated, slope, send_activated = upper
    sends = tie(
        [combined_turned[0], first_turned[0], send_activated, tokens_turned[0]], [upper]
    )
    others = [other(x) for x in sends]
    parts_d = tie([both_d[0], z_d], [upper])
    parts_d = [*parts_d, *[other(x) for x in parts_d]]
    unpacked = unpack_d(me, parts_d, after=[others[0], others[1], others[3]])
    turned_down = unpacked[0]
    downed = down_norm(me, activated, turned_down, normal, vectors, cotangent)
    layer_out, feed_grad, second_grad, sums_two = downed
    other_tokens = others[3]

    other_feed = other(feed_grad)
    hidden = hidden_back(me, feed_grad, turned_down, slope, after=[downed])
    hidden_grad, sums_up = hidden
    (hidden_grad,) = tie([hidden_grad], [hidden, other_feed, others[2]])
    other_hidden = other(hidden_grad)
    grad_d = gradient_d(
        me, feed_grad, other_feed, activated, others[2], after=[hidden]
    )
    core_d = scatter_near(grad_d)
    first = first_back(
        me, hidden_grad, full_up, second_grad, normal, inverse, vectors, after=[grad_d]
    )
    residual_grad, attention_grad, *halves, sums_one = first
    halves = [other(x) for x in halves]

    def back(part, kept, before, after):
        return attend_back(
            me, attention_grad, full_out, order, kept,
            part * pairs, pairs, before, after,
        )

    grads_a = back(0, seen_a[:3], (), [first])
    grads_b = back(1, seen_b[:3], grads_a, [])
    grads_c = back(2, seen_c[:3], grads_b, halves)
    half_d = add_plane(me, core_d, after=[grads_c])
    plane_d = scatter_far(half_d)
    projected_grad, sums_bias = grads_c
    grad_vectors = all_sums(me, sums_bias, sums_one, sums_two, sums_up)
    projected_grad, grad_vectors = tie([projected_grad, grad_vectors], [half_d])
    other_grads = other(projected_grad), other(grad_vectors)
    grad_ou = gradient_ou(
        me,
        (combined_turned[1], others[0]),
        (first_turned[1], others[1]),
        (hidden_grad, other_hidden),
        (attention_grad, *halves),
        after=[half_d],
    )
    core_ou = scatter_near(grad_ou)
    last_d = add_last(me, plane_d, after=[grad_ou], cost=22 * MICROSECOND)
    z_d = scatter_z(last_d)
    grad_q = gradient_q(
        me, tokens_turned[1], other_tokens, projected_grad, other_grads[0], grad_vectors,
        other_grads[1], after=[last_d],
    )
    near_q = grad_q[0], swap(grad_q[1], "mp", 1)
    moved = tokens_back(me, projected_grad, full_qkv, residual_grad, after=[grad_q])
    grad_tokens = moved[0]
    near_d = add_z(me, z_d, after=[moved])
    sum_d = scatter_z_far(near_d)
    half_ou = add_plane(me, core_ou, after=[near_d], cost=4 * MICROSECOND)
    plane_ou = scatter_far(half_ou)
    last_ou = add_last(me, plane_ou, after=[half_ou])
    z_ou = scatter_z(last_ou)
    first_q = add_first(me, *near_q, after=[last_ou])
    core_q = scatter_near(first_q)
    done_d = finish_d(me, sum_d, after=[first_q])
    near_ou = add_z(me, z_ou, after=[done_d])
    sum_ou = scatter_z_far(near_ou)
    half_q = add_plane(me, core_q, after=[near_ou])
    plane_q = scatter_far(half_q)
    sum_q = scatter_z_far(add_both(me, plane_q, after=[]))
    done_ou = finish_ou(me, sum_ou)
    shard_out, shard_up = done_ou
    shard_qkv, *shard_vectors = finish_q(me, sum_q)
    shard_down = done_d[0].T
    grad_list = [v.reshape(-1) for v in shard_vectors]
    return (
        layer_out,
        grad_tokens,
        shard_qkv,
        grad_list[0],
        grad_list[1],
        shard_out,
        grad_list[2],
        grad_list[3],
        grad_list[4],
        shard_up,
        grad_list[8],
        shard_down,
        grad_list[5],
        grad_list[6],
        grad_list[7],
    )


def solution(mesh):
    in_specs = (
        P(("dp", "mp"), None),
        P("dp", "mp"),
        P(("dp", "mp")),
        P(("dp", "mp")),
        P("dp", "mp"),
        P(("dp", "mp")),
        P(("dp", "mp")),
        P(("dp", "mp")),
        P("dp", "mp"),
        P(("dp", "mp")),
        P("dp", "mp"),
        P(("dp", "mp")),
        P(("dp", "mp")),
        P(("dp", "mp")),
        P(("dp", "mp"), None, None),
        P(("dp", "mp"), None),
        P(("dp", "mp"), None),
        P(("dp", "mp"), None),
    )
    out_specs = (
        P(("dp", "mp"), None),
        P(("dp", "mp"), None),
        P("dp", "mp"),
        P(("dp", "mp")),
        P(("dp", "mp")),
        P("dp", "mp"),
        P(("dp", "mp")),
        P(("dp", "mp")),
        P(("dp", "mp")),
        P("dp", "mp"),
        P(("dp", "mp")),
        P("dp", "mp"),
        P(("dp", "mp")),
        P(("dp", "mp")),
        P(("dp", "mp")),
    )
    blocks = mesh.shape["dp"] == 8 and mesh.shape["mp"] == 4
    local = local_block if blocks else local_general
    return jax.shard_map(local, mesh=mesh, in_specs=in_specs, out_specs=out_specs, check_vma=False)
```

```python
import functools
import math

import jax
import jax.numpy as jnp
from jax import lax
from jax.experimental import pallas as pl
from jax.experimental.pallas import tpu as pltpu
from jax.sharding import PartitionSpec as P

HEADS = 12
HEAD_DIM = 64
CLUSTER = 128


epsilon = 1e-12
masked_score = -1e30


def product(left_side, right_side):
    return jnp.dot(left_side, right_side, preferred_element_type=jnp.float32)


def times_back(left_side, right_side):
    return lax.dot_general(
        left_side, right_side, (((1,), (1,)), ((), ())), preferred_element_type=jnp.float32
    )


def outer_sum(left_side, right_side):
    return lax.dot_general(
        left_side, right_side, (((0,), (0,)), ((), ())), preferred_element_type=jnp.float32
    )


def norm_forward(hidden, norm_gain, norm_shift):
    average = jnp.mean(hidden, axis=-1, keepdims=True)
    centred = hidden - average
    variance = jnp.mean(centred * centred, axis=-1, keepdims=True)
    inverse = lax.rsqrt(variance + epsilon)
    normal = centred * inverse
    return (normal * norm_gain + norm_shift, normal, inverse)


def norm_backward(upstream, normal, inverse, norm_gain):
    scaled = upstream * norm_gain
    return inverse * (
        scaled
        - jnp.mean(scaled, axis=-1, keepdims=True)
        - normal * jnp.mean(scaled * normal, axis=-1, keepdims=True)
    )


def gelu_exact(inputs):
    return jax.nn.gelu(inputs, approximate=False)


def local_general(
    tokens,
    w_qkv,
    bias_query,
    bias_value,
    w_out,
    bias_out,
    gain_one,
    shift_one,
    w_up,
    bias_up,
    w_down,
    bias_down,
    gain_two,
    shift_two,
    cluster_order,
    segment_ids,
    padding,
    cotangent,
):
    model_width = HEADS * HEAD_DIM
    length = tokens.shape[0]
    groups = length // CLUSTER
    score_scale = HEAD_DIM ** (-0.5)
    vectors = jnp.stack(
        [bias_query, bias_value, bias_out, gain_one, shift_one, bias_down, gain_two, shift_two]
    ).astype(jnp.bfloat16)
    vector_up = bias_up.astype(jnp.bfloat16)[None, :]
    part_qkv = w_qkv.astype(jnp.bfloat16)
    part_out = w_out.astype(jnp.bfloat16)
    part_up = w_up.astype(jnp.bfloat16)
    part_down = w_down.astype(jnp.bfloat16)
    column_qkv, column_out, column_up, column_down, column_vectors, column_bias = (
        lax.all_gather(part_qkv, "mp", axis=1, tiled=True),
        lax.all_gather(part_out, "mp", axis=1, tiled=True),
        lax.all_gather(part_up, "mp", axis=1, tiled=True),
        lax.all_gather(part_down, "mp", axis=1, tiled=True),
        lax.all_gather(vectors, "mp", axis=1, tiled=True),
        lax.all_gather(vector_up, "mp", axis=1, tiled=True),
    )
    full_qkv, full_out, full_up, full_down, full_vectors, full_bias = (
        lax.all_gather(column_qkv, "dp", axis=0, tiled=True),
        lax.all_gather(column_out, "dp", axis=0, tiled=True),
        lax.all_gather(column_up, "dp", axis=0, tiled=True),
        lax.all_gather(column_down, "dp", axis=0, tiled=True),
        lax.all_gather(column_vectors, "dp", axis=1, tiled=True),
        lax.all_gather(column_bias, "dp", axis=1, tiled=True),
    )
    small_params = full_vectors.astype(jnp.float32)
    hidden_bias = full_bias[0].astype(jnp.float32)
    ordering = cluster_order[0]
    segment = segment_ids[0]
    present = padding[0]
    positions = jnp.arange(length, dtype=jnp.int32)
    placement = (ordering[:, :, None] == positions[None, None, :]).astype(jnp.bfloat16)

    def to_clusters(matrix):
        per_head = matrix.reshape(length, HEADS, HEAD_DIM)
        moved = jnp.einsum("hip,phd->hid", placement, per_head, preferred_element_type=jnp.float32)
        return moved.astype(jnp.bfloat16).reshape(HEADS, groups, CLUSTER, HEAD_DIM)

    def from_clusters(blocks):
        per_head = blocks.astype(jnp.bfloat16).reshape(HEADS, length, HEAD_DIM)
        moved = jnp.einsum("hip,hid->phd", placement, per_head, preferred_element_type=jnp.float32)
        return moved.astype(jnp.bfloat16).reshape(length, model_width)

    segment_blocks = jnp.take(segment, ordering).reshape(HEADS, groups, CLUSTER)
    present_blocks = jnp.take(present, ordering).reshape(HEADS, groups, CLUSTER)
    same_doc = segment_blocks[..., :, None] == segment_blocks[..., None, :]
    itself = jnp.eye(CLUSTER, dtype=bool)
    allowed = same_doc & ((present_blocks[..., None, :] == 1) | itself)

    def scores_of(query_blocks, key_blocks):
        raw_scores = (
            jnp.einsum(
                "hncd,hnmd->hncm", query_blocks, key_blocks, preferred_element_type=jnp.float32
            )
            * score_scale
        )
        return jnp.where(allowed, raw_scores, masked_score)

    projected = product(tokens, full_qkv)
    query = (projected[:, :model_width] + small_params[0]).astype(jnp.bfloat16)
    keys = projected[:, model_width : 2 * model_width].astype(jnp.bfloat16)
    values = (projected[:, 2 * model_width :] + small_params[1]).astype(jnp.bfloat16)
    query_blocks = to_clusters(query)
    key_blocks = to_clusters(keys)
    value_blocks = to_clusters(values)
    masked = scores_of(query_blocks, key_blocks)
    highest = jnp.max(masked, axis=-1, keepdims=True)
    exponent = jnp.exp(masked - highest)
    row_total = jnp.sum(exponent, axis=-1, keepdims=True)
    soft_weights = exponent / row_total
    log_total = highest + jnp.log(row_total)
    soft_low = soft_weights.astype(jnp.bfloat16)
    combined = from_clusters(
        jnp.einsum("hncm,hnmd->hncd", soft_low, value_blocks, preferred_element_type=jnp.float32)
    )
    attention = product(combined, full_out) + small_params[2]
    first_norm, first_normal, first_inverse = norm_forward(
        tokens.astype(jnp.float32) + attention, small_params[3], small_params[4]
    )
    first_low = first_norm.astype(jnp.bfloat16)
    hidden = product(first_low, full_up) + hidden_bias
    activated, gelu_pull = jax.vjp(gelu_exact, hidden)
    activated_low = activated.astype(jnp.bfloat16)
    feed_out = product(activated_low, full_down) + small_params[5]
    output, second_normal, second_inverse = norm_forward(
        first_norm + feed_out, small_params[6], small_params[7]
    )
    layer_out = output.astype(jnp.bfloat16)
    again_qkv, again_out, again_up, again_down = (
        lax.all_gather(part_qkv, "mp", axis=1, tiled=True),
        lax.all_gather(part_out, "mp", axis=1, tiled=True),
        lax.all_gather(part_up, "mp", axis=1, tiled=True),
        lax.all_gather(part_down, "mp", axis=1, tiled=True),
    )
    back_qkv, back_out, back_up, back_down = (
        lax.all_gather(again_qkv, "dp", axis=0, tiled=True),
        lax.all_gather(again_out, "dp", axis=0, tiled=True),
        lax.all_gather(again_up, "dp", axis=0, tiled=True),
        lax.all_gather(again_down, "dp", axis=0, tiled=True),
    )
    grad_gain_two = jnp.sum(cotangent * second_normal, axis=0)
    grad_shift_two = jnp.sum(cotangent, axis=0)
    second_grad = norm_backward(cotangent, second_normal, second_inverse, small_params[6])
    feed_grad = second_grad.astype(jnp.bfloat16)
    grad_bias_down = jnp.sum(feed_grad.astype(jnp.float32), axis=0)
    grad_w_down = outer_sum(activated_low, feed_grad)
    hidden_grad = gelu_pull(times_back(feed_grad, back_down))[0].astype(jnp.bfloat16)
    grad_bias_up = jnp.sum(hidden_grad.astype(jnp.float32), axis=0)
    grad_w_up = outer_sum(first_low, hidden_grad)
    first_grad = times_back(hidden_grad, back_up) + second_grad
    grad_gain_one = jnp.sum(first_grad * first_normal, axis=0)
    grad_shift_one = jnp.sum(first_grad, axis=0)
    residual_grad = norm_backward(first_grad, first_normal, first_inverse, small_params[3])
    attention_grad = residual_grad.astype(jnp.bfloat16)
    grad_bias_out = jnp.sum(attention_grad.astype(jnp.float32), axis=0)
    grad_w_out = outer_sum(combined, attention_grad)
    combined_grad = to_clusters(times_back(attention_grad, back_out).astype(jnp.bfloat16))
    masked_again = scores_of(query_blocks, key_blocks)
    soft_again = jnp.exp(masked_again - log_total)
    soft_again_low = soft_again.astype(jnp.bfloat16)
    value_sums = jnp.einsum(
        "hncm,hncd->hnmd", soft_again_low, combined_grad, preferred_element_type=jnp.float32
    )
    soft_grad = jnp.einsum(
        "hncd,hnmd->hncm", combined_grad, value_blocks, preferred_element_type=jnp.float32
    )
    score_grad = (
        soft_again * (soft_grad - jnp.sum(soft_grad * soft_again, axis=-1, keepdims=True))
    ).astype(jnp.bfloat16)
    query_sums = (
        jnp.einsum("hncm,hnmd->hncd", score_grad, key_blocks, preferred_element_type=jnp.float32)
        * score_scale
    )
    key_sums = (
        jnp.einsum("hncm,hncd->hnmd", score_grad, query_blocks, preferred_element_type=jnp.float32)
        * score_scale
    )
    query_grad = from_clusters(query_sums)
    key_grad = from_clusters(key_sums)
    value_grad = from_clusters(value_sums)
    grad_bias_query = jnp.sum(query_grad.astype(jnp.float32), axis=0)
    grad_bias_value = jnp.sum(value_grad.astype(jnp.float32), axis=0)
    projected_grad = jnp.concatenate([query_grad, key_grad, value_grad], axis=1)
    grad_w_qkv = outer_sum(tokens, projected_grad)
    grad_tokens = times_back(projected_grad, back_qkv) + residual_grad
    grad_vectors = jnp.stack(
        [
            grad_bias_query,
            grad_bias_value,
            grad_bias_out,
            grad_gain_one,
            grad_shift_one,
            grad_bias_down,
            grad_gain_two,
            grad_shift_two,
        ]
    )
    grad_up_row = grad_bias_up[None, :]
    row_qkv, row_out, row_up, row_down, row_vectors, row_bias = (
        lax.psum_scatter(
            grad_w_qkv.astype(jnp.bfloat16), "dp", scatter_dimension=0, tiled=True
        ).astype(jnp.float32),
        lax.psum_scatter(
            grad_w_out.astype(jnp.bfloat16), "dp", scatter_dimension=0, tiled=True
        ).astype(jnp.float32),
        lax.psum_scatter(
            grad_w_up.astype(jnp.bfloat16), "dp", scatter_dimension=0, tiled=True
        ).astype(jnp.float32),
        lax.psum_scatter(
            grad_w_down.astype(jnp.bfloat16), "dp", scatter_dimension=0, tiled=True
        ).astype(jnp.float32),
        lax.psum_scatter(
            grad_vectors.astype(jnp.bfloat16), "dp", scatter_dimension=1, tiled=True
        ).astype(jnp.float32),
        lax.psum_scatter(
            grad_up_row.astype(jnp.bfloat16), "dp", scatter_dimension=1, tiled=True
        ).astype(jnp.float32),
    )
    shard_qkv, shard_out, shard_up, shard_down, shard_vectors, shard_bias = (
        lax.psum_scatter(
            row_qkv.astype(jnp.bfloat16), "mp", scatter_dimension=1, tiled=True
        ).astype(jnp.float32),
        lax.psum_scatter(
            row_out.astype(jnp.bfloat16), "mp", scatter_dimension=1, tiled=True
        ).astype(jnp.float32),
        lax.psum_scatter(row_up.astype(jnp.bfloat16), "mp", scatter_dimension=1, tiled=True).astype(
            jnp.float32
        ),
        lax.psum_scatter(
            row_down.astype(jnp.bfloat16), "mp", scatter_dimension=1, tiled=True
        ).astype(jnp.float32),
        lax.psum_scatter(
            row_vectors.astype(jnp.bfloat16), "mp", scatter_dimension=1, tiled=True
        ).astype(jnp.float32),
        lax.psum_scatter(
            row_bias.astype(jnp.bfloat16), "mp", scatter_dimension=1, tiled=True
        ).astype(jnp.float32),
    )
    return (
        layer_out,
        grad_tokens,
        shard_qkv,
        shard_vectors[0],
        shard_vectors[1],
        shard_out,
        shard_vectors[2],
        shard_vectors[3],
        shard_vectors[4],
        shard_up,
        shard_bias[0],
        shard_down,
        shard_vectors[5],
        shard_vectors[6],
        shard_vectors[7],
    )


LANES = 128
QKV_ROWS = 96
UP_TILES = 6
DOWN_TILES = 3
PACK_Q = 4 * QKV_ROWS + QKV_ROWS // 2 + 16
PACK_OU = QKV_ROWS + QKV_ROWS // 2 + UP_TILES * QKV_ROWS
PACK_D = DOWN_TILES * 192
VECTOR_ROW = 4 * QKV_ROWS + QKV_ROWS // 2
UP_ROW = QKV_ROWS + QKV_ROWS // 2


def whole():
    return pl.BlockSpec(memory_space=pltpu.VMEM)


def far():
    return pl.BlockSpec(memory_space=pltpu.HBM)


def kept_far(arrays):
    return [pltpu.with_memory_space_constraint(x, pltpu.HBM) for x in arrays]


def near(x):
    return pltpu.with_memory_space_constraint(x, pltpu.VMEM)


def near_shape(shape, dtype=jnp.bfloat16):
    return pltpu.VMEM(shape, dtype)


def waited(after):
    return [kept_far([x.token])[0] if isinstance(x, Results) else x for x in after]


def anywhere(after):
    return [far() if isinstance(x, Results) else pl.BlockSpec(memory_space=pl.ANY) for x in after]


class Results(list):
    token = None


TOKEN = pltpu.HBM((8, 128), jnp.float32)


def place():
    return lax.axis_index("dp"), lax.axis_index("mp")


SHORT = pl.CostEstimate(flops=1, bytes_accessed=1, transcendentals=0)
MICROSECOND = 1_153_000_000


class Place(tuple):
    def arrived(self, index, part=None):
        copies, here = self.late[index]
        for i in range(len(copies)) if part is None else [part]:
            if copies[i] is not None:
                copies[i].wait()
                copies[i] = None
        return here

    def send(self, index, where=None, source=None):
        here, there = self.far[index]
        source = here if source is None else source
        if where is not None:
            source, there = source.at[where], there.at[where]
        copy = pltpu.make_async_copy(source, there, self.sems.at[len(self.sent)])
        copy.start()
        self.sent.append(copy)


def call(
    body, out_shapes, operands, scratch=(), staged=0, late=(), far_outs=None, sends=None, after=(),
    aliases=None, vmem=10, cost=0, name=None,
):
    operands = operands[1:]
    far_outs = far_outs or {}
    sends = len(far_outs) if sends is None else sends
    count, outs, copied = len(operands), len(out_shapes), staged + len(late)
    spread = [(0, 1)] * staged + [x or (0, 1) for x in late]
    starts = [sum(n for _, n in spread[:i]) for i in range(copied)]

    def with_copies(*refs):
        sources, rest = refs[:copied], refs[copied:count]
        results = list(refs[count + len(after) : count + len(after) + outs])
        own = refs[count + len(after) + outs + 1 :]
        mine, own = own[: len(scratch)], own[len(scratch) :]
        arrived, own = own[:copied], list(own[copied:])
        me = Place(place())
        me.sent, me.far = [], {}
        if copied:
            sem = own.pop(0)
            copies = []
            for source, here, (axis, parts), start in zip(sources, arrived, spread, starts):
                size = here.shape[axis] // parts
                copies.append([])
                for i in range(parts):
                    cut = (slice(None),) * axis + (slice(i * size, (i + 1) * size),)
                    copies[-1].append(
                        pltpu.make_async_copy(source.at[cut], here.at[cut], sem.at[start + i])
                    )
            for copy in sum(copies, []):
                copy.start()
            for (copy,) in copies[:staged]:
                copy.wait()
            me.late = list(zip(copies[staged:], arrived[staged:]))
        if far_outs:
            me.sems = own.pop(0)
            for index, has_room in far_outs.items():
                here = own.pop(0) if has_room else None
                me.far[index] = (here, results[index])
                results[index] = here
        body(me, *arrived[:staged], *rest, *results, *mine)
        for copy in me.sent:
            copy.wait()

    room = [pltpu.VMEM(x.shape, x.dtype) for x in operands[:copied]]
    if copied:
        room.append(pltpu.SemaphoreType.DMA((sum(n for _, n in spread),)))
    if far_outs:
        room.append(pltpu.SemaphoreType.DMA((sends,)))
        room += [pltpu.VMEM(out_shapes[i].shape, out_shapes[i].dtype) for i in far_outs if far_outs[i]]
    given = [
        pltpu.HBM(x.shape, x.dtype) if i in far_outs else x for i, x in enumerate(out_shapes)
    ]
    *results, token = pl.pallas_call(
        with_copies,
        out_shape=[*given, TOKEN],
        in_specs=[pl.BlockSpec(memory_space=pl.ANY)] * staged
        + [far()] * len(late)
        + [whole()] * (count - copied)
        + anywhere(after),
        out_specs=[far() if i in far_outs else whole() for i in range(outs)] + [far()],
        scratch_shapes=list(scratch) + room,
        input_output_aliases=aliases or {},
        compiler_params=pltpu.CompilerParams(vmem_limit_bytes=vmem * 1024 * 1024),
        cost_estimate=SHORT if not cost else pl.CostEstimate(cost, 1, 0),
        name=name,
    )(
        *operands[:staged],
        *kept_far(operands[staged:copied]),
        *operands[copied:],
        *waited(after),
    )
    results = Results(results)
    results.token = token
    return results


def tie(arrays, after):
    count = len(arrays)

    def body(*refs):
        pass

    return pl.pallas_call(
        body,
        out_shape=[shape_of(x.shape, x.dtype) for x in arrays],
        in_specs=[pl.BlockSpec(memory_space=pl.ANY)] * count + anywhere(after),
        out_specs=[pl.BlockSpec(memory_space=pl.ANY)] * count,
        input_output_aliases={i: i for i in range(count)},
        compiler_params=pltpu.CompilerParams(vmem_limit_bytes=1024 * 1024),
        cost_estimate=SHORT,
        name="tie",
    )(*arrays, *waited(after))


def shape_of(shape, dtype=jnp.bfloat16):
    return jax.ShapeDtypeStruct(shape, dtype)


def halves_beside(single):
    half = single.shape[0] // 2
    return jnp.concatenate([single[:half], single[half:]], axis=1)


def pack_columns(odd, low, tiles, base, target):
    @pl.when(odd)
    def _():
        for t in range(tiles):
            target[base + t * 96 : base + (t + 1) * 96, :] = low[
                :, 64 + t * LANES : 64 + (t + 1) * LANES
            ].astype(jnp.bfloat16)
        target[base + tiles * 96 : base + tiles * 96 + 48, :] = halves_beside(low[:, :64]).astype(
            jnp.bfloat16
        )

    @pl.when(jnp.logical_not(odd))
    def _():
        for t in range(tiles):
            target[base + t * 96 : base + (t + 1) * 96, :] = low[
                :, t * LANES : (t + 1) * LANES
            ].astype(jnp.bfloat16)
        target[base + tiles * 96 : base + tiles * 96 + 48, :] = halves_beside(
            low[:, tiles * LANES : tiles * LANES + 64]
        ).astype(jnp.bfloat16)


def pack_q_body(me, *refs):
    w_qkv, vectors, target, own = refs[0], refs[1:10], refs[10], refs[11]
    pack_columns(lax.rem(me[1], 2) == 1, w_qkv[...], 4, 0, target)
    rows = lax.broadcasted_iota(jnp.int32, (16, LANES), 0)
    tail = jnp.zeros((16, LANES), jnp.float32)
    for v in range(9):
        value = vectors[v][...]
        wide = jnp.concatenate(
            [value, jnp.zeros((1, LANES - value.shape[1]), jnp.float32)], axis=1
        )
        tail = jnp.where(rows == v, jnp.broadcast_to(wide, (16, LANES)), tail)
    target[VECTOR_ROW:, :] = tail.astype(jnp.bfloat16)
    me.send(0)
    own[...] = target[...]


def pack_q(me, w_qkv, vectors, bias_up):
    small = [v.reshape(1, -1) for v in (*vectors, bias_up)]
    return call(
        pack_q_body, [shape_of((PACK_Q, LANES))] * 2, [me, *kept_far([w_qkv, *small])], staged=10, far_outs={0: True},
        name="pack_q",
    )


def pack_rest_body(me, w_out, w_up, w_down, to_ou, upper_d, lower_d, to_d):
    for t in range(DOWN_TILES):
        to_d[t * 192 : (t + 1) * 192, :] = w_down[:, t * LANES : (t + 1) * LANES].astype(
            jnp.bfloat16
        )
    upper_d[...] = to_d[: PACK_D // 2, :]
    lower_d[...] = to_d[PACK_D // 2 :, :]
    me.send(1)
    me.send(2)
    pack_columns(lax.rem(me[1], 2) == 1, w_out[...], 1, 0, to_ou)
    for t in range(UP_TILES):
        to_ou[UP_ROW + t * 96 : UP_ROW + (t + 1) * 96, :] = w_up[
            :, t * LANES : (t + 1) * LANES
        ].astype(jnp.bfloat16)


def pack_rest(me, w_out, w_up, w_down, after):
    return call(
        pack_rest_body,
        [
            near_shape((PACK_OU, LANES)),
            shape_of((PACK_D // 2, LANES)),
            shape_of((PACK_D // 2, LANES)),
            near_shape((PACK_D, LANES)),
        ],
        [me, *kept_far([w_out, w_up, w_down.T])],
        staged=3,
        far_outs={1: True, 2: True},
        after=after,
        name="pack_rest",
    )


def swap(x, axis, bit):
    size = lax.axis_size(axis)
    return lax.ppermute(x, axis, [(i, i ^ bit) for i in range(size)])


CORE, ALONG_X, ALONG_Y = 1, 2, 4


def gather_z(x, own=None):
    return [x if own is None else own] + [swap(x, "mp", k) for k in (1, 2, 3)]


def beside(me, groups, shapes, after=(), name="beside", cost=0):
    sources = []
    for x, _ in groups:
        if all(x is not y for y in sources):
            sources.append(x)

    def body(me, *refs):
        for x, (index, where) in groups:
            source = refs[next(n for n, y in enumerate(sources) if x is y)]
            refs[len(sources) + index][where] = source[...]

    return call(body, [shape_of(s) for s in shapes], [me, *sources], after=after, name=name, cost=cost)


def beside_two(me, a, b, after=(), cost=0):
    return beside(me, [(a, (0, 0)), (b, (0, 1))], [(2, *a.shape)], after, "beside_two", cost)


def gather_near(me, parts, after=()):
    shape = (2, *parts[0].shape)
    found = beside(
        me,
        [(parts[0], (0, 0)), (parts[1], (0, 1)), (parts[2], (1, 0)), (parts[3], (1, 1))],
        [shape, shape],
        after,
        "beside_z",
    )
    first, second = found
    result = Results([first, swap(first, "dp", ALONG_X), second, swap(second, "dp", ALONG_Y)])
    result.token = found.token
    return result


def gather_far(me, parts, after=(), cost=0):
    shape = (2, *parts[0].shape)
    groups = [(parts[i], (i // 2, i % 2)) for i in range(4)]
    found = beside(me, groups, [shape, shape], after, "beside_near", cost)
    first, second = found
    result = Results([first, second, swap(first, "dp", ALONG_Y), swap(second, "dp", ALONG_X)])
    result.token = found.token
    return result


def gather_core(parts):
    return list(parts) + [swap(x, "dp", CORE) for x in parts]


def gathered_blocks(me, refs, steps=(1, 2)):
    for index, ref in enumerate(refs):
        core, far, half = index // 4, index % 4 // 2, index % 2
        for mid in range(2):
            for low in range(2):
                kx, ky = (far, mid) if half else (mid, far)
                along_z = steps[0] * low + steps[1] * half
                yield me[0] ^ (core + 2 * kx + 4 * ky), me[1] ^ along_z, ref.at[mid, low]


def split_pairs(refs):
    return [ref.at[i] for ref in refs for i in range(2)]


def place_columns(block, base, tiles, dp, mp, width, weights, singles):
    start = pl.multiple_of(mp * width + 64 * lax.rem(mp, 2), LANES)
    rows = pl.ds(pl.multiple_of(dp * 96, 32), 96)
    for t in range(tiles):
        weights[rows, pl.ds(pl.multiple_of(start + t * LANES, LANES), LANES)] = block[
            base + t * 96 : base + (t + 1) * 96, :
        ]
    singles[mp, pl.ds(pl.multiple_of(dp * 48, 16), 48), :] = block[
        base + tiles * 96 : base + tiles * 96 + 48, :
    ]


def place_singles(width, weights, singles):
    for pair in range(2):
        column = 2 * pair * width + (width // LANES) * LANES
        for dp in range(8):
            left = singles[2 * pair, dp * 48 : (dp + 1) * 48, :].astype(jnp.float32)
            right = singles[2 * pair + 1, dp * 48 : (dp + 1) * 48, :].astype(jnp.float32)
            upper = jnp.concatenate([left[:, :64], right[:, :64]], axis=1)
            lower = jnp.concatenate([left[:, 64:], right[:, 64:]], axis=1)
            weights[dp * 96 : dp * 96 + 48, column : column + LANES] = upper.astype(jnp.bfloat16)
            weights[dp * 96 + 48 : (dp + 1) * 96, column : column + LANES] = lower.astype(
                jnp.bfloat16
            )


def unpack_q_body(me, *refs):
    blocks, weights, vectors, bias_up, singles, tails = refs[:8], *refs[8:]
    for dp, mp, block in gathered_blocks(me, blocks, (2, 1)):
        place_columns(block, 0, 4, dp, mp, 576, weights, singles)
        tails[dp * 4 + mp] = block[VECTOR_ROW:, :].astype(jnp.float32)
    place_singles(576, weights, singles)
    lane = lax.broadcasted_iota(jnp.int32, (16, LANES), 1)

    def spread(width, count):
        found = [jnp.zeros((16, LANES), jnp.float32) for _ in range(count)]
        for device in range(32):
            start, tile = device * width % LANES, device * width // LANES
            piece = tails[device]
            moved = pltpu.roll(piece, start, axis=1) if start else piece
            found[tile] = jnp.where((lane >= start) & (lane < start + width), moved, found[tile])
            if start + width > LANES:
                found[tile + 1] = jnp.where(lane < start + width - LANES, moved, found[tile + 1])
        return found

    for t, value in enumerate(spread(24, 6)):
        vectors[:, t * LANES : (t + 1) * LANES] = value[:8]
    for t, value in enumerate(spread(96, 24)):
        bias_up[:, t * LANES : (t + 1) * LANES] = value[8:9]


def unpack_ou_body(me, *refs):
    blocks, w_out, w_up, singles = refs[:8], *refs[8:]
    for dp, mp, block in gathered_blocks(me, blocks, (2, 1)):
        place_columns(block, 0, 1, dp, mp, 192, w_out, singles)
        rows = pl.ds(pl.multiple_of(dp * 96, 32), 96)
        for t in range(UP_TILES):
            w_up[rows, pl.ds(pl.multiple_of(mp * 768 + t * LANES, LANES), LANES)] = block[
                UP_ROW + t * 96 : UP_ROW + (t + 1) * 96, :
            ]
    place_singles(192, w_out, singles)


def unpack_ou(me, parts, after=()):
    return call(
        unpack_ou_body,
        [near_shape((768, 768)), near_shape((768, 3072))],
        [me, *parts],
        [pltpu.VMEM((4, 384, LANES), jnp.bfloat16)],
        after=after,
        name="unpack_ou",
    )


def spread_d_body(me, mine, upper_x, lower_y, upper, lower):
    half = PACK_D // 2
    upper[0], upper[1] = mine[:half, :], upper_x[...]
    lower[0], lower[1] = mine[half:, :], lower_y[...]


def spread_d(me, mine, upper_x, lower_y, after=()):
    shape = near_shape((2, PACK_D // 2, LANES))
    return call(
        spread_d_body, [shape, shape], [me, mine, upper_x, lower_y], after=after, name="spread_d"
    )


def whole_d_body(me, upper, upper_y, lower, lower_x, out):
    half = PACK_D // 2
    for kx in range(2):
        for ky in range(2):
            out[2 * ky + kx, :half, :] = (upper_y if ky else upper)[kx]
            out[2 * ky + kx, half:, :] = (lower_x if kx else lower)[ky]


def whole_d(me, upper, upper_y, lower, lower_x, after=()):
    return call(
        whole_d_body, [near_shape((4, PACK_D, LANES))], [me, upper, upper_y, lower, lower_x],
        after=after, name="whole_d",
    )


def unpack_d_body(me, *refs):
    blocks, turned = refs[:4], refs[4]
    for index, ref in enumerate(blocks):
        for far in range(2):
            for plane in range(4):
                dp, mp = me[0] ^ (2 * plane + index // 2), me[1] ^ (2 * far + index % 2)
                rows = pl.ds(pl.multiple_of(mp * 192, 64), 192)
                for t in range(DOWN_TILES):
                    turned[rows, pl.ds(pl.multiple_of(dp * 384 + t * LANES, LANES), LANES)] = ref[
                        far, plane, t * 192 : (t + 1) * 192, :
                    ]


def unpack_d(me, parts, after=()):
    return call(
        unpack_d_body, [near_shape((768, 3072))], [me, *parts], after=after, name="unpack_d"
    )


def turn_body(me, source, send, keep, turned):
    value = source[...].T
    for dp in range(8):
        k = me[0] ^ dp
        slot = (1 - (k & 1)) * 4 + (k >> 1)
        turned[pl.ds(pl.multiple_of(slot * 96, 32), 96), :] = value[dp * 96 : (dp + 1) * 96, :]
    send[...] = turned[:384, :]
    keep[...] = turned[384:, :]


def turn(me, source, after=()):
    n = source.shape[0]
    return call(
        turn_body,
        [shape_of((384, n)), near_shape((384, n))],
        [me, source],
        [pltpu.VMEM((768, n), jnp.bfloat16)],
        after=after,
        name="turn",
    )


def dot(a, b):
    return jnp.dot(a, b, preferred_element_type=jnp.float32)


def dot_nt(a, b):
    return lax.dot_general(a, b, (((1,), (1,)), ((), ())), preferred_element_type=jnp.float32)


def dot_tn(a, b):
    return lax.dot_general(a, b, (((0,), (0,)), ((), ())), preferred_element_type=jnp.float32)


def part_of(targets, kp, mp):
    ky, kx = kp // 2, kp % 2
    if mp < 2:
        return targets[ky].at[kx, mp]
    return targets[2 + kx].at[ky, mp - 2]


def store_columns(target, base, tiles, first, value):
    for t in range(tiles):
        target[base + t * 96 : base + (t + 1) * 96, :] = value[
            :, first + t * LANES : first + (t + 1) * LANES
        ].astype(jnp.bfloat16)


def store_single(target, base, odd, value):
    upper, lower = value[:48], value[48:]
    low_lanes = lax.broadcasted_iota(jnp.int32, (48, LANES), 1) < 64
    if odd:
        both = jnp.where(low_lanes, pltpu.roll(upper, 64, axis=1), lower)
    else:
        both = jnp.where(low_lanes, upper, pltpu.roll(lower, 64, axis=1))
    target[base : base + 48, :] = both.astype(jnp.bfloat16)


def column_gradient(lefts, rights, targets, base, tiles, width):
    def product(columns):
        return dot(lefts[0], rights[0][:, columns]) + dot(lefts[1], rights[1][:, columns])

    for pair in range(2):
        first = 2 * pair * width
        middle = first + tiles * LANES
        for begin, mp in ((first, 2 * pair), (middle + LANES, 2 * pair + 1)):
            value = product(slice(begin, begin + tiles * LANES))
            for kp in range(4):
                store_columns(
                    targets(kp, mp), base, tiles, 0, value[kp * 96 : (kp + 1) * 96]
                )
        value = product(slice(middle, middle + LANES))
        for kp in range(4):
            for mp in (2 * pair, 2 * pair + 1):
                store_single(
                    targets(kp, mp), base + tiles * 96, mp % 2,
                    value[kp * 96 : (kp + 1) * 96],
                )


def parts_shape(rows):
    return [near_shape((2, 2, rows, LANES)), shape_of((2, 2, rows, LANES))] * 2


def gradient_q_body(
    me, keep, other_keep, grads, other_grads, vectors, other_vectors, mine, send, room
):
    targets = lambda kp, mp: room.at[me[1] ^ mp, kp]
    lefts, rights = (keep[...], other_keep[...]), (grads, other_grads)
    column_gradient(lefts, rights, targets, 0, 4, 576)
    sums = vectors[...] + other_vectors[...]
    lane = lax.broadcasted_iota(jnp.int32, (16, LANES), 1)
    rows = lax.broadcasted_iota(jnp.int32, (16, LANES), 0)

    def cut(source, width, device):
        start, tile = device * width % LANES, device * width // LANES
        value = source[:, tile * LANES : (tile + 1) * LANES]
        moved = pltpu.roll(value, LANES - start, axis=1) if start else value
        if start + width > LANES:
            after = source[:, (tile + 1) * LANES : (tile + 2) * LANES]
            after = pltpu.roll(after, LANES - start, axis=1)
            here = lax.broadcasted_iota(jnp.int32, value.shape, 1)
            moved = jnp.where(here < LANES - start, moved, after)
        return moved

    for kp in range(4):
        plane = (me[0] >> 1) ^ kp
        for mp in range(4):
            tail = jnp.zeros((16, LANES), jnp.float32)
            for dp in range(8):
                device = dp * 4 + mp
                row = 8 + device // 8
                up = jnp.broadcast_to(cut(sums[row : row + 1], 96, device % 8), (8, LANES))
                found = jnp.concatenate([cut(sums[:8], 24, device), up], axis=0)
                owner = dp == 2 * plane + (me[0] & 1)
                tail = jnp.where(owner, found, tail)
            tail = jnp.where((rows < 8) & (lane >= 24), 0.0, tail).astype(jnp.bfloat16)
            targets(kp, mp)[VECTOR_ROW:, :] = tail
    for kz in range(4):
        (send if kz % 2 else mine)[kz // 2] = room[kz]


def gradient_q(me, keep, other_keep, grads, other_grads, vectors, other_vectors, after=()):
    return call(
        gradient_q_body,
        [near_shape((2, 4, PACK_Q, LANES)), shape_of((2, 4, PACK_Q, LANES))],
        [me, keep, other_keep, grads, other_grads, vectors, other_vectors],
        [pltpu.VMEM((4, 4, PACK_Q, LANES), jnp.bfloat16)],
        after=after,
        name="gradient_q",
    )


def gradient_ou_body(me, *refs):
    combined, first_low, hidden_grad = (refs[i : i + 2] for i in (0, 2, 4))
    attention_grad, room = (refs[6], refs[13]), refs[13]
    targets = functools.partial(part_of, refs[9:13])
    room[:, :384] = refs[7][...]
    room[:, 384:] = refs[8][...]
    column_gradient([x[...] for x in combined], attention_grad, targets, 0, 1, 192)
    lefts = [x[...] for x in first_low]
    for mp in range(4):
        columns = slice(mp * 768, (mp + 1) * 768)
        value = dot(lefts[0], hidden_grad[0][:, columns])
        value = value + dot(lefts[1], hidden_grad[1][:, columns])
        for kp in range(4):
            store_columns(
                targets(kp, mp), UP_ROW, UP_TILES, 0, value[kp * 96 : (kp + 1) * 96]
            )


def gradient_ou(me, combined, first_low, hidden_grad, attention_grad, after=()):
    return call(
        gradient_ou_body,
        parts_shape(PACK_OU),
        [me, *combined, *first_low, *hidden_grad, *attention_grad],
        [pltpu.VMEM(attention_grad[0].shape, jnp.bfloat16)],
        after=after,
        name="gradient_ou",
    )


def gradient_d_body(me, feed_grad, other_feed_grad, activated, other_activated, *refs):
    targets, turned, other_turned = refs[:4], refs[4], refs[5]
    turned[...] = feed_grad[...].T
    other_turned[...] = other_feed_grad[...].T
    for kp in range(4):
        dp = me[0] ^ (2 * kp)
        block = activated[:, pl.ds(pl.multiple_of(dp * 384, LANES), 384)]
        value = dot(turned[...], block)
        value = value + dot(other_turned[...], other_activated[:, kp * 384 : (kp + 1) * 384])
        for mp in range(4):
            target = part_of(targets, kp, mp)
            for t in range(DOWN_TILES):
                target[t * 192 : (t + 1) * 192, :] = value[
                    mp * 192 : (mp + 1) * 192, t * LANES : (t + 1) * LANES
                ].astype(jnp.bfloat16)


def gradient_d(me, feed_grad, other_feed_grad, activated, other_activated, after=()):
    return call(
        gradient_d_body,
        parts_shape(PACK_D),
        [me, feed_grad, other_feed_grad, activated, other_activated],
        [pltpu.VMEM((768, feed_grad.shape[0]), jnp.bfloat16)] * 2,
        after=after,
        name="gradient_d",
    )


def sums_body(me, bias, one, two, up, out):
    out[0:2, :], out[2:5, :], out[5:8, :] = bias[...], one[...], two[...]
    for i in range(4):
        out[8 + i : 9 + i, :] = up[:, i * 768 : (i + 1) * 768]


def all_sums(me, *sums):
    return call(sums_body, [shape_of((12, 768), jnp.float32)], [me, *sums], name="sums")[0]


def add(a, b):
    return a.astype(jnp.float32) + b.astype(jnp.float32)


def add_plane_body(me, first, first_in, second, second_in, *outs):
    for keep, send, a, b in ((*outs[:2], first, first_in), (*outs[2:], second, second_in)):
        keep[...] = add(a[0], b[0]).astype(jnp.bfloat16)
        send[...] = add(a[1], b[1]).astype(jnp.bfloat16)


def add_last_body(me, first, first_in, second, second_in, *refs):
    keep, send, room = refs
    for mp in range(4):
        a, b = (first, first_in) if mp < 2 else (second, second_in)
        room[me[1] ^ mp] = add(a[mp % 2], b[mp % 2]).astype(jnp.bfloat16)
    for k in range(4):
        (send if k % 2 else keep)[k // 2] = room[k]


def add_first_body(me, mine, arrived, *outs):
    for kp in range(4):
        ky, kx = kp // 2, kp % 2
        outs[ky][kx] = add(mine[0, kp], arrived[0, kp]).astype(jnp.bfloat16)
        outs[2 + kx][ky] = add(mine[1, kp], arrived[1, kp]).astype(jnp.bfloat16)


def add_first(me, mine, arrived, after=()):
    rows = mine.shape[2]
    return call(
        add_first_body,
        [near_shape((2, rows, LANES)), shape_of((2, rows, LANES))] * 2,
        [me, mine, arrived],
        after=after,
        name="add_first",
    )


def add_both_body(me, first, first_in, second, second_in, keep, send):
    keep[...] = add(first[...], first_in[...])
    send[...] = add(second[...], second_in[...]).astype(jnp.bfloat16)


def add_both(me, parts, after=()):
    shape = parts[0].shape
    return call(
        add_both_body,
        [near_shape(shape, jnp.float32), shape_of(shape)],
        [me, *parts],
        after=after,
        name="add_both",
    )


def add_z_body(me, mine, arrived, keep, send):
    keep[...] = add(mine[0], arrived[0])
    send[...] = add(mine[1], arrived[1]).astype(jnp.bfloat16)


def scatter_near(parts):
    first, first_send, second, second_send = parts
    return first, swap(first_send, "dp", ALONG_Y), second, swap(second_send, "dp", ALONG_X)


def add_plane(me, parts, after=(), cost=0):
    shape = parts[0].shape[1:]
    return call(
        add_plane_body,
        [near_shape(shape), shape_of(shape)] * 2,
        [me, *parts],
        after=after,
        cost=cost,
        name="add_plane",
    )


def scatter_far(parts):
    first, first_send, second, second_send = parts
    return first, swap(first_send, "dp", ALONG_X), second, swap(second_send, "dp", ALONG_Y)


def add_last(me, parts, after=(), cost=0):
    rows = parts[0].shape[1]
    return call(
        add_last_body,
        [near_shape((2, rows, LANES)), shape_of((2, rows, LANES))],
        [me, *parts],
        [pltpu.VMEM((4, rows, LANES), jnp.bfloat16)],
        after=after,
        cost=cost,
        name="add_last",
    )


def scatter_z(parts):
    return parts[0], swap(parts[1], "mp", 1)


def add_z(me, parts, after=()):
    rows = parts[0].shape[1]
    return call(
        add_z_body,
        [near_shape((rows, LANES), jnp.float32), shape_of((rows, LANES))],
        [me, *parts],
        after=after,
        name="add_z",
    )


def scatter_z_far(parts):
    return parts[0], swap(parts[1], "mp", 2)


def total(refs, rows):
    value = refs[0][rows, :].astype(jnp.float32)
    for ref in refs[1:]:
        value = value + ref[rows, :].astype(jnp.float32)
    return value


def finish_columns(me, refs, base, tiles, out):
    odd = lax.rem(me[1], 2) == 1
    full = [total(refs, pl.ds(base + t * 96, 96)) for t in range(tiles)]
    single = total(refs, pl.ds(base + tiles * 96, 48))
    single = jnp.concatenate([single[:, :64], single[:, 64:]], axis=0)

    @pl.when(odd)
    def _():
        out[...] = jnp.concatenate([single, *full], axis=1)

    @pl.when(jnp.logical_not(odd))
    def _():
        out[...] = jnp.concatenate([*full, single], axis=1)


def finish_q_body(me, *refs):
    parts, out, outs = refs[:2], refs[2], refs[3:]
    finish_columns(me, parts, 0, 4, out)
    tail = total(parts, pl.ds(VECTOR_ROW, 16))
    for v in range(8):
        outs[v][...] = tail[v : v + 1, :24]
    outs[8][...] = tail[8:9, :96]


def finish_q(me, parts):
    f = jnp.float32
    return call(
        finish_q_body,
        [shape_of((96, 576), f)] + [shape_of((1, 24), f)] * 8 + [shape_of((1, 96), f)],
        [me, *parts],
        name="finish_q",
    )


def finish_ou_body(me, *refs):
    parts, w_out, w_up = refs[:2], refs[2], refs[3]
    finish_columns(me, parts, 0, 1, w_out)
    for t in range(UP_TILES):
        w_up[:, t * LANES : (t + 1) * LANES] = total(parts, pl.ds(UP_ROW + t * 96, 96))


def finish_ou(me, parts, after=()):
    f = jnp.float32
    return call(
        finish_ou_body, [shape_of((96, 192), f), shape_of((96, 768), f)], [me, *parts],
        after=after, name="finish_ou",
    )


def finish_d_body(me, *refs):
    parts, out = refs[:2], refs[2]
    for t in range(DOWN_TILES):
        out[:, t * LANES : (t + 1) * LANES] = total(parts, pl.ds(t * 192, 192))


def finish_d(me, parts, after=()):
    f = jnp.float32
    return call(finish_d_body, [shape_of((192, 384), f)], [me, *parts], after=after, name="finish_d")


PAIRS = HEADS // 2


def iota(shape, axis):
    return lax.broadcasted_iota(jnp.int32, shape, axis)


def place_matrix(order, head):
    length = order.shape[1]
    row = order[head : head + 1, :].astype(jnp.int16)
    token = iota((length, length), 0).astype(jnp.int16)
    return jnp.where(token == row, jnp.bfloat16(1.0), jnp.bfloat16(0.0))


def project_body(me, *refs):
    blocks, tokens = split_pairs(refs[:4]), refs[4]
    weights, vectors, bias_up, qkv, singles, tails = refs[5:]
    unpack_q_body(me, *blocks, weights, vectors, bias_up, singles, tails)
    for c in range(9):
        columns = slice(c * 256, (c + 1) * 256)
        value = dot(tokens[...], weights[:, columns])
        if c < 3:
            value = value + vectors[0:1, c * 256 : (c + 1) * 256]
        elif c >= 6:
            value = value + vectors[1:2, (c - 6) * 256 : (c - 5) * 256]
        qkv[:, columns] = value.astype(jnp.bfloat16)


def project(me, parts, tokens, after=()):
    return call(
        project_body,
        [
            near_shape((768, 2304)),
            near_shape((8, 768), jnp.float32),
            near_shape((1, 3072), jnp.float32),
            near_shape((tokens.shape[0], 2304)),
        ],
        [me, *parts, tokens],
        [pltpu.VMEM((4, 384, LANES), jnp.bfloat16), pltpu.VMEM((32, 16, LANES), jnp.float32)],
        after=after,
        name="project",
    )


def attend_body(first_pair, pairs, me, qkv, order, facts, *refs):
    swapped, values, soft, combined = refs[-4:]
    length = qkv.shape[0]
    groups = length // CLUSTER
    blocks = [slice(g * CLUSTER, (g + 1) * CLUSTER) for g in range(groups)]
    low = iota((length, LANES), 1) < 64
    itself = iota((CLUSTER, CLUSTER), 0) == iota((CLUSTER, CLUSTER), 1)
    pick = [
        jnp.where(iota((16, LANES), 1) == lane, 1.0, 0.0).astype(jnp.bfloat16) for lane in (64, 0)
    ]
    scale = HEAD_DIM ** (-0.5)

    for place in range(pairs):
        pair = first_pair + place

        def columns(base, pair=pair):
            return slice(base + pair * LANES, base + (pair + 1) * LANES)

        query = qkv[:, columns(0)].astype(jnp.float32)
        keys = qkv[:, columns(768)].astype(jnp.float32)
        value = qkv[:, columns(1536)].astype(jnp.float32)
        known = facts[...]
        tiles = (
            (jnp.where(low, query, pltpu.roll(keys, 64, axis=1)), jnp.where(low, value, known)),
            (jnp.where(low, pltpu.roll(query, 64, axis=1), keys), jnp.where(low, known, value)),
        )
        moved, to_tokens = [], []
        for h in range(2):
            back = place_matrix(order, 2 * pair + h)
            to_tokens.append(back)
            tile = jnp.concatenate([t.astype(jnp.bfloat16) for t in tiles[h]], axis=1)
            moved.append(dot_tn(back, tile))
        query_slots, key_slots, value_slots, codes, rows_of = [], [], [], [], []
        for h in range(2):
            both = moved[h][:, :LANES]
            query_slots.append(jnp.where(low, both, 0.0).astype(jnp.bfloat16))
            key_slots.append(pltpu.roll(both, 64, axis=1).astype(jnp.bfloat16))
            value_slots.append(moved[h][:, LANES:].astype(jnp.bfloat16))
            swapped[2 * place + h] = key_slots[h]
            values[2 * place + h] = value_slots[h]
            lane = 64 * (1 - h)
            code = moved[h][:, LANES + lane : LANES + lane + 1]
            row = dot_nt(pick[h], value_slots[h])[0:1]
            codes.append(jnp.where(code >= 32.0, code - 32.0, code))
            rows_of.append(row)
        scores = [
            [dot_nt(query_slots[h][b], key_slots[h][b]) for b in blocks] for h in range(2)
        ]
        found = []
        for h in range(2):
            outs = []
            for g, b in enumerate(blocks):
                allowed = (codes[h][b] == rows_of[h][:, b]) | itself
                value = jnp.where(allowed, scores[h][g] * scale, masked_score)
                value = jnp.exp(value - jnp.max(value, axis=1, keepdims=True))
                weights = value / jnp.sum(value, axis=1, keepdims=True)
                soft[2 * place + h, b, :] = weights
                outs.append(weights.astype(jnp.bfloat16))
            found.append(
                [dot(outs[g], value_slots[h][b]) for g, b in enumerate(blocks)]
            )
        result = None
        for h in range(2):
            value = jnp.concatenate(found[h], axis=0)
            value = jnp.where(low if h == 0 else jnp.logical_not(low), value, 0.0)
            value = dot(to_tokens[h], value.astype(jnp.bfloat16))
            result = value if result is None else result + value
        combined[:, columns(0)] = result.astype(jnp.bfloat16)


def attend(me, qkv, order, facts, first_pair, pairs, combined=None, after=()):
    length = qkv.shape[0]
    operands = [me, qkv, order, facts]
    if combined is not None:
        operands.append(combined)
    return call(
        functools.partial(attend_body, first_pair, pairs),
        [
            near_shape((2 * pairs, length, LANES)),
            near_shape((2 * pairs, length, LANES)),
            near_shape((2 * pairs, length, CLUSTER), jnp.float32),
            near_shape((length, 768)),
        ],
        operands,
        after=after,
        aliases={3: 3} if combined is not None else None,
        name="attend",
    )


def by_rows(first, count, step, body):
    for i in range(first, first + count, step):
        body(slice(i, i + step))


def mean(value):
    return jnp.mean(value, axis=1, keepdims=True)


def fold(value):
    return jnp.sum(value.reshape(value.shape[0] // 8, 8, value.shape[1]), axis=0)


def out_norm_body(me, combined, w_out, tokens, vectors, first_low, normal, inverse, total_ref):

    def rows_of(rows):
        value = total_ref[rows, :] + vectors[2:3] + tokens[rows, :].astype(jnp.float32)
        centred = value - mean(value)
        scale = lax.rsqrt(mean(centred * centred) + epsilon)
        norm = centred * scale
        normal[rows, :] = norm
        inverse[rows, :] = jnp.broadcast_to(scale, (scale.shape[0], LANES))
        first_low[rows, :] = (norm * vectors[3:4] + vectors[4:5]).astype(jnp.bfloat16)

    half = tokens.shape[0] // 2
    for first in (0, half):
        rows = slice(first, first + half)
        total_ref[rows, :] = dot(combined[rows, :], w_out[...])
        by_rows(first, half, 32, rows_of)


def out_norm(me, combined, w_out, tokens, vectors, after=()):
    n = tokens.shape[0]
    f = jnp.float32
    return call(
        out_norm_body,
        [near_shape((n, 768)), near_shape((n, 768), f), near_shape((n, LANES), f)],
        [me, combined, w_out, tokens, vectors],
        [pltpu.VMEM((n, 768), jnp.float32)],
        after=after,
        name="out_norm",
    )


def up_body(me, first_low, w_up, bias_up, activated, slope, send):
    width = w_up.shape[1] // 8
    for i in range(8):
        columns = slice(i * width, (i + 1) * width)
        hidden = dot(first_low[...], w_up[:, columns]) + bias_up[:, columns]
        half = 0.5 + 0.5 * lax.erf(hidden * (0.5**0.5))
        low = (hidden * half).astype(jnp.bfloat16)
        activated[:, columns] = low
        bell = jnp.exp(-0.5 * hidden * hidden) * (2.0 * math.pi) ** (-0.5)
        slope[:, columns] = (half + hidden * bell).astype(jnp.bfloat16)
    for i in range(8):
        k = me[0] ^ i

        @pl.when((k & 1) == 1)
        def _():
            there = pl.ds(pl.multiple_of((k >> 1) * width, LANES), width)
            send[:, there] = activated[:, i * width : (i + 1) * width]


def up(me, first_low, w_up, bias_up, after=()):
    n, width = first_low.shape[0], w_up.shape[1]
    return call(
        up_body,
        [near_shape((n, width)), near_shape((n, width)), shape_of((n, width // 2))],
        [me, first_low, w_up, bias_up],
        after=after,
        name="up",
    )


def down_norm_body(
    me, activated, turned, normal, vectors, out, feed_grad, second_grad, sums, feed, acc
):
    acc[...] = jnp.zeros_like(acc)

    def rows_of(rows):
        value = normal[rows, :] * vectors[3:4] + vectors[4:5] + feed[rows, :] + vectors[5:6]
        centred = value - mean(value)
        inverse = lax.rsqrt(mean(centred * centred) + epsilon)
        norm = centred * inverse
        out[rows, :] = (norm * vectors[6:7] + vectors[7:8]).astype(jnp.bfloat16)
        upstream = me.arrived(0)[rows, :]
        scaled = upstream * vectors[6:7]
        back = inverse * (scaled - mean(scaled) - norm * mean(scaled * norm))
        second_grad[rows, :] = back
        low = back.astype(jnp.bfloat16)
        feed_grad[rows, :] = low
        acc[0] += fold(low.astype(jnp.float32))
        acc[1] += fold(upstream * norm)
        acc[2] += fold(upstream)

    half = out.shape[0] // 2
    for first in (0, half):
        rows = slice(first, first + half)
        feed[rows, :] = dot_nt(activated[rows, :], turned[...])
        by_rows(first, half, 32, rows_of)
    me.send(0)
    for i in range(3):
        sums[i : i + 1, :] = jnp.sum(acc[i], axis=0, keepdims=True)


def down_norm(me, activated, turned, normal, vectors, cotangent, after=()):
    n = cotangent.shape[0]
    return call(
        down_norm_body,
        [
            shape_of((n, 768)),
            near_shape((n, 768)),
            near_shape((n, 768), jnp.float32),
            near_shape((3, 768), jnp.float32),
        ],
        [me, cotangent, activated, turned, normal, vectors],
        [pltpu.VMEM((n, 768), jnp.float32), pltpu.VMEM((3, 8, 768), jnp.float32)],
        late=[None],
        far_outs={0: True},
        after=after,
        name="down_norm",
    )


def hidden_back_body(me, feed_grad, turned, slope, hidden_grad, sums):
    for i in range(hidden_grad.shape[1] // 256):
        columns = slice(i * 256, (i + 1) * 256)
        value = dot(feed_grad[...], turned[:, columns]) * slope[:, columns].astype(jnp.float32)
        low = value.astype(jnp.bfloat16)
        hidden_grad[:, columns] = low
        sums[:, columns] = jnp.sum(low.astype(jnp.float32), axis=0, keepdims=True)


def hidden_back(me, feed_grad, turned, slope, after=()):
    return call(
        hidden_back_body,
        [near_shape(slope.shape), near_shape((1, slope.shape[1]), jnp.float32)],
        [me, feed_grad, turned, slope],
        after=after,
        name="hidden_back",
    )


def first_back_body(
    me, hidden_grad, w_up, second_grad, normal, inverse, vectors, residual, low_out, left, right, sums, back,
    acc,
):
    acc[...] = jnp.zeros_like(acc)

    def rows_of(rows):
        upstream = back[rows, :] + second_grad[rows, :]
        norm = normal[rows, :]
        scaled = upstream * vectors[3:4]
        value = inverse[rows, 0:1] * (scaled - mean(scaled) - norm * mean(scaled * norm))
        residual[rows, :] = value
        low = value.astype(jnp.bfloat16)
        low_out[rows, :] = low
        left[rows, :] = low[:, :384]
        right[rows, :] = low[:, 384:]
        acc[0] += fold(low.astype(jnp.float32))
        acc[1] += fold(upstream * norm)
        acc[2] += fold(upstream)

    half = normal.shape[0] // 2
    for first in (0, half):
        rows = slice(first, first + half)
        back[rows, :] = dot_nt(hidden_grad[rows, :], w_up[...])
        by_rows(first, half, 32, rows_of)
    for i in range(3):
        sums[i : i + 1, :] = jnp.sum(acc[i], axis=0, keepdims=True)


def first_back(me, hidden_grad, w_up, second_grad, normal, inverse, vectors, after=()):
    n = normal.shape[0]
    return call(
        first_back_body,
        [
            near_shape((n, 768), jnp.float32),
            near_shape((n, 768)),
            shape_of((n, 384)),
            shape_of((n, 384)),
            near_shape((3, 768), jnp.float32),
        ],
        [me, hidden_grad, w_up, second_grad, normal, inverse, vectors],
        [pltpu.VMEM((n, 768), jnp.float32), pltpu.VMEM((3, 8, 768), jnp.float32)],
        after=after,
        name="first_back",
    )


def attend_back_body(
    first_pair, pairs, me, attention_grad, w_out, order, swapped, values, soft, *refs
):
    grads, sums, upstream = refs[-3:]
    length = attention_grad.shape[0]
    groups = length // CLUSTER
    blocks = [slice(g * CLUSTER, (g + 1) * CLUSTER) for g in range(groups)]
    low = iota((length, LANES), 1) < 64
    low_rows = iota((CLUSTER, LANES), 1) < 64
    scale = HEAD_DIM ** (-0.5)
    mine = slice(first_pair * LANES, (first_pair + pairs) * LANES)
    upstream[...] = dot_nt(attention_grad[...], w_out[mine, :]).astype(jnp.bfloat16)

    for place in range(pairs):
        pair = first_pair + place

        def columns(base, pair=pair):
            return slice(base + pair * LANES, base + (pair + 1) * LANES)

        both = upstream[:, slice(place * LANES, (place + 1) * LANES)]
        to_tokens, moved = [], []
        for h in range(2):
            to_tokens.append(place_matrix(order, 2 * pair + h))
            value = dot_tn(to_tokens[h], both)
            value = jnp.where(low if h == 0 else jnp.logical_not(low), value, 0.0)
            moved.append(value.astype(jnp.bfloat16))
        back = []
        for h in range(2):
            kept = 2 * place + h
            keys = [swapped[kept, b, :] for b in blocks]
            weights = [soft[kept, b, :] for b in blocks]
            soft_grad = [dot_nt(moved[h][b], values[kept, b, :]) for b in blocks]
            value_grad = [
                dot_tn(weights[g].astype(jnp.bfloat16), moved[h][b]) for g, b in enumerate(blocks)
            ]
            score_grad = []
            for g in range(groups):
                middle = jnp.sum(soft_grad[g] * weights[g], axis=1, keepdims=True)
                score_grad.append((weights[g] * (soft_grad[g] - middle)).astype(jnp.bfloat16))
            query_grad = [dot(score_grad[g], keys[g]) for g in range(groups)]
            key_grad = [dot_tn(score_grad[g], keys[g]) for g in range(groups)]
            parts = [
                jnp.concatenate(
                    [
                        (jnp.where(low_rows, query_grad[g], key_grad[g]) * scale).astype(
                            jnp.bfloat16
                        ),
                        value_grad[g].astype(jnp.bfloat16),
                    ],
                    axis=1,
                )
                for g in range(groups)
            ]
            back.append(dot(to_tokens[h], jnp.concatenate(parts, axis=0)))
        first, second = back[0][:, :LANES], back[1][:, :LANES]
        query = jnp.where(low, first, pltpu.roll(second, 64, axis=1))
        keys = jnp.where(low, pltpu.roll(first, 64, axis=1), second)
        value = back[0][:, LANES:] + back[1][:, LANES:]
        grads[:, columns(0)] = query.astype(jnp.bfloat16)
        grads[:, columns(768)] = keys.astype(jnp.bfloat16)
        grads[:, columns(1536)] = value.astype(jnp.bfloat16)
        sums[0:1, columns(0)] = jnp.sum(query, axis=0, keepdims=True)
        sums[1:2, columns(0)] = jnp.sum(value, axis=0, keepdims=True)


def attend_back(
    me, attention_grad, w_out, order, kept, first_pair, pairs, before=(), after=()
):
    length = attention_grad.shape[0]
    return call(
        functools.partial(attend_back_body, first_pair, pairs),
        [near_shape((length, 2304)), near_shape((2, 768), jnp.float32)],
        [me, attention_grad, w_out, order, *kept, *before],
        [pltpu.VMEM((length, pairs * LANES), jnp.bfloat16)],
        after=after,
        aliases={6: 0, 7: 1} if before else None,
        name="attend_back",
    )


def tokens_back_body(me, grads, weights, residual, out):
    for c in range(3):
        columns = slice(c * 256, (c + 1) * 256)
        out[:, columns] = dot_nt(grads[...], weights[columns, :]) + residual[:, columns]
        me.send(0, (slice(None), columns))


def tokens_back(me, grads, weights, residual, after=()):
    return call(
        tokens_back_body,
        [shape_of(residual.shape, jnp.float32)],
        [me, grads, weights, residual],
        far_outs={0: True},
        sends=3,
        after=after,
        name="tokens_back",
    )


def local_block(
    tokens,
    w_qkv,
    bias_query,
    bias_value,
    w_out,
    bias_out,
    gain_one,
    shift_one,
    w_up,
    bias_up,
    w_down,
    bias_down,
    gain_two,
    shift_two,
    cluster_order,
    segment_ids,
    padding,
    cotangent,
):
    length = tokens.shape[0]
    me = None
    vector_list = [
        bias_query, bias_value, bias_out, gain_one, shift_one, bias_down, gain_two, shift_two
    ]
    order = cluster_order[0]
    facts = (segment_ids[0] + 32 * (1 - padding[0])).astype(jnp.float32)
    facts = jnp.broadcast_to(facts[:, None], (length, 128))

    def other(x):
        return swap(x, "dp", CORE)

    blocks_q = pack_q(me, w_qkv, vector_list, bias_up)
    far_z_q = swap(blocks_q[0], "mp", 2)
    blocks_rest = pack_rest(me, w_out, w_up, w_down, after=[blocks_q])
    block_ou, upper, lower, block_d = blocks_rest
    far_z_ou = swap(block_ou, "mp", 2)
    upper_x, lower_y = swap(upper, "dp", ALONG_X), swap(lower, "dp", ALONG_Y)
    tokens_turned = turn(me, tokens, after=[blocks_rest])
    spread = spread_d(me, block_d, upper_x, lower_y, after=[tokens_turned])
    upper, lower = spread
    upper_y, lower_x = swap(upper, "dp", ALONG_Y), swap(lower, "dp", ALONG_X)
    near_z_q = beside_two(
        me, blocks_q[1], far_z_q, after=[spread], cost=20 * MICROSECOND // 10
    )
    z_q = near_z_q[0], swap(near_z_q[0], "mp", 1)
    near_z_ou = beside_two(me, block_ou, far_z_ou, after=[near_z_q])
    z_ou = near_z_ou[0], swap(near_z_ou[0], "mp", 1)
    near_d = whole_d(me, upper, upper_y, lower, lower_x, after=[near_z_ou])
    z_q = tie(z_q, [near_d])
    near_q = [z_q[0], swap(z_q[0], "dp", ALONG_X), z_q[1], swap(z_q[1], "dp", ALONG_Y)]
    far_q = gather_far(me, near_q, after=[near_d])
    far_d = swap(near_d[0], "mp", 2)
    z_ou = tie(z_ou, [far_q])
    near_ou = [z_ou[0], swap(z_ou[0], "dp", ALONG_X), z_ou[1], swap(z_ou[1], "dp", ALONG_Y)]
    pairs_q = beside(
        me,
        [(x, (i // 2, i % 2)) for i, x in enumerate(far_q)],
        [(2, *far_q[0].shape)] * 2,
        (),
        "beside_far",
    )
    parts_q = list(pairs_q)
    parts_q = [*parts_q, *[other(x) for x in parts_q]]
    far_ou = gather_far(me, near_ou, after=[pairs_q], cost=5 * MICROSECOND // 10)
    both_d = beside_two(
        me, near_d[0], far_d, after=[far_ou], cost=82 * MICROSECOND // 10
    )
    z_d = swap(both_d[0], "mp", 1)
    projected = project(me, parts_q, tokens, after=[both_d])
    full_qkv, vectors, full_bias_up, qkv = projected

    pairs = PAIRS // 3

    def forward(part, before, after):
        return attend(
            me, qkv, order, facts, part * pairs, pairs, before, after=after
        )

    seen_a = forward(0, None, [projected])
    seen_b = forward(1, seen_a[-1], [seen_a])
    far_ou = tie(far_ou, [seen_b])
    seen_c = forward(2, seen_b[-1], far_ou[:1])
    combined = seen_c[-1]
    combined_turned = turn(me, combined)
    full_out, full_up = unpack_ou(me, gather_core(far_ou), after=[combined_turned])
    normed = out_norm(me, combined, full_out, tokens, vectors)
    first_low, normal, inverse = normed
    first_turned = turn(me, first_low)
    upper = up(me, first_low, full_up, full_bias_up, after=[first_turned])
    activated, slope, send_activated = upper
    sends = tie(
        [combined_turned[0], first_turned[0], send_activated, tokens_turned[0]], [upper]
    )
    others = [other(x) for x in sends]
    parts_d = tie([both_d[0], z_d], [upper])
    parts_d = [*parts_d, *[other(x) for x in parts_d]]
    unpacked = unpack_d(me, parts_d, after=[others[0], others[1], others[3]])
    turned_down = unpacked[0]
    downed = down_norm(me, activated, turned_down, normal, vectors, cotangent)
    layer_out, feed_grad, second_grad, sums_two = downed
    other_tokens = others[3]

    other_feed = other(feed_grad)
    hidden = hidden_back(me, feed_grad, turned_down, slope, after=[downed])
    hidden_grad, sums_up = hidden
    (hidden_grad,) = tie([hidden_grad], [hidden, other_feed, others[2]])
    other_hidden = other(hidden_grad)
    grad_d = gradient_d(
        me, feed_grad, other_feed, activated, others[2], after=[hidden]
    )
    core_d = scatter_near(grad_d)
    first = first_back(
        me, hidden_grad, full_up, second_grad, normal, inverse, vectors, after=[grad_d]
    )
    residual_grad, attention_grad, *halves, sums_one = first
    halves = [other(x) for x in halves]

    def back(part, kept, before, after):
        return attend_back(
            me, attention_grad, full_out, order, kept,
            part * pairs, pairs, before, after,
        )

    grads_a = back(0, seen_a[:3], (), [first])
    grads_b = back(1, seen_b[:3], grads_a, [])
    grads_c = back(2, seen_c[:3], grads_b, halves)
    half_d = add_plane(me, core_d, after=[grads_c])
    plane_d = scatter_far(half_d)
    projected_grad, sums_bias = grads_c
    grad_vectors = all_sums(me, sums_bias, sums_one, sums_two, sums_up)
    projected_grad, grad_vectors = tie([projected_grad, grad_vectors], [half_d])
    other_grads = other(projected_grad), other(grad_vectors)
    grad_ou = gradient_ou(
        me,
        (combined_turned[1], others[0]),
        (first_turned[1], others[1]),
        (hidden_grad, other_hidden),
        (attention_grad, *halves),
        after=[half_d],
    )
    core_ou = scatter_near(grad_ou)
    last_d = add_last(me, plane_d, after=[grad_ou], cost=22 * MICROSECOND)
    z_d = scatter_z(last_d)
    grad_q = gradient_q(
        me, tokens_turned[1], other_tokens, projected_grad, other_grads[0], grad_vectors,
        other_grads[1], after=[last_d],
    )
    near_q = grad_q[0], swap(grad_q[1], "mp", 1)
    moved = tokens_back(me, projected_grad, full_qkv, residual_grad, after=[grad_q])
    grad_tokens = moved[0]
    near_d = add_z(me, z_d, after=[moved])
    sum_d = scatter_z_far(near_d)
    half_ou = add_plane(me, core_ou, after=[near_d], cost=4 * MICROSECOND)
    plane_ou = scatter_far(half_ou)
    last_ou = add_last(me, plane_ou, after=[half_ou])
    z_ou = scatter_z(last_ou)
    first_q = add_first(me, *near_q, after=[last_ou])
    core_q = scatter_near(first_q)
    half_q = add_plane(me, core_q, after=[first_q])
    plane_q = scatter_far(half_q)
    near_ou = add_z(me, z_ou, after=[half_q])
    sum_ou = scatter_z_far(near_ou)
    done_d = finish_d(me, sum_d, after=[near_ou])
    sum_q = scatter_z_far(add_both(me, plane_q, after=[done_d]))
    done_ou = finish_ou(me, sum_ou)
    shard_out, shard_up = done_ou
    shard_qkv, *shard_vectors = finish_q(me, sum_q)
    shard_down = done_d[0].T
    grad_list = [v.reshape(-1) for v in shard_vectors]
    return (
        layer_out,
        grad_tokens,
        shard_qkv,
        grad_list[0],
        grad_list[1],
        shard_out,
        grad_list[2],
        grad_list[3],
        grad_list[4],
        shard_up,
        grad_list[8],
        shard_down,
        grad_list[5],
        grad_list[6],
        grad_list[7],
    )


def solution(mesh):
    in_specs = (
        P(("dp", "mp"), None),
        P("dp", "mp"),
        P(("dp", "mp")),
        P(("dp", "mp")),
        P("dp", "mp"),
        P(("dp", "mp")),
        P(("dp", "mp")),
        P(("dp", "mp")),
        P("dp", "mp"),
        P(("dp", "mp")),
        P("dp", "mp"),
        P(("dp", "mp")),
        P(("dp", "mp")),
        P(("dp", "mp")),
        P(("dp", "mp"), None, None),
        P(("dp", "mp"), None),
        P(("dp", "mp"), None),
        P(("dp", "mp"), None),
    )
    out_specs = (
        P(("dp", "mp"), None),
        P(("dp", "mp"), None),
        P("dp", "mp"),
        P(("dp", "mp")),
        P(("dp", "mp")),
        P("dp", "mp"),
        P(("dp", "mp")),
        P(("dp", "mp")),
        P(("dp", "mp")),
        P("dp", "mp"),
        P(("dp", "mp")),
        P("dp", "mp"),
        P(("dp", "mp")),
        P(("dp", "mp")),
        P(("dp", "mp")),
    )
    blocks = mesh.shape["dp"] == 8 and mesh.shape["mp"] == 4
    local = local_block if blocks else local_general
    return jax.shard_map(local, mesh=mesh, in_specs=in_specs, out_specs=out_specs, check_vma=False)
```

```python
import functools
import math

import jax
import jax.numpy as jnp
from jax import lax
from jax.experimental import pallas as pl
from jax.experimental.pallas import tpu as pltpu
from jax.sharding import PartitionSpec as P

HEADS = 12
HEAD_DIM = 64
CLUSTER = 128


epsilon = 1e-12
masked_score = -1e30


def product(left_side, right_side):
    return jnp.dot(left_side, right_side, preferred_element_type=jnp.float32)


def times_back(left_side, right_side):
    return lax.dot_general(
        left_side, right_side, (((1,), (1,)), ((), ())), preferred_element_type=jnp.float32
    )


def outer_sum(left_side, right_side):
    return lax.dot_general(
        left_side, right_side, (((0,), (0,)), ((), ())), preferred_element_type=jnp.float32
    )


def norm_forward(hidden, norm_gain, norm_shift):
    average = jnp.mean(hidden, axis=-1, keepdims=True)
    centred = hidden - average
    variance = jnp.mean(centred * centred, axis=-1, keepdims=True)
    inverse = lax.rsqrt(variance + epsilon)
    normal = centred * inverse
    return (normal * norm_gain + norm_shift, normal, inverse)


def norm_backward(upstream, normal, inverse, norm_gain):
    scaled = upstream * norm_gain
    return inverse * (
        scaled
        - jnp.mean(scaled, axis=-1, keepdims=True)
        - normal * jnp.mean(scaled * normal, axis=-1, keepdims=True)
    )


def gelu_exact(inputs):
    return jax.nn.gelu(inputs, approximate=False)


def local_general(
    tokens,
    w_qkv,
    bias_query,
    bias_value,
    w_out,
    bias_out,
    gain_one,
    shift_one,
    w_up,
    bias_up,
    w_down,
    bias_down,
    gain_two,
    shift_two,
    cluster_order,
    segment_ids,
    padding,
    cotangent,
):
    model_width = HEADS * HEAD_DIM
    length = tokens.shape[0]
    groups = length // CLUSTER
    score_scale = HEAD_DIM ** (-0.5)
    vectors = jnp.stack(
        [bias_query, bias_value, bias_out, gain_one, shift_one, bias_down, gain_two, shift_two]
    ).astype(jnp.bfloat16)
    vector_up = bias_up.astype(jnp.bfloat16)[None, :]
    part_qkv = w_qkv.astype(jnp.bfloat16)
    part_out = w_out.astype(jnp.bfloat16)
    part_up = w_up.astype(jnp.bfloat16)
    part_down = w_down.astype(jnp.bfloat16)
    column_qkv, column_out, column_up, column_down, column_vectors, column_bias = (
        lax.all_gather(part_qkv, "mp", axis=1, tiled=True),
        lax.all_gather(part_out, "mp", axis=1, tiled=True),
        lax.all_gather(part_up, "mp", axis=1, tiled=True),
        lax.all_gather(part_down, "mp", axis=1, tiled=True),
        lax.all_gather(vectors, "mp", axis=1, tiled=True),
        lax.all_gather(vector_up, "mp", axis=1, tiled=True),
    )
    full_qkv, full_out, full_up, full_down, full_vectors, full_bias = (
        lax.all_gather(column_qkv, "dp", axis=0, tiled=True),
        lax.all_gather(column_out, "dp", axis=0, tiled=True),
        lax.all_gather(column_up, "dp", axis=0, tiled=True),
        lax.all_gather(column_down, "dp", axis=0, tiled=True),
        lax.all_gather(column_vectors, "dp", axis=1, tiled=True),
        lax.all_gather(column_bias, "dp", axis=1, tiled=True),
    )
    small_params = full_vectors.astype(jnp.float32)
    hidden_bias = full_bias[0].astype(jnp.float32)
    ordering = cluster_order[0]
    segment = segment_ids[0]
    present = padding[0]
    positions = jnp.arange(length, dtype=jnp.int32)
    placement = (ordering[:, :, None] == positions[None, None, :]).astype(jnp.bfloat16)

    def to_clusters(matrix):
        per_head = matrix.reshape(length, HEADS, HEAD_DIM)
        moved = jnp.einsum("hip,phd->hid", placement, per_head, preferred_element_type=jnp.float32)
        return moved.astype(jnp.bfloat16).reshape(HEADS, groups, CLUSTER, HEAD_DIM)

    def from_clusters(blocks):
        per_head = blocks.astype(jnp.bfloat16).reshape(HEADS, length, HEAD_DIM)
        moved = jnp.einsum("hip,hid->phd", placement, per_head, preferred_element_type=jnp.float32)
        return moved.astype(jnp.bfloat16).reshape(length, model_width)

    segment_blocks = jnp.take(segment, ordering).reshape(HEADS, groups, CLUSTER)
    present_blocks = jnp.take(present, ordering).reshape(HEADS, groups, CLUSTER)
    same_doc = segment_blocks[..., :, None] == segment_blocks[..., None, :]
    itself = jnp.eye(CLUSTER, dtype=bool)
    allowed = same_doc & ((present_blocks[..., None, :] == 1) | itself)

    def scores_of(query_blocks, key_blocks):
        raw_scores = (
            jnp.einsum(
                "hncd,hnmd->hncm", query_blocks, key_blocks, preferred_element_type=jnp.float32
            )
            * score_scale
        )
        return jnp.where(allowed, raw_scores, masked_score)

    projected = product(tokens, full_qkv)
    query = (projected[:, :model_width] + small_params[0]).astype(jnp.bfloat16)
    keys = projected[:, model_width : 2 * model_width].astype(jnp.bfloat16)
    values = (projected[:, 2 * model_width :] + small_params[1]).astype(jnp.bfloat16)
    query_blocks = to_clusters(query)
    key_blocks = to_clusters(keys)
    value_blocks = to_clusters(values)
    masked = scores_of(query_blocks, key_blocks)
    highest = jnp.max(masked, axis=-1, keepdims=True)
    exponent = jnp.exp(masked - highest)
    row_total = jnp.sum(exponent, axis=-1, keepdims=True)
    soft_weights = exponent / row_total
    log_total = highest + jnp.log(row_total)
    soft_low = soft_weights.astype(jnp.bfloat16)
    combined = from_clusters(
        jnp.einsum("hncm,hnmd->hncd", soft_low, value_blocks, preferred_element_type=jnp.float32)
    )
    attention = product(combined, full_out) + small_params[2]
    first_norm, first_normal, first_inverse = norm_forward(
        tokens.astype(jnp.float32) + attention, small_params[3], small_params[4]
    )
    first_low = first_norm.astype(jnp.bfloat16)
    hidden = product(first_low, full_up) + hidden_bias
    activated, gelu_pull = jax.vjp(gelu_exact, hidden)
    activated_low = activated.astype(jnp.bfloat16)
    feed_out = product(activated_low, full_down) + small_params[5]
    output, second_normal, second_inverse = norm_forward(
        first_norm + feed_out, small_params[6], small_params[7]
    )
    layer_out = output.astype(jnp.bfloat16)
    again_qkv, again_out, again_up, again_down = (
        lax.all_gather(part_qkv, "mp", axis=1, tiled=True),
        lax.all_gather(part_out, "mp", axis=1, tiled=True),
        lax.all_gather(part_up, "mp", axis=1, tiled=True),
        lax.all_gather(part_down, "mp", axis=1, tiled=True),
    )
    back_qkv, back_out, back_up, back_down = (
        lax.all_gather(again_qkv, "dp", axis=0, tiled=True),
        lax.all_gather(again_out, "dp", axis=0, tiled=True),
        lax.all_gather(again_up, "dp", axis=0, tiled=True),
        lax.all_gather(again_down, "dp", axis=0, tiled=True),
    )
    grad_gain_two = jnp.sum(cotangent * second_normal, axis=0)
    grad_shift_two = jnp.sum(cotangent, axis=0)
    second_grad = norm_backward(cotangent, second_normal, second_inverse, small_params[6])
    feed_grad = second_grad.astype(jnp.bfloat16)
    grad_bias_down = jnp.sum(feed_grad.astype(jnp.float32), axis=0)
    grad_w_down = outer_sum(activated_low, feed_grad)
    hidden_grad = gelu_pull(times_back(feed_grad, back_down))[0].astype(jnp.bfloat16)
    grad_bias_up = jnp.sum(hidden_grad.astype(jnp.float32), axis=0)
    grad_w_up = outer_sum(first_low, hidden_grad)
    first_grad = times_back(hidden_grad, back_up) + second_grad
    grad_gain_one = jnp.sum(first_grad * first_normal, axis=0)
    grad_shift_one = jnp.sum(first_grad, axis=0)
    residual_grad = norm_backward(first_grad, first_normal, first_inverse, small_params[3])
    attention_grad = residual_grad.astype(jnp.bfloat16)
    grad_bias_out = jnp.sum(attention_grad.astype(jnp.float32), axis=0)
    grad_w_out = outer_sum(combined, attention_grad)
    combined_grad = to_clusters(times_back(attention_grad, back_out).astype(jnp.bfloat16))
    masked_again = scores_of(query_blocks, key_blocks)
    soft_again = jnp.exp(masked_again - log_total)
    soft_again_low = soft_again.astype(jnp.bfloat16)
    value_sums = jnp.einsum(
        "hncm,hncd->hnmd", soft_again_low, combined_grad, preferred_element_type=jnp.float32
    )
    soft_grad = jnp.einsum(
        "hncd,hnmd->hncm", combined_grad, value_blocks, preferred_element_type=jnp.float32
    )
    score_grad = (
        soft_again * (soft_grad - jnp.sum(soft_grad * soft_again, axis=-1, keepdims=True))
    ).astype(jnp.bfloat16)
    query_sums = (
        jnp.einsum("hncm,hnmd->hncd", score_grad, key_blocks, preferred_element_type=jnp.float32)
        * score_scale
    )
    key_sums = (
        jnp.einsum("hncm,hncd->hnmd", score_grad, query_blocks, preferred_element_type=jnp.float32)
        * score_scale
    )
    query_grad = from_clusters(query_sums)
    key_grad = from_clusters(key_sums)
    value_grad = from_clusters(value_sums)
    grad_bias_query = jnp.sum(query_grad.astype(jnp.float32), axis=0)
    grad_bias_value = jnp.sum(value_grad.astype(jnp.float32), axis=0)
    projected_grad = jnp.concatenate([query_grad, key_grad, value_grad], axis=1)
    grad_w_qkv = outer_sum(tokens, projected_grad)
    grad_tokens = times_back(projected_grad, back_qkv) + residual_grad
    grad_vectors = jnp.stack(
        [
            grad_bias_query,
            grad_bias_value,
            grad_bias_out,
            grad_gain_one,
            grad_shift_one,
            grad_bias_down,
            grad_gain_two,
            grad_shift_two,
        ]
    )
    grad_up_row = grad_bias_up[None, :]
    row_qkv, row_out, row_up, row_down, row_vectors, row_bias = (
        lax.psum_scatter(
            grad_w_qkv.astype(jnp.bfloat16), "dp", scatter_dimension=0, tiled=True
        ).astype(jnp.float32),
        lax.psum_scatter(
            grad_w_out.astype(jnp.bfloat16), "dp", scatter_dimension=0, tiled=True
        ).astype(jnp.float32),
        lax.psum_scatter(
            grad_w_up.astype(jnp.bfloat16), "dp", scatter_dimension=0, tiled=True
        ).astype(jnp.float32),
        lax.psum_scatter(
            grad_w_down.astype(jnp.bfloat16), "dp", scatter_dimension=0, tiled=True
        ).astype(jnp.float32),
        lax.psum_scatter(
            grad_vectors.astype(jnp.bfloat16), "dp", scatter_dimension=1, tiled=True
        ).astype(jnp.float32),
        lax.psum_scatter(
            grad_up_row.astype(jnp.bfloat16), "dp", scatter_dimension=1, tiled=True
        ).astype(jnp.float32),
    )
    shard_qkv, shard_out, shard_up, shard_down, shard_vectors, shard_bias = (
        lax.psum_scatter(
            row_qkv.astype(jnp.bfloat16), "mp", scatter_dimension=1, tiled=True
        ).astype(jnp.float32),
        lax.psum_scatter(
            row_out.astype(jnp.bfloat16), "mp", scatter_dimension=1, tiled=True
        ).astype(jnp.float32),
        lax.psum_scatter(row_up.astype(jnp.bfloat16), "mp", scatter_dimension=1, tiled=True).astype(
            jnp.float32
        ),
        lax.psum_scatter(
            row_down.astype(jnp.bfloat16), "mp", scatter_dimension=1, tiled=True
        ).astype(jnp.float32),
        lax.psum_scatter(
            row_vectors.astype(jnp.bfloat16), "mp", scatter_dimension=1, tiled=True
        ).astype(jnp.float32),
        lax.psum_scatter(
            row_bias.astype(jnp.bfloat16), "mp", scatter_dimension=1, tiled=True
        ).astype(jnp.float32),
    )
    return (
        layer_out,
        grad_tokens,
        shard_qkv,
        shard_vectors[0],
        shard_vectors[1],
        shard_out,
        shard_vectors[2],
        shard_vectors[3],
        shard_vectors[4],
        shard_up,
        shard_bias[0],
        shard_down,
        shard_vectors[5],
        shard_vectors[6],
        shard_vectors[7],
    )


LANES = 128
QKV_ROWS = 96
UP_TILES = 6
DOWN_TILES = 3
PACK_Q = 4 * QKV_ROWS + QKV_ROWS // 2 + 16
PACK_OU = QKV_ROWS + QKV_ROWS // 2 + UP_TILES * QKV_ROWS
PACK_D = DOWN_TILES * 192
VECTOR_ROW = 4 * QKV_ROWS + QKV_ROWS // 2
UP_ROW = QKV_ROWS + QKV_ROWS // 2


def whole():
    return pl.BlockSpec(memory_space=pltpu.VMEM)


def far():
    return pl.BlockSpec(memory_space=pltpu.HBM)


def kept_far(arrays):
    return [pltpu.with_memory_space_constraint(x, pltpu.HBM) for x in arrays]


def near(x):
    return pltpu.with_memory_space_constraint(x, pltpu.VMEM)


def near_shape(shape, dtype=jnp.bfloat16):
    return pltpu.VMEM(shape, dtype)


def waited(after):
    return [kept_far([x.token])[0] if isinstance(x, Results) else x for x in after]


def anywhere(after):
    return [far() if isinstance(x, Results) else pl.BlockSpec(memory_space=pl.ANY) for x in after]


class Results(list):
    token = None


TOKEN = pltpu.HBM((8, 128), jnp.float32)


def place():
    return lax.axis_index("dp"), lax.axis_index("mp")


SHORT = pl.CostEstimate(flops=1, bytes_accessed=1, transcendentals=0)
MICROSECOND = 1_153_000_000


class Place(tuple):
    def arrived(self, index, part=None):
        copies, here = self.late[index]
        for i in range(len(copies)) if part is None else [part]:
            if copies[i] is not None:
                copies[i].wait()
                copies[i] = None
        return here

    def send(self, index, where=None, source=None):
        here, there = self.far[index]
        source = here if source is None else source
        if where is not None:
            source, there = source.at[where], there.at[where]
        copy = pltpu.make_async_copy(source, there, self.sems.at[len(self.sent)])
        copy.start()
        self.sent.append(copy)


def call(
    body, out_shapes, operands, scratch=(), staged=0, late=(), far_outs=None, sends=None, after=(),
    aliases=None, vmem=10, cost=0, name=None,
):
    operands = operands[1:]
    far_outs = far_outs or {}
    sends = len(far_outs) if sends is None else sends
    count, outs, copied = len(operands), len(out_shapes), staged + len(late)
    spread = [(0, 1)] * staged + [x or (0, 1) for x in late]
    starts = [sum(n for _, n in spread[:i]) for i in range(copied)]

    def with_copies(*refs):
        sources, rest = refs[:copied], refs[copied:count]
        results = list(refs[count + len(after) : count + len(after) + outs])
        own = refs[count + len(after) + outs + 1 :]
        mine, own = own[: len(scratch)], own[len(scratch) :]
        arrived, own = own[:copied], list(own[copied:])
        me = Place(place())
        me.sent, me.far = [], {}
        if copied:
            sem = own.pop(0)
            copies = []
            for source, here, (axis, parts), start in zip(sources, arrived, spread, starts):
                size = here.shape[axis] // parts
                copies.append([])
                for i in range(parts):
                    cut = (slice(None),) * axis + (slice(i * size, (i + 1) * size),)
                    copies[-1].append(
                        pltpu.make_async_copy(source.at[cut], here.at[cut], sem.at[start + i])
                    )
            for copy in sum(copies, []):
                copy.start()
            for (copy,) in copies[:staged]:
                copy.wait()
            me.late = list(zip(copies[staged:], arrived[staged:]))
        if far_outs:
            me.sems = own.pop(0)
            for index, has_room in far_outs.items():
                here = own.pop(0) if has_room else None
                me.far[index] = (here, results[index])
                results[index] = here
        body(me, *arrived[:staged], *rest, *results, *mine)
        for copy in me.sent:
            copy.wait()

    room = [pltpu.VMEM(x.shape, x.dtype) for x in operands[:copied]]
    if copied:
        room.append(pltpu.SemaphoreType.DMA((sum(n for _, n in spread),)))
    if far_outs:
        room.append(pltpu.SemaphoreType.DMA((sends,)))
        room += [pltpu.VMEM(out_shapes[i].shape, out_shapes[i].dtype) for i in far_outs if far_outs[i]]
    given = [
        pltpu.HBM(x.shape, x.dtype) if i in far_outs else x for i, x in enumerate(out_shapes)
    ]
    *results, token = pl.pallas_call(
        with_copies,
        out_shape=[*given, TOKEN],
        in_specs=[pl.BlockSpec(memory_space=pl.ANY)] * staged
        + [far()] * len(late)
        + [whole()] * (count - copied)
        + anywhere(after),
        out_specs=[far() if i in far_outs else whole() for i in range(outs)] + [far()],
        scratch_shapes=list(scratch) + room,
        input_output_aliases=aliases or {},
        compiler_params=pltpu.CompilerParams(vmem_limit_bytes=vmem * 1024 * 1024),
        cost_estimate=SHORT if not cost else pl.CostEstimate(cost, 1, 0),
        name=name,
    )(
        *operands[:staged],
        *kept_far(operands[staged:copied]),
        *operands[copied:],
        *waited(after),
    )
    results = Results(results)
    results.token = token
    return results


def tie(arrays, after):
    count = len(arrays)

    def body(*refs):
        pass

    return pl.pallas_call(
        body,
        out_shape=[shape_of(x.shape, x.dtype) for x in arrays],
        in_specs=[pl.BlockSpec(memory_space=pl.ANY)] * count + anywhere(after),
        out_specs=[pl.BlockSpec(memory_space=pl.ANY)] * count,
        input_output_aliases={i: i for i in range(count)},
        compiler_params=pltpu.CompilerParams(vmem_limit_bytes=1024 * 1024),
        cost_estimate=SHORT,
        name="tie",
    )(*arrays, *waited(after))


def shape_of(shape, dtype=jnp.bfloat16):
    return jax.ShapeDtypeStruct(shape, dtype)


def halves_beside(single):
    half = single.shape[0] // 2
    return jnp.concatenate([single[:half], single[half:]], axis=1)


def pack_columns(odd, low, tiles, base, target):
    @pl.when(odd)
    def _():
        for t in range(tiles):
            target[base + t * 96 : base + (t + 1) * 96, :] = low[
                :, 64 + t * LANES : 64 + (t + 1) * LANES
            ].astype(jnp.bfloat16)
        target[base + tiles * 96 : base + tiles * 96 + 48, :] = halves_beside(low[:, :64]).astype(
            jnp.bfloat16
        )

    @pl.when(jnp.logical_not(odd))
    def _():
        for t in range(tiles):
            target[base + t * 96 : base + (t + 1) * 96, :] = low[
                :, t * LANES : (t + 1) * LANES
            ].astype(jnp.bfloat16)
        target[base + tiles * 96 : base + tiles * 96 + 48, :] = halves_beside(
            low[:, tiles * LANES : tiles * LANES + 64]
        ).astype(jnp.bfloat16)


def pack_q_body(me, *refs):
    w_qkv, vectors, target, own = refs[0], refs[1:10], refs[10], refs[11]
    pack_columns(lax.rem(me[1], 2) == 1, w_qkv[...], 4, 0, target)
    rows = lax.broadcasted_iota(jnp.int32, (16, LANES), 0)
    tail = jnp.zeros((16, LANES), jnp.float32)
    for v in range(9):
        value = vectors[v][...]
        wide = jnp.concatenate(
            [value, jnp.zeros((1, LANES - value.shape[1]), jnp.float32)], axis=1
        )
        tail = jnp.where(rows == v, jnp.broadcast_to(wide, (16, LANES)), tail)
    target[VECTOR_ROW:, :] = tail.astype(jnp.bfloat16)
    me.send(0)
    own[...] = target[...]


def pack_q(me, w_qkv, vectors, bias_up):
    small = [v.reshape(1, -1) for v in (*vectors, bias_up)]
    return call(
        pack_q_body, [shape_of((PACK_Q, LANES))] * 2, [me, *kept_far([w_qkv, *small])], staged=10, far_outs={0: True},
        name="pack_q",
    )


def pack_rest_body(me, w_out, w_up, w_down, to_ou, upper_d, lower_d, to_d):
    for t in range(DOWN_TILES):
        to_d[t * 192 : (t + 1) * 192, :] = w_down[:, t * LANES : (t + 1) * LANES].astype(
            jnp.bfloat16
        )
    upper_d[...] = to_d[: PACK_D // 2, :]
    lower_d[...] = to_d[PACK_D // 2 :, :]
    me.send(1)
    me.send(2)
    pack_columns(lax.rem(me[1], 2) == 1, w_out[...], 1, 0, to_ou)
    for t in range(UP_TILES):
        to_ou[UP_ROW + t * 96 : UP_ROW + (t + 1) * 96, :] = w_up[
            :, t * LANES : (t + 1) * LANES
        ].astype(jnp.bfloat16)


def pack_rest(me, w_out, w_up, w_down, after):
    return call(
        pack_rest_body,
        [
            near_shape((PACK_OU, LANES)),
            shape_of((PACK_D // 2, LANES)),
            shape_of((PACK_D // 2, LANES)),
            near_shape((PACK_D, LANES)),
        ],
        [me, *kept_far([w_out, w_up, w_down.T])],
        staged=3,
        far_outs={1: True, 2: True},
        after=after,
        name="pack_rest",
    )


def swap(x, axis, bit):
    size = lax.axis_size(axis)
    return lax.ppermute(x, axis, [(i, i ^ bit) for i in range(size)])


CORE, ALONG_X, ALONG_Y = 1, 2, 4


def gather_z(x, own=None):
    return [x if own is None else own] + [swap(x, "mp", k) for k in (1, 2, 3)]


def beside(me, groups, shapes, after=(), name="beside", cost=0):
    sources = []
    for x, _ in groups:
        if all(x is not y for y in sources):
            sources.append(x)

    def body(me, *refs):
        for x, (index, where) in groups:
            source = refs[next(n for n, y in enumerate(sources) if x is y)]
            refs[len(sources) + index][where] = source[...]

    return call(body, [shape_of(s) for s in shapes], [me, *sources], after=after, name=name, cost=cost)


def beside_two(me, a, b, after=(), cost=0):
    return beside(me, [(a, (0, 0)), (b, (0, 1))], [(2, *a.shape)], after, "beside_two", cost)


def gather_near(me, parts, after=()):
    shape = (2, *parts[0].shape)
    found = beside(
        me,
        [(parts[0], (0, 0)), (parts[1], (0, 1)), (parts[2], (1, 0)), (parts[3], (1, 1))],
        [shape, shape],
        after,
        "beside_z",
    )
    first, second = found
    result = Results([first, swap(first, "dp", ALONG_X), second, swap(second, "dp", ALONG_Y)])
    result.token = found.token
    return result


def gather_far(me, parts, after=(), cost=0):
    shape = (2, *parts[0].shape)
    groups = [(parts[i], (i // 2, i % 2)) for i in range(4)]
    found = beside(me, groups, [shape, shape], after, "beside_near", cost)
    first, second = found
    result = Results([first, second, swap(first, "dp", ALONG_Y), swap(second, "dp", ALONG_X)])
    result.token = found.token
    return result


def gather_core(parts):
    return list(parts) + [swap(x, "dp", CORE) for x in parts]


def gathered_blocks(me, refs, steps=(1, 2)):
    for index, ref in enumerate(refs):
        core, far, half = index // 4, index % 4 // 2, index % 2
        for mid in range(2):
            for low in range(2):
                kx, ky = (far, mid) if half else (mid, far)
                along_z = steps[0] * low + steps[1] * half
                yield me[0] ^ (core + 2 * kx + 4 * ky), me[1] ^ along_z, ref.at[mid, low]


def split_pairs(refs):
    return [ref.at[i] for ref in refs for i in range(2)]


def place_columns(block, base, tiles, dp, mp, width, weights, singles):
    start = pl.multiple_of(mp * width + 64 * lax.rem(mp, 2), LANES)
    rows = pl.ds(pl.multiple_of(dp * 96, 32), 96)
    for t in range(tiles):
        weights[rows, pl.ds(pl.multiple_of(start + t * LANES, LANES), LANES)] = block[
            base + t * 96 : base + (t + 1) * 96, :
        ]
    singles[mp, pl.ds(pl.multiple_of(dp * 48, 16), 48), :] = block[
        base + tiles * 96 : base + tiles * 96 + 48, :
    ]


def place_singles(width, weights, singles):
    for pair in range(2):
        column = 2 * pair * width + (width // LANES) * LANES
        for dp in range(8):
            left = singles[2 * pair, dp * 48 : (dp + 1) * 48, :].astype(jnp.float32)
            right = singles[2 * pair + 1, dp * 48 : (dp + 1) * 48, :].astype(jnp.float32)
            upper = jnp.concatenate([left[:, :64], right[:, :64]], axis=1)
            lower = jnp.concatenate([left[:, 64:], right[:, 64:]], axis=1)
            weights[dp * 96 : dp * 96 + 48, column : column + LANES] = upper.astype(jnp.bfloat16)
            weights[dp * 96 + 48 : (dp + 1) * 96, column : column + LANES] = lower.astype(
                jnp.bfloat16
            )


def unpack_q_body(me, *refs):
    blocks, weights, vectors, bias_up, singles, tails = refs[:8], *refs[8:]
    for dp, mp, block in gathered_blocks(me, blocks, (2, 1)):
        place_columns(block, 0, 4, dp, mp, 576, weights, singles)
        tails[dp * 4 + mp] = block[VECTOR_ROW:, :].astype(jnp.float32)
    place_singles(576, weights, singles)
    lane = lax.broadcasted_iota(jnp.int32, (16, LANES), 1)

    def spread(width, count):
        found = [jnp.zeros((16, LANES), jnp.float32) for _ in range(count)]
        for device in range(32):
            start, tile = device * width % LANES, device * width // LANES
            piece = tails[device]
            moved = pltpu.roll(piece, start, axis=1) if start else piece
            found[tile] = jnp.where((lane >= start) & (lane < start + width), moved, found[tile])
            if start + width > LANES:
                found[tile + 1] = jnp.where(lane < start + width - LANES, moved, found[tile + 1])
        return found

    for t, value in enumerate(spread(24, 6)):
        vectors[:, t * LANES : (t + 1) * LANES] = value[:8]
    for t, value in enumerate(spread(96, 24)):
        bias_up[:, t * LANES : (t + 1) * LANES] = value[8:9]


def unpack_ou_body(me, *refs):
    blocks, w_out, w_up, singles = refs[:8], *refs[8:]
    for dp, mp, block in gathered_blocks(me, blocks, (2, 1)):
        place_columns(block, 0, 1, dp, mp, 192, w_out, singles)
        rows = pl.ds(pl.multiple_of(dp * 96, 32), 96)
        for t in range(UP_TILES):
            w_up[rows, pl.ds(pl.multiple_of(mp * 768 + t * LANES, LANES), LANES)] = block[
                UP_ROW + t * 96 : UP_ROW + (t + 1) * 96, :
            ]
    place_singles(192, w_out, singles)


def unpack_ou(me, parts, after=()):
    return call(
        unpack_ou_body,
        [near_shape((768, 768)), near_shape((768, 3072))],
        [me, *parts],
        [pltpu.VMEM((4, 384, LANES), jnp.bfloat16)],
        after=after,
        name="unpack_ou",
    )


def spread_d_body(me, mine, upper_x, lower_y, upper, lower):
    half = PACK_D // 2
    upper[0], upper[1] = mine[:half, :], upper_x[...]
    lower[0], lower[1] = mine[half:, :], lower_y[...]


def spread_d(me, mine, upper_x, lower_y, after=()):
    shape = near_shape((2, PACK_D // 2, LANES))
    return call(
        spread_d_body, [shape, shape], [me, mine, upper_x, lower_y], after=after, name="spread_d"
    )


def whole_d_body(me, upper, upper_y, lower, lower_x, out):
    half = PACK_D // 2
    for kx in range(2):
        for ky in range(2):
            out[2 * ky + kx, :half, :] = (upper_y if ky else upper)[kx]
            out[2 * ky + kx, half:, :] = (lower_x if kx else lower)[ky]


def whole_d(me, upper, upper_y, lower, lower_x, after=()):
    return call(
        whole_d_body, [near_shape((4, PACK_D, LANES))], [me, upper, upper_y, lower, lower_x],
        after=after, name="whole_d",
    )


def unpack_d_body(me, both, both_z, other, other_far, other_z, turned):
    for core in range(2):
        for kz in range(4):
            for plane in range(4):
                if core and kz % 2 == 0:
                    block = (other_far if kz else other).at[plane]
                else:
                    source = (other_z if core else both_z) if kz % 2 else both
                    block = source.at[kz // 2, plane]
                dp, mp = me[0] ^ (2 * plane + core), me[1] ^ kz
                rows = pl.ds(pl.multiple_of(mp * 192, 64), 192)
                for t in range(DOWN_TILES):
                    turned[rows, pl.ds(pl.multiple_of(dp * 384 + t * LANES, LANES), LANES)] = block[
                        t * 192 : (t + 1) * 192, :
                    ]


def unpack_d(me, parts, after=()):
    return call(
        unpack_d_body, [near_shape((768, 3072))], [me, *parts], after=after, name="unpack_d"
    )


def turn_body(me, source, send, keep, turned):
    value = source[...].T
    for dp in range(8):
        k = me[0] ^ dp
        slot = (1 - (k & 1)) * 4 + (k >> 1)
        turned[pl.ds(pl.multiple_of(slot * 96, 32), 96), :] = value[dp * 96 : (dp + 1) * 96, :]
    send[...] = turned[:384, :]
    keep[...] = turned[384:, :]


def turn(me, source, after=()):
    n = source.shape[0]
    return call(
        turn_body,
        [shape_of((384, n)), near_shape((384, n))],
        [me, source],
        [pltpu.VMEM((768, n), jnp.bfloat16)],
        after=after,
        name="turn",
    )


def dot(a, b):
    return jnp.dot(a, b, preferred_element_type=jnp.float32)


def dot_nt(a, b):
    return lax.dot_general(a, b, (((1,), (1,)), ((), ())), preferred_element_type=jnp.float32)


def dot_tn(a, b):
    return lax.dot_general(a, b, (((0,), (0,)), ((), ())), preferred_element_type=jnp.float32)


def part_of(targets, kp, mp):
    ky, kx = kp // 2, kp % 2
    if mp < 2:
        return targets[ky].at[kx, mp]
    return targets[2 + kx].at[ky, mp - 2]


def store_columns(target, base, tiles, first, value):
    for t in range(tiles):
        target[base + t * 96 : base + (t + 1) * 96, :] = value[
            :, first + t * LANES : first + (t + 1) * LANES
        ].astype(jnp.bfloat16)


def store_single(target, base, odd, value):
    upper, lower = value[:48], value[48:]
    low_lanes = lax.broadcasted_iota(jnp.int32, (48, LANES), 1) < 64
    if odd:
        both = jnp.where(low_lanes, pltpu.roll(upper, 64, axis=1), lower)
    else:
        both = jnp.where(low_lanes, upper, pltpu.roll(lower, 64, axis=1))
    target[base : base + 48, :] = both.astype(jnp.bfloat16)


def column_gradient(lefts, rights, targets, base, tiles, width):
    def product(columns):
        return dot(lefts[0], rights[0][:, columns]) + dot(lefts[1], rights[1][:, columns])

    for pair in range(2):
        first = 2 * pair * width
        middle = first + tiles * LANES
        for begin, mp in ((first, 2 * pair), (middle + LANES, 2 * pair + 1)):
            value = product(slice(begin, begin + tiles * LANES))
            for kp in range(4):
                store_columns(
                    targets(kp, mp), base, tiles, 0, value[kp * 96 : (kp + 1) * 96]
                )
        value = product(slice(middle, middle + LANES))
        for kp in range(4):
            for mp in (2 * pair, 2 * pair + 1):
                store_single(
                    targets(kp, mp), base + tiles * 96, mp % 2,
                    value[kp * 96 : (kp + 1) * 96],
                )


def parts_shape(rows):
    return [near_shape((2, 2, rows, LANES)), shape_of((2, 2, rows, LANES))] * 2


def gradient_q_body(
    me, keep, other_keep, grads, other_grads, vectors, other_vectors, mine, send, room
):
    targets = lambda kp, mp: room.at[me[1] ^ mp, kp]
    lefts, rights = (keep[...], other_keep[...]), (grads, other_grads)
    column_gradient(lefts, rights, targets, 0, 4, 576)
    sums = vectors[...] + other_vectors[...]
    lane = lax.broadcasted_iota(jnp.int32, (16, LANES), 1)
    rows = lax.broadcasted_iota(jnp.int32, (16, LANES), 0)

    def cut(source, width, device):
        start, tile = device * width % LANES, device * width // LANES
        value = source[:, tile * LANES : (tile + 1) * LANES]
        moved = pltpu.roll(value, LANES - start, axis=1) if start else value
        if start + width > LANES:
            after = source[:, (tile + 1) * LANES : (tile + 2) * LANES]
            after = pltpu.roll(after, LANES - start, axis=1)
            here = lax.broadcasted_iota(jnp.int32, value.shape, 1)
            moved = jnp.where(here < LANES - start, moved, after)
        return moved

    for kp in range(4):
        plane = (me[0] >> 1) ^ kp
        for mp in range(4):
            tail = jnp.zeros((16, LANES), jnp.float32)
            for dp in range(8):
                device = dp * 4 + mp
                row = 8 + device // 8
                up = jnp.broadcast_to(cut(sums[row : row + 1], 96, device % 8), (8, LANES))
                found = jnp.concatenate([cut(sums[:8], 24, device), up], axis=0)
                owner = dp == 2 * plane + (me[0] & 1)
                tail = jnp.where(owner, found, tail)
            tail = jnp.where((rows < 8) & (lane >= 24), 0.0, tail).astype(jnp.bfloat16)
            targets(kp, mp)[VECTOR_ROW:, :] = tail
    for kz in range(4):
        (send if kz % 2 else mine)[kz // 2] = room[kz]


def gradient_q(me, keep, other_keep, grads, other_grads, vectors, other_vectors, after=()):
    return call(
        gradient_q_body,
        [near_shape((2, 4, PACK_Q, LANES)), shape_of((2, 4, PACK_Q, LANES))],
        [me, keep, other_keep, grads, other_grads, vectors, other_vectors],
        [pltpu.VMEM((4, 4, PACK_Q, LANES), jnp.bfloat16)],
        after=after,
        name="gradient_q",
    )


def gradient_ou_body(me, *refs):
    combined, first_low, hidden_grad = (refs[i : i + 2] for i in (0, 2, 4))
    attention_grad, room = (refs[6], refs[13]), refs[13]
    targets = functools.partial(part_of, refs[9:13])
    room[:, :384] = refs[7][...]
    room[:, 384:] = refs[8][...]
    column_gradient([x[...] for x in combined], attention_grad, targets, 0, 1, 192)
    lefts = [x[...] for x in first_low]
    for mp in range(4):
        columns = slice(mp * 768, (mp + 1) * 768)
        value = dot(lefts[0], hidden_grad[0][:, columns])
        value = value + dot(lefts[1], hidden_grad[1][:, columns])
        for kp in range(4):
            store_columns(
                targets(kp, mp), UP_ROW, UP_TILES, 0, value[kp * 96 : (kp + 1) * 96]
            )


def gradient_ou(me, combined, first_low, hidden_grad, attention_grad, after=()):
    return call(
        gradient_ou_body,
        parts_shape(PACK_OU),
        [me, *combined, *first_low, *hidden_grad, *attention_grad],
        [pltpu.VMEM(attention_grad[0].shape, jnp.bfloat16)],
        after=after,
        name="gradient_ou",
    )


def gradient_d_body(me, feed_grad, other_feed_grad, activated, other_activated, *refs):
    targets, turned, other_turned = refs[:4], refs[4], refs[5]
    turned[...] = feed_grad[...].T
    other_turned[...] = other_feed_grad[...].T
    for kp in range(4):
        dp = me[0] ^ (2 * kp)
        block = activated[:, pl.ds(pl.multiple_of(dp * 384, LANES), 384)]
        value = dot(turned[...], block)
        value = value + dot(other_turned[...], other_activated[:, kp * 384 : (kp + 1) * 384])
        for mp in range(4):
            target = part_of(targets, kp, mp)
            for t in range(DOWN_TILES):
                target[t * 192 : (t + 1) * 192, :] = value[
                    mp * 192 : (mp + 1) * 192, t * LANES : (t + 1) * LANES
                ].astype(jnp.bfloat16)


def gradient_d(me, feed_grad, other_feed_grad, activated, other_activated, after=()):
    return call(
        gradient_d_body,
        parts_shape(PACK_D),
        [me, feed_grad, other_feed_grad, activated, other_activated],
        [pltpu.VMEM((768, feed_grad.shape[0]), jnp.bfloat16)] * 2,
        after=after,
        name="gradient_d",
    )


def sums_body(me, bias, one, two, up, out):
    out[0:2, :], out[2:5, :], out[5:8, :] = bias[...], one[...], two[...]
    for i in range(4):
        out[8 + i : 9 + i, :] = up[:, i * 768 : (i + 1) * 768]


def all_sums(me, *sums):
    return call(sums_body, [shape_of((12, 768), jnp.float32)], [me, *sums], name="sums")[0]


def add(a, b):
    return a.astype(jnp.float32) + b.astype(jnp.float32)


def add_plane_body(me, first, first_in, second, second_in, *outs):
    for keep, send, a, b in ((*outs[:2], first, first_in), (*outs[2:], second, second_in)):
        keep[...] = add(a[0], b[0]).astype(jnp.bfloat16)
        send[...] = add(a[1], b[1]).astype(jnp.bfloat16)


def add_last_body(me, first, first_in, second, second_in, *refs):
    keep, send, room = refs
    for mp in range(4):
        a, b = (first, first_in) if mp < 2 else (second, second_in)
        room[me[1] ^ mp] = add(a[mp % 2], b[mp % 2]).astype(jnp.bfloat16)
    for k in range(4):
        (send if k % 2 else keep)[k // 2] = room[k]


def add_first_body(me, mine, arrived, *outs):
    for kp in range(4):
        ky, kx = kp // 2, kp % 2
        outs[ky][kx] = add(mine[0, kp], arrived[0, kp]).astype(jnp.bfloat16)
        outs[2 + kx][ky] = add(mine[1, kp], arrived[1, kp]).astype(jnp.bfloat16)


def add_first(me, mine, arrived, after=()):
    rows = mine.shape[2]
    return call(
        add_first_body,
        [near_shape((2, rows, LANES)), shape_of((2, rows, LANES))] * 2,
        [me, mine, arrived],
        after=after,
        name="add_first",
    )


def add_both_body(me, first, first_in, second, second_in, keep, send):
    keep[...] = add(first[...], first_in[...])
    send[...] = add(second[...], second_in[...]).astype(jnp.bfloat16)


def add_both(me, parts, after=()):
    shape = parts[0].shape
    return call(
        add_both_body,
        [near_shape(shape, jnp.float32), shape_of(shape)],
        [me, *parts],
        after=after,
        name="add_both",
    )


def add_z_body(me, mine, arrived, keep, send):
    keep[...] = add(mine[0], arrived[0])
    send[...] = add(mine[1], arrived[1]).astype(jnp.bfloat16)


def scatter_near(parts):
    first, first_send, second, second_send = parts
    return first, swap(first_send, "dp", ALONG_Y), second, swap(second_send, "dp", ALONG_X)


def add_plane(me, parts, after=(), cost=0):
    shape = parts[0].shape[1:]
    return call(
        add_plane_body,
        [near_shape(shape), shape_of(shape)] * 2,
        [me, *parts],
        after=after,
        cost=cost,
        name="add_plane",
    )


def scatter_far(parts):
    first, first_send, second, second_send = parts
    return first, swap(first_send, "dp", ALONG_X), second, swap(second_send, "dp", ALONG_Y)


def add_last(me, parts, after=(), cost=0):
    rows = parts[0].shape[1]
    return call(
        add_last_body,
        [near_shape((2, rows, LANES)), shape_of((2, rows, LANES))],
        [me, *parts],
        [pltpu.VMEM((4, rows, LANES), jnp.bfloat16)],
        after=after,
        cost=cost,
        name="add_last",
    )


def scatter_z(parts):
    return parts[0], swap(parts[1], "mp", 1)


def add_z(me, parts, after=()):
    rows = parts[0].shape[1]
    return call(
        add_z_body,
        [near_shape((rows, LANES), jnp.float32), shape_of((rows, LANES))],
        [me, *parts],
        after=after,
        name="add_z",
    )


def scatter_z_far(parts):
    return parts[0], swap(parts[1], "mp", 2)


def total(refs, rows):
    value = refs[0][rows, :].astype(jnp.float32)
    for ref in refs[1:]:
        value = value + ref[rows, :].astype(jnp.float32)
    return value


def finish_columns(me, refs, base, tiles, out):
    odd = lax.rem(me[1], 2) == 1
    full = [total(refs, pl.ds(base + t * 96, 96)) for t in range(tiles)]
    single = total(refs, pl.ds(base + tiles * 96, 48))
    single = jnp.concatenate([single[:, :64], single[:, 64:]], axis=0)

    @pl.when(odd)
    def _():
        out[...] = jnp.concatenate([single, *full], axis=1)

    @pl.when(jnp.logical_not(odd))
    def _():
        out[...] = jnp.concatenate([*full, single], axis=1)


def finish_q_body(me, *refs):
    parts, out, outs = refs[:2], refs[2], refs[3:]
    finish_columns(me, parts, 0, 4, out)
    tail = total(parts, pl.ds(VECTOR_ROW, 16))
    for v in range(8):
        outs[v][...] = tail[v : v + 1, :24]
    outs[8][...] = tail[8:9, :96]


def finish_q(me, parts, after=()):
    f = jnp.float32
    return call(
        finish_q_body,
        [shape_of((96, 576), f)] + [shape_of((1, 24), f)] * 8 + [shape_of((1, 96), f)],
        [me, *parts],
        after=after,
        name="finish_q",
    )


def finish_ou_body(me, *refs):
    parts, w_out, w_up = refs[:2], refs[2], refs[3]
    finish_columns(me, parts, 0, 1, w_out)
    for t in range(UP_TILES):
        w_up[:, t * LANES : (t + 1) * LANES] = total(parts, pl.ds(UP_ROW + t * 96, 96))


def finish_ou(me, parts, after=()):
    f = jnp.float32
    return call(
        finish_ou_body, [shape_of((96, 192), f), shape_of((96, 768), f)], [me, *parts],
        after=after, name="finish_ou",
    )


def finish_d_body(me, *refs):
    parts, out = refs[:2], refs[2]
    for t in range(DOWN_TILES):
        out[:, t * LANES : (t + 1) * LANES] = total(parts, pl.ds(t * 192, 192))


def finish_d(me, parts, after=()):
    f = jnp.float32
    return call(finish_d_body, [shape_of((192, 384), f)], [me, *parts], after=after, name="finish_d")


PAIRS = HEADS // 2


def iota(shape, axis):
    return lax.broadcasted_iota(jnp.int32, shape, axis)


def place_matrix(order, head):
    length = order.shape[1]
    row = order[head : head + 1, :].astype(jnp.int16)
    token = iota((length, length), 0).astype(jnp.int16)
    return jnp.where(token == row, jnp.bfloat16(1.0), jnp.bfloat16(0.0))


def project_body(me, *refs):
    blocks, tokens = split_pairs(refs[:4]), refs[4]
    weights, vectors, bias_up, qkv, singles, tails = refs[5:]
    unpack_q_body(me, *blocks, weights, vectors, bias_up, singles, tails)
    for c in range(9):
        columns = slice(c * 256, (c + 1) * 256)
        value = dot(tokens[...], weights[:, columns])
        if c < 3:
            value = value + vectors[0:1, c * 256 : (c + 1) * 256]
        elif c >= 6:
            value = value + vectors[1:2, (c - 6) * 256 : (c - 5) * 256]
        qkv[:, columns] = value.astype(jnp.bfloat16)


def project(me, parts, tokens, after=()):
    return call(
        project_body,
        [
            near_shape((768, 2304)),
            near_shape((8, 768), jnp.float32),
            near_shape((1, 3072), jnp.float32),
            near_shape((tokens.shape[0], 2304)),
        ],
        [me, *parts, tokens],
        [pltpu.VMEM((4, 384, LANES), jnp.bfloat16), pltpu.VMEM((32, 16, LANES), jnp.float32)],
        after=after,
        name="project",
    )


def attend_body(first_pair, pairs, me, qkv, order, facts, *refs):
    swapped, values, soft, combined = refs[-4:]
    length = qkv.shape[0]
    groups = length // CLUSTER
    blocks = [slice(g * CLUSTER, (g + 1) * CLUSTER) for g in range(groups)]
    low = iota((length, LANES), 1) < 64
    itself = iota((CLUSTER, CLUSTER), 0) == iota((CLUSTER, CLUSTER), 1)
    pick = [
        jnp.where(iota((16, LANES), 1) == lane, 1.0, 0.0).astype(jnp.bfloat16) for lane in (64, 0)
    ]
    scale = HEAD_DIM ** (-0.5)

    for place in range(pairs):
        pair = first_pair + place

        def columns(base, pair=pair):
            return slice(base + pair * LANES, base + (pair + 1) * LANES)

        query = qkv[:, columns(0)].astype(jnp.float32)
        keys = qkv[:, columns(768)].astype(jnp.float32)
        value = qkv[:, columns(1536)].astype(jnp.float32)
        known = facts[...]
        tiles = (
            (jnp.where(low, query, pltpu.roll(keys, 64, axis=1)), jnp.where(low, value, known)),
            (jnp.where(low, pltpu.roll(query, 64, axis=1), keys), jnp.where(low, known, value)),
        )
        moved, to_tokens = [], []
        for h in range(2):
            back = place_matrix(order, 2 * pair + h)
            to_tokens.append(back)
            tile = jnp.concatenate([t.astype(jnp.bfloat16) for t in tiles[h]], axis=1)
            moved.append(dot_tn(back, tile))
        query_slots, key_slots, value_slots, codes, rows_of = [], [], [], [], []
        for h in range(2):
            both = moved[h][:, :LANES]
            query_slots.append(jnp.where(low, both, 0.0).astype(jnp.bfloat16))
            key_slots.append(pltpu.roll(both, 64, axis=1).astype(jnp.bfloat16))
            value_slots.append(moved[h][:, LANES:].astype(jnp.bfloat16))
            swapped[2 * place + h] = key_slots[h]
            values[2 * place + h] = value_slots[h]
            lane = 64 * (1 - h)
            code = moved[h][:, LANES + lane : LANES + lane + 1]
            row = dot_nt(pick[h], value_slots[h])[0:1]
            codes.append(jnp.where(code >= 32.0, code - 32.0, code))
            rows_of.append(row)
        scores = [
            [dot_nt(query_slots[h][b], key_slots[h][b]) for b in blocks] for h in range(2)
        ]
        found = []
        for h in range(2):
            outs = []
            for g, b in enumerate(blocks):
                allowed = (codes[h][b] == rows_of[h][:, b]) | itself
                value = jnp.where(allowed, scores[h][g] * scale, masked_score)
                value = jnp.exp(value - jnp.max(value, axis=1, keepdims=True))
                weights = value / jnp.sum(value, axis=1, keepdims=True)
                soft[2 * place + h, b, :] = weights
                outs.append(weights.astype(jnp.bfloat16))
            found.append(
                [dot(outs[g], value_slots[h][b]) for g, b in enumerate(blocks)]
            )
        result = None
        for h in range(2):
            value = jnp.concatenate(found[h], axis=0)
            value = jnp.where(low if h == 0 else jnp.logical_not(low), value, 0.0)
            value = dot(to_tokens[h], value.astype(jnp.bfloat16))
            result = value if result is None else result + value
        combined[:, columns(0)] = result.astype(jnp.bfloat16)


def attend(me, qkv, order, facts, first_pair, pairs, combined=None, after=()):
    length = qkv.shape[0]
    operands = [me, qkv, order, facts]
    if combined is not None:
        operands.append(combined)
    return call(
        functools.partial(attend_body, first_pair, pairs),
        [
            near_shape((2 * pairs, length, LANES)),
            near_shape((2 * pairs, length, LANES)),
            near_shape((2 * pairs, length, CLUSTER), jnp.float32),
            near_shape((length, 768)),
        ],
        operands,
        after=after,
        aliases={3: 3} if combined is not None else None,
        name="attend",
    )


def by_rows(first, count, step, body):
    for i in range(first, first + count, step):
        body(slice(i, i + step))


def mean(value):
    return jnp.mean(value, axis=1, keepdims=True)


def fold(value):
    return jnp.sum(value.reshape(value.shape[0] // 8, 8, value.shape[1]), axis=0)


def out_norm_body(me, combined, w_out, tokens, vectors, first_low, normal, inverse, total_ref):

    def rows_of(rows):
        value = total_ref[rows, :] + vectors[2:3] + tokens[rows, :].astype(jnp.float32)
        centred = value - mean(value)
        scale = lax.rsqrt(mean(centred * centred) + epsilon)
        norm = centred * scale
        normal[rows, :] = norm
        inverse[rows, :] = jnp.broadcast_to(scale, (scale.shape[0], LANES))
        first_low[rows, :] = (norm * vectors[3:4] + vectors[4:5]).astype(jnp.bfloat16)

    half = tokens.shape[0] // 2
    for first in (0, half):
        rows = slice(first, first + half)
        total_ref[rows, :] = dot(combined[rows, :], w_out[...])
        by_rows(first, half, 32, rows_of)


def out_norm(me, combined, w_out, tokens, vectors, after=()):
    n = tokens.shape[0]
    f = jnp.float32
    return call(
        out_norm_body,
        [near_shape((n, 768)), near_shape((n, 768), f), near_shape((n, LANES), f)],
        [me, combined, w_out, tokens, vectors],
        [pltpu.VMEM((n, 768), jnp.float32)],
        after=after,
        name="out_norm",
    )


def up_body(me, first_low, w_up, bias_up, activated, slope, send):
    width = w_up.shape[1] // 8
    for i in range(8):
        columns = slice(i * width, (i + 1) * width)
        hidden = dot(first_low[...], w_up[:, columns]) + bias_up[:, columns]
        half = 0.5 + 0.5 * lax.erf(hidden * (0.5**0.5))
        low = (hidden * half).astype(jnp.bfloat16)
        activated[:, columns] = low
        bell = jnp.exp(-0.5 * hidden * hidden) * (2.0 * math.pi) ** (-0.5)
        slope[:, columns] = (half + hidden * bell).astype(jnp.bfloat16)
    for i in range(8):
        k = me[0] ^ i

        @pl.when((k & 1) == 1)
        def _():
            there = pl.ds(pl.multiple_of((k >> 1) * width, LANES), width)
            send[:, there] = activated[:, i * width : (i + 1) * width]


def up(me, first_low, w_up, bias_up, after=()):
    n, width = first_low.shape[0], w_up.shape[1]
    return call(
        up_body,
        [near_shape((n, width)), near_shape((n, width)), shape_of((n, width // 2))],
        [me, first_low, w_up, bias_up],
        after=after,
        name="up",
    )


def down_norm_body(
    me, activated, turned, normal, vectors, out, feed_grad, second_grad, sums, feed, acc
):
    acc[...] = jnp.zeros_like(acc)

    def rows_of(rows):
        value = normal[rows, :] * vectors[3:4] + vectors[4:5] + feed[rows, :] + vectors[5:6]
        centred = value - mean(value)
        inverse = lax.rsqrt(mean(centred * centred) + epsilon)
        norm = centred * inverse
        out[rows, :] = (norm * vectors[6:7] + vectors[7:8]).astype(jnp.bfloat16)
        upstream = me.arrived(0)[rows, :]
        scaled = upstream * vectors[6:7]
        back = inverse * (scaled - mean(scaled) - norm * mean(scaled * norm))
        second_grad[rows, :] = back
        low = back.astype(jnp.bfloat16)
        feed_grad[rows, :] = low
        acc[0] += fold(low.astype(jnp.float32))
        acc[1] += fold(upstream * norm)
        acc[2] += fold(upstream)

    half = out.shape[0] // 2
    for first in (0, half):
        rows = slice(first, first + half)
        feed[rows, :] = dot_nt(activated[rows, :], turned[...])
        by_rows(first, half, 32, rows_of)
    me.send(0)
    for i in range(3):
        sums[i : i + 1, :] = jnp.sum(acc[i], axis=0, keepdims=True)


def down_norm(me, activated, turned, normal, vectors, cotangent, after=()):
    n = cotangent.shape[0]
    return call(
        down_norm_body,
        [
            shape_of((n, 768)),
            near_shape((n, 768)),
            near_shape((n, 768), jnp.float32),
            near_shape((3, 768), jnp.float32),
        ],
        [me, cotangent, activated, turned, normal, vectors],
        [pltpu.VMEM((n, 768), jnp.float32), pltpu.VMEM((3, 8, 768), jnp.float32)],
        late=[None],
        far_outs={0: True},
        after=after,
        name="down_norm",
    )


def hidden_back_body(me, feed_grad, turned, slope, hidden_grad, sums):
    for i in range(hidden_grad.shape[1] // 256):
        columns = slice(i * 256, (i + 1) * 256)
        value = dot(feed_grad[...], turned[:, columns]) * slope[:, columns].astype(jnp.float32)
        low = value.astype(jnp.bfloat16)
        hidden_grad[:, columns] = low
        sums[:, columns] = jnp.sum(low.astype(jnp.float32), axis=0, keepdims=True)


def hidden_back(me, feed_grad, turned, slope, after=()):
    return call(
        hidden_back_body,
        [near_shape(slope.shape), near_shape((1, slope.shape[1]), jnp.float32)],
        [me, feed_grad, turned, slope],
        after=after,
        name="hidden_back",
    )


def first_back_body(
    me, hidden_grad, w_up, second_grad, normal, inverse, vectors, residual, low_out, left, right, sums, back,
    acc,
):
    acc[...] = jnp.zeros_like(acc)

    def rows_of(rows):
        upstream = back[rows, :] + second_grad[rows, :]
        norm = normal[rows, :]
        scaled = upstream * vectors[3:4]
        value = inverse[rows, 0:1] * (scaled - mean(scaled) - norm * mean(scaled * norm))
        residual[rows, :] = value
        low = value.astype(jnp.bfloat16)
        low_out[rows, :] = low
        left[rows, :] = low[:, :384]
        right[rows, :] = low[:, 384:]
        acc[0] += fold(low.astype(jnp.float32))
        acc[1] += fold(upstream * norm)
        acc[2] += fold(upstream)

    half = normal.shape[0] // 2
    for first in (0, half):
        rows = slice(first, first + half)
        back[rows, :] = dot_nt(hidden_grad[rows, :], w_up[...])
        by_rows(first, half, 32, rows_of)
    for i in range(3):
        sums[i : i + 1, :] = jnp.sum(acc[i], axis=0, keepdims=True)


def first_back(me, hidden_grad, w_up, second_grad, normal, inverse, vectors, after=()):
    n = normal.shape[0]
    return call(
        first_back_body,
        [
            near_shape((n, 768), jnp.float32),
            near_shape((n, 768)),
            shape_of((n, 384)),
            shape_of((n, 384)),
            near_shape((3, 768), jnp.float32),
        ],
        [me, hidden_grad, w_up, second_grad, normal, inverse, vectors],
        [pltpu.VMEM((n, 768), jnp.float32), pltpu.VMEM((3, 8, 768), jnp.float32)],
        after=after,
        name="first_back",
    )


def attend_back_body(
    first_pair, pairs, me, attention_grad, w_out, order, swapped, values, soft, *refs
):
    grads, sums, upstream = refs[-3:]
    length = attention_grad.shape[0]
    groups = length // CLUSTER
    blocks = [slice(g * CLUSTER, (g + 1) * CLUSTER) for g in range(groups)]
    low = iota((length, LANES), 1) < 64
    low_rows = iota((CLUSTER, LANES), 1) < 64
    scale = HEAD_DIM ** (-0.5)
    mine = slice(first_pair * LANES, (first_pair + pairs) * LANES)
    upstream[...] = dot_nt(attention_grad[...], w_out[mine, :]).astype(jnp.bfloat16)

    for place in range(pairs):
        pair = first_pair + place

        def columns(base, pair=pair):
            return slice(base + pair * LANES, base + (pair + 1) * LANES)

        both = upstream[:, slice(place * LANES, (place + 1) * LANES)]
        to_tokens, moved = [], []
        for h in range(2):
            to_tokens.append(place_matrix(order, 2 * pair + h))
            value = dot_tn(to_tokens[h], both)
            value = jnp.where(low if h == 0 else jnp.logical_not(low), value, 0.0)
            moved.append(value.astype(jnp.bfloat16))
        back = []
        for h in range(2):
            kept = 2 * place + h
            keys = [swapped[kept, b, :] for b in blocks]
            weights = [soft[kept, b, :] for b in blocks]
            soft_grad = [dot_nt(moved[h][b], values[kept, b, :]) for b in blocks]
            value_grad = [
                dot_tn(weights[g].astype(jnp.bfloat16), moved[h][b]) for g, b in enumerate(blocks)
            ]
            score_grad = []
            for g in range(groups):
                middle = jnp.sum(soft_grad[g] * weights[g], axis=1, keepdims=True)
                score_grad.append((weights[g] * (soft_grad[g] - middle)).astype(jnp.bfloat16))
            query_grad = [dot(score_grad[g], keys[g]) for g in range(groups)]
            key_grad = [dot_tn(score_grad[g], keys[g]) for g in range(groups)]
            parts = [
                jnp.concatenate(
                    [
                        (jnp.where(low_rows, query_grad[g], key_grad[g]) * scale).astype(
                            jnp.bfloat16
                        ),
                        value_grad[g].astype(jnp.bfloat16),
                    ],
                    axis=1,
                )
                for g in range(groups)
            ]
            back.append(dot(to_tokens[h], jnp.concatenate(parts, axis=0)))
        first, second = back[0][:, :LANES], back[1][:, :LANES]
        query = jnp.where(low, first, pltpu.roll(second, 64, axis=1))
        keys = jnp.where(low, pltpu.roll(first, 64, axis=1), second)
        value = back[0][:, LANES:] + back[1][:, LANES:]
        grads[:, columns(0)] = query.astype(jnp.bfloat16)
        grads[:, columns(768)] = keys.astype(jnp.bfloat16)
        grads[:, columns(1536)] = value.astype(jnp.bfloat16)
        sums[0:1, columns(0)] = jnp.sum(query, axis=0, keepdims=True)
        sums[1:2, columns(0)] = jnp.sum(value, axis=0, keepdims=True)


def attend_back(
    me, attention_grad, w_out, order, kept, first_pair, pairs, before=(), after=()
):
    length = attention_grad.shape[0]
    return call(
        functools.partial(attend_back_body, first_pair, pairs),
        [near_shape((length, 2304)), near_shape((2, 768), jnp.float32)],
        [me, attention_grad, w_out, order, *kept, *before],
        [pltpu.VMEM((length, pairs * LANES), jnp.bfloat16)],
        after=after,
        aliases={6: 0, 7: 1} if before else None,
        name="attend_back",
    )


def tokens_back_body(me, grads, weights, residual, out):
    for c in range(3):
        columns = slice(c * 256, (c + 1) * 256)
        out[:, columns] = dot_nt(grads[...], weights[columns, :]) + residual[:, columns]
        me.send(0, (slice(None), columns))


def tokens_back(me, grads, weights, residual, after=()):
    return call(
        tokens_back_body,
        [shape_of(residual.shape, jnp.float32)],
        [me, grads, weights, residual],
        far_outs={0: True},
        sends=3,
        after=after,
        name="tokens_back",
    )


def local_block(
    tokens,
    w_qkv,
    bias_query,
    bias_value,
    w_out,
    bias_out,
    gain_one,
    shift_one,
    w_up,
    bias_up,
    w_down,
    bias_down,
    gain_two,
    shift_two,
    cluster_order,
    segment_ids,
    padding,
    cotangent,
):
    length = tokens.shape[0]
    me = None
    vector_list = [
        bias_query, bias_value, bias_out, gain_one, shift_one, bias_down, gain_two, shift_two
    ]
    order = cluster_order[0]
    facts = (segment_ids[0] + 32 * (1 - padding[0])).astype(jnp.float32)
    facts = jnp.broadcast_to(facts[:, None], (length, 128))

    def other(x):
        return swap(x, "dp", CORE)

    blocks_q = pack_q(me, w_qkv, vector_list, bias_up)
    far_z_q = swap(blocks_q[0], "mp", 2)
    blocks_rest = pack_rest(me, w_out, w_up, w_down, after=[blocks_q])
    block_ou, upper, lower, block_d = blocks_rest
    far_z_ou = swap(block_ou, "mp", 2)
    upper_x, lower_y = swap(upper, "dp", ALONG_X), swap(lower, "dp", ALONG_Y)
    tokens_turned = turn(me, tokens, after=[blocks_rest])
    spread = spread_d(me, block_d, upper_x, lower_y, after=[tokens_turned])
    upper, lower = spread
    upper_y, lower_x = swap(upper, "dp", ALONG_Y), swap(lower, "dp", ALONG_X)
    near_z_q = beside_two(
        me, blocks_q[1], far_z_q, after=[spread], cost=20 * MICROSECOND // 10
    )
    z_q = near_z_q[0], swap(near_z_q[0], "mp", 1)
    near_z_ou = beside_two(me, block_ou, far_z_ou, after=[near_z_q])
    z_ou = near_z_ou[0], swap(near_z_ou[0], "mp", 1)
    near_d = whole_d(me, upper, upper_y, lower, lower_x, after=[near_z_ou])
    z_q = tie(z_q, [near_d])
    near_q = [z_q[0], swap(z_q[0], "dp", ALONG_X), z_q[1], swap(z_q[1], "dp", ALONG_Y)]
    far_q = gather_far(me, near_q, after=[near_d])
    far_d = swap(near_d[0], "mp", 2)
    z_ou = tie(z_ou, [far_q])
    near_ou = [z_ou[0], swap(z_ou[0], "dp", ALONG_X), z_ou[1], swap(z_ou[1], "dp", ALONG_Y)]
    pairs_q = beside(
        me,
        [(x, (i // 2, i % 2)) for i, x in enumerate(far_q)],
        [(2, *far_q[0].shape)] * 2,
        (),
        "beside_far",
    )
    parts_q = list(pairs_q)
    parts_q = [*parts_q, *[other(x) for x in parts_q]]
    far_ou = gather_far(me, near_ou, after=[pairs_q], cost=5 * MICROSECOND // 10)
    both_d = beside_two(
        me, near_d[0], far_d, after=[far_ou], cost=82 * MICROSECOND // 10
    )
    z_d = swap(both_d[0], "mp", 1)
    projected = project(me, parts_q, tokens, after=[both_d])
    full_qkv, vectors, full_bias_up, qkv = projected

    pairs = PAIRS // 3

    def forward(part, before, after):
        return attend(
            me, qkv, order, facts, part * pairs, pairs, before, after=after
        )

    seen_a = forward(0, None, [projected])
    seen_b = forward(1, seen_a[-1], [seen_a])
    early_d = [other(x) for x in tie([near_d[0], far_d], [both_d])]
    far_ou = tie(far_ou, [seen_b, *early_d])
    seen_c = forward(2, seen_b[-1], far_ou[:1])
    combined = seen_c[-1]
    combined_turned = turn(me, combined)
    full_out, full_up = unpack_ou(me, gather_core(far_ou), after=[combined_turned])
    normed = out_norm(me, combined, full_out, tokens, vectors)
    first_low, normal, inverse = normed
    first_turned = turn(me, first_low)
    upper = up(me, first_low, full_up, full_bias_up, after=[first_turned])
    activated, slope, send_activated = upper
    sends = tie([combined_turned[0], first_turned[0], tokens_turned[0]], [upper])
    others = [other(x) for x in sends]
    (z_d,) = tie([z_d], [upper])
    unpacked = unpack_d(me, [both_d[0], z_d, *early_d, other(z_d)], after=others)
    others.insert(2, other(tie([send_activated], [unpacked])[0]))
    turned_down = unpacked[0]
    downed = down_norm(me, activated, turned_down, normal, vectors, cotangent)
    layer_out, feed_grad, second_grad, sums_two = downed
    other_tokens = others[3]

    other_feed = other(feed_grad)
    hidden = hidden_back(me, feed_grad, turned_down, slope, after=[downed])
    hidden_grad, sums_up = hidden
    (hidden_grad,) = tie([hidden_grad], [hidden, other_feed, others[2]])
    other_hidden = other(hidden_grad)
    grad_d = gradient_d(
        me, feed_grad, other_feed, activated, others[2], after=[hidden]
    )
    core_d = scatter_near(grad_d)
    first = first_back(
        me, hidden_grad, full_up, second_grad, normal, inverse, vectors, after=[grad_d]
    )
    residual_grad, attention_grad, *halves, sums_one = first
    halves = [other(x) for x in halves]

    def back(part, kept, before, after):
        return attend_back(
            me, attention_grad, full_out, order, kept,
            part * pairs, pairs, before, after,
        )

    grads_a = back(0, seen_a[:3], (), [first])
    grads_b = back(1, seen_b[:3], grads_a, [])
    grads_c = back(2, seen_c[:3], grads_b, halves)
    half_d = add_plane(me, core_d, after=[grads_c])
    plane_d = scatter_far(half_d)
    projected_grad, sums_bias = grads_c
    grad_vectors = all_sums(me, sums_bias, sums_one, sums_two, sums_up)
    projected_grad, grad_vectors = tie([projected_grad, grad_vectors], [half_d])
    other_grads = other(projected_grad), other(grad_vectors)
    grad_ou = gradient_ou(
        me,
        (combined_turned[1], others[0]),
        (first_turned[1], others[1]),
        (hidden_grad, other_hidden),
        (attention_grad, *halves),
        after=[half_d],
    )
    core_ou = scatter_near(grad_ou)
    last_d = add_last(me, plane_d, after=[grad_ou], cost=22 * MICROSECOND)
    z_d = scatter_z(last_d)
    grad_q = gradient_q(
        me, tokens_turned[1], other_tokens, projected_grad, other_grads[0], grad_vectors,
        other_grads[1], after=[last_d],
    )
    near_q = grad_q[0], swap(grad_q[1], "mp", 1)
    moved = tokens_back(me, projected_grad, full_qkv, residual_grad, after=[grad_q])
    grad_tokens = moved[0]
    near_d = add_z(me, z_d, after=[moved])
    sum_d = scatter_z_far(near_d)
    half_ou = add_plane(me, core_ou, after=[near_d], cost=4 * MICROSECOND)
    plane_ou = scatter_far(half_ou)
    last_ou = add_last(me, plane_ou, after=[half_ou])
    z_ou = scatter_z(last_ou)
    first_q = add_first(me, *near_q, after=[last_ou])
    core_q = scatter_near(first_q)
    half_q = add_plane(me, core_q, after=[first_q])
    plane_q = scatter_far(half_q)
    near_ou = add_z(me, z_ou, after=[half_q])
    sum_ou = scatter_z_far(near_ou)
    done_d = finish_d(me, sum_d, after=[near_ou])
    sum_q = scatter_z_far(add_both(me, plane_q, after=[done_d]))
    done_ou = finish_ou(me, sum_ou)
    shard_out, shard_up = done_ou
    shard_qkv, *shard_vectors = finish_q(me, sum_q, after=[done_ou])
    shard_down = done_d[0].T
    grad_list = [v.reshape(-1) for v in shard_vectors]
    return (
        layer_out,
        grad_tokens,
        shard_qkv,
        grad_list[0],
        grad_list[1],
        shard_out,
        grad_list[2],
        grad_list[3],
        grad_list[4],
        shard_up,
        grad_list[8],
        shard_down,
        grad_list[5],
        grad_list[6],
        grad_list[7],
    )


def solution(mesh):
    in_specs = (
        P(("dp", "mp"), None),
        P("dp", "mp"),
        P(("dp", "mp")),
        P(("dp", "mp")),
        P("dp", "mp"),
        P(("dp", "mp")),
        P(("dp", "mp")),
        P(("dp", "mp")),
        P("dp", "mp"),
        P(("dp", "mp")),
        P("dp", "mp"),
        P(("dp", "mp")),
        P(("dp", "mp")),
        P(("dp", "mp")),
        P(("dp", "mp"), None, None),
        P(("dp", "mp"), None),
        P(("dp", "mp"), None),
        P(("dp", "mp"), None),
    )
    out_specs = (
        P(("dp", "mp"), None),
        P(("dp", "mp"), None),
        P("dp", "mp"),
        P(("dp", "mp")),
        P(("dp", "mp")),
        P("dp", "mp"),
        P(("dp", "mp")),
        P(("dp", "mp")),
        P(("dp", "mp")),
        P("dp", "mp"),
        P(("dp", "mp")),
        P("dp", "mp"),
        P(("dp", "mp")),
        P(("dp", "mp")),
        P(("dp", "mp")),
    )
    blocks = mesh.shape["dp"] == 8 and mesh.shape["mp"] == 4
    local = local_block if blocks else local_general
    return jax.shard_map(local, mesh=mesh, in_specs=in_specs, out_specs=out_specs, check_vma=False)
```

```python
import functools
import math

import jax
import jax.numpy as jnp
from jax import lax
from jax.experimental import pallas as pl
from jax.experimental.pallas import tpu as pltpu
from jax.sharding import PartitionSpec as P

HEADS = 12
HEAD_DIM = 64
CLUSTER = 128


epsilon = 1e-12
masked_score = -1e30


def product(left_side, right_side):
    return jnp.dot(left_side, right_side, preferred_element_type=jnp.float32)


def times_back(left_side, right_side):
    return lax.dot_general(
        left_side, right_side, (((1,), (1,)), ((), ())), preferred_element_type=jnp.float32
    )


def outer_sum(left_side, right_side):
    return lax.dot_general(
        left_side, right_side, (((0,), (0,)), ((), ())), preferred_element_type=jnp.float32
    )


def norm_forward(hidden, norm_gain, norm_shift):
    average = jnp.mean(hidden, axis=-1, keepdims=True)
    centred = hidden - average
    variance = jnp.mean(centred * centred, axis=-1, keepdims=True)
    inverse = lax.rsqrt(variance + epsilon)
    normal = centred * inverse
    return (normal * norm_gain + norm_shift, normal, inverse)


def norm_backward(upstream, normal, inverse, norm_gain):
    scaled = upstream * norm_gain
    return inverse * (
        scaled
        - jnp.mean(scaled, axis=-1, keepdims=True)
        - normal * jnp.mean(scaled * normal, axis=-1, keepdims=True)
    )


def gelu_exact(inputs):
    return jax.nn.gelu(inputs, approximate=False)


def local_general(
    tokens,
    w_qkv,
    bias_query,
    bias_value,
    w_out,
    bias_out,
    gain_one,
    shift_one,
    w_up,
    bias_up,
    w_down,
    bias_down,
    gain_two,
    shift_two,
    cluster_order,
    segment_ids,
    padding,
    cotangent,
):
    model_width = HEADS * HEAD_DIM
    length = tokens.shape[0]
    groups = length // CLUSTER
    score_scale = HEAD_DIM ** (-0.5)
    vectors = jnp.stack(
        [bias_query, bias_value, bias_out, gain_one, shift_one, bias_down, gain_two, shift_two]
    ).astype(jnp.bfloat16)
    vector_up = bias_up.astype(jnp.bfloat16)[None, :]
    part_qkv = w_qkv.astype(jnp.bfloat16)
    part_out = w_out.astype(jnp.bfloat16)
    part_up = w_up.astype(jnp.bfloat16)
    part_down = w_down.astype(jnp.bfloat16)
    column_qkv, column_out, column_up, column_down, column_vectors, column_bias = (
        lax.all_gather(part_qkv, "mp", axis=1, tiled=True),
        lax.all_gather(part_out, "mp", axis=1, tiled=True),
        lax.all_gather(part_up, "mp", axis=1, tiled=True),
        lax.all_gather(part_down, "mp", axis=1, tiled=True),
        lax.all_gather(vectors, "mp", axis=1, tiled=True),
        lax.all_gather(vector_up, "mp", axis=1, tiled=True),
    )
    full_qkv, full_out, full_up, full_down, full_vectors, full_bias = (
        lax.all_gather(column_qkv, "dp", axis=0, tiled=True),
        lax.all_gather(column_out, "dp", axis=0, tiled=True),
        lax.all_gather(column_up, "dp", axis=0, tiled=True),
        lax.all_gather(column_down, "dp", axis=0, tiled=True),
        lax.all_gather(column_vectors, "dp", axis=1, tiled=True),
        lax.all_gather(column_bias, "dp", axis=1, tiled=True),
    )
    small_params = full_vectors.astype(jnp.float32)
    hidden_bias = full_bias[0].astype(jnp.float32)
    ordering = cluster_order[0]
    segment = segment_ids[0]
    present = padding[0]
    positions = jnp.arange(length, dtype=jnp.int32)
    placement = (ordering[:, :, None] == positions[None, None, :]).astype(jnp.bfloat16)

    def to_clusters(matrix):
        per_head = matrix.reshape(length, HEADS, HEAD_DIM)
        moved = jnp.einsum("hip,phd->hid", placement, per_head, preferred_element_type=jnp.float32)
        return moved.astype(jnp.bfloat16).reshape(HEADS, groups, CLUSTER, HEAD_DIM)

    def from_clusters(blocks):
        per_head = blocks.astype(jnp.bfloat16).reshape(HEADS, length, HEAD_DIM)
        moved = jnp.einsum("hip,hid->phd", placement, per_head, preferred_element_type=jnp.float32)
        return moved.astype(jnp.bfloat16).reshape(length, model_width)

    segment_blocks = jnp.take(segment, ordering).reshape(HEADS, groups, CLUSTER)
    present_blocks = jnp.take(present, ordering).reshape(HEADS, groups, CLUSTER)
    same_doc = segment_blocks[..., :, None] == segment_blocks[..., None, :]
    itself = jnp.eye(CLUSTER, dtype=bool)
    allowed = same_doc & ((present_blocks[..., None, :] == 1) | itself)

    def scores_of(query_blocks, key_blocks):
        raw_scores = (
            jnp.einsum(
                "hncd,hnmd->hncm", query_blocks, key_blocks, preferred_element_type=jnp.float32
            )
            * score_scale
        )
        return jnp.where(allowed, raw_scores, masked_score)

    projected = product(tokens, full_qkv)
    query = (projected[:, :model_width] + small_params[0]).astype(jnp.bfloat16)
    keys = projected[:, model_width : 2 * model_width].astype(jnp.bfloat16)
    values = (projected[:, 2 * model_width :] + small_params[1]).astype(jnp.bfloat16)
    query_blocks = to_clusters(query)
    key_blocks = to_clusters(keys)
    value_blocks = to_clusters(values)
    masked = scores_of(query_blocks, key_blocks)
    highest = jnp.max(masked, axis=-1, keepdims=True)
    exponent = jnp.exp(masked - highest)
    row_total = jnp.sum(exponent, axis=-1, keepdims=True)
    soft_weights = exponent / row_total
    log_total = highest + jnp.log(row_total)
    soft_low = soft_weights.astype(jnp.bfloat16)
    combined = from_clusters(
        jnp.einsum("hncm,hnmd->hncd", soft_low, value_blocks, preferred_element_type=jnp.float32)
    )
    attention = product(combined, full_out) + small_params[2]
    first_norm, first_normal, first_inverse = norm_forward(
        tokens.astype(jnp.float32) + attention, small_params[3], small_params[4]
    )
    first_low = first_norm.astype(jnp.bfloat16)
    hidden = product(first_low, full_up) + hidden_bias
    activated, gelu_pull = jax.vjp(gelu_exact, hidden)
    activated_low = activated.astype(jnp.bfloat16)
    feed_out = product(activated_low, full_down) + small_params[5]
    output, second_normal, second_inverse = norm_forward(
        first_norm + feed_out, small_params[6], small_params[7]
    )
    layer_out = output.astype(jnp.bfloat16)
    again_qkv, again_out, again_up, again_down = (
        lax.all_gather(part_qkv, "mp", axis=1, tiled=True),
        lax.all_gather(part_out, "mp", axis=1, tiled=True),
        lax.all_gather(part_up, "mp", axis=1, tiled=True),
        lax.all_gather(part_down, "mp", axis=1, tiled=True),
    )
    back_qkv, back_out, back_up, back_down = (
        lax.all_gather(again_qkv, "dp", axis=0, tiled=True),
        lax.all_gather(again_out, "dp", axis=0, tiled=True),
        lax.all_gather(again_up, "dp", axis=0, tiled=True),
        lax.all_gather(again_down, "dp", axis=0, tiled=True),
    )
    grad_gain_two = jnp.sum(cotangent * second_normal, axis=0)
    grad_shift_two = jnp.sum(cotangent, axis=0)
    second_grad = norm_backward(cotangent, second_normal, second_inverse, small_params[6])
    feed_grad = second_grad.astype(jnp.bfloat16)
    grad_bias_down = jnp.sum(feed_grad.astype(jnp.float32), axis=0)
    grad_w_down = outer_sum(activated_low, feed_grad)
    hidden_grad = gelu_pull(times_back(feed_grad, back_down))[0].astype(jnp.bfloat16)
    grad_bias_up = jnp.sum(hidden_grad.astype(jnp.float32), axis=0)
    grad_w_up = outer_sum(first_low, hidden_grad)
    first_grad = times_back(hidden_grad, back_up) + second_grad
    grad_gain_one = jnp.sum(first_grad * first_normal, axis=0)
    grad_shift_one = jnp.sum(first_grad, axis=0)
    residual_grad = norm_backward(first_grad, first_normal, first_inverse, small_params[3])
    attention_grad = residual_grad.astype(jnp.bfloat16)
    grad_bias_out = jnp.sum(attention_grad.astype(jnp.float32), axis=0)
    grad_w_out = outer_sum(combined, attention_grad)
    combined_grad = to_clusters(times_back(attention_grad, back_out).astype(jnp.bfloat16))
    masked_again = scores_of(query_blocks, key_blocks)
    soft_again = jnp.exp(masked_again - log_total)
    soft_again_low = soft_again.astype(jnp.bfloat16)
    value_sums = jnp.einsum(
        "hncm,hncd->hnmd", soft_again_low, combined_grad, preferred_element_type=jnp.float32
    )
    soft_grad = jnp.einsum(
        "hncd,hnmd->hncm", combined_grad, value_blocks, preferred_element_type=jnp.float32
    )
    score_grad = (
        soft_again * (soft_grad - jnp.sum(soft_grad * soft_again, axis=-1, keepdims=True))
    ).astype(jnp.bfloat16)
    query_sums = (
        jnp.einsum("hncm,hnmd->hncd", score_grad, key_blocks, preferred_element_type=jnp.float32)
        * score_scale
    )
    key_sums = (
        jnp.einsum("hncm,hncd->hnmd", score_grad, query_blocks, preferred_element_type=jnp.float32)
        * score_scale
    )
    query_grad = from_clusters(query_sums)
    key_grad = from_clusters(key_sums)
    value_grad = from_clusters(value_sums)
    grad_bias_query = jnp.sum(query_grad.astype(jnp.float32), axis=0)
    grad_bias_value = jnp.sum(value_grad.astype(jnp.float32), axis=0)
    projected_grad = jnp.concatenate([query_grad, key_grad, value_grad], axis=1)
    grad_w_qkv = outer_sum(tokens, projected_grad)
    grad_tokens = times_back(projected_grad, back_qkv) + residual_grad
    grad_vectors = jnp.stack(
        [
            grad_bias_query,
            grad_bias_value,
            grad_bias_out,
            grad_gain_one,
            grad_shift_one,
            grad_bias_down,
            grad_gain_two,
            grad_shift_two,
        ]
    )
    grad_up_row = grad_bias_up[None, :]
    row_qkv, row_out, row_up, row_down, row_vectors, row_bias = (
        lax.psum_scatter(
            grad_w_qkv.astype(jnp.bfloat16), "dp", scatter_dimension=0, tiled=True
        ).astype(jnp.float32),
        lax.psum_scatter(
            grad_w_out.astype(jnp.bfloat16), "dp", scatter_dimension=0, tiled=True
        ).astype(jnp.float32),
        lax.psum_scatter(
            grad_w_up.astype(jnp.bfloat16), "dp", scatter_dimension=0, tiled=True
        ).astype(jnp.float32),
        lax.psum_scatter(
            grad_w_down.astype(jnp.bfloat16), "dp", scatter_dimension=0, tiled=True
        ).astype(jnp.float32),
        lax.psum_scatter(
            grad_vectors.astype(jnp.bfloat16), "dp", scatter_dimension=1, tiled=True
        ).astype(jnp.float32),
        lax.psum_scatter(
            grad_up_row.astype(jnp.bfloat16), "dp", scatter_dimension=1, tiled=True
        ).astype(jnp.float32),
    )
    shard_qkv, shard_out, shard_up, shard_down, shard_vectors, shard_bias = (
        lax.psum_scatter(
            row_qkv.astype(jnp.bfloat16), "mp", scatter_dimension=1, tiled=True
        ).astype(jnp.float32),
        lax.psum_scatter(
            row_out.astype(jnp.bfloat16), "mp", scatter_dimension=1, tiled=True
        ).astype(jnp.float32),
        lax.psum_scatter(row_up.astype(jnp.bfloat16), "mp", scatter_dimension=1, tiled=True).astype(
            jnp.float32
        ),
        lax.psum_scatter(
            row_down.astype(jnp.bfloat16), "mp", scatter_dimension=1, tiled=True
        ).astype(jnp.float32),
        lax.psum_scatter(
            row_vectors.astype(jnp.bfloat16), "mp", scatter_dimension=1, tiled=True
        ).astype(jnp.float32),
        lax.psum_scatter(
            row_bias.astype(jnp.bfloat16), "mp", scatter_dimension=1, tiled=True
        ).astype(jnp.float32),
    )
    return (
        layer_out,
        grad_tokens,
        shard_qkv,
        shard_vectors[0],
        shard_vectors[1],
        shard_out,
        shard_vectors[2],
        shard_vectors[3],
        shard_vectors[4],
        shard_up,
        shard_bias[0],
        shard_down,
        shard_vectors[5],
        shard_vectors[6],
        shard_vectors[7],
    )


LANES = 128
QKV_ROWS = 96
UP_TILES = 6
DOWN_TILES = 3
PACK_Q = 4 * QKV_ROWS + QKV_ROWS // 2 + 16
PACK_OU = QKV_ROWS + QKV_ROWS // 2 + UP_TILES * QKV_ROWS
PACK_D = DOWN_TILES * 192
VECTOR_ROW = 4 * QKV_ROWS + QKV_ROWS // 2
UP_ROW = QKV_ROWS + QKV_ROWS // 2


def whole():
    return pl.BlockSpec(memory_space=pltpu.VMEM)


def far():
    return pl.BlockSpec(memory_space=pltpu.HBM)


def kept_far(arrays):
    return [pltpu.with_memory_space_constraint(x, pltpu.HBM) for x in arrays]


def near(x):
    return pltpu.with_memory_space_constraint(x, pltpu.VMEM)


def near_shape(shape, dtype=jnp.bfloat16):
    return pltpu.VMEM(shape, dtype)


def waited(after):
    return [kept_far([x.token])[0] if isinstance(x, Results) else x for x in after]


def anywhere(after):
    return [far() if isinstance(x, Results) else pl.BlockSpec(memory_space=pl.ANY) for x in after]


class Results(list):
    token = None


TOKEN = pltpu.HBM((8, 128), jnp.float32)


def place():
    return lax.axis_index("dp"), lax.axis_index("mp")


SHORT = pl.CostEstimate(flops=1, bytes_accessed=1, transcendentals=0)
MICROSECOND = 1_153_000_000


class Place(tuple):
    def arrived(self, index, part=None):
        copies, here = self.late[index]
        for i in range(len(copies)) if part is None else [part]:
            if copies[i] is not None:
                copies[i].wait()
                copies[i] = None
        return here

    def send(self, index, where=None, source=None):
        here, there = self.far[index]
        source = here if source is None else source
        if where is not None:
            source, there = source.at[where], there.at[where]
        copy = pltpu.make_async_copy(source, there, self.sems.at[len(self.sent)])
        copy.start()
        self.sent.append(copy)


def call(
    body, out_shapes, operands, scratch=(), staged=0, late=(), far_outs=None, sends=None, after=(),
    aliases=None, vmem=10, cost=0, name=None,
):
    operands = operands[1:]
    far_outs = far_outs or {}
    sends = len(far_outs) if sends is None else sends
    count, outs, copied = len(operands), len(out_shapes), staged + len(late)
    spread = [(0, 1)] * staged + [x or (0, 1) for x in late]
    starts = [sum(n for _, n in spread[:i]) for i in range(copied)]

    def with_copies(*refs):
        sources, rest = refs[:copied], refs[copied:count]
        results = list(refs[count + len(after) : count + len(after) + outs])
        own = refs[count + len(after) + outs + 1 :]
        mine, own = own[: len(scratch)], own[len(scratch) :]
        arrived, own = own[:copied], list(own[copied:])
        me = Place(place())
        me.sent, me.far = [], {}
        if copied:
            sem = own.pop(0)
            copies = []
            for source, here, (axis, parts), start in zip(sources, arrived, spread, starts):
                size = here.shape[axis] // parts
                copies.append([])
                for i in range(parts):
                    cut = (slice(None),) * axis + (slice(i * size, (i + 1) * size),)
                    copies[-1].append(
                        pltpu.make_async_copy(source.at[cut], here.at[cut], sem.at[start + i])
                    )
            for copy in sum(copies, []):
                copy.start()
            for (copy,) in copies[:staged]:
                copy.wait()
            me.late = list(zip(copies[staged:], arrived[staged:]))
        if far_outs:
            me.sems = own.pop(0)
            for index, has_room in far_outs.items():
                here = own.pop(0) if has_room else None
                me.far[index] = (here, results[index])
                results[index] = here
        body(me, *arrived[:staged], *rest, *results, *mine)
        for copy in me.sent:
            copy.wait()

    room = [pltpu.VMEM(x.shape, x.dtype) for x in operands[:copied]]
    if copied:
        room.append(pltpu.SemaphoreType.DMA((sum(n for _, n in spread),)))
    if far_outs:
        room.append(pltpu.SemaphoreType.DMA((sends,)))
        room += [pltpu.VMEM(out_shapes[i].shape, out_shapes[i].dtype) for i in far_outs if far_outs[i]]
    given = [
        pltpu.HBM(x.shape, x.dtype) if i in far_outs else x for i, x in enumerate(out_shapes)
    ]
    *results, token = pl.pallas_call(
        with_copies,
        out_shape=[*given, TOKEN],
        in_specs=[pl.BlockSpec(memory_space=pl.ANY)] * staged
        + [far()] * len(late)
        + [whole()] * (count - copied)
        + anywhere(after),
        out_specs=[far() if i in far_outs else whole() for i in range(outs)] + [far()],
        scratch_shapes=list(scratch) + room,
        input_output_aliases=aliases or {},
        compiler_params=pltpu.CompilerParams(vmem_limit_bytes=vmem * 1024 * 1024),
        cost_estimate=SHORT if not cost else pl.CostEstimate(cost, 1, 0),
        name=name,
    )(
        *operands[:staged],
        *kept_far(operands[staged:copied]),
        *operands[copied:],
        *waited(after),
    )
    results = Results(results)
    results.token = token
    return results


def tie(arrays, after):
    count = len(arrays)

    def body(*refs):
        pass

    return pl.pallas_call(
        body,
        out_shape=[shape_of(x.shape, x.dtype) for x in arrays],
        in_specs=[pl.BlockSpec(memory_space=pl.ANY)] * count + anywhere(after),
        out_specs=[pl.BlockSpec(memory_space=pl.ANY)] * count,
        input_output_aliases={i: i for i in range(count)},
        compiler_params=pltpu.CompilerParams(vmem_limit_bytes=1024 * 1024),
        cost_estimate=SHORT,
        name="tie",
    )(*arrays, *waited(after))


def shape_of(shape, dtype=jnp.bfloat16):
    return jax.ShapeDtypeStruct(shape, dtype)


def halves_beside(single):
    half = single.shape[0] // 2
    return jnp.concatenate([single[:half], single[half:]], axis=1)


def pack_columns(odd, low, tiles, base, target):
    @pl.when(odd)
    def _():
        for t in range(tiles):
            target[base + t * 96 : base + (t + 1) * 96, :] = low[
                :, 64 + t * LANES : 64 + (t + 1) * LANES
            ].astype(jnp.bfloat16)
        target[base + tiles * 96 : base + tiles * 96 + 48, :] = halves_beside(low[:, :64]).astype(
            jnp.bfloat16
        )

    @pl.when(jnp.logical_not(odd))
    def _():
        for t in range(tiles):
            target[base + t * 96 : base + (t + 1) * 96, :] = low[
                :, t * LANES : (t + 1) * LANES
            ].astype(jnp.bfloat16)
        target[base + tiles * 96 : base + tiles * 96 + 48, :] = halves_beside(
            low[:, tiles * LANES : tiles * LANES + 64]
        ).astype(jnp.bfloat16)


def pack_q_body(me, *refs):
    w_qkv, vectors, target, own = refs[0], refs[1:10], refs[10], refs[11]
    pack_columns(lax.rem(me[1], 2) == 1, w_qkv[...], 4, 0, target)
    rows = lax.broadcasted_iota(jnp.int32, (16, LANES), 0)
    tail = jnp.zeros((16, LANES), jnp.float32)
    for v in range(9):
        value = vectors[v][...]
        wide = jnp.concatenate(
            [value, jnp.zeros((1, LANES - value.shape[1]), jnp.float32)], axis=1
        )
        tail = jnp.where(rows == v, jnp.broadcast_to(wide, (16, LANES)), tail)
    target[VECTOR_ROW:, :] = tail.astype(jnp.bfloat16)
    me.send(0)
    own[...] = target[...]


def pack_q(me, w_qkv, vectors, bias_up):
    small = [v.reshape(1, -1) for v in (*vectors, bias_up)]
    return call(
        pack_q_body, [shape_of((PACK_Q, LANES))] * 2, [me, *kept_far([w_qkv, *small])], staged=10, far_outs={0: True},
        name="pack_q",
    )


def pack_rest_body(me, w_out, w_up, w_down, to_ou, upper_d, lower_d, to_d):
    for t in range(DOWN_TILES):
        to_d[t * 192 : (t + 1) * 192, :] = w_down[:, t * LANES : (t + 1) * LANES].astype(
            jnp.bfloat16
        )
    upper_d[...] = to_d[: PACK_D // 2, :]
    lower_d[...] = to_d[PACK_D // 2 :, :]
    me.send(1)
    me.send(2)
    pack_columns(lax.rem(me[1], 2) == 1, w_out[...], 1, 0, to_ou)
    for t in range(UP_TILES):
        to_ou[UP_ROW + t * 96 : UP_ROW + (t + 1) * 96, :] = w_up[
            :, t * LANES : (t + 1) * LANES
        ].astype(jnp.bfloat16)


def pack_rest(me, w_out, w_up, w_down, after):
    return call(
        pack_rest_body,
        [
            near_shape((PACK_OU, LANES)),
            shape_of((PACK_D // 2, LANES)),
            shape_of((PACK_D // 2, LANES)),
            near_shape((PACK_D, LANES)),
        ],
        [me, *kept_far([w_out, w_up, w_down.T])],
        staged=3,
        far_outs={1: True, 2: True},
        after=after,
        name="pack_rest",
    )


def swap(x, axis, bit):
    size = lax.axis_size(axis)
    return lax.ppermute(x, axis, [(i, i ^ bit) for i in range(size)])


CORE, ALONG_X, ALONG_Y = 1, 2, 4


def gather_z(x, own=None):
    return [x if own is None else own] + [swap(x, "mp", k) for k in (1, 2, 3)]


def beside(me, groups, shapes, after=(), name="beside", cost=0):
    sources = []
    for x, _ in groups:
        if all(x is not y for y in sources):
            sources.append(x)

    def body(me, *refs):
        for x, (index, where) in groups:
            source = refs[next(n for n, y in enumerate(sources) if x is y)]
            refs[len(sources) + index][where] = source[...]

    return call(body, [shape_of(s) for s in shapes], [me, *sources], after=after, name=name, cost=cost)


def beside_two(me, a, b, after=(), cost=0):
    return beside(me, [(a, (0, 0)), (b, (0, 1))], [(2, *a.shape)], after, "beside_two", cost)


def gather_near(me, parts, after=()):
    shape = (2, *parts[0].shape)
    found = beside(
        me,
        [(parts[0], (0, 0)), (parts[1], (0, 1)), (parts[2], (1, 0)), (parts[3], (1, 1))],
        [shape, shape],
        after,
        "beside_z",
    )
    first, second = found
    result = Results([first, swap(first, "dp", ALONG_X), second, swap(second, "dp", ALONG_Y)])
    result.token = found.token
    return result


def gather_far(me, parts, after=(), cost=0):
    shape = (2, *parts[0].shape)
    groups = [(parts[i], (i // 2, i % 2)) for i in range(4)]
    found = beside(me, groups, [shape, shape], after, "beside_near", cost)
    first, second = found
    result = Results([first, second, swap(first, "dp", ALONG_Y), swap(second, "dp", ALONG_X)])
    result.token = found.token
    return result


def gather_core(parts):
    return list(parts) + [swap(x, "dp", CORE) for x in parts]


def gathered_blocks(me, refs, steps=(1, 2)):
    for index, ref in enumerate(refs):
        core, far, half = index // 4, index % 4 // 2, index % 2
        for mid in range(2):
            for low in range(2):
                kx, ky = (far, mid) if half else (mid, far)
                along_z = steps[0] * low + steps[1] * half
                yield me[0] ^ (core + 2 * kx + 4 * ky), me[1] ^ along_z, ref.at[mid, low]


def split_pairs(refs):
    return [ref.at[i] for ref in refs for i in range(2)]


def place_columns(block, base, tiles, dp, mp, width, weights, singles):
    start = pl.multiple_of(mp * width + 64 * lax.rem(mp, 2), LANES)
    rows = pl.ds(pl.multiple_of(dp * 96, 32), 96)
    for t in range(tiles):
        weights[rows, pl.ds(pl.multiple_of(start + t * LANES, LANES), LANES)] = block[
            base + t * 96 : base + (t + 1) * 96, :
        ]
    singles[mp, pl.ds(pl.multiple_of(dp * 48, 16), 48), :] = block[
        base + tiles * 96 : base + tiles * 96 + 48, :
    ]


def place_singles(width, weights, singles):
    for pair in range(2):
        column = 2 * pair * width + (width // LANES) * LANES
        for dp in range(8):
            left = singles[2 * pair, dp * 48 : (dp + 1) * 48, :].astype(jnp.float32)
            right = singles[2 * pair + 1, dp * 48 : (dp + 1) * 48, :].astype(jnp.float32)
            upper = jnp.concatenate([left[:, :64], right[:, :64]], axis=1)
            lower = jnp.concatenate([left[:, 64:], right[:, 64:]], axis=1)
            weights[dp * 96 : dp * 96 + 48, column : column + LANES] = upper.astype(jnp.bfloat16)
            weights[dp * 96 + 48 : (dp + 1) * 96, column : column + LANES] = lower.astype(
                jnp.bfloat16
            )


def unpack_q_body(me, *refs):
    blocks, weights, vectors, bias_up, singles, tails = refs[:8], *refs[8:]
    for dp, mp, block in gathered_blocks(me, blocks, (2, 1)):
        place_columns(block, 0, 4, dp, mp, 576, weights, singles)
        tails[dp * 4 + mp] = block[VECTOR_ROW:, :].astype(jnp.float32)
    place_singles(576, weights, singles)
    lane = lax.broadcasted_iota(jnp.int32, (16, LANES), 1)

    def spread(width, count):
        found = [jnp.zeros((16, LANES), jnp.float32) for _ in range(count)]
        for device in range(32):
            start, tile = device * width % LANES, device * width // LANES
            piece = tails[device]
            moved = pltpu.roll(piece, start, axis=1) if start else piece
            found[tile] = jnp.where((lane >= start) & (lane < start + width), moved, found[tile])
            if start + width > LANES:
                found[tile + 1] = jnp.where(lane < start + width - LANES, moved, found[tile + 1])
        return found

    for t, value in enumerate(spread(24, 6)):
        vectors[:, t * LANES : (t + 1) * LANES] = value[:8]
    for t, value in enumerate(spread(96, 24)):
        bias_up[:, t * LANES : (t + 1) * LANES] = value[8:9]


def unpack_ou_body(me, *refs):
    blocks, w_out, w_up, singles = refs[:8], *refs[8:]
    for dp, mp, block in gathered_blocks(me, blocks, (2, 1)):
        place_columns(block, 0, 1, dp, mp, 192, w_out, singles)
        rows = pl.ds(pl.multiple_of(dp * 96, 32), 96)
        for t in range(UP_TILES):
            w_up[rows, pl.ds(pl.multiple_of(mp * 768 + t * LANES, LANES), LANES)] = block[
                UP_ROW + t * 96 : UP_ROW + (t + 1) * 96, :
            ]
    place_singles(192, w_out, singles)


def unpack_ou(me, parts, after=()):
    return call(
        unpack_ou_body,
        [near_shape((768, 768)), near_shape((768, 3072))],
        [me, *parts],
        [pltpu.VMEM((4, 384, LANES), jnp.bfloat16)],
        after=after,
        name="unpack_ou",
    )


def spread_d_body(me, mine, upper_x, lower_y, upper, lower):
    half = PACK_D // 2
    upper[0], upper[1] = mine[:half, :], upper_x[...]
    lower[0], lower[1] = mine[half:, :], lower_y[...]


def spread_d(me, mine, upper_x, lower_y, after=()):
    shape = near_shape((2, PACK_D // 2, LANES))
    return call(
        spread_d_body, [shape, shape], [me, mine, upper_x, lower_y], after=after, name="spread_d"
    )


def whole_d_body(me, upper, upper_y, lower, lower_x, out):
    half = PACK_D // 2
    for kx in range(2):
        for ky in range(2):
            out[2 * ky + kx, :half, :] = (upper_y if ky else upper)[kx]
            out[2 * ky + kx, half:, :] = (lower_x if kx else lower)[ky]


def whole_d(me, upper, upper_y, lower, lower_x, after=()):
    return call(
        whole_d_body, [near_shape((4, PACK_D, LANES))], [me, upper, upper_y, lower, lower_x],
        after=after, name="whole_d",
    )


def unpack_d_body(me, both, both_z, other, other_far, other_z, turned):
    for core in range(2):
        for kz in range(4):
            for plane in range(4):
                if core and kz % 2 == 0:
                    block = (other_far if kz else other).at[plane]
                else:
                    source = (other_z if core else both_z) if kz % 2 else both
                    block = source.at[kz // 2, plane]
                dp, mp = me[0] ^ (2 * plane + core), me[1] ^ kz
                rows = pl.ds(pl.multiple_of(mp * 192, 64), 192)
                for t in range(DOWN_TILES):
                    turned[rows, pl.ds(pl.multiple_of(dp * 384 + t * LANES, LANES), LANES)] = block[
                        t * 192 : (t + 1) * 192, :
                    ]


def unpack_d(me, parts, after=()):
    return call(
        unpack_d_body, [near_shape((768, 3072))], [me, *parts], after=after, name="unpack_d"
    )


def turn_body(me, source, send, keep, turned):
    value = source[...].T
    for dp in range(8):
        k = me[0] ^ dp
        slot = (1 - (k & 1)) * 4 + (k >> 1)
        turned[pl.ds(pl.multiple_of(slot * 96, 32), 96), :] = value[dp * 96 : (dp + 1) * 96, :]
    send[...] = turned[:384, :]
    keep[...] = turned[384:, :]


def turn(me, source, after=()):
    n = source.shape[0]
    return call(
        turn_body,
        [shape_of((384, n)), near_shape((384, n))],
        [me, source],
        [pltpu.VMEM((768, n), jnp.bfloat16)],
        after=after,
        name="turn",
    )


def dot(a, b):
    return jnp.dot(a, b, preferred_element_type=jnp.float32)


def dot_nt(a, b):
    return lax.dot_general(a, b, (((1,), (1,)), ((), ())), preferred_element_type=jnp.float32)


def dot_tn(a, b):
    return lax.dot_general(a, b, (((0,), (0,)), ((), ())), preferred_element_type=jnp.float32)


def part_of(targets, kp, mp):
    ky, kx = kp // 2, kp % 2
    if mp < 2:
        return targets[ky].at[kx, mp]
    return targets[2 + kx].at[ky, mp - 2]


def store_columns(target, base, tiles, first, value):
    for t in range(tiles):
        target[base + t * 96 : base + (t + 1) * 96, :] = value[
            :, first + t * LANES : first + (t + 1) * LANES
        ].astype(jnp.bfloat16)


def store_single(target, base, odd, value):
    upper, lower = value[:48], value[48:]
    low_lanes = lax.broadcasted_iota(jnp.int32, (48, LANES), 1) < 64
    if odd:
        both = jnp.where(low_lanes, pltpu.roll(upper, 64, axis=1), lower)
    else:
        both = jnp.where(low_lanes, upper, pltpu.roll(lower, 64, axis=1))
    target[base : base + 48, :] = both.astype(jnp.bfloat16)


def column_gradient(lefts, rights, targets, base, tiles, width):
    def product(columns):
        return dot(lefts[0], rights[0][:, columns]) + dot(lefts[1], rights[1][:, columns])

    for pair in range(2):
        first = 2 * pair * width
        middle = first + tiles * LANES
        for begin, mp in ((first, 2 * pair), (middle + LANES, 2 * pair + 1)):
            value = product(slice(begin, begin + tiles * LANES))
            for kp in range(4):
                store_columns(
                    targets(kp, mp), base, tiles, 0, value[kp * 96 : (kp + 1) * 96]
                )
        value = product(slice(middle, middle + LANES))
        for kp in range(4):
            for mp in (2 * pair, 2 * pair + 1):
                store_single(
                    targets(kp, mp), base + tiles * 96, mp % 2,
                    value[kp * 96 : (kp + 1) * 96],
                )


def parts_shape(rows):
    return [near_shape((2, 2, rows, LANES)), shape_of((2, 2, rows, LANES))] * 2


def gradient_q_body(
    me, keep, other_keep, grads, other_grads, vectors, other_vectors, mine, send, room
):
    targets = lambda kp, mp: room.at[me[1] ^ mp, kp]
    lefts, rights = (keep[...], other_keep[...]), (grads, other_grads)
    column_gradient(lefts, rights, targets, 0, 4, 576)
    sums = vectors[...] + other_vectors[...]
    lane = lax.broadcasted_iota(jnp.int32, (16, LANES), 1)
    rows = lax.broadcasted_iota(jnp.int32, (16, LANES), 0)

    def cut(source, width, device):
        start, tile = device * width % LANES, device * width // LANES
        value = source[:, tile * LANES : (tile + 1) * LANES]
        moved = pltpu.roll(value, LANES - start, axis=1) if start else value
        if start + width > LANES:
            after = source[:, (tile + 1) * LANES : (tile + 2) * LANES]
            after = pltpu.roll(after, LANES - start, axis=1)
            here = lax.broadcasted_iota(jnp.int32, value.shape, 1)
            moved = jnp.where(here < LANES - start, moved, after)
        return moved

    for kp in range(4):
        plane = (me[0] >> 1) ^ kp
        for mp in range(4):
            tail = jnp.zeros((16, LANES), jnp.float32)
            for dp in range(8):
                device = dp * 4 + mp
                row = 8 + device // 8
                up = jnp.broadcast_to(cut(sums[row : row + 1], 96, device % 8), (8, LANES))
                found = jnp.concatenate([cut(sums[:8], 24, device), up], axis=0)
                owner = dp == 2 * plane + (me[0] & 1)
                tail = jnp.where(owner, found, tail)
            tail = jnp.where((rows < 8) & (lane >= 24), 0.0, tail).astype(jnp.bfloat16)
            targets(kp, mp)[VECTOR_ROW:, :] = tail
    for kz in range(4):
        (send if kz % 2 else mine)[kz // 2] = room[kz]


def gradient_q(me, keep, other_keep, grads, other_grads, vectors, other_vectors, after=()):
    return call(
        gradient_q_body,
        [near_shape((2, 4, PACK_Q, LANES)), shape_of((2, 4, PACK_Q, LANES))],
        [me, keep, other_keep, grads, other_grads, vectors, other_vectors],
        [pltpu.VMEM((4, 4, PACK_Q, LANES), jnp.bfloat16)],
        after=after,
        name="gradient_q",
    )


def gradient_ou_body(me, *refs):
    combined, first_low, hidden_grad = (refs[i : i + 2] for i in (0, 2, 4))
    attention_grad, room = (refs[6], refs[13]), refs[13]
    targets = functools.partial(part_of, refs[9:13])
    room[:, :384] = refs[7][...]
    room[:, 384:] = refs[8][...]
    column_gradient([x[...] for x in combined], attention_grad, targets, 0, 1, 192)
    lefts = [x[...] for x in first_low]
    for mp in range(4):
        columns = slice(mp * 768, (mp + 1) * 768)
        value = dot(lefts[0], hidden_grad[0][:, columns])
        value = value + dot(lefts[1], hidden_grad[1][:, columns])
        for kp in range(4):
            store_columns(
                targets(kp, mp), UP_ROW, UP_TILES, 0, value[kp * 96 : (kp + 1) * 96]
            )


def gradient_ou(me, combined, first_low, hidden_grad, attention_grad, after=()):
    return call(
        gradient_ou_body,
        parts_shape(PACK_OU),
        [me, *combined, *first_low, *hidden_grad, *attention_grad],
        [pltpu.VMEM(attention_grad[0].shape, jnp.bfloat16)],
        after=after,
        name="gradient_ou",
    )


def gradient_d_body(me, feed_grad, other_feed_grad, activated, other_activated, *refs):
    targets, turned, other_turned = refs[:4], refs[4], refs[5]
    turned[...] = feed_grad[...].T
    other_turned[...] = other_feed_grad[...].T
    for kp in range(4):
        dp = me[0] ^ (2 * kp)
        block = activated[:, pl.ds(pl.multiple_of(dp * 384, LANES), 384)]
        value = dot(turned[...], block)
        value = value + dot(other_turned[...], other_activated[:, kp * 384 : (kp + 1) * 384])
        for mp in range(4):
            target = part_of(targets, kp, mp)
            for t in range(DOWN_TILES):
                target[t * 192 : (t + 1) * 192, :] = value[
                    mp * 192 : (mp + 1) * 192, t * LANES : (t + 1) * LANES
                ].astype(jnp.bfloat16)


def gradient_d(me, feed_grad, other_feed_grad, activated, other_activated, after=()):
    return call(
        gradient_d_body,
        parts_shape(PACK_D),
        [me, feed_grad, other_feed_grad, activated, other_activated],
        [pltpu.VMEM((768, feed_grad.shape[0]), jnp.bfloat16)] * 2,
        after=after,
        name="gradient_d",
    )


def sums_body(me, bias, one, two, up, out):
    out[0:2, :], out[2:5, :], out[5:8, :] = bias[...], one[...], two[...]
    for i in range(4):
        out[8 + i : 9 + i, :] = up[:, i * 768 : (i + 1) * 768]


def all_sums(me, *sums):
    return call(sums_body, [shape_of((12, 768), jnp.float32)], [me, *sums], name="sums")[0]


def add(a, b):
    return a.astype(jnp.float32) + b.astype(jnp.float32)


def add_plane_body(me, first, first_in, second, second_in, *outs):
    for keep, send, a, b in ((*outs[:2], first, first_in), (*outs[2:], second, second_in)):
        keep[...] = add(a[0], b[0]).astype(jnp.bfloat16)
        send[...] = add(a[1], b[1]).astype(jnp.bfloat16)


def add_last_body(me, first, first_in, second, second_in, *refs):
    keep, send, room = refs
    for mp in range(4):
        a, b = (first, first_in) if mp < 2 else (second, second_in)
        room[me[1] ^ mp] = add(a[mp % 2], b[mp % 2]).astype(jnp.bfloat16)
    for k in range(4):
        (send if k % 2 else keep)[k // 2] = room[k]


def add_first_body(me, mine, arrived, *outs):
    for kp in range(4):
        ky, kx = kp // 2, kp % 2
        outs[ky][kx] = add(mine[0, kp], arrived[0, kp]).astype(jnp.bfloat16)
        outs[2 + kx][ky] = add(mine[1, kp], arrived[1, kp]).astype(jnp.bfloat16)


def add_first(me, mine, arrived, after=()):
    rows = mine.shape[2]
    return call(
        add_first_body,
        [near_shape((2, rows, LANES)), shape_of((2, rows, LANES))] * 2,
        [me, mine, arrived],
        after=after,
        name="add_first",
    )


def add_both_body(me, first, first_in, second, second_in, keep, send):
    keep[...] = add(first[...], first_in[...])
    send[...] = add(second[...], second_in[...]).astype(jnp.bfloat16)


def add_both(me, parts, after=()):
    shape = parts[0].shape
    return call(
        add_both_body,
        [near_shape(shape, jnp.float32), shape_of(shape)],
        [me, *parts],
        after=after,
        name="add_both",
    )


def add_z_body(me, mine, arrived, keep, send):
    keep[...] = add(mine[0], arrived[0])
    send[...] = add(mine[1], arrived[1]).astype(jnp.bfloat16)


def scatter_near(parts):
    first, first_send, second, second_send = parts
    return first, swap(first_send, "dp", ALONG_Y), second, swap(second_send, "dp", ALONG_X)


def add_plane(me, parts, after=(), cost=0):
    shape = parts[0].shape[1:]
    return call(
        add_plane_body,
        [near_shape(shape), shape_of(shape)] * 2,
        [me, *parts],
        after=after,
        cost=cost,
        name="add_plane",
    )


def scatter_far(parts):
    first, first_send, second, second_send = parts
    return first, swap(first_send, "dp", ALONG_X), second, swap(second_send, "dp", ALONG_Y)


def add_last(me, parts, after=(), cost=0):
    rows = parts[0].shape[1]
    return call(
        add_last_body,
        [near_shape((2, rows, LANES)), shape_of((2, rows, LANES))],
        [me, *parts],
        [pltpu.VMEM((4, rows, LANES), jnp.bfloat16)],
        after=after,
        cost=cost,
        name="add_last",
    )


def scatter_z(parts):
    return parts[0], swap(parts[1], "mp", 1)


def add_z(me, parts, after=()):
    rows = parts[0].shape[1]
    return call(
        add_z_body,
        [near_shape((rows, LANES), jnp.float32), shape_of((rows, LANES))],
        [me, *parts],
        after=after,
        name="add_z",
    )


def scatter_z_far(parts):
    return parts[0], swap(parts[1], "mp", 2)


def total(refs, rows):
    value = refs[0][rows, :].astype(jnp.float32)
    for ref in refs[1:]:
        value = value + ref[rows, :].astype(jnp.float32)
    return value


def finish_columns(me, refs, base, tiles, out):
    odd = lax.rem(me[1], 2) == 1
    full = [total(refs, pl.ds(base + t * 96, 96)) for t in range(tiles)]
    single = total(refs, pl.ds(base + tiles * 96, 48))
    single = jnp.concatenate([single[:, :64], single[:, 64:]], axis=0)

    @pl.when(odd)
    def _():
        out[...] = jnp.concatenate([single, *full], axis=1)

    @pl.when(jnp.logical_not(odd))
    def _():
        out[...] = jnp.concatenate([*full, single], axis=1)


def finish_q_body(me, *refs):
    parts, out, outs = refs[:2], refs[2], refs[3:]
    finish_columns(me, parts, 0, 4, out)
    tail = total(parts, pl.ds(VECTOR_ROW, 16))
    for v in range(8):
        outs[v][...] = tail[v : v + 1, :24]
    outs[8][...] = tail[8:9, :96]


def finish_q(me, parts, after=()):
    f = jnp.float32
    return call(
        finish_q_body,
        [shape_of((96, 576), f)] + [shape_of((1, 24), f)] * 8 + [shape_of((1, 96), f)],
        [me, *parts],
        after=after,
        name="finish_q",
    )


def finish_ou_body(me, *refs):
    parts, w_out, w_up = refs[:2], refs[2], refs[3]
    finish_columns(me, parts, 0, 1, w_out)
    for t in range(UP_TILES):
        w_up[:, t * LANES : (t + 1) * LANES] = total(parts, pl.ds(UP_ROW + t * 96, 96))


def finish_ou(me, parts, after=()):
    f = jnp.float32
    return call(
        finish_ou_body, [shape_of((96, 192), f), shape_of((96, 768), f)], [me, *parts],
        after=after, name="finish_ou",
    )


def finish_d_body(me, *refs):
    parts, out = refs[:2], refs[2]
    for t in range(DOWN_TILES):
        out[:, t * LANES : (t + 1) * LANES] = total(parts, pl.ds(t * 192, 192))


def finish_d(me, parts, after=()):
    f = jnp.float32
    return call(finish_d_body, [shape_of((192, 384), f)], [me, *parts], after=after, name="finish_d")


PAIRS = HEADS // 2


def iota(shape, axis):
    return lax.broadcasted_iota(jnp.int32, shape, axis)


def place_matrix(order, head):
    length = order.shape[1]
    row = order[head : head + 1, :].astype(jnp.int16)
    token = iota((length, length), 0).astype(jnp.int16)
    return jnp.where(token == row, jnp.bfloat16(1.0), jnp.bfloat16(0.0))


def project_body(me, *refs):
    blocks, tokens = split_pairs(refs[:4]), refs[4]
    weights, vectors, bias_up, qkv, singles, tails = refs[5:]
    unpack_q_body(me, *blocks, weights, vectors, bias_up, singles, tails)
    for c in range(9):
        columns = slice(c * 256, (c + 1) * 256)
        value = dot(tokens[...], weights[:, columns])
        if c < 3:
            value = value + vectors[0:1, c * 256 : (c + 1) * 256]
        elif c >= 6:
            value = value + vectors[1:2, (c - 6) * 256 : (c - 5) * 256]
        qkv[:, columns] = value.astype(jnp.bfloat16)


def project(me, parts, tokens, after=()):
    return call(
        project_body,
        [
            near_shape((768, 2304)),
            near_shape((8, 768), jnp.float32),
            near_shape((1, 3072), jnp.float32),
            near_shape((tokens.shape[0], 2304)),
        ],
        [me, *parts, tokens],
        [pltpu.VMEM((4, 384, LANES), jnp.bfloat16), pltpu.VMEM((32, 16, LANES), jnp.float32)],
        after=after,
        name="project",
    )


def attend_body(first_pair, pairs, me, qkv, order, facts, *refs):
    swapped, values, soft, combined = refs[-4:]
    length = qkv.shape[0]
    groups = length // CLUSTER
    blocks = [slice(g * CLUSTER, (g + 1) * CLUSTER) for g in range(groups)]
    low = iota((length, LANES), 1) < 64
    itself = iota((CLUSTER, CLUSTER), 0) == iota((CLUSTER, CLUSTER), 1)
    pick = [
        jnp.where(iota((16, LANES), 1) == lane, 1.0, 0.0).astype(jnp.bfloat16) for lane in (64, 0)
    ]
    scale = HEAD_DIM ** (-0.5)

    for place in range(pairs):
        pair = first_pair + place

        def columns(base, pair=pair):
            return slice(base + pair * LANES, base + (pair + 1) * LANES)

        query = qkv[:, columns(0)].astype(jnp.float32)
        keys = qkv[:, columns(768)].astype(jnp.float32)
        value = qkv[:, columns(1536)].astype(jnp.float32)
        known = facts[...]
        tiles = (
            (jnp.where(low, query, pltpu.roll(keys, 64, axis=1)), jnp.where(low, value, known)),
            (jnp.where(low, pltpu.roll(query, 64, axis=1), keys), jnp.where(low, known, value)),
        )
        moved, to_tokens = [], []
        for h in range(2):
            back = place_matrix(order, 2 * pair + h)
            to_tokens.append(back)
            tile = jnp.concatenate([t.astype(jnp.bfloat16) for t in tiles[h]], axis=1)
            moved.append(dot_tn(back, tile))
        query_slots, key_slots, value_slots, codes, rows_of = [], [], [], [], []
        for h in range(2):
            both = moved[h][:, :LANES]
            query_slots.append(jnp.where(low, both, 0.0).astype(jnp.bfloat16))
            key_slots.append(pltpu.roll(both, 64, axis=1).astype(jnp.bfloat16))
            value_slots.append(moved[h][:, LANES:].astype(jnp.bfloat16))
            swapped[2 * place + h] = key_slots[h]
            values[2 * place + h] = value_slots[h]
            lane = 64 * (1 - h)
            code = moved[h][:, LANES + lane : LANES + lane + 1]
            row = dot_nt(pick[h], value_slots[h])[0:1]
            codes.append(jnp.where(code >= 32.0, code - 32.0, code))
            rows_of.append(row)
        scores = [
            [dot_nt(query_slots[h][b], key_slots[h][b]) for b in blocks] for h in range(2)
        ]
        found = []
        for h in range(2):
            outs = []
            for g, b in enumerate(blocks):
                allowed = (codes[h][b] == rows_of[h][:, b]) | itself
                value = jnp.where(allowed, scores[h][g] * scale, masked_score)
                value = jnp.exp(value - jnp.max(value, axis=1, keepdims=True))
                weights = value / jnp.sum(value, axis=1, keepdims=True)
                soft[2 * place + h, b, :] = weights
                outs.append(weights.astype(jnp.bfloat16))
            found.append(
                [dot(outs[g], value_slots[h][b]) for g, b in enumerate(blocks)]
            )
        result = None
        for h in range(2):
            value = jnp.concatenate(found[h], axis=0)
            value = jnp.where(low if h == 0 else jnp.logical_not(low), value, 0.0)
            value = dot(to_tokens[h], value.astype(jnp.bfloat16))
            result = value if result is None else result + value
        combined[:, columns(0)] = result.astype(jnp.bfloat16)


def attend(me, qkv, order, facts, first_pair, pairs, combined=None, after=()):
    length = qkv.shape[0]
    operands = [me, qkv, order, facts]
    if combined is not None:
        operands.append(combined)
    return call(
        functools.partial(attend_body, first_pair, pairs),
        [
            near_shape((2 * pairs, length, LANES)),
            near_shape((2 * pairs, length, LANES)),
            near_shape((2 * pairs, length, CLUSTER), jnp.float32),
            near_shape((length, 768)),
        ],
        operands,
        after=after,
        aliases={3: 3} if combined is not None else None,
        name="attend",
    )


def by_rows(first, count, step, body):
    for i in range(first, first + count, step):
        body(slice(i, i + step))


def mean(value):
    return jnp.mean(value, axis=1, keepdims=True)


def fold(value):
    return jnp.sum(value.reshape(value.shape[0] // 8, 8, value.shape[1]), axis=0)


def out_norm_body(me, combined, w_out, tokens, vectors, first_low, normal, inverse, total_ref):

    def rows_of(rows):
        value = total_ref[rows, :] + vectors[2:3] + tokens[rows, :].astype(jnp.float32)
        centred = value - mean(value)
        scale = lax.rsqrt(mean(centred * centred) + epsilon)
        norm = centred * scale
        normal[rows, :] = norm
        inverse[rows, :] = jnp.broadcast_to(scale, (scale.shape[0], LANES))
        first_low[rows, :] = (norm * vectors[3:4] + vectors[4:5]).astype(jnp.bfloat16)

    half = tokens.shape[0] // 2
    for first in (0, half):
        rows = slice(first, first + half)
        total_ref[rows, :] = dot(combined[rows, :], w_out[...])
        by_rows(first, half, 32, rows_of)


def out_norm(me, combined, w_out, tokens, vectors, after=()):
    n = tokens.shape[0]
    f = jnp.float32
    return call(
        out_norm_body,
        [near_shape((n, 768)), near_shape((n, 768), f), near_shape((n, LANES), f)],
        [me, combined, w_out, tokens, vectors],
        [pltpu.VMEM((n, 768), jnp.float32)],
        after=after,
        name="out_norm",
    )


def up_body(me, first_low, w_up, bias_up, activated, slope, send):
    width = w_up.shape[1] // 8
    for i in range(8):
        columns = slice(i * width, (i + 1) * width)
        hidden = dot(first_low[...], w_up[:, columns]) + bias_up[:, columns]
        half = 0.5 + 0.5 * lax.erf(hidden * (0.5**0.5))
        low = (hidden * half).astype(jnp.bfloat16)
        activated[:, columns] = low
        bell = jnp.exp(-0.5 * hidden * hidden) * (2.0 * math.pi) ** (-0.5)
        slope[:, columns] = (half + hidden * bell).astype(jnp.bfloat16)
    for i in range(8):
        k = me[0] ^ i

        @pl.when((k & 1) == 1)
        def _():
            there = pl.ds(pl.multiple_of((k >> 1) * width, LANES), width)
            send[:, there] = activated[:, i * width : (i + 1) * width]


def up(me, first_low, w_up, bias_up, after=()):
    n, width = first_low.shape[0], w_up.shape[1]
    return call(
        up_body,
        [near_shape((n, width)), near_shape((n, width)), shape_of((n, width // 2))],
        [me, first_low, w_up, bias_up],
        after=after,
        name="up",
    )


def down_norm_body(
    me, activated, turned, normal, vectors, out, feed_grad, second_grad, sums, feed, acc
):
    acc[...] = jnp.zeros_like(acc)

    def rows_of(rows):
        value = normal[rows, :] * vectors[3:4] + vectors[4:5] + feed[rows, :] + vectors[5:6]
        centred = value - mean(value)
        inverse = lax.rsqrt(mean(centred * centred) + epsilon)
        norm = centred * inverse
        out[rows, :] = (norm * vectors[6:7] + vectors[7:8]).astype(jnp.bfloat16)
        upstream = me.arrived(0)[rows, :]
        scaled = upstream * vectors[6:7]
        back = inverse * (scaled - mean(scaled) - norm * mean(scaled * norm))
        second_grad[rows, :] = back
        low = back.astype(jnp.bfloat16)
        feed_grad[rows, :] = low
        acc[0] += fold(low.astype(jnp.float32))
        acc[1] += fold(upstream * norm)
        acc[2] += fold(upstream)

    feed[...] = dot_nt(activated[...], turned[...])
    by_rows(0, out.shape[0], 32, rows_of)
    me.send(0)
    for i in range(3):
        sums[i : i + 1, :] = jnp.sum(acc[i], axis=0, keepdims=True)


def down_norm(me, activated, turned, normal, vectors, cotangent, after=()):
    n = cotangent.shape[0]
    return call(
        down_norm_body,
        [
            shape_of((n, 768)),
            near_shape((n, 768)),
            near_shape((n, 768), jnp.float32),
            near_shape((3, 768), jnp.float32),
        ],
        [me, cotangent, activated, turned, normal, vectors],
        [pltpu.VMEM((n, 768), jnp.float32), pltpu.VMEM((3, 8, 768), jnp.float32)],
        late=[None],
        far_outs={0: True},
        after=after,
        name="down_norm",
    )


def hidden_back_body(me, feed_grad, turned, slope, hidden_grad, sums):
    for i in range(hidden_grad.shape[1] // 256):
        columns = slice(i * 256, (i + 1) * 256)
        value = dot(feed_grad[...], turned[:, columns]) * slope[:, columns].astype(jnp.float32)
        low = value.astype(jnp.bfloat16)
        hidden_grad[:, columns] = low
        sums[:, columns] = jnp.sum(low.astype(jnp.float32), axis=0, keepdims=True)


def hidden_back(me, feed_grad, turned, slope, after=()):
    return call(
        hidden_back_body,
        [near_shape(slope.shape), near_shape((1, slope.shape[1]), jnp.float32)],
        [me, feed_grad, turned, slope],
        after=after,
        name="hidden_back",
    )


def first_back_body(
    me, hidden_grad, w_up, second_grad, normal, inverse, vectors, residual, low_out, left, right, sums, back,
    acc,
):
    acc[...] = jnp.zeros_like(acc)

    def rows_of(rows):
        upstream = back[rows, :] + second_grad[rows, :]
        norm = normal[rows, :]
        scaled = upstream * vectors[3:4]
        value = inverse[rows, 0:1] * (scaled - mean(scaled) - norm * mean(scaled * norm))
        residual[rows, :] = value
        low = value.astype(jnp.bfloat16)
        low_out[rows, :] = low
        left[rows, :] = low[:, :384]
        right[rows, :] = low[:, 384:]
        acc[0] += fold(low.astype(jnp.float32))
        acc[1] += fold(upstream * norm)
        acc[2] += fold(upstream)

    back[...] = dot_nt(hidden_grad[...], w_up[...])
    by_rows(0, normal.shape[0], 32, rows_of)
    for i in range(3):
        sums[i : i + 1, :] = jnp.sum(acc[i], axis=0, keepdims=True)


def first_back(me, hidden_grad, w_up, second_grad, normal, inverse, vectors, after=()):
    n = normal.shape[0]
    return call(
        first_back_body,
        [
            near_shape((n, 768), jnp.float32),
            near_shape((n, 768)),
            shape_of((n, 384)),
            shape_of((n, 384)),
            near_shape((3, 768), jnp.float32),
        ],
        [me, hidden_grad, w_up, second_grad, normal, inverse, vectors],
        [pltpu.VMEM((n, 768), jnp.float32), pltpu.VMEM((3, 8, 768), jnp.float32)],
        after=after,
        name="first_back",
    )


def attend_back_body(
    first_pair, pairs, me, attention_grad, w_out, order, swapped, values, soft, *refs
):
    grads, sums, upstream = refs[-3:]
    length = attention_grad.shape[0]
    groups = length // CLUSTER
    blocks = [slice(g * CLUSTER, (g + 1) * CLUSTER) for g in range(groups)]
    low = iota((length, LANES), 1) < 64
    low_rows = iota((CLUSTER, LANES), 1) < 64
    scale = HEAD_DIM ** (-0.5)
    mine = slice(first_pair * LANES, (first_pair + pairs) * LANES)
    upstream[...] = dot_nt(attention_grad[...], w_out[mine, :]).astype(jnp.bfloat16)

    for place in range(pairs):
        pair = first_pair + place

        def columns(base, pair=pair):
            return slice(base + pair * LANES, base + (pair + 1) * LANES)

        both = upstream[:, slice(place * LANES, (place + 1) * LANES)]
        to_tokens, moved = [], []
        for h in range(2):
            to_tokens.append(place_matrix(order, 2 * pair + h))
            value = dot_tn(to_tokens[h], both)
            value = jnp.where(low if h == 0 else jnp.logical_not(low), value, 0.0)
            moved.append(value.astype(jnp.bfloat16))
        back = []
        for h in range(2):
            kept = 2 * place + h
            keys = [swapped[kept, b, :] for b in blocks]
            weights = [soft[kept, b, :] for b in blocks]
            soft_grad = [dot_nt(moved[h][b], values[kept, b, :]) for b in blocks]
            value_grad = [
                dot_tn(weights[g].astype(jnp.bfloat16), moved[h][b]) for g, b in enumerate(blocks)
            ]
            score_grad = []
            for g in range(groups):
                middle = jnp.sum(soft_grad[g] * weights[g], axis=1, keepdims=True)
                score_grad.append((weights[g] * (soft_grad[g] - middle)).astype(jnp.bfloat16))
            query_grad = [dot(score_grad[g], keys[g]) for g in range(groups)]
            key_grad = [dot_tn(score_grad[g], keys[g]) for g in range(groups)]
            parts = [
                jnp.concatenate(
                    [
                        (jnp.where(low_rows, query_grad[g], key_grad[g]) * scale).astype(
                            jnp.bfloat16
                        ),
                        value_grad[g].astype(jnp.bfloat16),
                    ],
                    axis=1,
                )
                for g in range(groups)
            ]
            back.append(dot(to_tokens[h], jnp.concatenate(parts, axis=0)))
        first, second = back[0][:, :LANES], back[1][:, :LANES]
        query = jnp.where(low, first, pltpu.roll(second, 64, axis=1))
        keys = jnp.where(low, pltpu.roll(first, 64, axis=1), second)
        value = back[0][:, LANES:] + back[1][:, LANES:]
        grads[:, columns(0)] = query.astype(jnp.bfloat16)
        grads[:, columns(768)] = keys.astype(jnp.bfloat16)
        grads[:, columns(1536)] = value.astype(jnp.bfloat16)
        sums[0:1, columns(0)] = jnp.sum(query, axis=0, keepdims=True)
        sums[1:2, columns(0)] = jnp.sum(value, axis=0, keepdims=True)


def attend_back(
    me, attention_grad, w_out, order, kept, first_pair, pairs, before=(), after=()
):
    length = attention_grad.shape[0]
    return call(
        functools.partial(attend_back_body, first_pair, pairs),
        [near_shape((length, 2304)), near_shape((2, 768), jnp.float32)],
        [me, attention_grad, w_out, order, *kept, *before],
        [pltpu.VMEM((length, pairs * LANES), jnp.bfloat16)],
        after=after,
        aliases={6: 0, 7: 1} if before else None,
        name="attend_back",
    )


def tokens_back_body(me, grads, weights, residual, out):
    for c in range(3):
        columns = slice(c * 256, (c + 1) * 256)
        out[:, columns] = dot_nt(grads[...], weights[columns, :]) + residual[:, columns]
        me.send(0, (slice(None), columns))


def tokens_back(me, grads, weights, residual, after=()):
    return call(
        tokens_back_body,
        [shape_of(residual.shape, jnp.float32)],
        [me, grads, weights, residual],
        far_outs={0: True},
        sends=3,
        after=after,
        name="tokens_back",
    )


def local_block(
    tokens,
    w_qkv,
    bias_query,
    bias_value,
    w_out,
    bias_out,
    gain_one,
    shift_one,
    w_up,
    bias_up,
    w_down,
    bias_down,
    gain_two,
    shift_two,
    cluster_order,
    segment_ids,
    padding,
    cotangent,
):
    length = tokens.shape[0]
    me = None
    vector_list = [
        bias_query, bias_value, bias_out, gain_one, shift_one, bias_down, gain_two, shift_two
    ]
    order = cluster_order[0]
    facts = (segment_ids[0] + 32 * (1 - padding[0])).astype(jnp.float32)
    facts = jnp.broadcast_to(facts[:, None], (length, 128))

    def other(x):
        return swap(x, "dp", CORE)

    blocks_q = pack_q(me, w_qkv, vector_list, bias_up)
    far_z_q = swap(blocks_q[0], "mp", 2)
    blocks_rest = pack_rest(me, w_out, w_up, w_down, after=[blocks_q])
    block_ou, upper, lower, block_d = blocks_rest
    far_z_ou = swap(block_ou, "mp", 2)
    upper_x, lower_y = swap(upper, "dp", ALONG_X), swap(lower, "dp", ALONG_Y)
    tokens_turned = turn(me, tokens, after=[blocks_rest])
    spread = spread_d(me, block_d, upper_x, lower_y, after=[tokens_turned])
    upper, lower = spread
    upper_y, lower_x = swap(upper, "dp", ALONG_Y), swap(lower, "dp", ALONG_X)
    near_z_q = beside_two(
        me, blocks_q[1], far_z_q, after=[spread], cost=20 * MICROSECOND // 10
    )
    z_q = near_z_q[0], swap(near_z_q[0], "mp", 1)
    near_z_ou = beside_two(me, block_ou, far_z_ou, after=[near_z_q])
    z_ou = near_z_ou[0], swap(near_z_ou[0], "mp", 1)
    near_d = whole_d(me, upper, upper_y, lower, lower_x, after=[near_z_ou])
    z_q = tie(z_q, [near_d])
    near_q = [z_q[0], swap(z_q[0], "dp", ALONG_X), z_q[1], swap(z_q[1], "dp", ALONG_Y)]
    far_q = gather_far(me, near_q, after=[near_d])
    far_d = swap(near_d[0], "mp", 2)
    z_ou = tie(z_ou, [far_q])
    near_ou = [z_ou[0], swap(z_ou[0], "dp", ALONG_X), z_ou[1], swap(z_ou[1], "dp", ALONG_Y)]
    pairs_q = beside(
        me,
        [(x, (i // 2, i % 2)) for i, x in enumerate(far_q)],
        [(2, *far_q[0].shape)] * 2,
        (),
        "beside_far",
    )
    parts_q = list(pairs_q)
    parts_q = [*parts_q, *[other(x) for x in parts_q]]
    far_ou = gather_far(me, near_ou, after=[pairs_q], cost=5 * MICROSECOND // 10)
    both_d = beside_two(
        me, near_d[0], far_d, after=[far_ou], cost=82 * MICROSECOND // 10
    )
    z_d = swap(both_d[0], "mp", 1)
    projected = project(me, parts_q, tokens, after=[both_d])
    full_qkv, vectors, full_bias_up, qkv = projected

    pairs = PAIRS // 3

    def forward(part, before, after):
        return attend(
            me, qkv, order, facts, part * pairs, pairs, before, after=after
        )

    seen_a = forward(0, None, [projected])
    seen_b = forward(1, seen_a[-1], [seen_a])
    early_d = [other(x) for x in tie([near_d[0], far_d], [both_d])]
    far_ou = tie(far_ou, [seen_b, *early_d])
    seen_c = forward(2, seen_b[-1], far_ou[:1])
    combined = seen_c[-1]
    combined_turned = turn(me, combined)
    full_out, full_up = unpack_ou(me, gather_core(far_ou), after=[combined_turned])
    normed = out_norm(me, combined, full_out, tokens, vectors)
    first_low, normal, inverse = normed
    first_turned = turn(me, first_low)
    upper = up(me, first_low, full_up, full_bias_up, after=[first_turned])
    activated, slope, send_activated = upper
    sends = tie([combined_turned[0], first_turned[0], tokens_turned[0]], [upper])
    others = [other(x) for x in sends]
    (z_d,) = tie([z_d], [upper])
    unpacked = unpack_d(me, [both_d[0], z_d, *early_d, other(z_d)], after=others)
    others.insert(2, other(tie([send_activated], [unpacked])[0]))
    turned_down = unpacked[0]
    downed = down_norm(me, activated, turned_down, normal, vectors, cotangent)
    layer_out, feed_grad, second_grad, sums_two = downed
    other_tokens = others[3]

    other_feed = other(feed_grad)
    hidden = hidden_back(me, feed_grad, turned_down, slope, after=[downed])
    hidden_grad, sums_up = hidden
    (hidden_grad,) = tie([hidden_grad], [hidden, other_feed, others[2]])
    other_hidden = other(hidden_grad)
    grad_d = gradient_d(
        me, feed_grad, other_feed, activated, others[2], after=[hidden]
    )
    core_d = scatter_near(grad_d)
    first = first_back(
        me, hidden_grad, full_up, second_grad, normal, inverse, vectors, after=[grad_d]
    )
    residual_grad, attention_grad, *halves, sums_one = first
    halves = [other(x) for x in halves]

    def back(part, kept, before, after):
        return attend_back(
            me, attention_grad, full_out, order, kept,
            part * pairs, pairs, before, after,
        )

    grads_a = back(0, seen_a[:3], (), [first])
    grads_b = back(1, seen_b[:3], grads_a, [])
    grads_c = back(2, seen_c[:3], grads_b, halves)
    half_d = add_plane(me, core_d, after=[grads_c])
    plane_d = scatter_far(half_d)
    projected_grad, sums_bias = grads_c
    grad_vectors = all_sums(me, sums_bias, sums_one, sums_two, sums_up)
    projected_grad, grad_vectors = tie([projected_grad, grad_vectors], [half_d])
    other_grads = other(projected_grad), other(grad_vectors)
    grad_ou = gradient_ou(
        me,
        (combined_turned[1], others[0]),
        (first_turned[1], others[1]),
        (hidden_grad, other_hidden),
        (attention_grad, *halves),
        after=[half_d],
    )
    core_ou = scatter_near(grad_ou)
    last_d = add_last(
        me, plane_d, after=[grad_ou, other_grads[1]], cost=22 * MICROSECOND
    )
    z_d = scatter_z(last_d)
    grad_q = gradient_q(
        me, tokens_turned[1], other_tokens, projected_grad, other_grads[0], grad_vectors,
        other_grads[1], after=[last_d],
    )
    near_q = grad_q[0], swap(grad_q[1], "mp", 1)
    moved = tokens_back(me, projected_grad, full_qkv, residual_grad, after=[grad_q])
    grad_tokens = moved[0]
    near_d = add_z(me, z_d, after=[moved])
    sum_d = scatter_z_far(near_d)
    half_ou = add_plane(me, core_ou, after=[near_d], cost=4 * MICROSECOND)
    plane_ou = scatter_far(half_ou)
    last_ou = add_last(me, plane_ou, after=[half_ou])
    z_ou = scatter_z(last_ou)
    first_q = add_first(me, *near_q, after=[last_ou])
    core_q = scatter_near(first_q)
    half_q = add_plane(me, core_q, after=[first_q])
    plane_q = scatter_far(half_q)
    near_ou = add_z(me, z_ou, after=[half_q])
    sum_ou = scatter_z_far(near_ou)
    done_d = finish_d(me, sum_d, after=[near_ou])
    sum_q = scatter_z_far(add_both(me, plane_q, after=[done_d]))
    done_ou = finish_ou(me, sum_ou)
    shard_out, shard_up = done_ou
    shard_qkv, *shard_vectors = finish_q(me, sum_q, after=[done_ou])
    shard_down = done_d[0].T
    grad_list = [v.reshape(-1) for v in shard_vectors]
    return (
        layer_out,
        grad_tokens,
        shard_qkv,
        grad_list[0],
        grad_list[1],
        shard_out,
        grad_list[2],
        grad_list[3],
        grad_list[4],
        shard_up,
        grad_list[8],
        shard_down,
        grad_list[5],
        grad_list[6],
        grad_list[7],
    )


def solution(mesh):
    in_specs = (
        P(("dp", "mp"), None),
        P("dp", "mp"),
        P(("dp", "mp")),
        P(("dp", "mp")),
        P("dp", "mp"),
        P(("dp", "mp")),
        P(("dp", "mp")),
        P(("dp", "mp")),
        P("dp", "mp"),
        P(("dp", "mp")),
        P("dp", "mp"),
        P(("dp", "mp")),
        P(("dp", "mp")),
        P(("dp", "mp")),
        P(("dp", "mp"), None, None),
        P(("dp", "mp"), None),
        P(("dp", "mp"), None),
        P(("dp", "mp"), None),
    )
    out_specs = (
        P(("dp", "mp"), None),
        P(("dp", "mp"), None),
        P("dp", "mp"),
        P(("dp", "mp")),
        P(("dp", "mp")),
        P("dp", "mp"),
        P(("dp", "mp")),
        P(("dp", "mp")),
        P(("dp", "mp")),
        P("dp", "mp"),
        P(("dp", "mp")),
        P("dp", "mp"),
        P(("dp", "mp")),
        P(("dp", "mp")),
        P(("dp", "mp")),
    )
    blocks = mesh.shape["dp"] == 8 and mesh.shape["mp"] == 4
    local = local_block if blocks else local_general
    return jax.shard_map(local, mesh=mesh, in_specs=in_specs, out_specs=out_specs, check_vma=False)
```

```python
import functools
import math

import jax
import jax.numpy as jnp
from jax import lax
from jax.experimental import pallas as pl
from jax.experimental.pallas import tpu as pltpu
from jax.sharding import PartitionSpec as P

HEADS = 12
HEAD_DIM = 64
CLUSTER = 128


epsilon = 1e-12
masked_score = -1e30


def product(left_side, right_side):
    return jnp.dot(left_side, right_side, preferred_element_type=jnp.float32)


def times_back(left_side, right_side):
    return lax.dot_general(
        left_side, right_side, (((1,), (1,)), ((), ())), preferred_element_type=jnp.float32
    )


def outer_sum(left_side, right_side):
    return lax.dot_general(
        left_side, right_side, (((0,), (0,)), ((), ())), preferred_element_type=jnp.float32
    )


def norm_forward(hidden, norm_gain, norm_shift):
    average = jnp.mean(hidden, axis=-1, keepdims=True)
    centred = hidden - average
    variance = jnp.mean(centred * centred, axis=-1, keepdims=True)
    inverse = lax.rsqrt(variance + epsilon)
    normal = centred * inverse
    return (normal * norm_gain + norm_shift, normal, inverse)


def norm_backward(upstream, normal, inverse, norm_gain):
    scaled = upstream * norm_gain
    return inverse * (
        scaled
        - jnp.mean(scaled, axis=-1, keepdims=True)
        - normal * jnp.mean(scaled * normal, axis=-1, keepdims=True)
    )


def gelu_exact(inputs):
    return jax.nn.gelu(inputs, approximate=False)


def local_general(
    tokens,
    w_qkv,
    bias_query,
    bias_value,
    w_out,
    bias_out,
    gain_one,
    shift_one,
    w_up,
    bias_up,
    w_down,
    bias_down,
    gain_two,
    shift_two,
    cluster_order,
    segment_ids,
    padding,
    cotangent,
):
    model_width = HEADS * HEAD_DIM
    length = tokens.shape[0]
    groups = length // CLUSTER
    score_scale = HEAD_DIM ** (-0.5)
    vectors = jnp.stack(
        [bias_query, bias_value, bias_out, gain_one, shift_one, bias_down, gain_two, shift_two]
    ).astype(jnp.bfloat16)
    vector_up = bias_up.astype(jnp.bfloat16)[None, :]
    part_qkv = w_qkv.astype(jnp.bfloat16)
    part_out = w_out.astype(jnp.bfloat16)
    part_up = w_up.astype(jnp.bfloat16)
    part_down = w_down.astype(jnp.bfloat16)
    column_qkv, column_out, column_up, column_down, column_vectors, column_bias = (
        lax.all_gather(part_qkv, "mp", axis=1, tiled=True),
        lax.all_gather(part_out, "mp", axis=1, tiled=True),
        lax.all_gather(part_up, "mp", axis=1, tiled=True),
        lax.all_gather(part_down, "mp", axis=1, tiled=True),
        lax.all_gather(vectors, "mp", axis=1, tiled=True),
        lax.all_gather(vector_up, "mp", axis=1, tiled=True),
    )
    full_qkv, full_out, full_up, full_down, full_vectors, full_bias = (
        lax.all_gather(column_qkv, "dp", axis=0, tiled=True),
        lax.all_gather(column_out, "dp", axis=0, tiled=True),
        lax.all_gather(column_up, "dp", axis=0, tiled=True),
        lax.all_gather(column_down, "dp", axis=0, tiled=True),
        lax.all_gather(column_vectors, "dp", axis=1, tiled=True),
        lax.all_gather(column_bias, "dp", axis=1, tiled=True),
    )
    small_params = full_vectors.astype(jnp.float32)
    hidden_bias = full_bias[0].astype(jnp.float32)
    ordering = cluster_order[0]
    segment = segment_ids[0]
    present = padding[0]
    positions = jnp.arange(length, dtype=jnp.int32)
    placement = (ordering[:, :, None] == positions[None, None, :]).astype(jnp.bfloat16)

    def to_clusters(matrix):
        per_head = matrix.reshape(length, HEADS, HEAD_DIM)
        moved = jnp.einsum("hip,phd->hid", placement, per_head, preferred_element_type=jnp.float32)
        return moved.astype(jnp.bfloat16).reshape(HEADS, groups, CLUSTER, HEAD_DIM)

    def from_clusters(blocks):
        per_head = blocks.astype(jnp.bfloat16).reshape(HEADS, length, HEAD_DIM)
        moved = jnp.einsum("hip,hid->phd", placement, per_head, preferred_element_type=jnp.float32)
        return moved.astype(jnp.bfloat16).reshape(length, model_width)

    segment_blocks = jnp.take(segment, ordering).reshape(HEADS, groups, CLUSTER)
    present_blocks = jnp.take(present, ordering).reshape(HEADS, groups, CLUSTER)
    same_doc = segment_blocks[..., :, None] == segment_blocks[..., None, :]
    itself = jnp.eye(CLUSTER, dtype=bool)
    allowed = same_doc & ((present_blocks[..., None, :] == 1) | itself)

    def scores_of(query_blocks, key_blocks):
        raw_scores = (
            jnp.einsum(
                "hncd,hnmd->hncm", query_blocks, key_blocks, preferred_element_type=jnp.float32
            )
            * score_scale
        )
        return jnp.where(allowed, raw_scores, masked_score)

    projected = product(tokens, full_qkv)
    query = (projected[:, :model_width] + small_params[0]).astype(jnp.bfloat16)
    keys = projected[:, model_width : 2 * model_width].astype(jnp.bfloat16)
    values = (projected[:, 2 * model_width :] + small_params[1]).astype(jnp.bfloat16)
    query_blocks = to_clusters(query)
    key_blocks = to_clusters(keys)
    value_blocks = to_clusters(values)
    masked = scores_of(query_blocks, key_blocks)
    highest = jnp.max(masked, axis=-1, keepdims=True)
    exponent = jnp.exp(masked - highest)
    row_total = jnp.sum(exponent, axis=-1, keepdims=True)
    soft_weights = exponent / row_total
    log_total = highest + jnp.log(row_total)
    soft_low = soft_weights.astype(jnp.bfloat16)
    combined = from_clusters(
        jnp.einsum("hncm,hnmd->hncd", soft_low, value_blocks, preferred_element_type=jnp.float32)
    )
    attention = product(combined, full_out) + small_params[2]
    first_norm, first_normal, first_inverse = norm_forward(
        tokens.astype(jnp.float32) + attention, small_params[3], small_params[4]
    )
    first_low = first_norm.astype(jnp.bfloat16)
    hidden = product(first_low, full_up) + hidden_bias
    activated, gelu_pull = jax.vjp(gelu_exact, hidden)
    activated_low = activated.astype(jnp.bfloat16)
    feed_out = product(activated_low, full_down) + small_params[5]
    output, second_normal, second_inverse = norm_forward(
        first_norm + feed_out, small_params[6], small_params[7]
    )
    layer_out = output.astype(jnp.bfloat16)
    again_qkv, again_out, again_up, again_down = (
        lax.all_gather(part_qkv, "mp", axis=1, tiled=True),
        lax.all_gather(part_out, "mp", axis=1, tiled=True),
        lax.all_gather(part_up, "mp", axis=1, tiled=True),
        lax.all_gather(part_down, "mp", axis=1, tiled=True),
    )
    back_qkv, back_out, back_up, back_down = (
        lax.all_gather(again_qkv, "dp", axis=0, tiled=True),
        lax.all_gather(again_out, "dp", axis=0, tiled=True),
        lax.all_gather(again_up, "dp", axis=0, tiled=True),
        lax.all_gather(again_down, "dp", axis=0, tiled=True),
    )
    grad_gain_two = jnp.sum(cotangent * second_normal, axis=0)
    grad_shift_two = jnp.sum(cotangent, axis=0)
    second_grad = norm_backward(cotangent, second_normal, second_inverse, small_params[6])
    feed_grad = second_grad.astype(jnp.bfloat16)
    grad_bias_down = jnp.sum(feed_grad.astype(jnp.float32), axis=0)
    grad_w_down = outer_sum(activated_low, feed_grad)
    hidden_grad = gelu_pull(times_back(feed_grad, back_down))[0].astype(jnp.bfloat16)
    grad_bias_up = jnp.sum(hidden_grad.astype(jnp.float32), axis=0)
    grad_w_up = outer_sum(first_low, hidden_grad)
    first_grad = times_back(hidden_grad, back_up) + second_grad
    grad_gain_one = jnp.sum(first_grad * first_normal, axis=0)
    grad_shift_one = jnp.sum(first_grad, axis=0)
    residual_grad = norm_backward(first_grad, first_normal, first_inverse, small_params[3])
    attention_grad = residual_grad.astype(jnp.bfloat16)
    grad_bias_out = jnp.sum(attention_grad.astype(jnp.float32), axis=0)
    grad_w_out = outer_sum(combined, attention_grad)
    combined_grad = to_clusters(times_back(attention_grad, back_out).astype(jnp.bfloat16))
    masked_again = scores_of(query_blocks, key_blocks)
    soft_again = jnp.exp(masked_again - log_total)
    soft_again_low = soft_again.astype(jnp.bfloat16)
    value_sums = jnp.einsum(
        "hncm,hncd->hnmd", soft_again_low, combined_grad, preferred_element_type=jnp.float32
    )
    soft_grad = jnp.einsum(
        "hncd,hnmd->hncm", combined_grad, value_blocks, preferred_element_type=jnp.float32
    )
    score_grad = (
        soft_again * (soft_grad - jnp.sum(soft_grad * soft_again, axis=-1, keepdims=True))
    ).astype(jnp.bfloat16)
    query_sums = (
        jnp.einsum("hncm,hnmd->hncd", score_grad, key_blocks, preferred_element_type=jnp.float32)
        * score_scale
    )
    key_sums = (
        jnp.einsum("hncm,hncd->hnmd", score_grad, query_blocks, preferred_element_type=jnp.float32)
        * score_scale
    )
    query_grad = from_clusters(query_sums)
    key_grad = from_clusters(key_sums)
    value_grad = from_clusters(value_sums)
    grad_bias_query = jnp.sum(query_grad.astype(jnp.float32), axis=0)
    grad_bias_value = jnp.sum(value_grad.astype(jnp.float32), axis=0)
    projected_grad = jnp.concatenate([query_grad, key_grad, value_grad], axis=1)
    grad_w_qkv = outer_sum(tokens, projected_grad)
    grad_tokens = times_back(projected_grad, back_qkv) + residual_grad
    grad_vectors = jnp.stack(
        [
            grad_bias_query,
            grad_bias_value,
            grad_bias_out,
            grad_gain_one,
            grad_shift_one,
            grad_bias_down,
            grad_gain_two,
            grad_shift_two,
        ]
    )
    grad_up_row = grad_bias_up[None, :]
    row_qkv, row_out, row_up, row_down, row_vectors, row_bias = (
        lax.psum_scatter(
            grad_w_qkv.astype(jnp.bfloat16), "dp", scatter_dimension=0, tiled=True
        ).astype(jnp.float32),
        lax.psum_scatter(
            grad_w_out.astype(jnp.bfloat16), "dp", scatter_dimension=0, tiled=True
        ).astype(jnp.float32),
        lax.psum_scatter(
            grad_w_up.astype(jnp.bfloat16), "dp", scatter_dimension=0, tiled=True
        ).astype(jnp.float32),
        lax.psum_scatter(
            grad_w_down.astype(jnp.bfloat16), "dp", scatter_dimension=0, tiled=True
        ).astype(jnp.float32),
        lax.psum_scatter(
            grad_vectors.astype(jnp.bfloat16), "dp", scatter_dimension=1, tiled=True
        ).astype(jnp.float32),
        lax.psum_scatter(
            grad_up_row.astype(jnp.bfloat16), "dp", scatter_dimension=1, tiled=True
        ).astype(jnp.float32),
    )
    shard_qkv, shard_out, shard_up, shard_down, shard_vectors, shard_bias = (
        lax.psum_scatter(
            row_qkv.astype(jnp.bfloat16), "mp", scatter_dimension=1, tiled=True
        ).astype(jnp.float32),
        lax.psum_scatter(
            row_out.astype(jnp.bfloat16), "mp", scatter_dimension=1, tiled=True
        ).astype(jnp.float32),
        lax.psum_scatter(row_up.astype(jnp.bfloat16), "mp", scatter_dimension=1, tiled=True).astype(
            jnp.float32
        ),
        lax.psum_scatter(
            row_down.astype(jnp.bfloat16), "mp", scatter_dimension=1, tiled=True
        ).astype(jnp.float32),
        lax.psum_scatter(
            row_vectors.astype(jnp.bfloat16), "mp", scatter_dimension=1, tiled=True
        ).astype(jnp.float32),
        lax.psum_scatter(
            row_bias.astype(jnp.bfloat16), "mp", scatter_dimension=1, tiled=True
        ).astype(jnp.float32),
    )
    return (
        layer_out,
        grad_tokens,
        shard_qkv,
        shard_vectors[0],
        shard_vectors[1],
        shard_out,
        shard_vectors[2],
        shard_vectors[3],
        shard_vectors[4],
        shard_up,
        shard_bias[0],
        shard_down,
        shard_vectors[5],
        shard_vectors[6],
        shard_vectors[7],
    )


LANES = 128
QKV_ROWS = 96
UP_TILES = 6
DOWN_TILES = 3
PACK_Q = 4 * QKV_ROWS + QKV_ROWS // 2 + 16
PACK_OU = QKV_ROWS + QKV_ROWS // 2 + UP_TILES * QKV_ROWS
PACK_D = DOWN_TILES * 192
VECTOR_ROW = 4 * QKV_ROWS + QKV_ROWS // 2
UP_ROW = QKV_ROWS + QKV_ROWS // 2


def whole():
    return pl.BlockSpec(memory_space=pltpu.VMEM)


def far():
    return pl.BlockSpec(memory_space=pltpu.HBM)


def kept_far(arrays):
    return [pltpu.with_memory_space_constraint(x, pltpu.HBM) for x in arrays]


def near(x):
    return pltpu.with_memory_space_constraint(x, pltpu.VMEM)


def near_shape(shape, dtype=jnp.bfloat16):
    return pltpu.VMEM(shape, dtype)


def waited(after):
    return [kept_far([x.token])[0] if isinstance(x, Results) else x for x in after]


def anywhere(after):
    return [far() if isinstance(x, Results) else pl.BlockSpec(memory_space=pl.ANY) for x in after]


class Results(list):
    token = None


TOKEN = pltpu.HBM((8, 128), jnp.float32)


def place():
    return lax.axis_index("dp"), lax.axis_index("mp")


SHORT = pl.CostEstimate(flops=1, bytes_accessed=1, transcendentals=0)
MICROSECOND = 1_153_000_000


class Place(tuple):
    def arrived(self, index, part=None):
        copies, here = self.late[index]
        for i in range(len(copies)) if part is None else [part]:
            if copies[i] is not None:
                copies[i].wait()
                copies[i] = None
        return here

    def send(self, index, where=None, source=None):
        here, there = self.far[index]
        source = here if source is None else source
        if where is not None:
            source, there = source.at[where], there.at[where]
        copy = pltpu.make_async_copy(source, there, self.sems.at[len(self.sent)])
        copy.start()
        self.sent.append(copy)


def call(
    body, out_shapes, operands, scratch=(), staged=0, late=(), far_outs=None, sends=None, after=(),
    aliases=None, vmem=10, cost=0, name=None,
):
    operands = operands[1:]
    far_outs = far_outs or {}
    sends = len(far_outs) if sends is None else sends
    count, outs, copied = len(operands), len(out_shapes), staged + len(late)
    spread = [(0, 1)] * staged + [x or (0, 1) for x in late]
    starts = [sum(n for _, n in spread[:i]) for i in range(copied)]

    def with_copies(*refs):
        sources, rest = refs[:copied], refs[copied:count]
        results = list(refs[count + len(after) : count + len(after) + outs])
        own = refs[count + len(after) + outs + 1 :]
        mine, own = own[: len(scratch)], own[len(scratch) :]
        arrived, own = own[:copied], list(own[copied:])
        me = Place(place())
        me.sent, me.far = [], {}
        if copied:
            sem = own.pop(0)
            copies = []
            for source, here, (axis, parts), start in zip(sources, arrived, spread, starts):
                size = here.shape[axis] // parts
                copies.append([])
                for i in range(parts):
                    cut = (slice(None),) * axis + (slice(i * size, (i + 1) * size),)
                    copies[-1].append(
                        pltpu.make_async_copy(source.at[cut], here.at[cut], sem.at[start + i])
                    )
            for copy in sum(copies, []):
                copy.start()
            for (copy,) in copies[:staged]:
                copy.wait()
            me.late = list(zip(copies[staged:], arrived[staged:]))
        if far_outs:
            me.sems = own.pop(0)
            for index, has_room in far_outs.items():
                here = own.pop(0) if has_room else None
                me.far[index] = (here, results[index])
                results[index] = here
        body(me, *arrived[:staged], *rest, *results, *mine)
        for copy in me.sent:
            copy.wait()

    room = [pltpu.VMEM(x.shape, x.dtype) for x in operands[:copied]]
    if copied:
        room.append(pltpu.SemaphoreType.DMA((sum(n for _, n in spread),)))
    if far_outs:
        room.append(pltpu.SemaphoreType.DMA((sends,)))
        room += [pltpu.VMEM(out_shapes[i].shape, out_shapes[i].dtype) for i in far_outs if far_outs[i]]
    given = [
        pltpu.HBM(x.shape, x.dtype) if i in far_outs else x for i, x in enumerate(out_shapes)
    ]
    *results, token = pl.pallas_call(
        with_copies,
        out_shape=[*given, TOKEN],
        in_specs=[pl.BlockSpec(memory_space=pl.ANY)] * staged
        + [far()] * len(late)
        + [whole()] * (count - copied)
        + anywhere(after),
        out_specs=[far() if i in far_outs else whole() for i in range(outs)] + [far()],
        scratch_shapes=list(scratch) + room,
        input_output_aliases=aliases or {},
        compiler_params=pltpu.CompilerParams(vmem_limit_bytes=vmem * 1024 * 1024),
        cost_estimate=SHORT if not cost else pl.CostEstimate(cost, 1, 0),
        name=name,
    )(
        *operands[:staged],
        *kept_far(operands[staged:copied]),
        *operands[copied:],
        *waited(after),
    )
    results = Results(results)
    results.token = token
    return results


def tie(arrays, after):
    count = len(arrays)

    def body(*refs):
        pass

    return pl.pallas_call(
        body,
        out_shape=[shape_of(x.shape, x.dtype) for x in arrays],
        in_specs=[pl.BlockSpec(memory_space=pl.ANY)] * count + anywhere(after),
        out_specs=[pl.BlockSpec(memory_space=pl.ANY)] * count,
        input_output_aliases={i: i for i in range(count)},
        compiler_params=pltpu.CompilerParams(vmem_limit_bytes=1024 * 1024),
        cost_estimate=SHORT,
        name="tie",
    )(*arrays, *waited(after))


def shape_of(shape, dtype=jnp.bfloat16):
    return jax.ShapeDtypeStruct(shape, dtype)


def halves_beside(single):
    half = single.shape[0] // 2
    return jnp.concatenate([single[:half], single[half:]], axis=1)


def pack_columns(odd, low, tiles, base, target):
    @pl.when(odd)
    def _():
        for t in range(tiles):
            target[base + t * 96 : base + (t + 1) * 96, :] = low[
                :, 64 + t * LANES : 64 + (t + 1) * LANES
            ].astype(jnp.bfloat16)
        target[base + tiles * 96 : base + tiles * 96 + 48, :] = halves_beside(low[:, :64]).astype(
            jnp.bfloat16
        )

    @pl.when(jnp.logical_not(odd))
    def _():
        for t in range(tiles):
            target[base + t * 96 : base + (t + 1) * 96, :] = low[
                :, t * LANES : (t + 1) * LANES
            ].astype(jnp.bfloat16)
        target[base + tiles * 96 : base + tiles * 96 + 48, :] = halves_beside(
            low[:, tiles * LANES : tiles * LANES + 64]
        ).astype(jnp.bfloat16)


def pack_q_body(me, *refs):
    w_qkv, vectors, target, own = refs[0], refs[1:10], refs[10], refs[11]
    pack_columns(lax.rem(me[1], 2) == 1, w_qkv[...], 4, 0, target)
    rows = lax.broadcasted_iota(jnp.int32, (16, LANES), 0)
    tail = jnp.zeros((16, LANES), jnp.float32)
    for v in range(9):
        value = vectors[v][...]
        wide = jnp.concatenate(
            [value, jnp.zeros((1, LANES - value.shape[1]), jnp.float32)], axis=1
        )
        tail = jnp.where(rows == v, jnp.broadcast_to(wide, (16, LANES)), tail)
    target[VECTOR_ROW:, :] = tail.astype(jnp.bfloat16)
    own[...] = target[...]


def pack_q(me, w_qkv, vectors, bias_up):
    small = [v.reshape(1, -1) for v in (*vectors, bias_up)]
    return call(
        pack_q_body, [near_shape((PACK_Q, LANES))] * 2, [me, *kept_far([w_qkv, *small])], staged=10,
        name="pack_q",
    )


def pack_rest_body(me, w_out, w_up, w_down, to_ou, upper_d, lower_d, to_d):
    for t in range(DOWN_TILES):
        to_d[t * 192 : (t + 1) * 192, :] = w_down[:, t * LANES : (t + 1) * LANES].astype(
            jnp.bfloat16
        )
    upper_d[...] = to_d[: PACK_D // 2, :]
    lower_d[...] = to_d[PACK_D // 2 :, :]
    pack_columns(lax.rem(me[1], 2) == 1, w_out[...], 1, 0, to_ou)
    for t in range(UP_TILES):
        to_ou[UP_ROW + t * 96 : UP_ROW + (t + 1) * 96, :] = w_up[
            :, t * LANES : (t + 1) * LANES
        ].astype(jnp.bfloat16)


def pack_rest(me, w_out, w_up, w_down, after):
    return call(
        pack_rest_body,
        [
            near_shape((PACK_OU, LANES)),
            near_shape((PACK_D // 2, LANES)),
            near_shape((PACK_D // 2, LANES)),
            near_shape((PACK_D, LANES)),
        ],
        [me, *kept_far([w_out, w_up, w_down.T])],
        staged=3,
        after=after,
        name="pack_rest",
    )


def swap(x, axis, bit):
    size = lax.axis_size(axis)
    return lax.ppermute(x, axis, [(i, i ^ bit) for i in range(size)])


CORE, ALONG_X, ALONG_Y = 1, 2, 4


def gather_z(x, own=None):
    return [x if own is None else own] + [swap(x, "mp", k) for k in (1, 2, 3)]


def beside(me, groups, shapes, after=(), name="beside", cost=0):
    sources = []
    for x, _ in groups:
        if all(x is not y for y in sources):
            sources.append(x)

    def body(me, *refs):
        for x, (index, where) in groups:
            source = refs[next(n for n, y in enumerate(sources) if x is y)]
            refs[len(sources) + index][where] = source[...]

    return call(body, [shape_of(s) for s in shapes], [me, *sources], after=after, name=name, cost=cost)


def beside_two(me, a, b, after=(), cost=0):
    return beside(me, [(a, (0, 0)), (b, (0, 1))], [(2, *a.shape)], after, "beside_two", cost)


def gather_near(me, parts, after=()):
    shape = (2, *parts[0].shape)
    found = beside(
        me,
        [(parts[0], (0, 0)), (parts[1], (0, 1)), (parts[2], (1, 0)), (parts[3], (1, 1))],
        [shape, shape],
        after,
        "beside_z",
    )
    first, second = found
    result = Results([first, swap(first, "dp", ALONG_X), second, swap(second, "dp", ALONG_Y)])
    result.token = found.token
    return result


def gather_far(me, parts, after=(), cost=0):
    shape = (2, *parts[0].shape)
    groups = [(parts[i], (i // 2, i % 2)) for i in range(4)]
    found = beside(me, groups, [shape, shape], after, "beside_near", cost)
    first, second = found
    result = Results([first, second, swap(first, "dp", ALONG_Y), swap(second, "dp", ALONG_X)])
    result.token = found.token
    return result


def gather_core(parts):
    return list(parts) + [swap(x, "dp", CORE) for x in parts]


def gathered_blocks(me, refs, steps=(1, 2)):
    for index, ref in enumerate(refs):
        core, far, half = index // 4, index % 4 // 2, index % 2
        for mid in range(2):
            for low in range(2):
                kx, ky = (far, mid) if half else (mid, far)
                along_z = steps[0] * low + steps[1] * half
                yield me[0] ^ (core + 2 * kx + 4 * ky), me[1] ^ along_z, ref.at[mid, low]


def split_pairs(refs):
    return [ref.at[i] for ref in refs for i in range(2)]


def place_columns(block, base, tiles, dp, mp, width, weights, singles):
    start = pl.multiple_of(mp * width + 64 * lax.rem(mp, 2), LANES)
    rows = pl.ds(pl.multiple_of(dp * 96, 32), 96)
    for t in range(tiles):
        weights[rows, pl.ds(pl.multiple_of(start + t * LANES, LANES), LANES)] = block[
            base + t * 96 : base + (t + 1) * 96, :
        ]
    singles[mp, pl.ds(pl.multiple_of(dp * 48, 16), 48), :] = block[
        base + tiles * 96 : base + tiles * 96 + 48, :
    ]


def place_singles(width, weights, singles):
    for pair in range(2):
        column = 2 * pair * width + (width // LANES) * LANES
        for dp in range(8):
            left = singles[2 * pair, dp * 48 : (dp + 1) * 48, :].astype(jnp.float32)
            right = singles[2 * pair + 1, dp * 48 : (dp + 1) * 48, :].astype(jnp.float32)
            upper = jnp.concatenate([left[:, :64], right[:, :64]], axis=1)
            lower = jnp.concatenate([left[:, 64:], right[:, 64:]], axis=1)
            weights[dp * 96 : dp * 96 + 48, column : column + LANES] = upper.astype(jnp.bfloat16)
            weights[dp * 96 + 48 : (dp + 1) * 96, column : column + LANES] = lower.astype(
                jnp.bfloat16
            )


def unpack_q_body(me, *refs):
    blocks, weights, vectors, bias_up, singles, tails = refs[:8], *refs[8:]
    for dp, mp, block in gathered_blocks(me, blocks, (2, 1)):
        place_columns(block, 0, 4, dp, mp, 576, weights, singles)
        tails[dp * 4 + mp] = block[VECTOR_ROW:, :].astype(jnp.float32)
    place_singles(576, weights, singles)
    lane = lax.broadcasted_iota(jnp.int32, (16, LANES), 1)

    def spread(width, count):
        found = [jnp.zeros((16, LANES), jnp.float32) for _ in range(count)]
        for device in range(32):
            start, tile = device * width % LANES, device * width // LANES
            piece = tails[device]
            moved = pltpu.roll(piece, start, axis=1) if start else piece
            found[tile] = jnp.where((lane >= start) & (lane < start + width), moved, found[tile])
            if start + width > LANES:
                found[tile + 1] = jnp.where(lane < start + width - LANES, moved, found[tile + 1])
        return found

    for t, value in enumerate(spread(24, 6)):
        vectors[:, t * LANES : (t + 1) * LANES] = value[:8]
    for t, value in enumerate(spread(96, 24)):
        bias_up[:, t * LANES : (t + 1) * LANES] = value[8:9]


def unpack_ou_body(me, *refs):
    blocks, w_out, w_up, singles = refs[:8], *refs[8:]
    for dp, mp, block in gathered_blocks(me, blocks, (2, 1)):
        place_columns(block, 0, 1, dp, mp, 192, w_out, singles)
        rows = pl.ds(pl.multiple_of(dp * 96, 32), 96)
        for t in range(UP_TILES):
            w_up[rows, pl.ds(pl.multiple_of(mp * 768 + t * LANES, LANES), LANES)] = block[
                UP_ROW + t * 96 : UP_ROW + (t + 1) * 96, :
            ]
    place_singles(192, w_out, singles)


def unpack_ou(me, parts, after=()):
    return call(
        unpack_ou_body,
        [near_shape((768, 768)), near_shape((768, 3072))],
        [me, *parts],
        [pltpu.VMEM((4, 384, LANES), jnp.bfloat16)],
        after=after,
        name="unpack_ou",
    )


def spread_d_body(me, mine, upper_x, lower_y, upper, lower):
    half = PACK_D // 2
    upper[0], upper[1] = mine[:half, :], upper_x[...]
    lower[0], lower[1] = mine[half:, :], lower_y[...]


def spread_d(me, mine, upper_x, lower_y, after=()):
    shape = near_shape((2, PACK_D // 2, LANES))
    return call(
        spread_d_body, [shape, shape], [me, mine, upper_x, lower_y], after=after, name="spread_d"
    )


def whole_d_body(me, upper, upper_y, lower, lower_x, out):
    half = PACK_D // 2
    for kx in range(2):
        for ky in range(2):
            out[2 * ky + kx, :half, :] = (upper_y if ky else upper)[kx]
            out[2 * ky + kx, half:, :] = (lower_x if kx else lower)[ky]


def whole_d(me, upper, upper_y, lower, lower_x, after=()):
    return call(
        whole_d_body, [near_shape((4, PACK_D, LANES))], [me, upper, upper_y, lower, lower_x],
        after=after, name="whole_d",
    )


def unpack_d_body(me, both, both_z, other, other_far, other_z, turned):
    for core in range(2):
        for kz in range(4):
            for plane in range(4):
                if core and kz % 2 == 0:
                    block = (other_far if kz else other).at[plane]
                else:
                    source = (other_z if core else both_z) if kz % 2 else both
                    block = source.at[kz // 2, plane]
                dp, mp = me[0] ^ (2 * plane + core), me[1] ^ kz
                rows = pl.ds(pl.multiple_of(mp * 192, 64), 192)
                for t in range(DOWN_TILES):
                    turned[rows, pl.ds(pl.multiple_of(dp * 384 + t * LANES, LANES), LANES)] = block[
                        t * 192 : (t + 1) * 192, :
                    ]


def unpack_d(me, parts, after=()):
    return call(
        unpack_d_body, [near_shape((768, 3072))], [me, *parts], after=after, name="unpack_d"
    )


def turn_body(me, source, send, keep, turned):
    value = source[...].T
    for dp in range(8):
        k = me[0] ^ dp
        slot = (1 - (k & 1)) * 4 + (k >> 1)
        turned[pl.ds(pl.multiple_of(slot * 96, 32), 96), :] = value[dp * 96 : (dp + 1) * 96, :]
    send[...] = turned[:384, :]
    keep[...] = turned[384:, :]


def turn(me, source, after=()):
    n = source.shape[0]
    return call(
        turn_body,
        [shape_of((384, n)), near_shape((384, n))],
        [me, source],
        [pltpu.VMEM((768, n), jnp.bfloat16)],
        after=after,
        name="turn",
    )


def dot(a, b):
    return jnp.dot(a, b, preferred_element_type=jnp.float32)


def dot_nt(a, b):
    return lax.dot_general(a, b, (((1,), (1,)), ((), ())), preferred_element_type=jnp.float32)


def dot_tn(a, b):
    return lax.dot_general(a, b, (((0,), (0,)), ((), ())), preferred_element_type=jnp.float32)


def part_of(targets, kp, mp):
    ky, kx = kp // 2, kp % 2
    if mp < 2:
        return targets[ky].at[kx, mp]
    return targets[2 + kx].at[ky, mp - 2]


def store_columns(target, base, tiles, first, value):
    for t in range(tiles):
        target[base + t * 96 : base + (t + 1) * 96, :] = value[
            :, first + t * LANES : first + (t + 1) * LANES
        ].astype(jnp.bfloat16)


def store_single(target, base, odd, value):
    upper, lower = value[:48], value[48:]
    low_lanes = lax.broadcasted_iota(jnp.int32, (48, LANES), 1) < 64
    if odd:
        both = jnp.where(low_lanes, pltpu.roll(upper, 64, axis=1), lower)
    else:
        both = jnp.where(low_lanes, upper, pltpu.roll(lower, 64, axis=1))
    target[base : base + 48, :] = both.astype(jnp.bfloat16)


def column_gradient(lefts, rights, targets, base, tiles, width):
    def product(columns):
        return dot(lefts[0], rights[0][:, columns]) + dot(lefts[1], rights[1][:, columns])

    for pair in range(2):
        first = 2 * pair * width
        middle = first + tiles * LANES
        for begin, mp in ((first, 2 * pair), (middle + LANES, 2 * pair + 1)):
            value = product(slice(begin, begin + tiles * LANES))
            for kp in range(4):
                store_columns(
                    targets(kp, mp), base, tiles, 0, value[kp * 96 : (kp + 1) * 96]
                )
        value = product(slice(middle, middle + LANES))
        for kp in range(4):
            for mp in (2 * pair, 2 * pair + 1):
                store_single(
                    targets(kp, mp), base + tiles * 96, mp % 2,
                    value[kp * 96 : (kp + 1) * 96],
                )


def parts_shape(rows):
    return [near_shape((2, 2, rows, LANES)), shape_of((2, 2, rows, LANES))] * 2


def gradient_q_body(
    me, keep, other_keep, grads, other_grads, vectors, other_vectors, mine, send, room
):
    targets = lambda kp, mp: room.at[me[1] ^ mp, kp]
    lefts, rights = (keep[...], other_keep[...]), (grads, other_grads)
    column_gradient(lefts, rights, targets, 0, 4, 576)
    sums = vectors[...] + other_vectors[...]
    lane = lax.broadcasted_iota(jnp.int32, (16, LANES), 1)
    rows = lax.broadcasted_iota(jnp.int32, (16, LANES), 0)

    def cut(source, width, device):
        start, tile = device * width % LANES, device * width // LANES
        value = source[:, tile * LANES : (tile + 1) * LANES]
        moved = pltpu.roll(value, LANES - start, axis=1) if start else value
        if start + width > LANES:
            after = source[:, (tile + 1) * LANES : (tile + 2) * LANES]
            after = pltpu.roll(after, LANES - start, axis=1)
            here = lax.broadcasted_iota(jnp.int32, value.shape, 1)
            moved = jnp.where(here < LANES - start, moved, after)
        return moved

    for kp in range(4):
        plane = (me[0] >> 1) ^ kp
        for mp in range(4):
            tail = jnp.zeros((16, LANES), jnp.float32)
            for dp in range(8):
                device = dp * 4 + mp
                row = 8 + device // 8
                up = jnp.broadcast_to(cut(sums[row : row + 1], 96, device % 8), (8, LANES))
                found = jnp.concatenate([cut(sums[:8], 24, device), up], axis=0)
                owner = dp == 2 * plane + (me[0] & 1)
                tail = jnp.where(owner, found, tail)
            tail = jnp.where((rows < 8) & (lane >= 24), 0.0, tail).astype(jnp.bfloat16)
            targets(kp, mp)[VECTOR_ROW:, :] = tail
    for kz in range(4):
        (send if kz % 2 else mine)[kz // 2] = room[kz]


def gradient_q(me, keep, other_keep, grads, other_grads, vectors, other_vectors, after=()):
    return call(
        gradient_q_body,
        [near_shape((2, 4, PACK_Q, LANES)), shape_of((2, 4, PACK_Q, LANES))],
        [me, keep, other_keep, grads, other_grads, vectors, other_vectors],
        [pltpu.VMEM((4, 4, PACK_Q, LANES), jnp.bfloat16)],
        after=after,
        name="gradient_q",
    )


def gradient_ou_body(me, *refs):
    combined, first_low, hidden_grad = (refs[i : i + 2] for i in (0, 2, 4))
    attention_grad, room = (refs[6], refs[13]), refs[13]
    targets = functools.partial(part_of, refs[9:13])
    room[:, :384] = refs[7][...]
    room[:, 384:] = refs[8][...]
    column_gradient([x[...] for x in combined], attention_grad, targets, 0, 1, 192)
    lefts = [x[...] for x in first_low]
    for mp in range(4):
        columns = slice(mp * 768, (mp + 1) * 768)
        value = dot(lefts[0], hidden_grad[0][:, columns])
        value = value + dot(lefts[1], hidden_grad[1][:, columns])
        for kp in range(4):
            store_columns(
                targets(kp, mp), UP_ROW, UP_TILES, 0, value[kp * 96 : (kp + 1) * 96]
            )


def gradient_ou(me, combined, first_low, hidden_grad, attention_grad, after=()):
    return call(
        gradient_ou_body,
        parts_shape(PACK_OU),
        [me, *combined, *first_low, *hidden_grad, *attention_grad],
        [pltpu.VMEM(attention_grad[0].shape, jnp.bfloat16)],
        after=after,
        name="gradient_ou",
    )


def gradient_d_body(me, feed_grad, other_feed_grad, activated, other_activated, *refs):
    targets, turned, other_turned = refs[:4], refs[4], refs[5]
    turned[...] = feed_grad[...].T
    other_turned[...] = other_feed_grad[...].T
    for kp in range(4):
        dp = me[0] ^ (2 * kp)
        block = activated[:, pl.ds(pl.multiple_of(dp * 384, LANES), 384)]
        value = dot(turned[...], block)
        value = value + dot(other_turned[...], other_activated[:, kp * 384 : (kp + 1) * 384])
        for mp in range(4):
            target = part_of(targets, kp, mp)
            for t in range(DOWN_TILES):
                target[t * 192 : (t + 1) * 192, :] = value[
                    mp * 192 : (mp + 1) * 192, t * LANES : (t + 1) * LANES
                ].astype(jnp.bfloat16)


def gradient_d(me, feed_grad, other_feed_grad, activated, other_activated, after=()):
    return call(
        gradient_d_body,
        parts_shape(PACK_D),
        [me, feed_grad, other_feed_grad, activated, other_activated],
        [pltpu.VMEM((768, feed_grad.shape[0]), jnp.bfloat16)] * 2,
        after=after,
        name="gradient_d",
    )


def sums_body(me, bias, one, two, up, out):
    out[0:2, :], out[2:5, :], out[5:8, :] = bias[...], one[...], two[...]
    for i in range(4):
        out[8 + i : 9 + i, :] = up[:, i * 768 : (i + 1) * 768]


def all_sums(me, *sums):
    return call(sums_body, [shape_of((12, 768), jnp.float32)], [me, *sums], name="sums")[0]


def add(a, b):
    return a.astype(jnp.float32) + b.astype(jnp.float32)


def add_plane_body(me, first, first_in, second, second_in, *outs):
    for keep, send, a, b in ((*outs[:2], first, first_in), (*outs[2:], second, second_in)):
        keep[...] = add(a[0], b[0]).astype(jnp.bfloat16)
        send[...] = add(a[1], b[1]).astype(jnp.bfloat16)


def add_last_body(me, first, first_in, second, second_in, *refs):
    keep, send, room = refs
    for mp in range(4):
        a, b = (first, first_in) if mp < 2 else (second, second_in)
        room[me[1] ^ mp] = add(a[mp % 2], b[mp % 2]).astype(jnp.bfloat16)
    for k in range(4):
        (send if k % 2 else keep)[k // 2] = room[k]


def add_first_body(me, mine, arrived, *outs):
    for kp in range(4):
        ky, kx = kp // 2, kp % 2
        outs[ky][kx] = add(mine[0, kp], arrived[0, kp]).astype(jnp.bfloat16)
        outs[2 + kx][ky] = add(mine[1, kp], arrived[1, kp]).astype(jnp.bfloat16)


def add_first(me, mine, arrived, after=()):
    rows = mine.shape[2]
    return call(
        add_first_body,
        [near_shape((2, rows, LANES)), shape_of((2, rows, LANES))] * 2,
        [me, mine, arrived],
        after=after,
        name="add_first",
    )


def add_both_body(me, first, first_in, second, second_in, keep, send):
    keep[...] = add(first[...], first_in[...])
    send[...] = add(second[...], second_in[...]).astype(jnp.bfloat16)


def add_both(me, parts, after=()):
    shape = parts[0].shape
    return call(
        add_both_body,
        [near_shape(shape, jnp.float32), shape_of(shape)],
        [me, *parts],
        after=after,
        name="add_both",
    )


def add_z_body(me, mine, arrived, keep, send):
    keep[...] = add(mine[0], arrived[0])
    send[...] = add(mine[1], arrived[1]).astype(jnp.bfloat16)


def scatter_near(parts):
    first, first_send, second, second_send = parts
    return first, swap(first_send, "dp", ALONG_Y), second, swap(second_send, "dp", ALONG_X)


def add_plane(me, parts, after=(), cost=0):
    shape = parts[0].shape[1:]
    return call(
        add_plane_body,
        [near_shape(shape), shape_of(shape)] * 2,
        [me, *parts],
        after=after,
        cost=cost,
        name="add_plane",
    )


def scatter_far(parts):
    first, first_send, second, second_send = parts
    return first, swap(first_send, "dp", ALONG_X), second, swap(second_send, "dp", ALONG_Y)


def add_last(me, parts, after=(), cost=0):
    rows = parts[0].shape[1]
    return call(
        add_last_body,
        [near_shape((2, rows, LANES)), shape_of((2, rows, LANES))],
        [me, *parts],
        [pltpu.VMEM((4, rows, LANES), jnp.bfloat16)],
        after=after,
        cost=cost,
        name="add_last",
    )


def scatter_z(parts):
    return parts[0], swap(parts[1], "mp", 1)


def add_z(me, parts, after=()):
    rows = parts[0].shape[1]
    return call(
        add_z_body,
        [near_shape((rows, LANES), jnp.float32), shape_of((rows, LANES))],
        [me, *parts],
        after=after,
        name="add_z",
    )


def scatter_z_far(parts):
    return parts[0], swap(parts[1], "mp", 2)


def total(refs, rows):
    value = refs[0][rows, :].astype(jnp.float32)
    for ref in refs[1:]:
        value = value + ref[rows, :].astype(jnp.float32)
    return value


def finish_columns(me, refs, base, tiles, out):
    odd = lax.rem(me[1], 2) == 1
    full = [total(refs, pl.ds(base + t * 96, 96)) for t in range(tiles)]
    single = total(refs, pl.ds(base + tiles * 96, 48))
    single = jnp.concatenate([single[:, :64], single[:, 64:]], axis=0)

    @pl.when(odd)
    def _():
        out[...] = jnp.concatenate([single, *full], axis=1)

    @pl.when(jnp.logical_not(odd))
    def _():
        out[...] = jnp.concatenate([*full, single], axis=1)


def finish_q_body(me, *refs):
    parts, out, outs = refs[:2], refs[2], refs[3:]
    finish_columns(me, parts, 0, 4, out)
    tail = total(parts, pl.ds(VECTOR_ROW, 16))
    for v in range(8):
        outs[v][...] = tail[v : v + 1, :24]
    outs[8][...] = tail[8:9, :96]


def finish_q(me, parts, after=()):
    f = jnp.float32
    return call(
        finish_q_body,
        [shape_of((96, 576), f)] + [shape_of((1, 24), f)] * 8 + [shape_of((1, 96), f)],
        [me, *parts],
        after=after,
        name="finish_q",
    )


def finish_ou_body(me, *refs):
    parts, w_out, w_up = refs[:2], refs[2], refs[3]
    finish_columns(me, parts, 0, 1, w_out)
    for t in range(UP_TILES):
        w_up[:, t * LANES : (t + 1) * LANES] = total(parts, pl.ds(UP_ROW + t * 96, 96))


def finish_ou(me, parts, after=()):
    f = jnp.float32
    return call(
        finish_ou_body, [shape_of((96, 192), f), shape_of((96, 768), f)], [me, *parts],
        after=after, name="finish_ou",
    )


def finish_d_body(me, *refs):
    parts, out = refs[:2], refs[2]
    for t in range(DOWN_TILES):
        out[:, t * LANES : (t + 1) * LANES] = total(parts, pl.ds(t * 192, 192))


def finish_d(me, parts, after=()):
    f = jnp.float32
    return call(finish_d_body, [shape_of((192, 384), f)], [me, *parts], after=after, name="finish_d")


PAIRS = HEADS // 2


def iota(shape, axis):
    return lax.broadcasted_iota(jnp.int32, shape, axis)


def place_matrix(order, head):
    length = order.shape[1]
    row = order[head : head + 1, :].astype(jnp.int16)
    token = iota((length, length), 0).astype(jnp.int16)
    return jnp.where(token == row, jnp.bfloat16(1.0), jnp.bfloat16(0.0))


def project_body(me, *refs):
    blocks, tokens = split_pairs(refs[:4]), refs[4]
    weights, vectors, bias_up, qkv, singles, tails = refs[5:]
    unpack_q_body(me, *blocks, weights, vectors, bias_up, singles, tails)
    for c in range(9):
        columns = slice(c * 256, (c + 1) * 256)
        value = dot(tokens[...], weights[:, columns])
        if c < 3:
            value = value + vectors[0:1, c * 256 : (c + 1) * 256]
        elif c >= 6:
            value = value + vectors[1:2, (c - 6) * 256 : (c - 5) * 256]
        qkv[:, columns] = value.astype(jnp.bfloat16)


def project(me, parts, tokens, after=()):
    return call(
        project_body,
        [
            near_shape((768, 2304)),
            near_shape((8, 768), jnp.float32),
            near_shape((1, 3072), jnp.float32),
            near_shape((tokens.shape[0], 2304)),
        ],
        [me, *parts, tokens],
        [pltpu.VMEM((4, 384, LANES), jnp.bfloat16), pltpu.VMEM((32, 16, LANES), jnp.float32)],
        after=after,
        name="project",
    )


def attend_body(first_pair, pairs, me, qkv, order, facts, *refs):
    swapped, values, soft, combined = refs[-4:]
    length = qkv.shape[0]
    groups = length // CLUSTER
    blocks = [slice(g * CLUSTER, (g + 1) * CLUSTER) for g in range(groups)]
    low = iota((length, LANES), 1) < 64
    itself = iota((CLUSTER, CLUSTER), 0) == iota((CLUSTER, CLUSTER), 1)
    pick = [
        jnp.where(iota((16, LANES), 1) == lane, 1.0, 0.0).astype(jnp.bfloat16) for lane in (64, 0)
    ]
    scale = HEAD_DIM ** (-0.5)

    for place in range(pairs):
        pair = first_pair + place

        def columns(base, pair=pair):
            return slice(base + pair * LANES, base + (pair + 1) * LANES)

        query = qkv[:, columns(0)].astype(jnp.float32)
        keys = qkv[:, columns(768)].astype(jnp.float32)
        value = qkv[:, columns(1536)].astype(jnp.float32)
        known = facts[...]
        tiles = (
            (jnp.where(low, query, pltpu.roll(keys, 64, axis=1)), jnp.where(low, value, known)),
            (jnp.where(low, pltpu.roll(query, 64, axis=1), keys), jnp.where(low, known, value)),
        )
        moved, to_tokens = [], []
        for h in range(2):
            back = place_matrix(order, 2 * pair + h)
            to_tokens.append(back)
            tile = jnp.concatenate([t.astype(jnp.bfloat16) for t in tiles[h]], axis=1)
            moved.append(dot_tn(back, tile))
        query_slots, key_slots, value_slots, codes, rows_of = [], [], [], [], []
        for h in range(2):
            both = moved[h][:, :LANES]
            query_slots.append(jnp.where(low, both, 0.0).astype(jnp.bfloat16))
            key_slots.append(pltpu.roll(both, 64, axis=1).astype(jnp.bfloat16))
            value_slots.append(moved[h][:, LANES:].astype(jnp.bfloat16))
            swapped[2 * place + h] = key_slots[h]
            values[2 * place + h] = value_slots[h]
            lane = 64 * (1 - h)
            code = moved[h][:, LANES + lane : LANES + lane + 1]
            row = dot_nt(pick[h], value_slots[h])[0:1]
            codes.append(jnp.where(code >= 32.0, code - 32.0, code))
            rows_of.append(row)
        scores = [
            [dot_nt(query_slots[h][b], key_slots[h][b]) for b in blocks] for h in range(2)
        ]
        found = []
        for h in range(2):
            outs = []
            for g, b in enumerate(blocks):
                allowed = (codes[h][b] == rows_of[h][:, b]) | itself
                value = jnp.where(allowed, scores[h][g] * scale, masked_score)
                value = jnp.exp(value - jnp.max(value, axis=1, keepdims=True))
                weights = value / jnp.sum(value, axis=1, keepdims=True)
                soft[2 * place + h, b, :] = weights
                outs.append(weights.astype(jnp.bfloat16))
            found.append(
                [dot(outs[g], value_slots[h][b]) for g, b in enumerate(blocks)]
            )
        result = None
        for h in range(2):
            value = jnp.concatenate(found[h], axis=0)
            value = jnp.where(low if h == 0 else jnp.logical_not(low), value, 0.0)
            value = dot(to_tokens[h], value.astype(jnp.bfloat16))
            result = value if result is None else result + value
        combined[:, columns(0)] = result.astype(jnp.bfloat16)


def attend(me, qkv, order, facts, first_pair, pairs, combined=None, after=()):
    length = qkv.shape[0]
    operands = [me, qkv, order, facts]
    if combined is not None:
        operands.append(combined)
    return call(
        functools.partial(attend_body, first_pair, pairs),
        [
            near_shape((2 * pairs, length, LANES)),
            near_shape((2 * pairs, length, LANES)),
            near_shape((2 * pairs, length, CLUSTER), jnp.float32),
            near_shape((length, 768)),
        ],
        operands,
        after=after,
        aliases={3: 3} if combined is not None else None,
        name="attend",
    )


def by_rows(first, count, step, body):
    for i in range(first, first + count, step):
        body(slice(i, i + step))


def mean(value):
    return jnp.mean(value, axis=1, keepdims=True)


def fold(value):
    return jnp.sum(value.reshape(value.shape[0] // 8, 8, value.shape[1]), axis=0)


def out_norm_body(me, combined, w_out, tokens, vectors, first_low, normal, inverse, total_ref):

    def rows_of(rows):
        value = total_ref[rows, :] + vectors[2:3] + tokens[rows, :].astype(jnp.float32)
        centred = value - mean(value)
        scale = lax.rsqrt(mean(centred * centred) + epsilon)
        norm = centred * scale
        normal[rows, :] = norm
        inverse[rows, :] = jnp.broadcast_to(scale, (scale.shape[0], LANES))
        first_low[rows, :] = (norm * vectors[3:4] + vectors[4:5]).astype(jnp.bfloat16)

    half = tokens.shape[0] // 2
    for first in (0, half):
        rows = slice(first, first + half)
        total_ref[rows, :] = dot(combined[rows, :], w_out[...])
        by_rows(first, half, 32, rows_of)


def out_norm(me, combined, w_out, tokens, vectors, after=()):
    n = tokens.shape[0]
    f = jnp.float32
    return call(
        out_norm_body,
        [near_shape((n, 768)), near_shape((n, 768), f), near_shape((n, LANES), f)],
        [me, combined, w_out, tokens, vectors],
        [pltpu.VMEM((n, 768), jnp.float32)],
        after=after,
        name="out_norm",
    )


def up_body(me, first_low, w_up, bias_up, activated, slope, send):
    width = w_up.shape[1] // 8
    for i in range(8):
        columns = slice(i * width, (i + 1) * width)
        hidden = dot(first_low[...], w_up[:, columns]) + bias_up[:, columns]
        half = 0.5 + 0.5 * lax.erf(hidden * (0.5**0.5))
        low = (hidden * half).astype(jnp.bfloat16)
        activated[:, columns] = low
        bell = jnp.exp(-0.5 * hidden * hidden) * (2.0 * math.pi) ** (-0.5)
        slope[:, columns] = (half + hidden * bell).astype(jnp.bfloat16)
    for i in range(8):
        k = me[0] ^ i

        @pl.when((k & 1) == 1)
        def _():
            there = pl.ds(pl.multiple_of((k >> 1) * width, LANES), width)
            send[:, there] = activated[:, i * width : (i + 1) * width]


def up(me, first_low, w_up, bias_up, after=()):
    n, width = first_low.shape[0], w_up.shape[1]
    return call(
        up_body,
        [near_shape((n, width)), near_shape((n, width)), shape_of((n, width // 2))],
        [me, first_low, w_up, bias_up],
        after=after,
        name="up",
    )


def down_norm_body(
    me, activated, turned, normal, vectors, out, feed_grad, second_grad, sums, feed, acc
):
    acc[...] = jnp.zeros_like(acc)

    def rows_of(rows):
        value = normal[rows, :] * vectors[3:4] + vectors[4:5] + feed[rows, :] + vectors[5:6]
        centred = value - mean(value)
        inverse = lax.rsqrt(mean(centred * centred) + epsilon)
        norm = centred * inverse
        out[rows, :] = (norm * vectors[6:7] + vectors[7:8]).astype(jnp.bfloat16)
        upstream = me.arrived(0)[rows, :]
        scaled = upstream * vectors[6:7]
        back = inverse * (scaled - mean(scaled) - norm * mean(scaled * norm))
        second_grad[rows, :] = back
        low = back.astype(jnp.bfloat16)
        feed_grad[rows, :] = low
        acc[0] += fold(low.astype(jnp.float32))
        acc[1] += fold(upstream * norm)
        acc[2] += fold(upstream)

    feed[...] = dot_nt(activated[...], turned[...])
    by_rows(0, out.shape[0], 32, rows_of)
    me.send(0)
    for i in range(3):
        sums[i : i + 1, :] = jnp.sum(acc[i], axis=0, keepdims=True)


def down_norm(me, activated, turned, normal, vectors, cotangent, after=()):
    n = cotangent.shape[0]
    return call(
        down_norm_body,
        [
            shape_of((n, 768)),
            near_shape((n, 768)),
            near_shape((n, 768), jnp.float32),
            near_shape((3, 768), jnp.float32),
        ],
        [me, cotangent, activated, turned, normal, vectors],
        [pltpu.VMEM((n, 768), jnp.float32), pltpu.VMEM((3, 8, 768), jnp.float32)],
        late=[None],
        far_outs={0: True},
        after=after,
        name="down_norm",
    )


def hidden_back_body(me, feed_grad, turned, slope, hidden_grad, sums):
    for i in range(hidden_grad.shape[1] // 256):
        columns = slice(i * 256, (i + 1) * 256)
        value = dot(feed_grad[...], turned[:, columns]) * slope[:, columns].astype(jnp.float32)
        low = value.astype(jnp.bfloat16)
        hidden_grad[:, columns] = low
        sums[:, columns] = jnp.sum(low.astype(jnp.float32), axis=0, keepdims=True)


def hidden_back(me, feed_grad, turned, slope, after=()):
    return call(
        hidden_back_body,
        [near_shape(slope.shape), near_shape((1, slope.shape[1]), jnp.float32)],
        [me, feed_grad, turned, slope],
        after=after,
        name="hidden_back",
    )


def first_back_body(
    me, hidden_grad, w_up, second_grad, normal, inverse, vectors, residual, low_out, left, right, sums, back,
    acc,
):
    acc[...] = jnp.zeros_like(acc)

    def rows_of(rows):
        upstream = back[rows, :] + second_grad[rows, :]
        norm = normal[rows, :]
        scaled = upstream * vectors[3:4]
        value = inverse[rows, 0:1] * (scaled - mean(scaled) - norm * mean(scaled * norm))
        residual[rows, :] = value
        low = value.astype(jnp.bfloat16)
        low_out[rows, :] = low
        left[rows, :] = low[:, :384]
        right[rows, :] = low[:, 384:]
        acc[0] += fold(low.astype(jnp.float32))
        acc[1] += fold(upstream * norm)
        acc[2] += fold(upstream)

    back[...] = dot_nt(hidden_grad[...], w_up[...])
    by_rows(0, normal.shape[0], 32, rows_of)
    for i in range(3):
        sums[i : i + 1, :] = jnp.sum(acc[i], axis=0, keepdims=True)


def first_back(me, hidden_grad, w_up, second_grad, normal, inverse, vectors, after=()):
    n = normal.shape[0]
    return call(
        first_back_body,
        [
            near_shape((n, 768), jnp.float32),
            near_shape((n, 768)),
            shape_of((n, 384)),
            shape_of((n, 384)),
            near_shape((3, 768), jnp.float32),
        ],
        [me, hidden_grad, w_up, second_grad, normal, inverse, vectors],
        [pltpu.VMEM((n, 768), jnp.float32), pltpu.VMEM((3, 8, 768), jnp.float32)],
        after=after,
        name="first_back",
    )


def attend_back_body(
    first_pair, pairs, me, attention_grad, w_out, order, swapped, values, soft, *refs
):
    grads, sums, upstream = refs[-3:]
    length = attention_grad.shape[0]
    groups = length // CLUSTER
    blocks = [slice(g * CLUSTER, (g + 1) * CLUSTER) for g in range(groups)]
    low = iota((length, LANES), 1) < 64
    low_rows = iota((CLUSTER, LANES), 1) < 64
    scale = HEAD_DIM ** (-0.5)
    mine = slice(first_pair * LANES, (first_pair + pairs) * LANES)
    upstream[...] = dot_nt(attention_grad[...], w_out[mine, :]).astype(jnp.bfloat16)

    for place in range(pairs):
        pair = first_pair + place

        def columns(base, pair=pair):
            return slice(base + pair * LANES, base + (pair + 1) * LANES)

        both = upstream[:, slice(place * LANES, (place + 1) * LANES)]
        to_tokens, moved = [], []
        for h in range(2):
            to_tokens.append(place_matrix(order, 2 * pair + h))
            value = dot_tn(to_tokens[h], both)
            value = jnp.where(low if h == 0 else jnp.logical_not(low), value, 0.0)
            moved.append(value.astype(jnp.bfloat16))
        back = []
        for h in range(2):
            kept = 2 * place + h
            keys = [swapped[kept, b, :] for b in blocks]
            weights = [soft[kept, b, :] for b in blocks]
            soft_grad = [dot_nt(moved[h][b], values[kept, b, :]) for b in blocks]
            value_grad = [
                dot_tn(weights[g].astype(jnp.bfloat16), moved[h][b]) for g, b in enumerate(blocks)
            ]
            score_grad = []
            for g in range(groups):
                middle = jnp.sum(soft_grad[g] * weights[g], axis=1, keepdims=True)
                score_grad.append((weights[g] * (soft_grad[g] - middle)).astype(jnp.bfloat16))
            query_grad = [dot(score_grad[g], keys[g]) for g in range(groups)]
            key_grad = [dot_tn(score_grad[g], keys[g]) for g in range(groups)]
            parts = [
                jnp.concatenate(
                    [
                        (jnp.where(low_rows, query_grad[g], key_grad[g]) * scale).astype(
                            jnp.bfloat16
                        ),
                        value_grad[g].astype(jnp.bfloat16),
                    ],
                    axis=1,
                )
                for g in range(groups)
            ]
            back.append(dot(to_tokens[h], jnp.concatenate(parts, axis=0)))
        first, second = back[0][:, :LANES], back[1][:, :LANES]
        query = jnp.where(low, first, pltpu.roll(second, 64, axis=1))
        keys = jnp.where(low, pltpu.roll(first, 64, axis=1), second)
        value = back[0][:, LANES:] + back[1][:, LANES:]
        grads[:, columns(0)] = query.astype(jnp.bfloat16)
        grads[:, columns(768)] = keys.astype(jnp.bfloat16)
        grads[:, columns(1536)] = value.astype(jnp.bfloat16)
        sums[0:1, columns(0)] = jnp.sum(query, axis=0, keepdims=True)
        sums[1:2, columns(0)] = jnp.sum(value, axis=0, keepdims=True)


def attend_back(
    me, attention_grad, w_out, order, kept, first_pair, pairs, before=(), after=()
):
    length = attention_grad.shape[0]
    return call(
        functools.partial(attend_back_body, first_pair, pairs),
        [near_shape((length, 2304)), near_shape((2, 768), jnp.float32)],
        [me, attention_grad, w_out, order, *kept, *before],
        [pltpu.VMEM((length, pairs * LANES), jnp.bfloat16)],
        after=after,
        aliases={6: 0, 7: 1} if before else None,
        name="attend_back",
    )


def tokens_back_body(me, grads, weights, residual, out):
    for c in range(3):
        columns = slice(c * 256, (c + 1) * 256)
        out[:, columns] = dot_nt(grads[...], weights[columns, :]) + residual[:, columns]
        me.send(0, (slice(None), columns))


def tokens_back(me, grads, weights, residual, after=()):
    return call(
        tokens_back_body,
        [shape_of(residual.shape, jnp.float32)],
        [me, grads, weights, residual],
        far_outs={0: True},
        sends=3,
        after=after,
        name="tokens_back",
    )


def local_block(
    tokens,
    w_qkv,
    bias_query,
    bias_value,
    w_out,
    bias_out,
    gain_one,
    shift_one,
    w_up,
    bias_up,
    w_down,
    bias_down,
    gain_two,
    shift_two,
    cluster_order,
    segment_ids,
    padding,
    cotangent,
):
    length = tokens.shape[0]
    me = None
    vector_list = [
        bias_query, bias_value, bias_out, gain_one, shift_one, bias_down, gain_two, shift_two
    ]
    order = cluster_order[0]
    facts = (segment_ids[0] + 32 * (1 - padding[0])).astype(jnp.float32)
    facts = jnp.broadcast_to(facts[:, None], (length, 128))

    def other(x):
        return swap(x, "dp", CORE)

    blocks_q = pack_q(me, w_qkv, vector_list, bias_up)
    far_z_q = swap(blocks_q[0], "mp", 2)
    blocks_rest = pack_rest(me, w_out, w_up, w_down, after=[blocks_q])
    block_ou, upper, lower, block_d = blocks_rest
    far_z_ou = swap(block_ou, "mp", 2)
    upper_x, lower_y = swap(upper, "dp", ALONG_X), swap(lower, "dp", ALONG_Y)
    tokens_turned = turn(me, tokens, after=[blocks_rest])
    spread = spread_d(me, block_d, upper_x, lower_y, after=[tokens_turned])
    upper, lower = spread
    upper_y, lower_x = swap(upper, "dp", ALONG_Y), swap(lower, "dp", ALONG_X)
    near_z_q = beside_two(
        me, blocks_q[1], far_z_q, after=[spread], cost=20 * MICROSECOND // 10
    )
    z_q = near_z_q[0], swap(near_z_q[0], "mp", 1)
    near_z_ou = beside_two(me, block_ou, far_z_ou, after=[near_z_q])
    z_ou = near_z_ou[0], swap(near_z_ou[0], "mp", 1)
    near_d = whole_d(me, upper, upper_y, lower, lower_x, after=[near_z_ou])
    z_q = tie(z_q, [near_d])
    near_q = [z_q[0], swap(z_q[0], "dp", ALONG_X), z_q[1], swap(z_q[1], "dp", ALONG_Y)]
    far_q = gather_far(me, near_q, after=[near_d])
    far_d = swap(near_d[0], "mp", 2)
    z_ou = tie(z_ou, [far_q])
    near_ou = [z_ou[0], swap(z_ou[0], "dp", ALONG_X), z_ou[1], swap(z_ou[1], "dp", ALONG_Y)]
    pairs_q = beside(
        me,
        [(x, (i // 2, i % 2)) for i, x in enumerate(far_q)],
        [(2, *far_q[0].shape)] * 2,
        (),
        "beside_far",
    )
    parts_q = list(pairs_q)
    parts_q = [*parts_q, *[other(x) for x in parts_q]]
    far_ou = gather_far(me, near_ou, after=[pairs_q], cost=5 * MICROSECOND // 10)
    both_d = beside_two(
        me, near_d[0], far_d, after=[far_ou], cost=82 * MICROSECOND // 10
    )
    z_d = swap(both_d[0], "mp", 1)
    projected = project(me, parts_q, tokens, after=[both_d])
    full_qkv, vectors, full_bias_up, qkv = projected

    pairs = PAIRS // 3

    def forward(part, before, after):
        return attend(
            me, qkv, order, facts, part * pairs, pairs, before, after=after
        )

    seen_a = forward(0, None, [projected])
    seen_b = forward(1, seen_a[-1], [seen_a])
    early_d = [other(x) for x in tie([near_d[0], far_d], [both_d])]
    far_ou = tie(far_ou, [seen_b, *early_d])
    seen_c = forward(2, seen_b[-1], far_ou[:1])
    combined = seen_c[-1]
    combined_turned = turn(me, combined)
    full_out, full_up = unpack_ou(me, gather_core(far_ou), after=[combined_turned])
    normed = out_norm(me, combined, full_out, tokens, vectors)
    first_low, normal, inverse = normed
    first_turned = turn(me, first_low)
    upper = up(me, first_low, full_up, full_bias_up, after=[first_turned])
    activated, slope, send_activated = upper
    sends = tie([combined_turned[0], first_turned[0], tokens_turned[0]], [upper])
    others = [other(x) for x in sends]
    (z_d,) = tie([z_d], [upper])
    unpacked = unpack_d(me, [both_d[0], z_d, *early_d, other(z_d)], after=others)
    others.insert(2, other(tie([send_activated], [unpacked])[0]))
    turned_down = unpacked[0]
    downed = down_norm(me, activated, turned_down, normal, vectors, cotangent)
    layer_out, feed_grad, second_grad, sums_two = downed
    other_tokens = others[3]

    other_feed = other(feed_grad)
    hidden = hidden_back(me, feed_grad, turned_down, slope, after=[downed])
    hidden_grad, sums_up = hidden
    (hidden_grad,) = tie([hidden_grad], [hidden, other_feed, others[2]])
    other_hidden = other(hidden_grad)
    grad_d = gradient_d(
        me, feed_grad, other_feed, activated, others[2], after=[hidden]
    )
    core_d = scatter_near(grad_d)
    first = first_back(
        me, hidden_grad, full_up, second_grad, normal, inverse, vectors, after=[grad_d]
    )
    residual_grad, attention_grad, *halves, sums_one = first
    halves = [other(x) for x in halves]

    def back(part, kept, before, after):
        return attend_back(
            me, attention_grad, full_out, order, kept,
            part * pairs, pairs, before, after,
        )

    grads_a = back(0, seen_a[:3], (), [first])
    grads_b = back(1, seen_b[:3], grads_a, [])
    grads_c = back(2, seen_c[:3], grads_b, halves)
    half_d = add_plane(me, core_d, after=[grads_c])
    plane_d = scatter_far(half_d)
    projected_grad, sums_bias = grads_c
    grad_vectors = all_sums(me, sums_bias, sums_one, sums_two, sums_up)
    projected_grad, grad_vectors = tie([projected_grad, grad_vectors], [half_d])
    other_grads = other(projected_grad), other(grad_vectors)
    grad_ou = gradient_ou(
        me,
        (combined_turned[1], others[0]),
        (first_turned[1], others[1]),
        (hidden_grad, other_hidden),
        (attention_grad, *halves),
        after=[half_d],
    )
    core_ou = scatter_near(grad_ou)
    last_d = add_last(
        me, plane_d, after=[grad_ou, other_grads[1]], cost=22 * MICROSECOND
    )
    z_d = scatter_z(last_d)
    grad_q = gradient_q(
        me, tokens_turned[1], other_tokens, projected_grad, other_grads[0], grad_vectors,
        other_grads[1], after=[last_d],
    )
    near_q = grad_q[0], swap(grad_q[1], "mp", 1)
    moved = tokens_back(me, projected_grad, full_qkv, residual_grad, after=[grad_q])
    grad_tokens = moved[0]
    near_d = add_z(me, z_d, after=[moved])
    sum_d = scatter_z_far(near_d)
    half_ou = add_plane(me, core_ou, after=[near_d], cost=4 * MICROSECOND)
    plane_ou = scatter_far(half_ou)
    last_ou = add_last(me, plane_ou, after=[half_ou])
    z_ou = scatter_z(last_ou)
    first_q = add_first(me, *near_q, after=[last_ou])
    core_q = scatter_near(first_q)
    half_q = add_plane(me, core_q, after=[first_q])
    plane_q = scatter_far(half_q)
    near_ou = add_z(me, z_ou, after=[half_q])
    sum_ou = scatter_z_far(near_ou)
    done_d = finish_d(me, sum_d, after=[near_ou])
    sum_q = scatter_z_far(add_both(me, plane_q, after=[done_d]))
    done_ou = finish_ou(me, sum_ou)
    shard_out, shard_up = done_ou
    shard_qkv, *shard_vectors = finish_q(me, sum_q, after=[done_ou])
    shard_down = done_d[0].T
    grad_list = [v.reshape(-1) for v in shard_vectors]
    return (
        layer_out,
        grad_tokens,
        shard_qkv,
        grad_list[0],
        grad_list[1],
        shard_out,
        grad_list[2],
        grad_list[3],
        grad_list[4],
        shard_up,
        grad_list[8],
        shard_down,
        grad_list[5],
        grad_list[6],
        grad_list[7],
    )


def solution(mesh):
    in_specs = (
        P(("dp", "mp"), None),
        P("dp", "mp"),
        P(("dp", "mp")),
        P(("dp", "mp")),
        P("dp", "mp"),
        P(("dp", "mp")),
        P(("dp", "mp")),
        P(("dp", "mp")),
        P("dp", "mp"),
        P(("dp", "mp")),
        P("dp", "mp"),
        P(("dp", "mp")),
        P(("dp", "mp")),
        P(("dp", "mp")),
        P(("dp", "mp"), None, None),
        P(("dp", "mp"), None),
        P(("dp", "mp"), None),
        P(("dp", "mp"), None),
    )
    out_specs = (
        P(("dp", "mp"), None),
        P(("dp", "mp"), None),
        P("dp", "mp"),
        P(("dp", "mp")),
        P(("dp", "mp")),
        P("dp", "mp"),
        P(("dp", "mp")),
        P(("dp", "mp")),
        P(("dp", "mp")),
        P("dp", "mp"),
        P(("dp", "mp")),
        P("dp", "mp"),
        P(("dp", "mp")),
        P(("dp", "mp")),
        P(("dp", "mp")),
    )
    blocks = mesh.shape["dp"] == 8 and mesh.shape["mp"] == 4
    local = local_block if blocks else local_general
    return jax.shard_map(local, mesh=mesh, in_specs=in_specs, out_specs=out_specs, check_vma=False)
```
